128 devices in a mesh: shard: 8 (over x, core), ctx: 4 (over z), tp: 4 (over y).
Axes of the slice: x: 4, y: 4, z: 4, core: 2. Of those that a mesh axis runs over, the one named last changes fastest.
Arguments:
- layer_input: bfloat16 [32768, 1536], P(('shard', 'ctx', 'tp')), may hold values from -4 to 4
- out_cotangent: bfloat16 [32768, 1536], P(('shard', 'ctx', 'tp')), may hold values from -4 to 4
- seq_lengths: int32 [8, 4], P('shard'), may hold values from 1 to 3584, as said below
- norm_gain: bfloat16 [1536], P(('shard', 'ctx')), may hold values from 0.5 to 1.5
- proj_gate: bfloat16 [1536, 3072], P(('shard', 'ctx'), 'tp'), may hold values from -0.15625 to 0.15625
- proj_input: bfloat16 [1536, 3072], P(('shard', 'ctx'), 'tp'), may hold values from -0.15625 to 0.15625
- proj_step: bfloat16 [1536, 48], P(('shard', 'ctx'), 'tp'), may hold values from -0.15625 to 0.15625
- proj_state: bfloat16 [1536, 256], P(('shard', 'ctx')), may hold values from -0.15625 to 0.15625
- conv_inner: bfloat16 [4, 48, 64], P(None, 'tp', ('shard', 'ctx')), may hold values from -3 to 3
- conv_inner_bias: bfloat16 [48, 64], P('tp', ('shard', 'ctx')), may hold values from -1 to 1
- conv_state: bfloat16 [4, 256], P(None, ('shard', 'ctx')), may hold values from -3 to 3
- conv_state_bias: bfloat16 [256], P(('shard', 'ctx')), may hold values from -1 to 1
- decay_log: float32 [48], P('tp'), may hold values from -1 to 1
- step_bias: float32 [48], P('tp'), may hold values from -9 to -3
- skip_scale: float32 [48], P('tp'), may hold values from 0.5 to 1.5
- gate_gain: bfloat16 [48, 64], P('tp', ('shard', 'ctx')), may hold values from 0.5 to 1.5
- proj_out: bfloat16 [3072, 1536], P('tp', ('shard', 'ctx')), may hold values from -0.109375 to 0.109375
Outputs:
- layer_output: bfloat16 [32768, 1536], P(('shard', 'ctx', 'tp'))
- input_grad: float32 [32768, 1536], P(('shard', 'ctx', 'tp'))
- grad_norm_gain: float32 [1536], P(('shard', 'ctx', 'tp'))
- grad_proj_gate: float32 [1536, 3072], P(('shard', 'ctx'), 'tp')
- grad_proj_input: float32 [1536, 3072], P(('shard', 'ctx'), 'tp')
- grad_proj_step: float32 [1536, 48], P(('shard', 'ctx'), 'tp')
- grad_proj_state: float32 [1536, 256], P(('shard', 'ctx', 'tp'))
- grad_conv_inner: float32 [4, 48, 64], P(None, 'tp', ('shard', 'ctx'))
- grad_conv_inner_bias: float32 [48, 64], P('tp', ('shard', 'ctx'))
- grad_conv_state: float32 [4, 256], P(None, ('shard', 'ctx', 'tp'))
- grad_conv_state_bias: float32 [256], P(('shard', 'ctx', 'tp'))
- grad_decay_log: float32 [48], P('tp')
- grad_step_bias: float32 [48], P('tp')
- grad_skip_scale: float32 [48], P('tp')
- grad_gate_gain: float32 [48, 64], P('tp', ('shard', 'ctx'))
- grad_proj_out: float32 [3072, 1536], P('tp', ('shard', 'ctx'))
The draws below stay inside these ranges and needn't reach their ends.
Inputs may be any that keep to these rules, and one draw needn't show every extreme that they name: `seq_lengths`: each row's lengths sum to 4096, and the longest in every row is exactly 3584.
All inputs are finite; a program needn't handle non-finite values.
Results may differ from the reference program's by a relative error of at most 0.013.
Values may be sent and summed in bfloat16 or wider, within the bound.
A program may use at most 320 MiB of HBM per device.

```python
import jax
import jax.numpy as jnp
from jax import lax

D = 1536
H = 48
P_SIZE = 64
N = 128
K = 4
STRETCH = 256
E = 3072
TOK_DEV = 1024
NSEQ = 4
GROUPS = 8
TOKENS = 32768
N_CTX = 4


def draw_seq_lengths(key, part):
    key = jax.random.fold_in(key, 17)
    group_span = N_CTX * TOK_DEV
    short_total = TOK_DEV // 2
    longest = group_span - short_total
    spare_extra = short_total - (NSEQ - 1)
    cut_key, place_key = jax.random.split(key)
    cut_points = jnp.sort(jax.random.randint(cut_key, (GROUPS, NSEQ - 2), 0, spare_extra + 1), axis=1).astype(jnp.int32)
    bounds = jnp.concatenate([jnp.zeros((GROUPS, 1), jnp.int32), cut_points, jnp.full((GROUPS, 1), spare_extra, jnp.int32)], axis=1)
    others = bounds[:, 1:] - bounds[:, :-1] + 1
    where_long = jax.random.randint(place_key, (GROUPS, 1), 0, NSEQ).astype(jnp.int32)
    slot_index = jnp.arange(NSEQ, dtype=jnp.int32)[None, :]
    before_long = jnp.concatenate([others, jnp.zeros((GROUPS, 1), jnp.int32)], axis=1)
    after_long = jnp.concatenate([jnp.zeros((GROUPS, 1), jnp.int32), others], axis=1)
    return jnp.where(slot_index < where_long, before_long, jnp.where(slot_index == where_long, longest, after_long)).astype(jnp.int32)


def shard_levels(stream_key, shape, cuts, smallest, top_value):
    factor_of = 1.0
    for position, parts in cuts:
        heights = jax.random.uniform(jax.random.fold_in(jax.random.fold_in(stream_key, 6), position), (parts,), jnp.float32, smallest / len(cuts), top_value / len(cuts))
        factor_of = factor_of * jnp.repeat(jnp.exp(heights), shape[position] // parts).reshape((-1,) + (1,) * (len(shape) - 1 - position))
    return factor_of


def bell_draw(rng, shape, scale, bound, cuts=(), kind=jnp.bfloat16):
    values = scale * jax.random.normal(rng, shape, jnp.float32)
    if cuts:
        values = values * shard_levels(rng, shape, cuts, -0.22, 0.18)
    return jnp.clip(values, -bound, bound).astype(kind)


def setup_inputs(seed: int = 0) -> dict:
    key_list = jax.random.split(jax.random.key(seed), 18)
    return {
        "layer_input": bell_draw(key_list[0], (TOKENS, D), 1.0, 4.0, ((0, 128),)),
        "out_cotangent": bell_draw(key_list[1], (TOKENS, D), 1.0, 4.0, ((0, 128),)),
        "seq_lengths": draw_seq_lengths(jax.random.fold_in(key_list[17], 71), 0),
        "norm_gain": jnp.clip(1.0 + 0.1 * jax.random.normal(key_list[3], (D,), jnp.float32), 0.5, 1.5).astype(jnp.bfloat16),
        "proj_gate": bell_draw(key_list[4], (D, E), D ** -0.5, 0.15625, ((0, 32), (1, 4))),
        "proj_input": bell_draw(key_list[5], (D, E), D ** -0.5, 0.15625, ((0, 32), (1, 4))),
        "proj_step": bell_draw(key_list[6], (D, H), D ** -0.5, 0.15625, ((0, 32), (1, 4))),
        "proj_state": bell_draw(key_list[7], (D, 2 * N), D ** -0.5, 0.15625, ((0, 32),)),
        "conv_inner": bell_draw(key_list[8], (K, H, P_SIZE), K ** -0.5, 3.0, ((1, 4), (2, 32))),
        "conv_inner_bias": bell_draw(key_list[9], (H, P_SIZE), 0.3, 1.0, ((0, 4), (1, 32))),
        "conv_state": bell_draw(key_list[10], (K, 2 * N), K ** -0.5, 3.0, ((1, 32),)),
        "conv_state_bias": bell_draw(key_list[11], (2 * N,), 0.3, 1.0, ((0, 32),)),
        "decay_log": jnp.clip(jax.random.uniform(key_list[12], (H,), jnp.float32, -1.0, 1.0) * shard_levels(key_list[12], (H,), ((0, 4),), -0.4, 0.0), -1.0, 1.0),
        "step_bias": jnp.clip(-9.0 + 6.0 * jax.random.uniform(key_list[13], (H,), jnp.float32) ** shard_levels(key_list[13], (H,), ((0, 4),), -0.2, 0.2), -9.0, -3.0),
        "skip_scale": jnp.clip(0.5 + 1.0 * jax.random.uniform(key_list[14], (H,), jnp.float32) ** shard_levels(key_list[14], (H,), ((0, 4),), -0.2, 0.2), 0.5, 1.5),
        "gate_gain": jnp.clip(1.0 + 0.1 * jax.random.normal(key_list[15], (H, P_SIZE), jnp.float32), 0.5, 1.5).astype(jnp.bfloat16),
        "proj_out": bell_draw(key_list[16], (E, D), E ** -0.5, 0.109375, ((0, 4), (1, 32))),
    }


EPS = 1e-05
HIGH = lax.Precision.HIGHEST

@jax.custom_vjp
def low(v):
    return lax.optimization_barrier(v.astype(jnp.bfloat16)).astype(jnp.float32)

@jax.custom_vjp
def low_back(v):
    return v

def low_keep(v):
    return (low(v), None)

def low_pass(kept, grad):
    return (grad,)

def back_keep(v):
    return (v, None)

def back_low(kept, grad):
    return (low(grad),)
low.defvjp(low_keep, low_pass)
low_back.defvjp(back_keep, back_low)

def silu_of(values_in):
    return values_in * jax.nn.sigmoid(values_in)

def segment_ids(seq_row, group_span):
    ends_at = jnp.cumsum(seq_row).astype(jnp.int32)
    places = jnp.arange(group_span, dtype=jnp.int32)
    return lax.optimization_barrier(jnp.sum((places[:, None] >= ends_at[None, :]).astype(jnp.int32), axis=1)).astype(jnp.int32)

def block_step(carried_in, pieces, decay_rate):
    state_now, seg_prev = carried_in
    inner_x, basis_b, basis_c, step_size, seg_here = pieces
    cum_rates = jnp.cumsum(step_size * decay_rate[None, :], axis=0)
    block_len = seg_here.shape[0]
    row_index = jnp.arange(block_len)
    keep_mask = (seg_here[:, None] == seg_here[None, :]) & (row_index[:, None] >= row_index[None, :])
    pair_mask = keep_mask[:, :, None]
    log_gaps = jnp.where(pair_mask, cum_rates[:, None, :] - cum_rates[None, :, :], 0.0)
    pair_weights = jnp.where(pair_mask, jnp.exp(log_gaps), 0.0) * step_size[None, :, :]
    inner_dot = jnp.einsum('tn,sn->ts', basis_c, basis_b, precision=HIGH)
    scores = inner_dot[:, :, None] * pair_weights
    local_out = jnp.einsum('tsh,shp->thp', scores, inner_x, precision=HIGH)
    live_rows = (seg_here == seg_prev).astype(cum_rates.dtype)
    carry_fade = jnp.exp(cum_rates) * live_rows[:, None]
    carry_out = jnp.einsum('tn,hpn->thp', basis_c, state_now, precision=HIGH) * carry_fade[:, :, None]
    last_seg = seg_here[block_len - 1]
    last_rate = cum_rates[block_len - 1]
    end_weights = jnp.exp(last_rate[None, :] - cum_rates) * (seg_here == last_seg).astype(cum_rates.dtype)[:, None] * step_size
    fresh_state = jnp.einsum('shp,sn->hpn', inner_x * end_weights[:, :, None], basis_b, precision=HIGH)
    kept_state = state_now * (jnp.exp(last_rate) * live_rows[block_len - 1])[:, None, None]
    return ((fresh_state + kept_state, last_seg), local_out + carry_out)

def group_forward(group_in, seg_here, params):
    norm_gain, proj_gate, proj_input, proj_step, proj_state, conv_inner, conv_inner_bias, conv_state, conv_state_bias, decay_log, step_bias, skip_scale, gate_gain, proj_out = params
    row_count = group_in.shape[0]
    inner_cols = proj_input.shape[1]
    head_count = decay_log.shape[0]
    head_width = inner_cols // head_count
    state_dims = proj_state.shape[1] // 2
    tap_count = conv_state.shape[0]
    normed = low(group_in * lax.rsqrt(lax.optimization_barrier(jnp.mean(group_in * group_in, axis=1, keepdims=True)) + EPS) * norm_gain[None, :])
    gate_pre = low_back(jnp.dot(normed, proj_gate, precision=HIGH))
    inner_pre = low(low_back(jnp.dot(normed, proj_input, precision=HIGH)))
    state_pre = low(low_back(jnp.dot(normed, proj_state, precision=HIGH)))
    step_pre = low_back(jnp.dot(normed, proj_step, precision=HIGH))
    conv_in = jnp.concatenate([inner_pre, state_pre], axis=1)
    conv_weights = jnp.concatenate([conv_inner.reshape(tap_count, inner_cols), conv_state], axis=1)
    conv_shifts = jnp.concatenate([conv_inner_bias.reshape(inner_cols), conv_state_bias])
    padded = jnp.concatenate([jnp.zeros((tap_count - 1, conv_in.shape[1]), conv_in.dtype), conv_in], axis=0)
    seg_padded = jnp.concatenate([jnp.full((tap_count - 1,), -1, jnp.int32), seg_here])
    summed = jnp.zeros_like(conv_in) + conv_shifts[None, :]
    for tap_index in range(tap_count):
        same_seg = (seg_padded[tap_index:tap_index + row_count] == seg_here).astype(conv_in.dtype)
        summed = summed + padded[tap_index:tap_index + row_count] * conv_weights[tap_index][None, :] * same_seg[:, None]
    conv_post = silu_of(summed)
    inner_x = low(conv_post[:, :inner_cols]).reshape(row_count, head_count, head_width)
    basis_b = low(conv_post[:, inner_cols:inner_cols + state_dims])
    basis_c = low(conv_post[:, inner_cols + state_dims:])
    step_size = jax.nn.softplus(step_pre + step_bias[None, :])
    decay_rate = -jnp.exp(decay_log)
    blocks = row_count // STRETCH

    def step_fn(carried_in, pieces):
        return block_step(carried_in, pieces, decay_rate)
    start_carry = (jnp.zeros((head_count, head_width, state_dims), group_in.dtype), jnp.array(-1, jnp.int32))
    _, outputs = lax.scan(jax.checkpoint(step_fn), start_carry, (inner_x.reshape(blocks, STRETCH, head_count, head_width), basis_b.reshape(blocks, STRETCH, state_dims), basis_c.reshape(blocks, STRETCH, state_dims), step_size.reshape(blocks, STRETCH, head_count), seg_here.reshape(blocks, STRETCH)))
    mixed_out = outputs.reshape(row_count, head_count, head_width) + skip_scale[None, :, None] * inner_x
    mixed_flat = mixed_out.reshape(row_count, inner_cols)
    gated_rows = mixed_flat * silu_of(gate_pre)
    branch = low(gated_rows * lax.rsqrt(lax.optimization_barrier(jnp.mean(gated_rows * gated_rows, axis=1, keepdims=True)) + EPS) * gate_gain.reshape(inner_cols)[None, :])
    return group_in + jnp.dot(branch, proj_out, precision=HIGH)

def reference(layer_input, out_cotangent, seq_lengths, norm_gain, proj_gate, proj_input, proj_step, proj_state, conv_inner, conv_inner_bias, conv_state, conv_state_bias, decay_log, step_bias, skip_scale, gate_gain, proj_out):
    group_count = seq_lengths.shape[0]
    group_span = layer_input.shape[0] // group_count
    model_width = layer_input.shape[1]
    seg_table = jnp.stack([segment_ids(seq_lengths[group_index], group_span) for group_index in range(group_count)])
    params = tuple((weight_in.astype(jnp.float32) for weight_in in (norm_gain, proj_gate, proj_input, proj_step, proj_state, conv_inner, conv_inner_bias, conv_state, conv_state_bias, decay_log, step_bias, skip_scale, gate_gain, proj_out)))
    inputs_wide = layer_input.astype(jnp.float32).reshape(group_count, group_span, model_width)

    def forward(all_in, all_params):

        def per_group(carried_in, pieces):
            return (carried_in, group_forward(pieces[0], pieces[1], all_params))
        _, outputs = lax.scan(jax.checkpoint(per_group), None, (all_in, seg_table))
        return outputs
    outputs, pullback = jax.vjp(forward, inputs_wide, params)
    input_grad, param_grads = pullback(out_cotangent.astype(jnp.float32).reshape(group_count, group_span, model_width))
    return (outputs.reshape(-1, model_width).astype(jnp.bfloat16), input_grad.reshape(-1, model_width), param_grads[0], param_grads[1], param_grads[2], param_grads[3], param_grads[4], param_grads[5], param_grads[6], param_grads[7], param_grads[8], param_grads[9], param_grads[10], param_grads[11], param_grads[12], param_grads[13])
```

```python
import functools

import jax
import jax.numpy as jnp
from jax import lax
from jax.experimental import pallas as pl
from jax.experimental.pallas import tpu as pltpu
from jax.sharding import PartitionSpec as P

MESH = pl.DeviceIdType.MESH
ANY = pl.ANY
F32 = jnp.float32
BF16 = jnp.bfloat16
EPS = 1e-05
LOG2E = 1.4426950408889634
HIGH = lax.Precision.HIGHEST

D = 1536
ROWS = 1024
HD = 768
HEADS = 12
PAIRS = 6
NS = 128
CONV = 1024
LEN = 128
CHUNKS = 8
E_ALL = 3072
C_OUT, C_GATE, C_IN, C_BC, C_MISC, WIDE = 0, 768, 1536, 2304, 2560, 2688
HALF_A, HALF_A1, HALF_B1 = 1408, 768, 2048


def dot(a, b):
    return jnp.dot(a, b, preferred_element_type=F32)


def dot_nt(a, b):
    return lax.dot_general(a, b, (((1,), (1,)), ((), ())), preferred_element_type=F32)


def dot_tn(a, b):
    return lax.dot_general(a, b, (((0,), (0,)), ((), ())), preferred_element_type=F32)


def dot_full(a, b):
    return jnp.dot(a, b, precision=HIGH, preferred_element_type=F32)


def iota(shape, axis):
    return lax.broadcasted_iota(jnp.int32, shape, axis)


def place():
    s = lax.axis_index("shard")
    return s // 2, s % 2, lax.axis_index("ctx"), lax.axis_index("tp")


def device(x, c, z, y):
    return {"shard": x * 2 + c, "ctx": z, "tp": y}


def enter(others):
    barrier = pltpu.get_barrier_semaphore()
    for other in others:
        pl.semaphore_signal(barrier, inc=1, device_id=other, device_id_type=MESH)
    pl.semaphore_wait(barrier, len(others))


class Sends:
    def __init__(self, send_sem, recv_sem):
        self.send_sem, self.recv_sem, self.copies = send_sem, recv_sem, []

    def __call__(self, src, dst, to):
        k = len(self.copies)
        copy = pltpu.make_async_remote_copy(
            src_ref=src,
            dst_ref=dst,
            send_sem=self.send_sem.at[k],
            recv_sem=self.recv_sem.at[k],
            device_id=to,
            device_id_type=MESH,
        )
        copy.start()
        self.copies.append(copy)
        return copy

    def finish(self):
        for copy in self.copies:
            copy.wait_send()


def sems(n):
    return [pltpu.SemaphoreType.DMA((n,)), pltpu.SemaphoreType.DMA((n,)), pltpu.SemaphoreType.DMA((4,))]


def comm_params(collective_id, vmem=None):
    return pltpu.CompilerParams(
        collective_id=collective_id, has_side_effects=True, vmem_limit_bytes=vmem
    )


def shape(dims, kind):
    return jax.ShapeDtypeStruct(dims, kind)


def gather_kernel(w_ref, x_ref, W, X, E, ssem, rsem, lsem):
    x, c, z, y = place()
    xr, xl, xo = (x + 1) % 4, (x + 3) % 4, (x + 2) % 4
    zr, zl, zo = (z + 1) % 4, (z + 3) % 4, (z + 2) % 4
    yr, yl = (y + 1) % 4, (y + 3) % 4
    dxr, dxl = device(xr, c, z, y), device(xl, c, z, y)
    dzr, dzl = device(x, c, zr, y), device(x, c, zl, y)
    dyr, dyl = device(x, c, z, yr), device(x, c, z, yl)
    dco = device(x, 1 - c, z, y)
    enter([dxr, dxl, dzr, dzl, dyr, dyl, dco])
    go = Sends(ssem, rsem)
    A, A1, A2 = pl.ds(0, HALF_A), pl.ds(0, HALF_A1), pl.ds(HALF_A1, HALF_A - HALF_A1)
    B = pl.ds(HALF_A, WIDE - HALF_A)
    B1, B2 = pl.ds(HALF_A, HALF_B1 - HALF_A), pl.ds(HALF_B1, WIDE - HALF_B1)
    H1, H2 = pl.ds(0, 128), pl.ds(128, 128)

    a_r = go(w_ref.at[:, A], W.at[x, c, z, :, A], dzr)
    b_r = go(w_ref.at[:, B], W.at[x, c, z, :, B], dxr)
    a_l = go(w_ref.at[:, A], W.at[x, c, z, :, A], dzl)
    b_l = go(w_ref.at[:, B], W.at[x, c, z, :, B], dxl)
    x_r = go(x_ref, X.at[y], dyr)
    x_l = go(x_ref, X.at[y], dyl)
    own = pltpu.make_async_copy(w_ref, W.at[x, c, z], lsem.at[0])
    own.start()
    own_x = pltpu.make_async_copy(x_ref, X.at[y], lsem.at[1])
    own_x.start()

    def on_x(xx, cols):
        return W.at[xx, c, :, :, cols]

    def on_z(zz, cols):
        return W.at[:, c, zz, :, cols]

    def same(ref, to):
        return go(ref, ref, to)

    a_r.wait_recv()
    a_fr = same(W.at[x, c, zl, :, A1], dzr)
    b_r.wait_recv()
    b_fr = same(W.at[xl, c, z, :, B1], dxr)
    a_l.wait_recv()
    a_fl = same(W.at[x, c, zr, :, A2], dzl)
    b_l.wait_recv()
    b_fl = same(W.at[xr, c, z, :, B2], dxl)
    own.wait()
    a_fr.wait_recv()
    a_fl.wait_recv()
    a2_r = same(on_x(x, A), dxr)
    a2_l = same(on_x(x, A), dxl)
    b_fr.wait_recv()
    b_fl.wait_recv()
    b2_r = same(on_z(z, B), dzr)
    b2_l = same(on_z(z, B), dzl)
    last = [same(on_x(x, A), dco), same(on_z(z, B), dco)]
    x_r.wait_recv()
    x_fr = same(X.at[yl, H1], dyr)
    x_l.wait_recv()
    x_fl = same(X.at[yr, H2], dyl)
    a2_r.wait_recv()
    f1 = same(on_x(xl, A1), dxr)
    last.append(same(on_x(xl, A), dco))
    b2_r.wait_recv()
    f3 = same(on_z(zl, B1), dzr)
    last.append(same(on_z(zl, B), dco))
    a2_l.wait_recv()
    f2 = same(on_x(xr, A2), dxl)
    last.append(same(on_x(xr, A), dco))
    b2_l.wait_recv()
    f4 = same(on_z(zr, B2), dzl)
    last.append(same(on_z(zr, B), dco))
    own_x.wait()
    x_fr.wait_recv()
    x_fl.wait_recv()
    edge = go(X.at[3, pl.ds(240, 16)], E, dzr)
    f1.wait_recv()
    last.append(same(on_x(xo, A1), dco))
    f3.wait_recv()
    last.append(same(on_z(zo, B1), dco))
    f2.wait_recv()
    last.append(same(on_x(xo, A2), dco))
    f4.wait_recv()
    last.append(same(on_z(zo, B2), dco))
    edge.wait_recv()
    for copy in last:
        copy.wait_recv()
    go.finish()


def gather(pack, rows):
    return pl.pallas_call(
        gather_kernel,
        out_shape=(
            shape((4, 2, 4, 48, WIDE), BF16),
            shape((4, 256, D), BF16),
            shape((16, D), BF16),
        ),
        in_specs=[pl.BlockSpec(memory_space=ANY)] * 2,
        out_specs=[pl.BlockSpec(memory_space=ANY)] * 3,
        scratch_shapes=sems(40),
        compiler_params=comm_params(0),
        name="gather_weights",
    )(pack, rows)


def swap_kernel(axis, own_ref, out_ref, ssem, rsem, lsem):
    x, c, z, y = place()

    def along(k):
        if axis == "ctx":
            return device(x, c, (z + k) % 4, y)
        return device(x, c, z, (y + k) % 4)

    me = z if axis == "ctx" else y
    others = [along(k) for k in (1, 3, 2)]
    enter(others)
    go = Sends(ssem, rsem)
    for other in others:
        go(own_ref, out_ref.at[me], other)
    own = pltpu.make_async_copy(own_ref, out_ref.at[me], lsem.at[0])
    own.start()
    own.wait()
    for copy in go.copies:
        copy.wait_recv()
    go.finish()


def swap(a, axis, collective_id, name):
    return pl.pallas_call(
        functools.partial(swap_kernel, axis),
        out_shape=shape((4,) + a.shape, a.dtype),
        in_specs=[pl.BlockSpec(memory_space=ANY)],
        out_specs=pl.BlockSpec(memory_space=ANY),
        scratch_shapes=sems(4),
        compiler_params=comm_params(collective_id),
        name=name,
    )(a)


def edge_kernel(own_ref, out_ref, ssem, rsem, lsem):
    x, c, z, y = place()
    before, after = device(x, c, (z + 3) % 4, y), device(x, c, (z + 1) % 4, y)
    enter([before, after])
    go = Sends(ssem, rsem)
    copy = go(own_ref, out_ref, before)
    copy.wait_recv()
    go.finish()


def edge_back(a, collective_id):
    return pl.pallas_call(
        edge_kernel,
        out_shape=shape(a.shape, a.dtype),
        in_specs=[pl.BlockSpec(memory_space=ANY)],
        out_specs=pl.BlockSpec(memory_space=ANY),
        scratch_shapes=sems(2),
        compiler_params=comm_params(collective_id),
        name="edge_back",
    )(a)


def spread_heads(v, p):
    r = v.shape[0]
    low = jnp.broadcast_to(v[:, 2 * p : 2 * p + 1], (r, 128))
    high = jnp.broadcast_to(v[:, 2 * p + 1 : 2 * p + 2], (r, 128))
    return jnp.where(iota((r, 128), 1) < 64, low, high)


def cols(p):
    return slice(128 * p, 128 * p + 128)


def stacked(pair):
    lane = iota(pair.shape, 1)
    zero = jnp.zeros_like(pair)
    return jnp.concatenate([jnp.where(lane < 64, pair, zero), jnp.where(lane < 64, zero, pair)], axis=0)


def in_two(v):
    high = v.astype(BF16)
    return high, (v - high.astype(F32)).astype(BF16)


def twice(v):
    return jnp.concatenate([v, v], axis=1)


def link_rows(decay):
    high, low = in_two(jnp.broadcast_to(decay, (8, HD)))
    return jnp.concatenate([high, low], axis=0)


def link_of(summ_ref, j):
    both = summ_ref[j, NS : NS + 16, :].astype(F32)
    return both[0:1] + both[8:9]


def head_sum(pair, p):
    lane, head = iota((128, 128), 0), iota((128, 128), 1)
    pick = jnp.where(head == 2 * p + lane // 64, 1.0, 0.0).astype(BF16)
    return dot(pair.astype(BF16), pick)


def triangle(kind):
    t, s = iota((LEN, LEN), 0), iota((LEN, LEN), 1)
    keep = {"incl": s <= t, "suffix": s >= t, "strict": s < t}[kind]
    return jnp.where(keep, 1.0, 0.0).astype(F32)


def fold8(v):
    return jnp.sum(v.reshape(v.shape[0] // 8, 8, v.shape[1]), axis=0)


def front_kernel(
    x_ref, w_ref, e_ref, gain_ref, conv_ref, step_ref, pos_ref,
    normed_ref, gate_ref, ci_ref, edge_ref, ds_ref, xbc_ref, xdt_ref, dt_ref, cum_ref, sig_ref, fresh_ref, summ_ref,
    buf, state, decay,
):
    step = pl.program_id(0)
    tile = x_ref.shape[0]

    def norm(rows):
        wide = rows.astype(F32)
        r = lax.rsqrt(jnp.mean(wide * wide, axis=1, keepdims=True) + EPS)
        return (wide * r * gain_ref[...]).astype(BF16)

    @pl.when(step == 0)
    def _():
        edge = dot(norm(e_ref[...]), w_ref[:, C_IN:C_MISC]).astype(BF16)
        edge_ref[...] = edge
        buf[0:8, :] = edge.astype(F32)[8:16]
        state[...] = jnp.zeros_like(state)
        decay[...] = jnp.ones_like(decay)

    @pl.when(step > 0)
    def _():
        buf[0:8, :] = buf[tile : tile + 8, :]

    normed = norm(x_ref[...])
    normed_ref[...] = normed
    gate_ref[...] = dot(normed, w_ref[:, C_GATE:C_IN])
    conv_in = dot(normed, w_ref[:, C_IN:C_MISC]).astype(BF16)
    ci_ref[...] = conv_in
    buf[8 : 8 + tile, :] = conv_in.astype(F32)
    step_pre = dot(normed, w_ref[:, C_MISC:WIDE])

    pos = pos_ref[...]
    for j in range(CONV // 128):
        lanes = cols(j)
        acc = buf[8 : 8 + tile, lanes] * conv_ref[3:4, lanes] + conv_ref[4:5, lanes]
        for back in (1, 2, 3):
            term = buf[8 - back : 8 - back + tile, lanes] * conv_ref[3 - back : 4 - back, lanes]
            acc = acc + jnp.where(pos >= back, term, 0.0)
        sig = jax.nn.sigmoid(acc)
        ds_ref[:, lanes] = sig * (1.0 + acc * (1.0 - sig))
        xbc_ref[:, lanes] = (acc * sig).astype(BF16)

    lane = iota((tile, 128), 1)
    pre = step_pre + step_ref[0:1, :]
    small = jnp.exp(-jnp.abs(pre))
    log1p = jnp.where(small < 1e-3, small * (1.0 - 0.5 * small + (1.0 / 3.0) * small * small), jnp.log(1.0 + small))
    dt = jnp.where(lane < HEADS, jnp.maximum(pre, 0.0) + log1p, 0.0)
    dt_ref[...] = dt
    sig_ref[...] = jax.nn.sigmoid(pre)
    rate = dt * step_ref[1:2, :]
    for sub in range(tile // LEN):
        rows = slice(LEN * sub, LEN * sub + LEN)
        cum = dot_full(triangle("incl"), rate[rows])
        cum_ref[rows, :] = cum
        last = cum[LEN - 1 : LEN, :]
        pos_last = pos[LEN * sub + LEN - 1 : LEN * sub + LEN, :]
        row = iota((LEN, 128), 0).astype(F32)
        fade = jnp.where((LEN - 1) - row <= pos_last, jnp.exp2(last - cum), 0.0)
        whole = jnp.where(pos_last > LEN - 1, jnp.exp2(last), 0.0)
        basis_t = jnp.transpose(xbc_ref[rows, HD : HD + NS].astype(F32)).astype(BF16)
        for p in range(PAIRS):
            xdt = (xbc_ref[rows, cols(p)].astype(F32) * spread_heads(dt[rows], p)).astype(BF16)
            xdt_ref[rows, cols(p)] = xdt
            ended = (xdt.astype(F32) * spread_heads(fade, p)).astype(BF16)
            fresh = dot(basis_t, ended)
            fresh_ref[sub, :, cols(p)] = fresh
            factor = spread_heads(whole, p)
            state[:, cols(p)] = state[:, cols(p)] * factor + fresh
            decay[:, cols(p)] = decay[:, cols(p)] * factor

    @pl.when(step == pl.num_programs(0) - 1)
    def _():
        summ_ref[0:NS, :] = state[...].astype(BF16)
        summ_ref[NS : NS + 16, :] = link_rows(decay[...])


def whole_spec(*dims):
    return pl.BlockSpec(dims, lambda i: (0,) * len(dims), pipeline_mode=pl.Buffered(1))


def rows_spec(r, c, back=None):
    if back is None:
        return pl.BlockSpec((r, c), lambda i: (i, 0))
    return pl.BlockSpec((r, c), lambda i: (back - i, 0))


def front(X, W, E, gain, conv, step, pos):
    tile = 256
    sub = tile // LEN
    return pl.pallas_call(
        front_kernel,
        grid=(ROWS // tile,),
        in_specs=[
            rows_spec(tile, D), whole_spec(D, WIDE), whole_spec(16, D), whole_spec(1, D), whole_spec(8, CONV),
            whole_spec(8, 128), rows_spec(tile, 128),
        ],
        out_specs=[
            rows_spec(tile, D), rows_spec(tile, HD), rows_spec(tile, CONV), whole_spec(16, CONV), rows_spec(tile, CONV),
            rows_spec(tile, CONV), rows_spec(tile, HD), rows_spec(tile, 128), rows_spec(tile, 128), rows_spec(tile, 128),
            pl.BlockSpec((sub, NS, HD), lambda i: (i, 0, 0)), whole_spec(NS + 16, HD),
        ],
        out_shape=[
            shape((ROWS, D), BF16), shape((ROWS, HD), F32), shape((ROWS, CONV), BF16), shape((16, CONV), BF16),
            shape((ROWS, CONV), F32), shape((ROWS, CONV), BF16), shape((ROWS, HD), BF16), shape((ROWS, 128), F32),
            shape((ROWS, 128), F32), shape((ROWS, 128), F32), shape((CHUNKS, NS, HD), F32), shape((NS + 16, HD), BF16),
        ],
        scratch_shapes=[pltpu.VMEM((8 + tile, CONV), F32), pltpu.VMEM((NS, HD), F32), pltpu.VMEM((1, HD), F32)],
        compiler_params=pltpu.CompilerParams(vmem_limit_bytes=56 << 20),
        cost_estimate=pl.CostEstimate(flops=2 * ROWS * D * 1920, bytes_accessed=40 << 20, transcendentals=ROWS * CONV),
        name="front",
    )(X, W, E, gain, conv, step, pos)


def scan_kernel(
    xbc_ref, xdt_ref, cum_ref, fresh_ref, gate_ref, pos_ref, summ_ref, cot_ref, w_ref, skip_ref, gain_ref,
    mixed_ref, db_ref, sums_ref, enter_ref,
    state,
):
    step = pl.program_id(0)
    tile = xbc_ref.shape[0]

    @pl.when(step == 0)
    def _():
        z = lax.axis_index("ctx")
        start = jnp.zeros((NS, HD), F32)
        for j in range(3):
            link = link_of(summ_ref, j)
            start = jnp.where(j < z, start * link + summ_ref[j, 0:NS, :].astype(F32), start)
        state[...] = start

    db_ref[...] = dot(cot_ref[...], w_ref[...])
    t, s = iota((LEN, LEN), 0), iota((LEN, LEN), 1)
    gap = (t - s).astype(F32)
    for sub in range(tile // LEN):
        rows = slice(LEN * sub, LEN * sub + LEN)
        pos = pos_ref[rows, :]
        keep = (gap >= 0) & (gap <= pos)
        cum = cum_ref[rows, :]
        cum_t = jnp.transpose(cum)
        basis = xbc_ref[rows, HD : HD + NS]
        basis_c = xbc_ref[rows, HD + NS : CONV]
        inner = dot_nt(basis_c, basis)
        fade = jnp.where(pos > t.astype(F32), jnp.exp2(cum), 0.0)
        whole = jnp.where(pos[LEN - 1 : LEN] > LEN - 1, jnp.exp2(cum[LEN - 1 : LEN]), 0.0)
        square = jnp.zeros((LEN, 128), F32)
        cross = jnp.zeros((LEN, 128), F32)
        for p in range(PAIRS):
            lanes = cols(p)
            entered = state[:, lanes].astype(BF16)
            enter_ref[sub, :, lanes] = entered
            parts = []
            for h in (2 * p, 2 * p + 1):
                span = jnp.where(keep, cum[:, h : h + 1] - cum_t[h : h + 1, :], -1e30)
                parts.append((jnp.exp2(span) * inner).astype(BF16))
            local = dot(jnp.concatenate(parts, axis=1), stacked(xdt_ref[rows, lanes]))
            out = local + dot(basis_c, entered) * spread_heads(fade, p)
            mixed = out + skip_ref[:, lanes] * xbc_ref[rows, lanes].astype(F32)
            mixed_ref[rows, lanes] = mixed
            gate = gate_ref[rows, lanes]
            gated = mixed * gate * jax.nn.sigmoid(gate)
            square = square + gated * gated
            cross = cross + gated * gain_ref[:, lanes] * db_ref[rows, lanes]
            state[:, lanes] = state[:, lanes] * spread_heads(whole, p) + fresh_ref[sub, :, lanes]
        sq = jnp.sum(square, axis=1, keepdims=True)
        cr = jnp.sum(cross, axis=1, keepdims=True)
        both = jnp.where(s == 0, sq, jnp.where(s == 1, cr, 0.0))
        sums_ref[8 * sub : 8 * sub + 8, :] = jnp.transpose(both)[0:8]


def scan(xbc, xdt, cum, fresh, gate, pos, summs, cot, W, skip, gain):
    tile = 256
    sub = tile // LEN
    return pl.pallas_call(
        scan_kernel,
        grid=(ROWS // tile,),
        in_specs=[
            rows_spec(tile, CONV), rows_spec(tile, HD), rows_spec(tile, 128),
            pl.BlockSpec((sub, NS, HD), lambda i: (i, 0, 0)), rows_spec(tile, HD), rows_spec(tile, 128),
            whole_spec(4, NS + 16, HD), rows_spec(tile, D), whole_spec(D, HD), whole_spec(1, HD), whole_spec(1, HD),
        ],
        out_specs=[
            rows_spec(tile, HD), rows_spec(tile, HD), rows_spec(8 * sub, 128),
            pl.BlockSpec((sub, NS, HD), lambda i: (i, 0, 0)),
        ],
        out_shape=[
            shape((ROWS, HD), F32), shape((ROWS, HD), F32), shape((8 * CHUNKS, 128), F32), shape((CHUNKS, NS, HD), BF16),
        ],
        scratch_shapes=[pltpu.VMEM((NS, HD), F32)],
        compiler_params=pltpu.CompilerParams(vmem_limit_bytes=56 << 20),
        cost_estimate=pl.CostEstimate(flops=2 * ROWS * D * 900, bytes_accessed=30 << 20, transcendentals=ROWS * CONV),
        name="scan",
    )(xbc, xdt, cum, fresh, gate, pos, summs, cot, W, skip, gain)


def turn_kernel(
    sums_ref, mixed_ref, gate_ref, db_ref, xbc_ref, cum_ref, pos_ref, w_ref, gain_ref,
    branch_ref, dgate_ref, dmix_ref, out_ref, gfresh_ref, summ_ref, acc_ref,
    state, decay,
):
    step = pl.program_id(0)
    tile = mixed_ref.shape[0]

    @pl.when(step == 0)
    def _():
        state[...] = jnp.zeros_like(state)
        decay[...] = jnp.ones_like(decay)
        acc_ref[...] = jnp.zeros_like(acc_ref)

    for sub in reversed(range(tile // LEN)):
        rows = slice(LEN * sub, LEN * sub + LEN)
        total = sums_ref[0, 8 * sub : 8 * sub + 8, :]
        for k in range(1, 4):
            total = total + sums_ref[k, 8 * sub : 8 * sub + 8, :]
        both = jnp.transpose(jnp.concatenate([total, jnp.zeros((120, 128), F32)], axis=0))
        r = lax.rsqrt(both[:, 0:1] * (1.0 / E_ALL) + EPS)
        slope = r * r * r * both[:, 1:2] * (1.0 / E_ALL)
        pos = pos_ref[rows, :]
        cum = cum_ref[rows, :]
        fade = jnp.where(pos > iota((LEN, 128), 0).astype(F32), jnp.exp2(cum), 0.0)
        whole = jnp.where(pos[LEN - 1 : LEN] > LEN - 1, jnp.exp2(cum[LEN - 1 : LEN]), 0.0)
        basis_t = jnp.transpose(xbc_ref[rows, HD + NS : CONV].astype(F32)).astype(BF16)
        for p in range(PAIRS):
            lanes = cols(p)
            mixed, gate, db = mixed_ref[rows, lanes], gate_ref[rows, lanes], db_ref[rows, lanes]
            gain = gain_ref[:, lanes]
            sig = jax.nn.sigmoid(gate)
            silu = gate * sig
            gated = mixed * silu
            scaled = gated * r
            branch_ref[rows, lanes] = (scaled * gain).astype(BF16)
            acc_ref[0:8, lanes] += fold8(db * scaled)
            dgated = r * gain * db - gated * slope
            dmix = dgated * silu
            dgate_ref[rows, lanes] = (dgated * mixed * sig * (1.0 + gate * (1.0 - sig))).astype(BF16)
            dmix_ref[rows, lanes] = dmix
            acc_ref[8:16, lanes] += fold8(dmix * xbc_ref[rows, lanes].astype(F32))
            fresh = dot(basis_t, (dmix * spread_heads(fade, p)).astype(BF16))
            gfresh_ref[sub, :, lanes] = fresh
            factor = spread_heads(whole, p)
            state[:, lanes] = state[:, lanes] * factor + fresh
            decay[:, lanes] = decay[:, lanes] * factor
    out_ref[...] = dot_nt(branch_ref[...], w_ref[...]).astype(BF16)

    @pl.when(step == pl.num_programs(0) - 1)
    def _():
        summ_ref[0:NS, :] = state[...].astype(BF16)
        summ_ref[NS : NS + 16, :] = link_rows(decay[...])


def turn(sums, mixed, gate, db, xbc, cum, pos, W, gain):
    tile = 256
    sub = tile // LEN
    top = ROWS // tile - 1
    return pl.pallas_call(
        turn_kernel,
        grid=(ROWS // tile,),
        in_specs=[
            pl.BlockSpec((4, 8 * sub, 128), lambda i: (0, top - i, 0)), rows_spec(tile, HD, top), rows_spec(tile, HD, top),
            rows_spec(tile, HD, top), rows_spec(tile, CONV, top), rows_spec(tile, 128, top), rows_spec(tile, 128, top),
            whole_spec(D, HD), whole_spec(1, HD),
        ],
        out_specs=[
            rows_spec(tile, HD, top), rows_spec(tile, HD, top), rows_spec(tile, HD, top), rows_spec(tile, D, top),
            pl.BlockSpec((sub, NS, HD), lambda i: (top - i, 0, 0)), whole_spec(NS + 16, HD), whole_spec(16, HD),
        ],
        out_shape=[
            shape((ROWS, HD), BF16), shape((ROWS, HD), BF16), shape((ROWS, HD), F32), shape((ROWS, D), BF16),
            shape((CHUNKS, NS, HD), F32), shape((NS + 16, HD), BF16), shape((16, HD), F32),
        ],
        scratch_shapes=[pltpu.VMEM((NS, HD), F32), pltpu.VMEM((1, HD), F32)],
        compiler_params=pltpu.CompilerParams(vmem_limit_bytes=56 << 20),
        cost_estimate=pl.CostEstimate(flops=2 * ROWS * D * 900, bytes_accessed=30 << 20, transcendentals=ROWS * CONV),
        name="turn",
    )(sums, mixed, gate, db, xbc, cum, pos, W, gain)


def back_kernel(
    xbc_ref, xdt_ref, dt_ref, cum_ref, sig_ref, dmix_ref, enter_ref, gfresh_ref, ds_ref, ci_ref, pos_ref,
    summ_ref, edge_ref, conv_ref, step_ref, skip_ref,
    din_ref, cgrad_ref, hgrad_ref, dedge_ref,
    state, dacc, posn,
):
    step = pl.program_id(0)

    @pl.when(step == 0)
    def _():
        z = lax.axis_index("ctx")
        start = jnp.zeros((NS, HD), F32)
        for j in (3, 2, 1):
            link = link_of(summ_ref, j)
            start = jnp.where(j > z, start * link + summ_ref[j, 0:NS, :].astype(F32), start)
        state[...] = start
        dacc[LEN : LEN + 8, :] = jnp.zeros((8, CONV), F32)
        posn[LEN : LEN + 8, :] = jnp.zeros((8, 128), F32)
        cgrad_ref[...] = jnp.zeros_like(cgrad_ref)
        hgrad_ref[...] = jnp.zeros_like(hgrad_ref)

    @pl.when(step > 0)
    def _():
        dacc[LEN : LEN + 8, :] = dacc[0:8, :]
        posn[LEN : LEN + 8, :] = posn[0:8, :]

    pos = pos_ref[...]
    posn[0:LEN, :] = pos
    row, lane = iota((LEN, LEN), 0), iota((LEN, LEN), 1)
    gap = (lane - row).astype(F32)
    keep = (gap >= 0) & (gap <= jnp.transpose(pos))
    cum, dt = cum_ref[...], dt_ref[...]
    cum_t = jnp.transpose(cum)
    last = cum[LEN - 1 : LEN]
    pos_last = pos[LEN - 1 : LEN]
    fade = jnp.where(pos > row.astype(F32), jnp.exp2(cum), 0.0)
    ends = jnp.where((LEN - 1) - row.astype(F32) <= pos_last, jnp.exp2(last - cum), 0.0)
    whole = jnp.where(pos_last > LEN - 1, jnp.exp2(last), 0.0)
    basis = xbc_ref[:, HD : HD + NS]
    basis_c = xbc_ref[:, HD + NS : CONV]
    inner = dot_nt(basis, basis_c)
    inner2 = jnp.concatenate([inner, inner], axis=1)
    d_inner = jnp.zeros((LEN, LEN), F32)
    d_b = jnp.zeros((LEN, NS), F32)
    d_c = jnp.zeros((LEN, NS), F32)
    into = jnp.zeros((LEN, 128), F32)
    direct = jnp.zeros((LEN, 128), F32)
    carry = jnp.zeros((LEN, 128), F32)
    later = jnp.zeros((LEN, 128), F32)
    across = jnp.zeros((8, 128), F32)
    sums_t = []
    for p in range(PAIRS):
        lanes = cols(p)
        xs = xbc_ref[:, lanes].astype(F32)
        xdt = xdt_ref[:, lanes]
        dy_wide = dmix_ref[:, lanes]
        dy, dy_low = in_two(dy_wide)
        entered = enter_ref[0, :, lanes]
        after = state[:, lanes]
        after_low = after.astype(BF16)
        dys = stacked(dy)
        spans = []
        for h in (2 * p, 2 * p + 1):
            spans.append(jnp.where(keep, cum_t[h : h + 1, :] - cum[:, h : h + 1], -1e30))
        decays = jnp.exp2(jnp.concatenate(spans, axis=1))
        scores = (decays * inner2).astype(BF16)
        d_scores = dot_nt(twice(xdt), jnp.concatenate([dys, stacked(dy_low)], axis=1)) * decays
        d_inner = d_inner + d_scores[:, :LEN] + d_scores[:, LEN:]
        prod = d_scores * inner2
        sums_t.append(jnp.sum(prod[:, :LEN], axis=0, keepdims=True))
        sums_t.append(jnp.sum(prod[:, LEN:], axis=0, keepdims=True))
        first = jnp.sum(prod[:, :LEN], axis=1, keepdims=True)
        second = jnp.sum(prod[:, LEN:], axis=1, keepdims=True)
        into = into + jnp.where(lane == 2 * p, first, jnp.where(lane == 2 * p + 1, second, 0.0))
        end_pair = spread_heads(ends, p)
        fade_pair = spread_heads(fade, p)
        z_state = dot(basis, after_low) * end_pair
        z = dot(scores, dys) + z_state
        direct = direct + head_sum(xs * z, p)
        later = later + head_sum(xdt.astype(F32) * z_state, p)
        carry = carry + head_sum(dy_wide * dot(basis_c, entered) * fade_pair, p)
        across = across + head_sum(fold8(after * entered.astype(F32)), p)
        d_x = spread_heads(dt, p) * z + skip_ref[:, lanes] * dy_wide
        dacc[0:LEN, lanes] = d_x * ds_ref[:, lanes]
        d_b = d_b + dot_nt(jnp.concatenate(in_two(xdt.astype(F32) * end_pair), axis=1), twice(after_low))
        d_c = d_c + dot_nt(jnp.concatenate(in_two(dy_wide * fade_pair), axis=1), twice(entered))
        state[:, lanes] = after * spread_heads(whole, p) + gfresh_ref[0, :, lanes]
    low = d_inner.astype(BF16)
    d_b = d_b + dot(low, basis_c)
    d_c = d_c + dot_tn(low, basis)
    dacc[0:LEN, HD : HD + NS] = d_b * ds_ref[:, HD : HD + NS]
    dacc[0:LEN, HD + NS : CONV] = d_c * ds_ref[:, HD + NS : CONV]
    out_of = jnp.transpose(jnp.concatenate(sums_t + [jnp.zeros((128 - HEADS, LEN), F32)], axis=0))
    d_rate = (
        dot_full(triangle("suffix"), out_of - into + carry)
        + dot_full(triangle("strict"), later)
        + whole * jnp.sum(across, axis=0, keepdims=True)
    )
    d_step = (direct + d_rate * step_ref[2:3, :]) * sig_ref[...]
    hgrad_ref[0:8, :] += fold8(d_rate * dt)
    hgrad_ref[8:16, :] += fold8(d_step)
    din_ref[:, CONV : CONV + 128] = d_step.astype(BF16)

    for j in range(CONV // 128):
        lanes = cols(j)
        here = dacc[0:LEN, lanes]
        ci = ci_ref[:, lanes].astype(F32)
        d_in = here * conv_ref[3:4, lanes]
        cgrad_ref[24:32, lanes] += fold8(here * ci)
        cgrad_ref[32:40, lanes] += fold8(here)
        for back in (1, 2, 3):
            moved = jnp.where(posn[back : back + LEN, :] >= back, dacc[back : back + LEN, lanes], 0.0)
            d_in = d_in + moved * conv_ref[3 - back : 4 - back, lanes]
            cgrad_ref[8 * (3 - back) : 8 * (3 - back) + 8, lanes] += fold8(moved * ci)
        din_ref[:, lanes] = d_in.astype(BF16)

    @pl.when(step == pl.num_programs(0) - 1)
    def _():
        dacc[8:16, :] = dacc[0:8, :]
        dacc[0:8, :] = jnp.zeros((8, CONV), F32)
        posn[8:16, :] = posn[0:8, :]
        posn[0:8, :] = jnp.zeros((8, 128), F32)
        for j in range(CONV // 128):
            lanes = cols(j)
            ci = edge_ref[:, lanes].astype(F32)[8:16]
            d_in = jnp.zeros((8, 128), F32)
            for back in (1, 2, 3):
                moved = jnp.where(posn[back : back + 8, :] >= back, dacc[back : back + 8, lanes], 0.0)
                d_in = d_in + moved * conv_ref[3 - back : 4 - back, lanes]
                cgrad_ref[8 * (3 - back) : 8 * (3 - back) + 8, lanes] += moved * ci
            dedge_ref[:, lanes] = d_in


def back(xbc, xdt, dt, cum, sig, dmix, entered, gfresh, ds, ci, pos, summs, edge, conv, step, skip):
    top = CHUNKS - 1

    def rows(c):
        return rows_spec(LEN, c, top)

    state = pl.BlockSpec((1, NS, HD), lambda i: (top - i, 0, 0))
    return pl.pallas_call(
        back_kernel,
        grid=(CHUNKS,),
        in_specs=[
            rows(CONV), rows(HD), rows(128), rows(128), rows(128), rows(HD), state, state, rows(CONV), rows(CONV), rows(128),
            whole_spec(4, NS + 16, HD), whole_spec(16, CONV), whole_spec(8, CONV), whole_spec(8, 128), whole_spec(1, HD),
        ],
        out_specs=[rows(CONV + 128), whole_spec(40, CONV), whole_spec(16, 128), whole_spec(8, CONV)],
        out_shape=[
            shape((ROWS, CONV + 128), BF16), shape((40, CONV), F32), shape((16, 128), F32), shape((8, CONV), F32),
        ],
        scratch_shapes=[
            pltpu.VMEM((NS, HD), F32), pltpu.VMEM((LEN + 8, CONV), F32), pltpu.VMEM((LEN + 8, 128), F32),
        ],
        compiler_params=pltpu.CompilerParams(vmem_limit_bytes=56 << 20),
        cost_estimate=pl.CostEstimate(flops=40 * ROWS * HD * 128, bytes_accessed=30 << 20, transcendentals=2 * ROWS * CONV),
        name="back",
    )(xbc, xdt, dt, cum, sig, dmix, entered, gfresh, ds, ci, pos, summs, edge, conv, step, skip)


def rows_kernel(dgate_ref, din_ref, edge_ref, w_ref, x_ref, out_ref, low_ref, ngain_ref):
    step = pl.program_id(0)
    tile = dgate_ref.shape[0]

    @pl.when(step == 0)
    def _():
        ngain_ref[...] = jnp.zeros_like(ngain_ref)

    low_ref[...] = din_ref[...]

    @pl.when((step == pl.num_programs(0) - 1) & (lax.axis_index("ctx") < 3))
    def _():
        tail = din_ref[tile - 16 : tile, 0:CONV].astype(F32)
        more = jnp.concatenate([jnp.zeros((8, CONV), F32), edge_ref[...]], axis=0)
        low_ref[tile - 16 : tile, 0:CONV] = (tail + more).astype(BF16)

    grad = dot_nt(dgate_ref[...], w_ref[:, C_GATE:C_IN]) + dot_nt(low_ref[...], w_ref[:, C_IN:WIDE])
    out_ref[...] = grad.astype(BF16)
    wide = x_ref[...].astype(F32)
    r = lax.rsqrt(jnp.mean(wide * wide, axis=1, keepdims=True) + EPS)
    ngain_ref[...] += fold8(grad * wide * r)


def rows_grad(dgate, din, edge, W, X):
    tile = 256
    return pl.pallas_call(
        rows_kernel,
        grid=(ROWS // tile,),
        in_specs=[
            rows_spec(tile, HD), rows_spec(tile, CONV + 128), whole_spec(8, CONV), whole_spec(D, WIDE), rows_spec(tile, D),
        ],
        out_specs=[rows_spec(tile, D), rows_spec(tile, CONV + 128), whole_spec(8, D)],
        out_shape=[shape((ROWS, D), BF16), shape((ROWS, CONV + 128), BF16), shape((8, D), F32)],
        compiler_params=pltpu.CompilerParams(vmem_limit_bytes=56 << 20),
        cost_estimate=pl.CostEstimate(flops=2 * ROWS * D * 1920, bytes_accessed=20 << 20, transcendentals=0),
        name="rows_grad",
    )(dgate, din, edge, W, X)


def weights_kernel(cot_ref, normed_ref, branch_ref, dgate_ref, din_ref, out_ref):
    normed_t = jnp.transpose(normed_ref[...])
    out_ref[:, C_OUT:C_GATE] = dot(jnp.transpose(cot_ref[...]), branch_ref[...]).astype(BF16)
    out_ref[:, C_GATE:C_IN] = dot(normed_t, dgate_ref[...]).astype(BF16)
    out_ref[:, C_IN:C_MISC] = dot(normed_t, din_ref[:, 0:CONV]).astype(BF16)
    out_ref[:, C_MISC:WIDE] = dot(normed_t, din_ref[:, CONV:]).astype(BF16)


def weights_grad(cot, normed, branch, dgate, din):
    tile = 256
    return pl.pallas_call(
        weights_kernel,
        grid=(D // tile,),
        in_specs=[
            pl.BlockSpec((ROWS, tile), lambda i: (0, i)), pl.BlockSpec((ROWS, tile), lambda i: (0, i)),
            whole_spec(ROWS, HD), whole_spec(ROWS, HD), whole_spec(ROWS, CONV + 128),
        ],
        out_specs=rows_spec(tile, WIDE),
        out_shape=shape((D, WIDE), BF16),
        compiler_params=pltpu.CompilerParams(vmem_limit_bytes=56 << 20),
        cost_estimate=pl.CostEstimate(flops=2 * ROWS * D * WIDE, bytes_accessed=20 << 20, transcendentals=0),
        name="weights_grad",
    )(cot, normed, branch, dgate, din)


def add(a, b):
    return a.astype(F32) + b.astype(F32)


def reduce_kernel(
    g_ref, n_ref, h_ref, gout_ref, nout_ref, yout_ref, hout_ref, hyout_ref,
    G, K, RA, SA, RB, SB, TA, TB, UA, UB, VA, VB, N, M, Q, Y, HZ, HX, HC, HY, ssem, rsem, lsem,
):
    x, c, z, y = place()
    xr, xl, xo = (x + 1) % 4, (x + 3) % 4, (x + 2) % 4
    zr, zl, zo = (z + 1) % 4, (z + 3) % 4, (z + 2) % 4
    yr, yl, yo = (y + 1) % 4, (y + 3) % 4, (y + 2) % 4
    dxr, dxl = device(xr, c, z, y), device(xl, c, z, y)
    dzr, dzl = device(x, c, zr, y), device(x, c, zl, y)
    dyr, dyl, dyo = device(x, c, z, yr), device(x, c, z, yl), device(x, c, z, yo)
    dco = device(x, 1 - c, z, y)
    dxo, dzo = device(xo, c, z, y), device(x, c, zo, y)
    load_g = pltpu.make_async_copy(g_ref, G, lsem.at[0])
    load_g.start()
    load_n = pltpu.make_async_copy(n_ref, N, lsem.at[1])
    load_n.start()
    enter([dxr, dxl, dxo, dzr, dzl, dzo, dyr, dyl, dyo, dco])
    go = Sends(ssem, rsem)
    nA, nB = HALF_A, WIDE - HALF_A
    A, B = pl.ds(0, nA), pl.ds(nA, nB)
    A1, A2 = pl.ds(0, HALF_A1), pl.ds(HALF_A1, nA - HALF_A1)
    B1, B2 = pl.ds(0, HALF_B1 - nA), pl.ds(HALF_B1 - nA, WIDE - HALF_B1)
    H1, H2 = pl.ds(0, 128), pl.ds(128, 128)

    n1 = go(n_ref.at[yo, H1], M.at[0], dyr)
    n2 = go(n_ref.at[yo, H2], M.at[1], dyl)
    HZ[z] = h_ref[...]
    hz = [go(HZ.at[z], HZ.at[z], d) for d in (dzr, dzl, dzo)]
    ka, kb = [], []
    for k in (xo, xr, xl, x):
        ka.append(go(g_ref.at[k, 1 - c, :, :, A], K.at[k, :, :, A], dco))
        j = {0: zo, 1: zr, 2: zl, 3: z}[len(kb)]
        kb.append(go(g_ref.at[:, 1 - c, j, :, B], K.at[:, j, :, B], dco))
    load_g.wait()

    def join_a(k):
        G[k, c, :, :, A] = add(G[k, c, :, :, A], K[k, :, :, A]).astype(BF16)

    def join_b(k):
        G[:, c, k, :, B] = add(G[:, c, k, :, B], K[:, k, :, B]).astype(BF16)

    ga = lambda k, part: G.at[k, c, :, :, part]
    gb = lambda k, part: G.at[:, c, k, :, part]
    GA1, GA2 = pl.ds(0, HALF_A1), pl.ds(HALF_A1, nA - HALF_A1)
    GB1, GB2 = pl.ds(nA, HALF_B1 - nA), pl.ds(HALF_B1, WIDE - HALF_B1)
    ka[0].wait_recv()
    join_a(xo)
    ra1 = go(ga(xo, GA1), RA.at[0, :, :, A1], dxr)
    ra2 = go(ga(xo, GA2), RA.at[0, :, :, A2], dxl)
    kb[0].wait_recv()
    join_b(zo)
    rb1 = go(gb(zo, GB1), RB.at[0, :, :, B1], dzr)
    rb2 = go(gb(zo, GB2), RB.at[0, :, :, B2], dzl)
    for copy in hz:
        copy.wait_recv()
    HX[x] = HZ[0] + HZ[1] + HZ[2] + HZ[3]
    hx = [go(HX.at[x], HX.at[x], d) for d in (dxr, dxl, dxo)]
    ka[1].wait_recv()
    join_a(xr)
    kb[1].wait_recv()
    join_b(zr)
    ka[2].wait_recv()
    join_a(xl)
    kb[2].wait_recv()
    join_b(zl)

    ra1.wait_recv()
    G[xr, c, :, :, GA1] = add(G[xr, c, :, :, GA1], RA[0, :, :, A1]).astype(BF16)
    sa_r = go(ga(xr, A), SA.at[0], dxr)
    rb1.wait_recv()
    G[:, c, zr, :, GB1] = add(G[:, c, zr, :, GB1], RB[0, :, :, B1]).astype(BF16)
    sb_r = go(gb(zr, B), SB.at[0], dzr)
    ra2.wait_recv()
    G[xl, c, :, :, GA2] = add(G[xl, c, :, :, GA2], RA[0, :, :, A2]).astype(BF16)
    sa_l = go(ga(xl, A), SA.at[1], dxl)
    rb2.wait_recv()
    G[:, c, zl, :, GB2] = add(G[:, c, zl, :, GB2], RB[0, :, :, B2]).astype(BF16)
    sb_l = go(gb(zl, B), SB.at[1], dzl)
    ka[3].wait_recv()
    kb[3].wait_recv()

    for copy in hx:
        copy.wait_recv()
    HC[c] = HX[0] + HX[1] + HX[2] + HX[3]
    hc = go(HC.at[c], HC.at[c], dco)
    load_n.wait()
    n1.wait_recv()
    N[yr, H1] = add(N[yr, H1], M[0]).astype(BF16)
    n3 = go(N.at[yr], Q.at[0], dyr)
    n2.wait_recv()
    N[yl, H2] = add(N[yl, H2], M[1]).astype(BF16)
    n4 = go(N.at[yl], Q.at[1], dyl)

    hc.wait_recv()
    HY[y] = HC[0] + HC[1]
    hout_ref[...] = HY[y]
    hy = [go(HY.at[y], HY.at[y], d) for d in (dyr, dyl, dyo)]

    sa_r.wait_recv()
    sa_l.wait_recv()
    own = add(G[x, c, :, :, A], K[x, :, :, A]) + add(SA[0], SA[1])
    TA[...] = own.astype(BF16)
    ta1 = go(TA.at[zo, :, A1], UA.at[:, A1], dzr)
    ta2 = go(TA.at[zo, :, A2], UA.at[:, A2], dzl)
    sb_r.wait_recv()
    sb_l.wait_recv()
    own = add(G[:, c, z, :, B], K[:, z, :, B]) + add(SB[0], SB[1])
    TB[...] = own.astype(BF16)
    tb1 = go(TB.at[xo, :, B1], UB.at[:, B1], dxr)
    tb2 = go(TB.at[xo, :, B2], UB.at[:, B2], dxl)
    ta1.wait_recv()
    TA[zr, :, A1] = add(TA[zr, :, A1], UA[:, A1]).astype(BF16)
    va_r = go(TA.at[zr], VA.at[0], dzr)
    ta2.wait_recv()
    TA[zl, :, A2] = add(TA[zl, :, A2], UA[:, A2]).astype(BF16)
    va_l = go(TA.at[zl], VA.at[1], dzl)
    tb1.wait_recv()
    TB[xr, :, B1] = add(TB[xr, :, B1], UB[:, B1]).astype(BF16)
    vb_r = go(TB.at[xr], VB.at[0], dxr)
    tb2.wait_recv()
    TB[xl, :, B2] = add(TB[xl, :, B2], UB[:, B2]).astype(BF16)
    vb_l = go(TB.at[xl], VB.at[1], dxl)
    vb_r.wait_recv()
    vb_l.wait_recv()
    gout_ref[:, B] = TB[x].astype(F32) + add(VB[0], VB[1])
    Y[y] = gout_ref[:, C_BC:C_MISC]
    ys = [go(Y.at[y], Y.at[y], d) for d in (dyr, dyl, dyo)]
    va_r.wait_recv()
    va_l.wait_recv()
    gout_ref[:, A] = TA[z].astype(F32) + add(VA[0], VA[1])
    for copy in hy:
        copy.wait_recv()
    hyout_ref[...] = HY[0] + HY[1] + HY[2] + HY[3]
    n3.wait_recv()
    n4.wait_recv()
    nout_ref[...] = N[y].astype(F32) + add(Q[0], Q[1])
    for copy in ys:
        copy.wait_recv()
    yout_ref[...] = Y[0] + Y[1] + Y[2] + Y[3]
    go.finish()


def reduce_all(g, n, h):
    nA, nB = HALF_A, WIDE - HALF_A
    return pl.pallas_call(
        reduce_kernel,
        out_shape=(shape((48, WIDE), F32), shape((256, D), F32), shape((48, C_MISC - C_BC), F32), shape((64, 128), F32), shape((64, 128), F32)),
        in_specs=[pl.BlockSpec(memory_space=ANY)] * 2 + [pl.BlockSpec(memory_space=pltpu.VMEM)],
        out_specs=[pl.BlockSpec(memory_space=pltpu.VMEM)] * 5,
        scratch_shapes=[
            pltpu.VMEM((4, 2, 4, 48, WIDE), BF16), pltpu.VMEM((4, 4, 48, WIDE), BF16),
            pltpu.VMEM((1, 4, 48, nA), BF16), pltpu.VMEM((2, 4, 48, nA), BF16),
            pltpu.VMEM((1, 4, 48, nB), BF16), pltpu.VMEM((2, 4, 48, nB), BF16),
            pltpu.VMEM((4, 48, nA), BF16), pltpu.VMEM((4, 48, nB), BF16),
            pltpu.VMEM((48, nA), BF16), pltpu.VMEM((48, nB), BF16),
            pltpu.VMEM((2, 48, nA), BF16), pltpu.VMEM((2, 48, nB), BF16),
            pltpu.VMEM((4, 256, D), BF16), pltpu.VMEM((2, 128, D), BF16), pltpu.VMEM((2, 256, D), BF16),
            pltpu.VMEM((4, 48, C_MISC - C_BC), F32),
            pltpu.VMEM((4, 64, 128), F32), pltpu.VMEM((4, 64, 128), F32), pltpu.VMEM((2, 64, 128), F32),
            pltpu.VMEM((4, 64, 128), F32),
        ] + sems(48),
        compiler_params=comm_params(5, 56 << 20),
        name="reduce_all",
    )(g, n, h)


def after(value, *others):
    return lax.optimization_barrier((value,) + others)[0]


def from_rows(blocks, r, first, count):
    return blocks[:, :r, first : first + count].transpose(1, 0, 2).reshape(r, 32 * count)


def per_device(
    layer_input, out_cotangent, seq_lengths, norm_gain, proj_gate, proj_input, proj_step, proj_state, conv_inner,
    conv_inner_bias, conv_state, conv_state_bias, decay_log, step_bias, skip_scale, gate_gain, proj_out,
):
    ctx = lax.axis_index("ctx")
    tp = lax.axis_index("tp")

    def column(a):
        return jnp.pad(a, ((0, 48 - a.shape[0]), (0, 0)))

    misc = jnp.concatenate(
        [
            proj_step, conv_inner.reshape(48, 2), column(conv_inner_bias), column(gate_gain), column(conv_state),
            column(conv_state_bias[None, :]), norm_gain[:, None], jnp.zeros((48, 93), BF16),
        ],
        axis=1,
    )
    pack = jnp.concatenate([proj_out.T, proj_gate, proj_input, proj_state, misc], axis=1)

    ends = jnp.cumsum(seq_lengths[0])
    token = ctx * ROWS + jnp.arange(ROWS, dtype=jnp.int32)
    begin = jnp.max(jnp.where(token[:, None] >= ends[None, :], ends[None, :], 0), axis=1)
    pos = jnp.broadcast_to((token - begin).astype(F32)[:, None], (ROWS, 128))

    rate = -jnp.exp(decay_log)
    step = jnp.pad(jnp.stack([step_bias, rate * LOG2E, rate]), ((0, 5), (0, 128 - HEADS)))
    skip = jnp.repeat(skip_scale, 64)[None, :]

    W, X, E = gather(pack, layer_input)
    W, X = W.reshape(D, WIDE), X.reshape(ROWS, D)
    cot_own = after(out_cotangent, E)
    cots = [cot_own] + [
        lax.ppermute(cot_own, "tp", [(j, (j + k) % 4) for j in range(4)]) for k in (1, 3, 2)
    ]

    blocks = W[:, C_MISC:].reshape(32, 48, 128).astype(F32)
    conv = jnp.concatenate(
        [
            jnp.concatenate([from_rows(blocks, 48, 12, 2).reshape(4, HD), from_rows(blocks, 4, 18, 8)], axis=1),
            jnp.concatenate([from_rows(blocks, 12, 14, 2).reshape(1, HD), from_rows(blocks, 1, 26, 8)], axis=1),
            jnp.zeros((3, CONV), F32),
        ]
    )
    gain = from_rows(blocks, 12, 16, 2).reshape(1, HD)
    ngain = blocks[:, :, 34].reshape(1, D)

    normed, gate, ci, edge, ds, xbc, xdt, dt, cum, sig, fresh, summ = front(X, W, E, ngain, conv, step, pos)
    summs = swap(summ, "ctx", 1, "swap_state")
    cot_all = jnp.zeros((4, 256, D), BF16)
    for k, part in zip((0, 1, 3, 2), cots):
        cot_all = lax.dynamic_update_slice(cot_all, part[None], ((tp - k) % 4, 0, 0))
    cot_all = cot_all.reshape(ROWS, D)
    mixed, db, sums, entered = scan(xbc, xdt, cum, fresh, gate, pos, summs, cot_all, W, skip, gain)
    sums = swap(sums, "tp", 2, "swap_sums")
    branch, dgate, dmix, out, gfresh, gsumm, tgrad = turn(sums, mixed, gate, db, xbc, cum, pos, W, gain)
    out = out.reshape(4, 256, D)
    out_parts = [lax.dynamic_index_in_dim(out, tp, 0, False)] + [
        lax.ppermute(
            lax.dynamic_index_in_dim(out, (tp + k) % 4, 0, False), "tp", [(j, (j + k) % 4) for j in range(4)]
        )
        for k in (1, 3, 2)
    ]
    gsumms = swap(gsumm, "ctx", 3, "swap_grad")
    din, cgrad, hgrad, dedge = back(
        xbc, xdt, dt, cum, sig, dmix, entered, gfresh, ds, ci, pos, gsumms, edge, conv, step, skip
    )
    dedge, *out_parts = lax.optimization_barrier((dedge, *out_parts))
    dedge = edge_back(dedge, 4)
    ngrad, din, nggrad = rows_grad(dgate, din, dedge, W, X)

    cg = jnp.sum(cgrad.reshape(5, 8, CONV), axis=1)
    tg = jnp.sum(tgrad.reshape(2, 8, HD), axis=1)
    hg = jnp.sum(hgrad.reshape(2, 8, 128), axis=1)
    heads = jnp.stack([hg[0, :HEADS] * rate, hg[1, :HEADS], tg[1].reshape(HEADS, 64).sum(axis=1)])
    heads = jnp.pad(heads, ((0, 3), (0, 128 - HEADS)))
    small = jnp.concatenate(
        [cg.reshape(40, 128), tg[0].reshape(6, 128), jnp.sum(nggrad, axis=0).reshape(12, 128), heads], axis=0
    )
    wgrad = weights_grad(cot_all, normed, branch, dgate, din)
    gsum, share, ysum, plane, every = reduce_all(wgrad.reshape(4, 2, 4, 48, WIDE), ngrad.reshape(4, 256, D), small)

    own = layer_input.astype(F32)
    out_share = sum(part.astype(F32) for part in out_parts)
    layer_output = (own + out_share).astype(BF16)
    scale = lax.rsqrt(jnp.mean(own * own, axis=1, keepdims=True) + EPS)
    weighted = share * ngain
    input_grad = (
        scale * weighted
        - own * (scale * scale * scale) * jnp.mean(own * weighted, axis=1, keepdims=True)
        + out_cotangent.astype(F32)
    )
    block = lax.axis_index("shard") * 4 + ctx
    conv_sum = plane[:40].reshape(5, CONV)[:, :HD].reshape(5, HEADS, 64)
    conv_sum = lax.dynamic_slice_in_dim(conv_sum, block * 2, 2, 2)
    gain_sum = lax.dynamic_slice_in_dim(plane[40:46].reshape(HEADS, 64), block * 2, 2, 1)
    state_sum = lax.dynamic_slice_in_dim(every[:40].reshape(5, CONV)[:, HD:], block * 8 + tp * 2, 2, 1)
    return (
        layer_output,
        input_grad,
        lax.dynamic_slice_in_dim(every[46:58].reshape(D), block * 48 + tp * 12, 12, 0),
        gsum[:, C_GATE:C_IN],
        gsum[:, C_IN:C_BC],
        gsum[:, C_MISC : C_MISC + HEADS],
        lax.dynamic_slice_in_dim(ysum, tp * 12, 12, 0),
        conv_sum[:4],
        conv_sum[4],
        state_sum[:4],
        state_sum[4],
        plane[58, :HEADS],
        plane[59, :HEADS],
        plane[60, :HEADS],
        gain_sum,
        gsum[:, C_OUT:C_GATE].T,
    )


def solution(mesh):
    both = ("shard", "ctx")
    every = ("shard", "ctx", "tp")
    return jax.shard_map(
        per_device,
        mesh=mesh,
        in_specs=(
            P(every, None), P(every, None), P("shard", None), P(both), P(both, "tp"), P(both, "tp"), P(both, "tp"),
            P(both, None), P(None, "tp", both), P("tp", both), P(None, both), P(both), P("tp"), P("tp"), P("tp"),
            P("tp", both), P("tp", both),
        ),
        out_specs=(
            P(every, None), P(every, None), P(every), P(both, "tp"), P(both, "tp"), P(both, "tp"), P(every, None),
            P(None, "tp", both), P("tp", both), P(None, every), P(every), P("tp"), P("tp"), P("tp"), P("tp", both),
            P("tp", both),
        ),
        check_vma=False,
    )
```

```python
import functools

import jax
import jax.numpy as jnp
from jax import lax
from jax.experimental import pallas as pl
from jax.experimental.pallas import tpu as pltpu
from jax.sharding import PartitionSpec as P

MESH = pl.DeviceIdType.MESH
ANY = pl.ANY
F32 = jnp.float32
BF16 = jnp.bfloat16
EPS = 1e-05
LOG2E = 1.4426950408889634
HIGH = lax.Precision.HIGHEST

D = 1536
ROWS = 1024
HD = 768
HEADS = 12
PAIRS = 6
NS = 128
CONV = 1024
LEN = 128
CHUNKS = 8
E_ALL = 3072
C_OUT, C_GATE, C_IN, C_BC, C_MISC, WIDE = 0, 768, 1536, 2304, 2560, 2688
HALF_A, HALF_A1, HALF_B1 = 1408, 768, 2048


def dot(a, b):
    return jnp.dot(a, b, preferred_element_type=F32)


def dot_nt(a, b):
    return lax.dot_general(a, b, (((1,), (1,)), ((), ())), preferred_element_type=F32)


def dot_tn(a, b):
    return lax.dot_general(a, b, (((0,), (0,)), ((), ())), preferred_element_type=F32)


def dot_full(a, b):
    return jnp.dot(a, b, precision=HIGH, preferred_element_type=F32)


def iota(shape, axis):
    return lax.broadcasted_iota(jnp.int32, shape, axis)


def place():
    s = lax.axis_index("shard")
    return s // 2, s % 2, lax.axis_index("ctx"), lax.axis_index("tp")


def device(x, c, z, y):
    return {"shard": x * 2 + c, "ctx": z, "tp": y}


def enter(others):
    barrier = pltpu.get_barrier_semaphore()
    for other in others:
        pl.semaphore_signal(barrier, inc=1, device_id=other, device_id_type=MESH)
    pl.semaphore_wait(barrier, len(others))


class Sends:
    def __init__(self, send_sem, recv_sem):
        self.send_sem, self.recv_sem, self.copies = send_sem, recv_sem, []

    def __call__(self, src, dst, to):
        k = len(self.copies)
        copy = pltpu.make_async_remote_copy(
            src_ref=src,
            dst_ref=dst,
            send_sem=self.send_sem.at[k],
            recv_sem=self.recv_sem.at[k],
            device_id=to,
            device_id_type=MESH,
        )
        copy.start()
        self.copies.append(copy)
        return copy

    def finish(self):
        for copy in self.copies:
            copy.wait_send()


class Flow:
    def __init__(self, send_sem, recv_sem):
        self.send_sem, self.recv_sem, self.known = send_sem, recv_sem, {}

    def add(self, name, src, dst, to):
        self.known[name] = (len(self.known), src, dst, to)

    def copy(self, name):
        k, src, dst, to = self.known[name]
        return pltpu.make_async_remote_copy(
            src_ref=src(),
            dst_ref=dst(),
            send_sem=self.send_sem.at[k],
            recv_sem=self.recv_sem.at[k],
            device_id=to,
            device_id_type=MESH,
        )

    def start(self, *names):
        for name in names:
            self.copy(name).start()

    def wait(self, *names):
        for name in names:
            self.copy(name).wait_recv()

    def finish(self):
        for name in self.known:
            self.copy(name).wait_send()


def sems(n):
    return [pltpu.SemaphoreType.DMA((n,)), pltpu.SemaphoreType.DMA((n,)), pltpu.SemaphoreType.DMA((4,))]


def comm_params(collective_id, vmem=None):
    return pltpu.CompilerParams(
        collective_id=collective_id, has_side_effects=True, vmem_limit_bytes=vmem
    )


def shape(dims, kind):
    return jax.ShapeDtypeStruct(dims, kind)


def gather_kernel(w_ref, x_ref, W, X, E, ssem, rsem, lsem):
    x, c, z, y = place()
    xr, xl, xo = (x + 1) % 4, (x + 3) % 4, (x + 2) % 4
    zr, zl, zo = (z + 1) % 4, (z + 3) % 4, (z + 2) % 4
    yr, yl = (y + 1) % 4, (y + 3) % 4
    dxr, dxl = device(xr, c, z, y), device(xl, c, z, y)
    dzr, dzl = device(x, c, zr, y), device(x, c, zl, y)
    dyr, dyl = device(x, c, z, yr), device(x, c, z, yl)
    dco = device(x, 1 - c, z, y)
    enter([dxr, dxl, dzr, dzl, dyr, dyl, dco])
    go = Sends(ssem, rsem)
    A, A1, A2 = pl.ds(0, HALF_A), pl.ds(0, HALF_A1), pl.ds(HALF_A1, HALF_A - HALF_A1)
    B = pl.ds(HALF_A, WIDE - HALF_A)
    B1, B2 = pl.ds(HALF_A, HALF_B1 - HALF_A), pl.ds(HALF_B1, WIDE - HALF_B1)
    H1, H2 = pl.ds(0, 128), pl.ds(128, 128)

    a_r = go(w_ref.at[:, A], W.at[x, c, z, :, A], dzr)
    b_r = go(w_ref.at[:, B], W.at[x, c, z, :, B], dxr)
    a_l = go(w_ref.at[:, A], W.at[x, c, z, :, A], dzl)
    b_l = go(w_ref.at[:, B], W.at[x, c, z, :, B], dxl)
    x_r = go(x_ref, X.at[y], dyr)
    x_l = go(x_ref, X.at[y], dyl)
    own = pltpu.make_async_copy(w_ref, W.at[x, c, z], lsem.at[0])
    own.start()
    own_x = pltpu.make_async_copy(x_ref, X.at[y], lsem.at[1])
    own_x.start()

    def on_x(xx, cols):
        return W.at[xx, c, :, :, cols]

    def on_z(zz, cols):
        return W.at[:, c, zz, :, cols]

    def same(ref, to):
        return go(ref, ref, to)

    a_r.wait_recv()
    a_fr = same(W.at[x, c, zl, :, A1], dzr)
    b_r.wait_recv()
    b_fr = same(W.at[xl, c, z, :, B1], dxr)
    a_l.wait_recv()
    a_fl = same(W.at[x, c, zr, :, A2], dzl)
    b_l.wait_recv()
    b_fl = same(W.at[xr, c, z, :, B2], dxl)
    own.wait()
    a_fr.wait_recv()
    a_fl.wait_recv()
    a2_r = same(on_x(x, A), dxr)
    a2_l = same(on_x(x, A), dxl)
    b_fr.wait_recv()
    b_fl.wait_recv()
    b2_r = same(on_z(z, B), dzr)
    b2_l = same(on_z(z, B), dzl)
    last = [same(on_x(x, A), dco), same(on_z(z, B), dco)]
    x_r.wait_recv()
    x_fr = same(X.at[yl, H1], dyr)
    x_l.wait_recv()
    x_fl = same(X.at[yr, H2], dyl)
    a2_r.wait_recv()
    f1 = same(on_x(xl, A1), dxr)
    last.append(same(on_x(xl, A), dco))
    b2_r.wait_recv()
    f3 = same(on_z(zl, B1), dzr)
    last.append(same(on_z(zl, B), dco))
    a2_l.wait_recv()
    f2 = same(on_x(xr, A2), dxl)
    last.append(same(on_x(xr, A), dco))
    b2_l.wait_recv()
    f4 = same(on_z(zr, B2), dzl)
    last.append(same(on_z(zr, B), dco))
    own_x.wait()
    x_fr.wait_recv()
    x_fl.wait_recv()
    edge = go(X.at[3, pl.ds(240, 16)], E, dzr)
    f1.wait_recv()
    last.append(same(on_x(xo, A1), dco))
    f3.wait_recv()
    last.append(same(on_z(zo, B1), dco))
    f2.wait_recv()
    last.append(same(on_x(xo, A2), dco))
    f4.wait_recv()
    last.append(same(on_z(zo, B2), dco))
    edge.wait_recv()
    for copy in last:
        copy.wait_recv()
    go.finish()


def gather(pack, rows):
    return pl.pallas_call(
        gather_kernel,
        out_shape=(
            shape((4, 2, 4, 48, WIDE), BF16),
            shape((4, 256, D), BF16),
            shape((16, D), BF16),
        ),
        in_specs=[pl.BlockSpec(memory_space=ANY)] * 2,
        out_specs=[pl.BlockSpec(memory_space=ANY)] * 3,
        scratch_shapes=sems(40),
        compiler_params=comm_params(0),
        name="gather_weights",
    )(pack, rows)


def swap_kernel(axis, own_ref, out_ref, ssem, rsem, lsem):
    x, c, z, y = place()

    def along(k):
        if axis == "ctx":
            return device(x, c, (z + k) % 4, y)
        return device(x, c, z, (y + k) % 4)

    me = z if axis == "ctx" else y
    others = [along(k) for k in (1, 3, 2)]
    enter(others)
    go = Sends(ssem, rsem)
    for other in others:
        go(own_ref, out_ref.at[me], other)
    own = pltpu.make_async_copy(own_ref, out_ref.at[me], lsem.at[0])
    own.start()
    own.wait()
    for copy in go.copies:
        copy.wait_recv()
    go.finish()


def swap(a, axis, collective_id, name):
    return pl.pallas_call(
        functools.partial(swap_kernel, axis),
        out_shape=shape((4,) + a.shape, a.dtype),
        in_specs=[pl.BlockSpec(memory_space=ANY)],
        out_specs=pl.BlockSpec(memory_space=ANY),
        scratch_shapes=sems(4),
        compiler_params=comm_params(collective_id),
        name=name,
    )(a)


def spread_heads(v, p):
    r = v.shape[0]
    low = jnp.broadcast_to(v[:, 2 * p : 2 * p + 1], (r, 128))
    high = jnp.broadcast_to(v[:, 2 * p + 1 : 2 * p + 2], (r, 128))
    return jnp.where(iota((r, 128), 1) < 64, low, high)


def cols(p):
    return slice(128 * p, 128 * p + 128)


def stacked(pair):
    lane = iota(pair.shape, 1)
    zero = jnp.zeros_like(pair)
    return jnp.concatenate([jnp.where(lane < 64, pair, zero), jnp.where(lane < 64, zero, pair)], axis=0)


def in_two(v):
    high = v.astype(BF16)
    return high, (v - high.astype(F32)).astype(BF16)


def twice(v):
    return jnp.concatenate([v, v], axis=1)


def link_rows(decay):
    high, low = in_two(jnp.broadcast_to(decay, (8, HD)))
    return jnp.concatenate([high, low], axis=0)


def link_of(summ_ref, j):
    both = summ_ref[j, NS : NS + 16, :].astype(F32)
    return both[0:1] + both[8:9]


def head_sum(pair, p):
    lane, head = iota((128, 128), 0), iota((128, 128), 1)
    pick = jnp.where(head == 2 * p + lane // 64, 1.0, 0.0).astype(BF16)
    return dot(pair.astype(BF16), pick)


def triangle(kind):
    t, s = iota((LEN, LEN), 0), iota((LEN, LEN), 1)
    keep = {"incl": s <= t, "suffix": s >= t, "strict": s < t}[kind]
    return jnp.where(keep, 1.0, 0.0).astype(F32)


def fold8(v):
    return jnp.sum(v.reshape(v.shape[0] // 8, 8, v.shape[1]), axis=0)


def front_kernel(
    x_ref, w_ref, e_ref, gain_ref, conv_ref, step_ref, pos_ref,
    normed_ref, gate_ref, ci_ref, edge_ref, ds_ref, xbc_ref, xdt_ref, dt_ref, cum_ref, sig_ref, fresh_ref, summ_ref,
    buf, state, decay,
):
    step = pl.program_id(0)
    tile = x_ref.shape[0]

    def norm(rows):
        wide = rows.astype(F32)
        r = lax.rsqrt(jnp.mean(wide * wide, axis=1, keepdims=True) + EPS)
        return (wide * r * gain_ref[...]).astype(BF16)

    @pl.when(step == 0)
    def _():
        edge = dot(norm(e_ref[...]), w_ref[:, C_IN:C_MISC]).astype(BF16)
        edge_ref[...] = edge
        buf[0:8, :] = edge.astype(F32)[8:16]
        state[...] = jnp.zeros_like(state)
        decay[...] = jnp.ones_like(decay)

    @pl.when(step > 0)
    def _():
        buf[0:8, :] = buf[tile : tile + 8, :]

    normed = norm(x_ref[...])
    normed_ref[...] = normed
    gate_ref[...] = dot(normed, w_ref[:, C_GATE:C_IN])
    conv_in = dot(normed, w_ref[:, C_IN:C_MISC]).astype(BF16)
    ci_ref[...] = conv_in
    buf[8 : 8 + tile, :] = conv_in.astype(F32)
    step_pre = dot(normed, w_ref[:, C_MISC:WIDE])

    pos = pos_ref[...]
    for j in range(CONV // 128):
        lanes = cols(j)
        acc = buf[8 : 8 + tile, lanes] * conv_ref[3:4, lanes] + conv_ref[4:5, lanes]
        for back in (1, 2, 3):
            term = buf[8 - back : 8 - back + tile, lanes] * conv_ref[3 - back : 4 - back, lanes]
            acc = acc + jnp.where(pos >= back, term, 0.0)
        sig = jax.nn.sigmoid(acc)
        ds_ref[:, lanes] = sig * (1.0 + acc * (1.0 - sig))
        xbc_ref[:, lanes] = (acc * sig).astype(BF16)

    lane = iota((tile, 128), 1)
    pre = step_pre + step_ref[0:1, :]
    small = jnp.exp(-jnp.abs(pre))
    log1p = jnp.where(small < 1e-3, small * (1.0 - 0.5 * small + (1.0 / 3.0) * small * small), jnp.log(1.0 + small))
    dt = jnp.where(lane < HEADS, jnp.maximum(pre, 0.0) + log1p, 0.0)
    dt_ref[...] = dt
    sig_ref[...] = jax.nn.sigmoid(pre)
    rate = dt * step_ref[1:2, :]
    for sub in range(tile // LEN):
        rows = slice(LEN * sub, LEN * sub + LEN)
        cum = dot_full(triangle("incl"), rate[rows])
        cum_ref[rows, :] = cum
        last = cum[LEN - 1 : LEN, :]
        pos_last = pos[LEN * sub + LEN - 1 : LEN * sub + LEN, :]
        row = iota((LEN, 128), 0).astype(F32)
        fade = jnp.where((LEN - 1) - row <= pos_last, jnp.exp2(last - cum), 0.0)
        whole = jnp.where(pos_last > LEN - 1, jnp.exp2(last), 0.0)
        basis_t = jnp.transpose(xbc_ref[rows, HD : HD + NS].astype(F32)).astype(BF16)
        for p in range(PAIRS):
            xdt = (xbc_ref[rows, cols(p)].astype(F32) * spread_heads(dt[rows], p)).astype(BF16)
            xdt_ref[rows, cols(p)] = xdt
            ended = (xdt.astype(F32) * spread_heads(fade, p)).astype(BF16)
            fresh = dot(basis_t, ended)
            fresh_ref[sub, :, cols(p)] = fresh
            factor = spread_heads(whole, p)
            state[:, cols(p)] = state[:, cols(p)] * factor + fresh
            decay[:, cols(p)] = decay[:, cols(p)] * factor

    @pl.when(step == pl.num_programs(0) - 1)
    def _():
        summ_ref[0:NS, :] = state[...].astype(BF16)
        summ_ref[NS : NS + 16, :] = link_rows(decay[...])


def whole_spec(*dims):
    return pl.BlockSpec(dims, lambda i: (0,) * len(dims), pipeline_mode=pl.Buffered(1))


def rows_spec(r, c, back=None):
    if back is None:
        return pl.BlockSpec((r, c), lambda i: (i, 0))
    return pl.BlockSpec((r, c), lambda i: (back - i, 0))


def front(X, W, E, gain, conv, step, pos):
    tile = 256
    sub = tile // LEN
    return pl.pallas_call(
        front_kernel,
        grid=(ROWS // tile,),
        in_specs=[
            rows_spec(tile, D), whole_spec(D, WIDE), whole_spec(16, D), whole_spec(1, D), whole_spec(8, CONV),
            whole_spec(8, 128), rows_spec(tile, 128),
        ],
        out_specs=[
            rows_spec(tile, D), rows_spec(tile, HD), rows_spec(tile, CONV), whole_spec(16, CONV), rows_spec(tile, CONV),
            rows_spec(tile, CONV), rows_spec(tile, HD), rows_spec(tile, 128), rows_spec(tile, 128), rows_spec(tile, 128),
            pl.BlockSpec((sub, NS, HD), lambda i: (i, 0, 0)), whole_spec(NS + 16, HD),
        ],
        out_shape=[
            shape((ROWS, D), BF16), shape((ROWS, HD), F32), shape((ROWS, CONV), BF16), shape((16, CONV), BF16),
            shape((ROWS, CONV), F32), shape((ROWS, CONV), BF16), shape((ROWS, HD), BF16), shape((ROWS, 128), F32),
            shape((ROWS, 128), F32), shape((ROWS, 128), F32), shape((CHUNKS, NS, HD), F32), shape((NS + 16, HD), BF16),
        ],
        scratch_shapes=[pltpu.VMEM((8 + tile, CONV), F32), pltpu.VMEM((NS, HD), F32), pltpu.VMEM((1, HD), F32)],
        compiler_params=pltpu.CompilerParams(vmem_limit_bytes=56 << 20),
        cost_estimate=pl.CostEstimate(flops=2 * ROWS * D * 1920, bytes_accessed=40 << 20, transcendentals=ROWS * CONV),
        name="front",
    )(X, W, E, gain, conv, step, pos)


def scan_kernel(
    xbc_ref, xdt_ref, cum_ref, fresh_ref, gate_ref, pos_ref, summ_ref, cot_ref, w_ref, skip_ref, gain_ref,
    mixed_ref, db_ref, sums_ref, enter_ref,
    state,
):
    step = pl.program_id(0)
    tile = xbc_ref.shape[0]

    @pl.when(step == 0)
    def _():
        z = lax.axis_index("ctx")
        start = jnp.zeros((NS, HD), F32)
        for j in range(3):
            link = link_of(summ_ref, j)
            start = jnp.where(j < z, start * link + summ_ref[j, 0:NS, :].astype(F32), start)
        state[...] = start

    db_ref[...] = dot(cot_ref[...], w_ref[...])
    t, s = iota((LEN, LEN), 0), iota((LEN, LEN), 1)
    gap = (t - s).astype(F32)
    for sub in range(tile // LEN):
        rows = slice(LEN * sub, LEN * sub + LEN)
        pos = pos_ref[rows, :]
        keep = (gap >= 0) & (gap <= pos)
        cum = cum_ref[rows, :]
        cum_t = jnp.transpose(cum)
        basis = xbc_ref[rows, HD : HD + NS]
        basis_c = xbc_ref[rows, HD + NS : CONV]
        inner = dot_nt(basis_c, basis)
        fade = jnp.where(pos > t.astype(F32), jnp.exp2(cum), 0.0)
        whole = jnp.where(pos[LEN - 1 : LEN] > LEN - 1, jnp.exp2(cum[LEN - 1 : LEN]), 0.0)
        square = jnp.zeros((LEN, 128), F32)
        cross = jnp.zeros((LEN, 128), F32)
        for p in range(PAIRS):
            lanes = cols(p)
            entered = state[:, lanes].astype(BF16)
            enter_ref[sub, :, lanes] = entered
            parts = []
            for h in (2 * p, 2 * p + 1):
                span = jnp.where(keep, cum[:, h : h + 1] - cum_t[h : h + 1, :], -1e30)
                parts.append((jnp.exp2(span) * inner).astype(BF16))
            local = dot(jnp.concatenate(parts, axis=1), stacked(xdt_ref[rows, lanes]))
            out = local + dot(basis_c, entered) * spread_heads(fade, p)
            mixed = out + skip_ref[:, lanes] * xbc_ref[rows, lanes].astype(F32)
            mixed_ref[rows, lanes] = mixed
            gate = gate_ref[rows, lanes]
            gated = mixed * gate * jax.nn.sigmoid(gate)
            square = square + gated * gated
            cross = cross + gated * gain_ref[:, lanes] * db_ref[rows, lanes]
            state[:, lanes] = state[:, lanes] * spread_heads(whole, p) + fresh_ref[sub, :, lanes]
        sq = jnp.sum(square, axis=1, keepdims=True)
        cr = jnp.sum(cross, axis=1, keepdims=True)
        both = jnp.where(s == 0, sq, jnp.where(s == 1, cr, 0.0))
        sums_ref[8 * sub : 8 * sub + 8, :] = jnp.transpose(both)[0:8]


def scan(xbc, xdt, cum, fresh, gate, pos, summs, cot, W, skip, gain):
    tile = 256
    sub = tile // LEN
    return pl.pallas_call(
        scan_kernel,
        grid=(ROWS // tile,),
        in_specs=[
            rows_spec(tile, CONV), rows_spec(tile, HD), rows_spec(tile, 128),
            pl.BlockSpec((sub, NS, HD), lambda i: (i, 0, 0)), rows_spec(tile, HD), rows_spec(tile, 128),
            whole_spec(4, NS + 16, HD), rows_spec(tile, D), whole_spec(D, HD), whole_spec(1, HD), whole_spec(1, HD),
        ],
        out_specs=[
            rows_spec(tile, HD), rows_spec(tile, HD), rows_spec(8 * sub, 128),
            pl.BlockSpec((sub, NS, HD), lambda i: (i, 0, 0)),
        ],
        out_shape=[
            shape((ROWS, HD), F32), shape((ROWS, HD), F32), shape((8 * CHUNKS, 128), F32), shape((CHUNKS, NS, HD), BF16),
        ],
        scratch_shapes=[pltpu.VMEM((NS, HD), F32)],
        compiler_params=pltpu.CompilerParams(vmem_limit_bytes=56 << 20),
        cost_estimate=pl.CostEstimate(flops=2 * ROWS * D * 900, bytes_accessed=30 << 20, transcendentals=ROWS * CONV),
        name="scan",
    )(xbc, xdt, cum, fresh, gate, pos, summs, cot, W, skip, gain)


def turn_kernel(
    sums_ref, mixed_ref, gate_ref, db_ref, xbc_ref, cum_ref, pos_ref, w_ref, gain_ref,
    branch_ref, dgate_ref, dmix_ref, out_ref, gfresh_ref, summ_ref, acc_ref,
    state, decay,
):
    step = pl.program_id(0)
    tile = mixed_ref.shape[0]

    @pl.when(step == 0)
    def _():
        state[...] = jnp.zeros_like(state)
        decay[...] = jnp.ones_like(decay)
        acc_ref[...] = jnp.zeros_like(acc_ref)

    for sub in reversed(range(tile // LEN)):
        rows = slice(LEN * sub, LEN * sub + LEN)
        total = sums_ref[0, 8 * sub : 8 * sub + 8, :]
        for k in range(1, 4):
            total = total + sums_ref[k, 8 * sub : 8 * sub + 8, :]
        both = jnp.transpose(jnp.concatenate([total, jnp.zeros((120, 128), F32)], axis=0))
        r = lax.rsqrt(both[:, 0:1] * (1.0 / E_ALL) + EPS)
        slope = r * r * r * both[:, 1:2] * (1.0 / E_ALL)
        pos = pos_ref[rows, :]
        cum = cum_ref[rows, :]
        fade = jnp.where(pos > iota((LEN, 128), 0).astype(F32), jnp.exp2(cum), 0.0)
        whole = jnp.where(pos[LEN - 1 : LEN] > LEN - 1, jnp.exp2(cum[LEN - 1 : LEN]), 0.0)
        basis_t = jnp.transpose(xbc_ref[rows, HD + NS : CONV].astype(F32)).astype(BF16)
        for p in range(PAIRS):
            lanes = cols(p)
            mixed, gate, db = mixed_ref[rows, lanes], gate_ref[rows, lanes], db_ref[rows, lanes]
            gain = gain_ref[:, lanes]
            sig = jax.nn.sigmoid(gate)
            silu = gate * sig
            gated = mixed * silu
            scaled = gated * r
            branch_ref[rows, lanes] = (scaled * gain).astype(BF16)
            acc_ref[0:8, lanes] += fold8(db * scaled)
            dgated = r * gain * db - gated * slope
            dmix = dgated * silu
            dgate_ref[rows, lanes] = (dgated * mixed * sig * (1.0 + gate * (1.0 - sig))).astype(BF16)
            dmix_ref[rows, lanes] = dmix
            acc_ref[8:16, lanes] += fold8(dmix * xbc_ref[rows, lanes].astype(F32))
            fresh = dot(basis_t, (dmix * spread_heads(fade, p)).astype(BF16))
            gfresh_ref[sub, :, lanes] = fresh
            factor = spread_heads(whole, p)
            state[:, lanes] = state[:, lanes] * factor + fresh
            decay[:, lanes] = decay[:, lanes] * factor
    out_ref[...] = dot_nt(branch_ref[...], w_ref[...]).astype(BF16)

    @pl.when(step == pl.num_programs(0) - 1)
    def _():
        summ_ref[0:NS, :] = state[...].astype(BF16)
        summ_ref[NS : NS + 16, :] = link_rows(decay[...])


def turn(sums, mixed, gate, db, xbc, cum, pos, W, gain):
    tile = 256
    sub = tile // LEN
    top = ROWS // tile - 1
    return pl.pallas_call(
        turn_kernel,
        grid=(ROWS // tile,),
        in_specs=[
            pl.BlockSpec((4, 8 * sub, 128), lambda i: (0, top - i, 0)), rows_spec(tile, HD, top), rows_spec(tile, HD, top),
            rows_spec(tile, HD, top), rows_spec(tile, CONV, top), rows_spec(tile, 128, top), rows_spec(tile, 128, top),
            whole_spec(D, HD), whole_spec(1, HD),
        ],
        out_specs=[
            rows_spec(tile, HD, top), rows_spec(tile, HD, top), rows_spec(tile, HD, top), rows_spec(tile, D, top),
            pl.BlockSpec((sub, NS, HD), lambda i: (top - i, 0, 0)), whole_spec(NS + 16, HD), whole_spec(16, HD),
        ],
        out_shape=[
            shape((ROWS, HD), BF16), shape((ROWS, HD), BF16), shape((ROWS, HD), F32), shape((ROWS, D), BF16),
            shape((CHUNKS, NS, HD), F32), shape((NS + 16, HD), BF16), shape((16, HD), F32),
        ],
        scratch_shapes=[pltpu.VMEM((NS, HD), F32), pltpu.VMEM((1, HD), F32)],
        compiler_params=pltpu.CompilerParams(vmem_limit_bytes=56 << 20),
        cost_estimate=pl.CostEstimate(flops=2 * ROWS * D * 900, bytes_accessed=30 << 20, transcendentals=ROWS * CONV),
        name="turn",
    )(sums, mixed, gate, db, xbc, cum, pos, W, gain)


def add(a, b):
    return a.astype(F32) + b.astype(F32)


class Reduce:
    def __init__(self, flow, tag, bufs, halves):
        self.flow, self.tag, self.bufs = flow, tag, bufs
        G, K, RA, SA, TA, UA, VA, RB, SB, TB, UB, VB = bufs
        nA, nA1, nB, nB1 = halves
        self.A, self.B = pl.ds(0, nA), pl.ds(nA, nB)
        self.A1, self.A2 = pl.ds(0, nA1), pl.ds(nA1, nA - nA1)
        self.B1, self.B2 = pl.ds(0, nB1), pl.ds(nB1, nB - nB1)
        self.GB1, self.GB2 = pl.ds(nA, nB1), pl.ds(nA + nB1, nB - nB1)
        x, c, z, y = place()
        self.c, self.at = c, (x, z)
        xr, xl, xo = (x + 1) % 4, (x + 3) % 4, (x + 2) % 4
        zr, zl, zo = (z + 1) % 4, (z + 3) % 4, (z + 2) % 4
        self.xs, self.zs = (xr, xl, xo), (zr, zl, zo)
        dxr, dxl = device(xr, c, z, y), device(xl, c, z, y)
        dzr, dzl = device(x, c, zr, y), device(x, c, zl, y)
        A, B, A1, A2, B1, B2, GB1, GB2 = self.A, self.B, self.A1, self.A2, self.B1, self.B2, self.GB1, self.GB2

        def put(name, src, dst, to):
            flow.add(tag + name, src, dst, to)

        for k in range(4):
            put("k%d" % k, lambda k=k: G.at[k, 1 - c], lambda k=k: K.at[k], device(x, 1 - c, z, y))
        put("ra1", lambda: G.at[xo, c, :, :, A1], lambda: RA.at[:, :, A1], dxr)
        put("ra2", lambda: G.at[xo, c, :, :, A2], lambda: RA.at[:, :, A2], dxl)
        put("rb1", lambda: G.at[:, c, zo, :, GB1], lambda: RB.at[:, :, B1], dzr)
        put("rb2", lambda: G.at[:, c, zo, :, GB2], lambda: RB.at[:, :, B2], dzl)
        put("sar", lambda: G.at[xr, c, :, :, A], lambda: SA.at[0], dxr)
        put("sal", lambda: G.at[xl, c, :, :, A], lambda: SA.at[1], dxl)
        put("sbr", lambda: G.at[:, c, zr, :, B], lambda: SB.at[0], dzr)
        put("sbl", lambda: G.at[:, c, zl, :, B], lambda: SB.at[1], dzl)
        put("ta1", lambda: TA.at[zo, :, A1], lambda: UA.at[:, A1], dzr)
        put("ta2", lambda: TA.at[zo, :, A2], lambda: UA.at[:, A2], dzl)
        put("tb1", lambda: TB.at[xo, :, B1], lambda: UB.at[:, B1], dxr)
        put("tb2", lambda: TB.at[xo, :, B2], lambda: UB.at[:, B2], dxl)
        put("var", lambda: TA.at[zr], lambda: VA.at[0], dzr)
        put("val", lambda: TA.at[zl], lambda: VA.at[1], dzl)
        put("vbr", lambda: TB.at[xr], lambda: VB.at[0], dxr)
        put("vbl", lambda: TB.at[xl], lambda: VB.at[1], dxl)

    def start(self, *names):
        self.flow.start(*[self.tag + name for name in names])

    def wait(self, *names):
        self.flow.wait(*[self.tag + name for name in names])

    def cores(self, k):
        self.start("k%d" % k)

    def first(self):
        G, K = self.bufs[:2]
        for k in range(4):
            self.wait("k%d" % k)
            for j in range(4):
                G[k, self.c, j] = add(G[k, self.c, j], K[k, j]).astype(BF16)
        self.start("ra1", "rb1", "ra2", "rb2")

    def second(self):
        G, K, RA, SA, TA, UA, VA, RB, SB, TB, UB, VB = self.bufs
        c, (xr, xl, _), (zr, zl, _) = self.c, self.xs, self.zs
        self.wait("ra1")
        G[xr, c, :, :, self.A1] = add(G[xr, c, :, :, self.A1], RA[:, :, self.A1]).astype(BF16)
        self.start("sar")
        self.wait("rb1")
        G[:, c, zr, :, self.GB1] = add(G[:, c, zr, :, self.GB1], RB[:, :, self.B1]).astype(BF16)
        self.start("sbr")
        self.wait("ra2")
        G[xl, c, :, :, self.A2] = add(G[xl, c, :, :, self.A2], RA[:, :, self.A2]).astype(BF16)
        self.start("sal")
        self.wait("rb2")
        G[:, c, zl, :, self.GB2] = add(G[:, c, zl, :, self.GB2], RB[:, :, self.B2]).astype(BF16)
        self.start("sbl")

    def third(self):
        G, K, RA, SA, TA, UA, VA, RB, SB, TB, UB, VB = self.bufs
        c, (x, z) = self.c, self.at
        self.wait("sar", "sal")
        TA[...] = (G[x, c, :, :, self.A].astype(F32) + add(SA[0], SA[1])).astype(BF16)
        self.start("ta1", "ta2")
        self.wait("sbr", "sbl")
        TB[...] = (G[:, c, z, :, self.B].astype(F32) + add(SB[0], SB[1])).astype(BF16)
        self.start("tb1", "tb2")

    def fourth(self):
        G, K, RA, SA, TA, UA, VA, RB, SB, TB, UB, VB = self.bufs
        (xr, xl, _), (zr, zl, _) = self.xs, self.zs
        self.wait("ta1")
        TA[zr, :, self.A1] = add(TA[zr, :, self.A1], UA[:, self.A1]).astype(BF16)
        self.start("var")
        self.wait("ta2")
        TA[zl, :, self.A2] = add(TA[zl, :, self.A2], UA[:, self.A2]).astype(BF16)
        self.start("val")
        self.wait("tb1")
        TB[xr, :, self.B1] = add(TB[xr, :, self.B1], UB[:, self.B1]).astype(BF16)
        self.start("vbr")
        self.wait("tb2")
        TB[xl, :, self.B2] = add(TB[xl, :, self.B2], UB[:, self.B2]).astype(BF16)
        self.start("vbl")

    def last(self, out_ref):
        G, K, RA, SA, TA, UA, VA, RB, SB, TB, UB, VB = self.bufs
        x, z = self.at
        self.wait("vbr", "vbl")
        out_ref[:, self.B] = TB[x].astype(F32) + add(VB[0], VB[1])
        self.wait("var", "val")
        out_ref[:, self.A] = TA[z].astype(F32) + add(VA[0], VA[1])


def reduce_bufs(halves):
    nA, nA1, nB, nB1 = halves

    def half(n):
        return [
            pltpu.VMEM((4, 48, n), BF16), pltpu.VMEM((2, 4, 48, n), BF16), pltpu.VMEM((4, 48, n), BF16),
            pltpu.VMEM((48, n), BF16), pltpu.VMEM((2, 48, n), BF16),
        ]

    return [pltpu.VMEM((4, 2, 4, 48, nA + nB), BF16), pltpu.VMEM((4, 4, 48, nA + nB), BF16)] + half(nA) + half(nB)


class RowSum:
    def __init__(self, flow, tag, N, M, Q, first_from=None):
        self.flow, self.tag, self.bufs = flow, tag, (N, M, Q)
        x, c, z, y = place()
        self.yr, self.yl, self.yo, self.y = (y + 1) % 4, (y + 3) % 4, (y + 2) % 4, y
        right, left = device(x, c, z, self.yr), device(x, c, z, self.yl)
        source = N if first_from is None else first_from
        self.h1, self.h2 = pl.ds(0, 128), pl.ds(128, 128)
        flow.add(tag + "1", lambda: source.at[self.yo, self.h1], lambda: M.at[0], right)
        flow.add(tag + "2", lambda: source.at[self.yo, self.h2], lambda: M.at[1], left)
        flow.add(tag + "3", lambda: N.at[self.yr], lambda: Q.at[0], right)
        flow.add(tag + "4", lambda: N.at[self.yl], lambda: Q.at[1], left)

    def first(self):
        self.flow.start(self.tag + "1", self.tag + "2")

    def second(self):
        N, M, Q = self.bufs
        self.flow.wait(self.tag + "1")
        N[self.yr, self.h1] = add(N[self.yr, self.h1], M[0]).astype(BF16)
        self.flow.start(self.tag + "3")
        self.flow.wait(self.tag + "2")
        N[self.yl, self.h2] = add(N[self.yl, self.h2], M[1]).astype(BF16)
        self.flow.start(self.tag + "4")

    def last(self, out_ref):
        N, M, Q = self.bufs
        self.flow.wait(self.tag + "3", self.tag + "4")
        out_ref[...] = N[self.y].astype(F32) + add(Q[0], Q[1])


def row_bufs():
    return [pltpu.VMEM((4, 256, D), BF16), pltpu.VMEM((2, 128, D), BF16), pltpu.VMEM((2, 256, D), BF16)]


MID = (768, 384, 768, 384)
TAIL = (640, 384, 512, 256)
PRE = 4


def middle_kernel(
    gsumm_ref, out_ref, cot_ref, normed_ref, branch_ref, dgate_ref,
    xbc_ref, xdt_ref, dt_ref, cum_ref, sig_ref, dmix_ref, enter_ref, gfresh_ref, ds_ref, ci_ref, pos_ref,
    edge_ref, conv_ref, step_ref, skip_ref,
    din_ref, cgrad_ref, hgrad_ref, dedge_ref, gout_ref, share_ref,
    state, dacc, posn, summ, edge_out, edge_in, *rest,
):
    bufs, (N, M, Q, ssem, rsem, lsem) = rest[:-6], rest[-6:]
    step = pl.program_id(0)
    steps = PRE + CHUNKS
    x, c, z, y = place()
    flow = Flow(ssem, rsem)
    reduce = Reduce(flow, "g", bufs, MID)
    rows = RowSum(flow, "n", N, M, Q, out_ref)
    others_z = [device(x, c, (z + k) % 4, y) for k in (1, 3, 2)]
    for k in range(3):
        flow.add("s%d" % k, lambda: gsumm_ref, lambda: summ.at[z], others_z[k])
    flow.add("e", lambda: edge_out, lambda: edge_in, others_z[1])
    load_n = pltpu.make_async_copy(out_ref, N, lsem.at[0])
    load_s = pltpu.make_async_copy(gsumm_ref, summ.at[z], lsem.at[1])

    @pl.when(step == 0)
    def _():
        load_s.start()
        load_n.start()
        enter(
            others_z
            + [device((x + 1) % 4, c, z, y), device((x + 3) % 4, c, z, y)]
            + [device(x, c, z, (y + 1) % 4), device(x, c, z, (y + 3) % 4), device(x, 1 - c, z, y)]
        )
        flow.start("s0", "s1", "s2")
        rows.first()

    for k in range(PRE):

        @pl.when(step == k)
        def _():
            G = bufs[0]
            out = dot(jnp.transpose(cot_ref[...]), branch_ref[...]).astype(BF16)
            gate = dot(jnp.transpose(normed_ref[...]), dgate_ref[...]).astype(BF16)
            G[k, :, :, :, 0:HD] = out.reshape(2, 4, 48, HD)
            G[k, :, :, :, HD : 2 * HD] = gate.reshape(2, 4, 48, HD)
            reduce.cores(k)

    @pl.when(step == PRE)
    def _():
        flow.wait("s0", "s1", "s2")
        load_s.wait()
        start = jnp.zeros((NS, HD), F32)
        for j in (3, 2, 1):
            link = link_of(summ, j)
            start = jnp.where(j > z, start * link + summ[j, 0:NS, :].astype(F32), start)
        state[...] = start
        dacc[LEN : LEN + 8, :] = jnp.zeros((8, CONV), F32)
        posn[LEN : LEN + 8, :] = jnp.zeros((8, 128), F32)
        cgrad_ref[...] = jnp.zeros_like(cgrad_ref)
        hgrad_ref[...] = jnp.zeros_like(hgrad_ref)
        reduce.first()

    @pl.when(step == PRE + 1)
    def _():
        load_n.wait()
        rows.second()

    @pl.when(step == PRE + 2)
    def _():
        reduce.second()

    @pl.when(step == PRE + 5)
    def _():
        reduce.third()

    @pl.when(step == PRE + 6)
    def _():
        reduce.fourth()

    @pl.when(step > PRE)
    def _():
        dacc[LEN : LEN + 8, :] = dacc[0:8, :]
        posn[LEN : LEN + 8, :] = posn[0:8, :]

    @pl.when(step >= PRE)
    def _():
        back_chunk(
            xbc_ref, xdt_ref, dt_ref, cum_ref, sig_ref, dmix_ref, enter_ref, gfresh_ref, ds_ref, ci_ref, pos_ref,
            conv_ref, step_ref, skip_ref, din_ref, cgrad_ref, hgrad_ref, state, dacc, posn,
        )

    @pl.when(step == steps - 1)
    def _():
        dacc[8:16, :] = dacc[0:8, :]
        dacc[0:8, :] = jnp.zeros((8, CONV), F32)
        posn[8:16, :] = posn[0:8, :]
        posn[0:8, :] = jnp.zeros((8, 128), F32)
        for j in range(CONV // 128):
            lanes = cols(j)
            ci = edge_ref[:, lanes].astype(F32)[8:16]
            d_in = jnp.zeros((8, 128), F32)
            for back in (1, 2, 3):
                moved = jnp.where(posn[back : back + 8, :] >= back, dacc[back : back + 8, lanes], 0.0)
                d_in = d_in + moved * conv_ref[3 - back : 4 - back, lanes]
                cgrad_ref[8 * (3 - back) : 8 * (3 - back) + 8, lanes] += moved * ci
            edge_out[:, lanes] = d_in
        flow.start("e")
        reduce.last(gout_ref)
        rows.last(share_ref)
        flow.wait("e")
        dedge_ref[...] = edge_in[...]
        flow.finish()


def back_chunk(
    xbc_ref, xdt_ref, dt_ref, cum_ref, sig_ref, dmix_ref, enter_ref, gfresh_ref, ds_ref, ci_ref, pos_ref,
    conv_ref, step_ref, skip_ref, din_ref, cgrad_ref, hgrad_ref, state, dacc, posn,
):
    pos = pos_ref[...]
    posn[0:LEN, :] = pos
    row, lane = iota((LEN, LEN), 0), iota((LEN, LEN), 1)
    gap = (lane - row).astype(F32)
    keep = (gap >= 0) & (gap <= jnp.transpose(pos))
    cum, dt = cum_ref[...], dt_ref[...]
    cum_t = jnp.transpose(cum)
    last = cum[LEN - 1 : LEN]
    pos_last = pos[LEN - 1 : LEN]
    fade = jnp.where(pos > row.astype(F32), jnp.exp2(cum), 0.0)
    ends = jnp.where((LEN - 1) - row.astype(F32) <= pos_last, jnp.exp2(last - cum), 0.0)
    whole = jnp.where(pos_last > LEN - 1, jnp.exp2(last), 0.0)
    basis = xbc_ref[:, HD : HD + NS]
    basis_c = xbc_ref[:, HD + NS : CONV]
    inner = dot_nt(basis, basis_c)
    inner2 = jnp.concatenate([inner, inner], axis=1)
    d_inner = jnp.zeros((LEN, LEN), F32)
    d_b = jnp.zeros((LEN, NS), F32)
    d_c = jnp.zeros((LEN, NS), F32)
    into = jnp.zeros((LEN, 128), F32)
    direct = jnp.zeros((LEN, 128), F32)
    carry = jnp.zeros((LEN, 128), F32)
    later = jnp.zeros((LEN, 128), F32)
    across = jnp.zeros((8, 128), F32)
    sums_t = []
    for p in range(PAIRS):
        lanes = cols(p)
        xs = xbc_ref[:, lanes].astype(F32)
        xdt = xdt_ref[:, lanes]
        dy_wide = dmix_ref[:, lanes]
        dy, dy_low = in_two(dy_wide)
        entered = enter_ref[0, :, lanes]
        after = state[:, lanes]
        after_low = after.astype(BF16)
        dys = stacked(dy)
        spans = []
        for h in (2 * p, 2 * p + 1):
            spans.append(jnp.where(keep, cum_t[h : h + 1, :] - cum[:, h : h + 1], -1e30))
        decays = jnp.exp2(jnp.concatenate(spans, axis=1))
        scores = (decays * inner2).astype(BF16)
        d_scores = dot_nt(twice(xdt), jnp.concatenate([dys, stacked(dy_low)], axis=1)) * decays
        d_inner = d_inner + d_scores[:, :LEN] + d_scores[:, LEN:]
        prod = d_scores * inner2
        sums_t.append(jnp.sum(prod[:, :LEN], axis=0, keepdims=True))
        sums_t.append(jnp.sum(prod[:, LEN:], axis=0, keepdims=True))
        first = jnp.sum(prod[:, :LEN], axis=1, keepdims=True)
        second = jnp.sum(prod[:, LEN:], axis=1, keepdims=True)
        into = into + jnp.where(lane == 2 * p, first, jnp.where(lane == 2 * p + 1, second, 0.0))
        end_pair = spread_heads(ends, p)
        fade_pair = spread_heads(fade, p)
        z_state = dot(basis, after_low) * end_pair
        z = dot(scores, dys) + z_state
        direct = direct + head_sum(xs * z, p)
        later = later + head_sum(xdt.astype(F32) * z_state, p)
        carry = carry + head_sum(dy_wide * dot(basis_c, entered) * fade_pair, p)
        across = across + head_sum(fold8(after * entered.astype(F32)), p)
        d_x = spread_heads(dt, p) * z + skip_ref[:, lanes] * dy_wide
        dacc[0:LEN, lanes] = d_x * ds_ref[:, lanes]
        d_b = d_b + dot_nt(jnp.concatenate(in_two(xdt.astype(F32) * end_pair), axis=1), twice(after_low))
        d_c = d_c + dot_nt(jnp.concatenate(in_two(dy_wide * fade_pair), axis=1), twice(entered))
        state[:, lanes] = after * spread_heads(whole, p) + gfresh_ref[0, :, lanes]
    low = d_inner.astype(BF16)
    d_b = d_b + dot(low, basis_c)
    d_c = d_c + dot_tn(low, basis)
    dacc[0:LEN, HD : HD + NS] = d_b * ds_ref[:, HD : HD + NS]
    dacc[0:LEN, HD + NS : CONV] = d_c * ds_ref[:, HD + NS : CONV]
    out_of = jnp.transpose(jnp.concatenate(sums_t + [jnp.zeros((128 - HEADS, LEN), F32)], axis=0))
    d_rate = (
        dot_full(triangle("suffix"), out_of - into + carry)
        + dot_full(triangle("strict"), later)
        + whole * jnp.sum(across, axis=0, keepdims=True)
    )
    d_step = (direct + d_rate * step_ref[2:3, :]) * sig_ref[...]
    hgrad_ref[0:8, :] += fold8(d_rate * dt)
    hgrad_ref[8:16, :] += fold8(d_step)
    din_ref[:, CONV : CONV + 128] = d_step.astype(BF16)

    for j in range(CONV // 128):
        lanes = cols(j)
        here = dacc[0:LEN, lanes]
        ci = ci_ref[:, lanes].astype(F32)
        d_in = here * conv_ref[3:4, lanes]
        cgrad_ref[24:32, lanes] += fold8(here * ci)
        cgrad_ref[32:40, lanes] += fold8(here)
        for back in (1, 2, 3):
            moved = jnp.where(posn[back : back + LEN, :] >= back, dacc[back : back + LEN, lanes], 0.0)
            d_in = d_in + moved * conv_ref[3 - back : 4 - back, lanes]
            cgrad_ref[8 * (3 - back) : 8 * (3 - back) + 8, lanes] += fold8(moved * ci)
        din_ref[:, lanes] = d_in.astype(BF16)


def middle(
    gsumm, out, cot, normed, branch, dgate, xbc, xdt, dt, cum, sig, dmix, entered, gfresh, ds, ci, pos, edge, conv, step, skip
):
    top = CHUNKS - 1

    def chunk(i):
        return jnp.minimum(top + PRE - i, top)

    def rows(c):
        return pl.BlockSpec((LEN, c), lambda i: (chunk(i), 0))

    def tiles():
        return pl.BlockSpec((ROWS, D // PRE), lambda i: (0, jnp.minimum(i, PRE - 1)))

    state = pl.BlockSpec((1, NS, HD), lambda i: (chunk(i), 0, 0))
    anywhere = pl.BlockSpec(memory_space=ANY)
    return pl.pallas_call(
        middle_kernel,
        grid=(PRE + CHUNKS,),
        in_specs=[
            anywhere, anywhere, tiles(), tiles(), whole_spec(ROWS, HD), whole_spec(ROWS, HD),
            rows(CONV), rows(HD), rows(128), rows(128), rows(128), rows(HD), state, state, rows(CONV), rows(CONV), rows(128),
            whole_spec(16, CONV), whole_spec(8, CONV), whole_spec(8, 128), whole_spec(1, HD),
        ],
        out_specs=[
            rows(CONV + 128), whole_spec(40, CONV), whole_spec(16, 128), whole_spec(8, CONV), whole_spec(48, 2 * HD),
            whole_spec(256, D),
        ],
        out_shape=[
            shape((ROWS, CONV + 128), BF16), shape((40, CONV), F32), shape((16, 128), F32), shape((8, CONV), F32),
            shape((48, 2 * HD), F32), shape((256, D), F32),
        ],
        scratch_shapes=[
            pltpu.VMEM((NS, HD), F32), pltpu.VMEM((LEN + 8, CONV), F32), pltpu.VMEM((LEN + 8, 128), F32),
            pltpu.VMEM((4, NS + 16, HD), BF16), pltpu.VMEM((8, CONV), F32), pltpu.VMEM((8, CONV), F32),
        ] + reduce_bufs(MID) + row_bufs() + sems(32),
        compiler_params=comm_params(3, 60 << 20),
        cost_estimate=pl.CostEstimate(flops=40 * ROWS * HD * 128, bytes_accessed=30 << 20, transcendentals=2 * ROWS * CONV),
        name="middle",
    )(gsumm, out, cot, normed, branch, dgate, xbc, xdt, dt, cum, sig, dmix, entered, gfresh, ds, ci, pos, edge, conv, step, skip)


def tail_kernel(
    dgate_ref, din_ref, w_ref, x_ref, normed_ref, edge_ref, cgrad_ref, tgrad_ref, hgrad_ref,
    gout_ref, share_ref, ysum_ref, plane_ref, every_ref,
    dgate, din, w, xs, normed, small, HZ, HX, HC, HY, Y, *rest,
):
    bufs, (N, M, Q, ssem, rsem, lsem) = rest[:-6], rest[-6:]
    x, c, z, y = place()
    xs_other = [device((x + k) % 4, c, z, y) for k in (1, 3, 2)]
    zs_other = [device(x, c, (z + k) % 4, y) for k in (1, 3, 2)]
    ys_other = [device(x, c, z, (y + k) % 4) for k in (1, 3, 2)]
    core = device(x, 1 - c, z, y)
    loads = [
        pltpu.make_async_copy(src, dst, lsem.at[k])
        for k, (src, dst) in enumerate(
            [(w_ref.at[:, C_GATE:WIDE], w), (dgate_ref, dgate), (din_ref, din), (x_ref, xs), (normed_ref, normed)]
        )
    ]
    for load in loads:
        load.start()
    enter(xs_other + zs_other + ys_other + [core])
    flow = Flow(ssem, rsem)
    reduce = Reduce(flow, "g", bufs, TAIL)
    rows = RowSum(flow, "n", N, M, Q)
    for k in range(3):
        flow.add("hz%d" % k, lambda: HZ.at[z], lambda: HZ.at[z], zs_other[k])
        flow.add("hx%d" % k, lambda: HX.at[x], lambda: HX.at[x], xs_other[k])
        flow.add("hy%d" % k, lambda: HY.at[y], lambda: HY.at[y], ys_other[k])
        flow.add("y%d" % k, lambda: Y.at[y], lambda: Y.at[y], ys_other[k])
    flow.add("hc", lambda: HC.at[c], lambda: HC.at[c], core)

    for load in loads[:3]:
        load.wait()
    end = din[ROWS - 16 : ROWS, 0:CONV].astype(F32)
    more = jnp.concatenate([jnp.zeros((8, CONV), F32), edge_ref[...]], axis=0)
    din[ROWS - 16 : ROWS, 0:CONV] = (end + more).astype(BF16)

    for k in range(40):
        j = k % 8
        small[k : k + 1, :] = jnp.sum(cgrad_ref[8 * (k // 8) : 8 * (k // 8) + 8, cols(j)], axis=0, keepdims=True)
    for j in range(6):
        small[40 + j : 41 + j, :] = jnp.sum(tgrad_ref[0:8, cols(j)], axis=0, keepdims=True)
        small[58 + j : 59 + j, :] = jnp.sum(tgrad_ref[8:16, cols(j)], axis=0, keepdims=True)
    small[64:65, :] = jnp.sum(hgrad_ref[0:8, :], axis=0, keepdims=True)
    small[65:66, :] = jnp.sum(hgrad_ref[8:16, :], axis=0, keepdims=True)
    small[66:72, :] = jnp.zeros((6, 128), F32)

    gains = jnp.zeros((8, D), F32)
    for k, block in enumerate((rows.yo, rows.yr, rows.yl, rows.y)):
        here = pl.ds(pl.multiple_of(block * 256, 256), 256)
        grad = dot_nt(dgate[here, :], w[:, 0:HD]) + dot_nt(din[here, :], w[:, HD : WIDE - C_GATE])
        N[block] = grad.astype(BF16)
        if k == 0:
            rows.first()
            loads[3].wait()
        wide = xs[here, :].astype(F32)
        r = lax.rsqrt(jnp.mean(wide * wide, axis=1, keepdims=True) + EPS)
        gains = gains + fold8(grad * wide * r)
    gains = jnp.sum(gains, axis=0, keepdims=True)
    for j in range(12):
        small[46 + j : 47 + j, :] = gains[:, cols(j)]
    HZ[z] = small[...]
    flow.start("hz0", "hz1", "hz2")
    loads[4].wait()
    G = bufs[0]
    for k in range(4):
        part = dot(jnp.transpose(normed[:, 384 * k : 384 * k + 384]), din[...]).astype(BF16)
        G[k] = part.reshape(2, 4, 48, CONV + 128)
        reduce.cores(k)
        if k == 0:
            rows.second()
    flow.wait("hz0", "hz1", "hz2")
    HX[x] = HZ[0] + HZ[1] + HZ[2] + HZ[3]
    flow.start("hx0", "hx1", "hx2")
    reduce.first()
    flow.wait("hx0", "hx1", "hx2")
    HC[c] = HX[0] + HX[1] + HX[2] + HX[3]
    flow.start("hc")
    reduce.second()
    flow.wait("hc")
    total = HC[0] + HC[1]
    HY[y] = total
    plane_ref[...] = total
    flow.start("hy0", "hy1", "hy2")
    reduce.third()
    flow.wait("hy0", "hy1", "hy2")
    every_ref[...] = HY[0] + HY[1] + HY[2] + HY[3]
    reduce.fourth()
    reduce.last(gout_ref)
    Y[y] = gout_ref[:, HD:CONV]
    flow.start("y0", "y1", "y2")
    rows.last(share_ref)
    flow.wait("y0", "y1", "y2")
    ysum_ref[...] = Y[0] + Y[1] + Y[2] + Y[3]
    flow.finish()


def tail(dgate, din, W, X, normed, edge, cgrad, tgrad, hgrad):
    vmem = pl.BlockSpec(memory_space=pltpu.VMEM)
    table = pltpu.VMEM((4, 72, 128), F32)
    return pl.pallas_call(
        tail_kernel,
        out_shape=(
            shape((48, CONV + 128), F32), shape((256, D), F32), shape((48, 2 * NS), F32), shape((72, 128), F32),
            shape((72, 128), F32),
        ),
        in_specs=[pl.BlockSpec(memory_space=ANY)] * 5 + [vmem] * 4,
        out_specs=[vmem] * 5,
        scratch_shapes=[
            pltpu.VMEM((ROWS, HD), BF16), pltpu.VMEM((ROWS, CONV + 128), BF16), pltpu.VMEM((D, WIDE - C_GATE), BF16),
            pltpu.VMEM((ROWS, D), BF16), pltpu.VMEM((ROWS, D), BF16), pltpu.VMEM((72, 128), F32),
            table, table, pltpu.VMEM((2, 72, 128), F32), table, pltpu.VMEM((4, 48, 2 * NS), F32),
        ] + reduce_bufs(TAIL) + row_bufs() + [
            pltpu.SemaphoreType.DMA((48,)), pltpu.SemaphoreType.DMA((48,)), pltpu.SemaphoreType.DMA((8,)),
        ],
        compiler_params=comm_params(5, 60 << 20),
        name="tail",
    )(dgate, din, W, X, normed, edge, cgrad, tgrad, hgrad)


def finish_kernel(
    x_ref, cot_ref, out_ref, share_ref, gain_ref, mid_ref, tail_ref, ysum_ref,
    lout_ref, grad_ref, gate_ref, in_ref, wout_ref, bc_ref,
):
    own = x_ref[...].astype(F32)
    lout_ref[...] = (own + out_ref[...]).astype(BF16)
    scale = lax.rsqrt(jnp.mean(own * own, axis=1, keepdims=True) + EPS)
    weighted = share_ref[...] * gain_ref[...]
    slope = scale * scale * scale * jnp.mean(own * weighted, axis=1, keepdims=True)
    grad_ref[...] = scale * weighted - own * slope + cot_ref[...].astype(F32)
    gate_ref[...] = mid_ref[:, HD : 2 * HD]
    in_ref[...] = tail_ref[:, 0:HD]
    wout_ref[...] = jnp.transpose(mid_ref[:, 0:HD])
    bc_ref[...] = ysum_ref[...]


def finish(rows, cot, out, share, gain, mid, tail, ysum):
    return pl.pallas_call(
        finish_kernel,
        out_shape=(
            shape((256, D), BF16), shape((256, D), F32), shape((48, HD), F32), shape((48, HD), F32), shape((HD, 48), F32),
            shape((48, 2 * NS), F32),
        ),
        in_specs=[pl.BlockSpec(memory_space=pltpu.VMEM)] * 8,
        out_specs=[pl.BlockSpec(memory_space=pltpu.VMEM)] * 6,
        compiler_params=pltpu.CompilerParams(vmem_limit_bytes=40 << 20),
        name="finish",
    )(rows, cot, out, share, gain, mid, tail, ysum)


def after(value, *others):
    return lax.optimization_barrier((value,) + others)[0]


def from_rows(blocks, r, first, count):
    return blocks[:, :r, first : first + count].transpose(1, 0, 2).reshape(r, 32 * count)


def per_device(
    layer_input, out_cotangent, seq_lengths, norm_gain, proj_gate, proj_input, proj_step, proj_state, conv_inner,
    conv_inner_bias, conv_state, conv_state_bias, decay_log, step_bias, skip_scale, gate_gain, proj_out,
):
    ctx = lax.axis_index("ctx")
    tp = lax.axis_index("tp")

    def column(a):
        return jnp.pad(a, ((0, 48 - a.shape[0]), (0, 0)))

    misc = jnp.concatenate(
        [
            proj_step, conv_inner.reshape(48, 2), column(conv_inner_bias), column(gate_gain), column(conv_state),
            column(conv_state_bias[None, :]), norm_gain[:, None], jnp.zeros((48, 93), BF16),
        ],
        axis=1,
    )
    pack = jnp.concatenate([proj_out.T, proj_gate, proj_input, proj_state, misc], axis=1)

    ends = jnp.cumsum(seq_lengths[0])
    token = ctx * ROWS + jnp.arange(ROWS, dtype=jnp.int32)
    begin = jnp.max(jnp.where(token[:, None] >= ends[None, :], ends[None, :], 0), axis=1)
    pos = jnp.broadcast_to((token - begin).astype(F32)[:, None], (ROWS, 128))

    rate = -jnp.exp(decay_log)
    step = jnp.pad(jnp.stack([step_bias, rate * LOG2E, rate]), ((0, 5), (0, 128 - HEADS)))
    skip = jnp.repeat(skip_scale, 64)[None, :]

    W, X, E = gather(pack, layer_input)
    W, X = W.reshape(D, WIDE), X.reshape(ROWS, D)
    cot_own = after(out_cotangent, E)
    cots = [cot_own] + [
        lax.ppermute(cot_own, "tp", [(j, (j + k) % 4) for j in range(4)]) for k in (1, 3, 2)
    ]

    blocks = W[:, C_MISC:].reshape(32, 48, 128).astype(F32)
    conv = jnp.concatenate(
        [
            jnp.concatenate([from_rows(blocks, 48, 12, 2).reshape(4, HD), from_rows(blocks, 4, 18, 8)], axis=1),
            jnp.concatenate([from_rows(blocks, 12, 14, 2).reshape(1, HD), from_rows(blocks, 1, 26, 8)], axis=1),
            jnp.zeros((3, CONV), F32),
        ]
    )
    gain = from_rows(blocks, 12, 16, 2).reshape(1, HD)
    ngain = blocks[:, :, 34].reshape(1, D)

    normed, gate, ci, edge, ds, xbc, xdt, dt, cum, sig, fresh, summ = front(X, W, E, ngain, conv, step, pos)
    summs = swap(summ, "ctx", 1, "swap_state")
    cot_all = jnp.zeros((4, 256, D), BF16)
    for k, part in zip((0, 1, 3, 2), cots):
        cot_all = lax.dynamic_update_slice(cot_all, part[None], ((tp - k) % 4, 0, 0))
    cot_all = cot_all.reshape(ROWS, D)
    mixed, db, sums, entered = scan(xbc, xdt, cum, fresh, gate, pos, summs, cot_all, W, skip, gain)
    sums = swap(sums, "tp", 2, "swap_sums")
    branch, dgate, dmix, out, gfresh, gsumm, tgrad = turn(sums, mixed, gate, db, xbc, cum, pos, W, gain)
    din, cgrad, hgrad, dedge, gmid, out_share = middle(
        gsumm, out.reshape(4, 256, D), cot_all, normed, branch, dgate,
        xbc, xdt, dt, cum, sig, dmix, entered, gfresh, ds, ci, pos, edge, conv, step, skip,
    )
    gtail, share, ysum, plane, every = tail(dgate, din, W, X, normed, dedge, cgrad, tgrad, hgrad)
    layer_output, input_grad, d_gate, d_input, d_out, d_state = finish(
        layer_input, out_cotangent, out_share, share, ngain, gmid, gtail, ysum
    )
    block = lax.axis_index("shard") * 4 + ctx
    conv_sum = plane[:40].reshape(5, CONV)[:, :HD].reshape(5, HEADS, 64)
    conv_sum = lax.dynamic_slice_in_dim(conv_sum, block * 2, 2, 2)
    gain_sum = lax.dynamic_slice_in_dim(plane[40:46].reshape(HEADS, 64), block * 2, 2, 1)
    state_sum = lax.dynamic_slice_in_dim(every[:40].reshape(5, CONV)[:, HD:], block * 8 + tp * 2, 2, 1)
    return (
        layer_output,
        input_grad,
        lax.dynamic_slice_in_dim(every[46:58].reshape(D), block * 48 + tp * 12, 12, 0),
        d_gate,
        d_input,
        gtail[:, CONV : CONV + HEADS],
        lax.dynamic_slice_in_dim(d_state, tp * 12, 12, 0),
        conv_sum[:4],
        conv_sum[4],
        state_sum[:4],
        state_sum[4],
        plane[64, :HEADS] * rate,
        plane[65, :HEADS],
        plane[58:64].reshape(HEADS, 64).sum(axis=1),
        gain_sum,
        d_out,
    )


def solution(mesh):
    both = ("shard", "ctx")
    every = ("shard", "ctx", "tp")
    return jax.shard_map(
        per_device,
        mesh=mesh,
        in_specs=(
            P(every, None), P(every, None), P("shard", None), P(both), P(both, "tp"), P(both, "tp"), P(both, "tp"),
            P(both, None), P(None, "tp", both), P("tp", both), P(None, both), P(both), P("tp"), P("tp"), P("tp"),
            P("tp", both), P("tp", both),
        ),
        out_specs=(
            P(every, None), P(every, None), P(every), P(both, "tp"), P(both, "tp"), P(both, "tp"), P(every, None),
            P(None, "tp", both), P("tp", both), P(None, every), P(every), P("tp"), P("tp"), P("tp"), P("tp", both),
            P("tp", both),
        ),
        check_vma=False,
    )
```

```python
import functools

import jax
import jax.numpy as jnp
from jax import lax
from jax.experimental import pallas as pl
from jax.experimental.pallas import tpu as pltpu
from jax.sharding import PartitionSpec as P

MESH = pl.DeviceIdType.MESH
ANY = pl.ANY
F32 = jnp.float32
BF16 = jnp.bfloat16
EPS = 1e-05
LOG2E = 1.4426950408889634
HIGH = lax.Precision.HIGHEST

D = 1536
ROWS = 1024
HD = 768
HEADS = 12
PAIRS = 6
NS = 128
CONV = 1024
LEN = 128
CHUNKS = 8
E_ALL = 3072
C_OUT, C_GATE, C_IN, C_BC, C_MISC, WIDE = 0, 768, 1536, 2304, 2560, 2688
HALF_A, HALF_A1, HALF_B1 = 1408, 768, 2048


def dot(a, b):
    return jnp.dot(a, b, preferred_element_type=F32)


def dot_nt(a, b):
    return lax.dot_general(a, b, (((1,), (1,)), ((), ())), preferred_element_type=F32)


def dot_tn(a, b):
    return lax.dot_general(a, b, (((0,), (0,)), ((), ())), preferred_element_type=F32)


def dot_full(a, b):
    return jnp.dot(a, b, precision=HIGH, preferred_element_type=F32)


def iota(shape, axis):
    return lax.broadcasted_iota(jnp.int32, shape, axis)


def place():
    s = lax.axis_index("shard")
    return s // 2, s % 2, lax.axis_index("ctx"), lax.axis_index("tp")


def device(x, c, z, y):
    return {"shard": x * 2 + c, "ctx": z, "tp": y}


def enter(others):
    barrier = pltpu.get_barrier_semaphore()
    for other in others:
        pl.semaphore_signal(barrier, inc=1, device_id=other, device_id_type=MESH)
    pl.semaphore_wait(barrier, len(others))


class Sends:
    def __init__(self, send_sem, recv_sem):
        self.send_sem, self.recv_sem, self.copies = send_sem, recv_sem, []

    def __call__(self, src, dst, to):
        k = len(self.copies)
        copy = pltpu.make_async_remote_copy(
            src_ref=src,
            dst_ref=dst,
            send_sem=self.send_sem.at[k],
            recv_sem=self.recv_sem.at[k],
            device_id=to,
            device_id_type=MESH,
        )
        copy.start()
        self.copies.append(copy)
        return copy

    def finish(self):
        for copy in self.copies:
            copy.wait_send()


class Flow:
    def __init__(self, send_sem, recv_sem):
        self.send_sem, self.recv_sem, self.known = send_sem, recv_sem, {}

    def add(self, name, src, dst, to):
        self.known[name] = (len(self.known), src, dst, to)

    def copy(self, name):
        k, src, dst, to = self.known[name]
        return pltpu.make_async_remote_copy(
            src_ref=src(),
            dst_ref=dst(),
            send_sem=self.send_sem.at[k],
            recv_sem=self.recv_sem.at[k],
            device_id=to,
            device_id_type=MESH,
        )

    def start(self, *names):
        for name in names:
            self.copy(name).start()

    def wait(self, *names):
        for name in names:
            self.copy(name).wait_recv()

    def finish(self):
        for name in self.known:
            self.copy(name).wait_send()


def sems(n):
    return [pltpu.SemaphoreType.DMA((n,)), pltpu.SemaphoreType.DMA((n,)), pltpu.SemaphoreType.DMA((4,))]


def comm_params(collective_id, vmem=None):
    return pltpu.CompilerParams(
        collective_id=collective_id, has_side_effects=True, vmem_limit_bytes=vmem
    )


def shape(dims, kind):
    return jax.ShapeDtypeStruct(dims, kind)


def spread_heads(v, p):
    r = v.shape[0]
    low = jnp.broadcast_to(v[:, 2 * p : 2 * p + 1], (r, 128))
    high = jnp.broadcast_to(v[:, 2 * p + 1 : 2 * p + 2], (r, 128))
    return jnp.where(iota((r, 128), 1) < 64, low, high)


def cols(p):
    return slice(128 * p, 128 * p + 128)


def stacked(pair):
    lane = iota(pair.shape, 1)
    zero = jnp.zeros_like(pair)
    return jnp.concatenate([jnp.where(lane < 64, pair, zero), jnp.where(lane < 64, zero, pair)], axis=0)


def in_two(v):
    high = v.astype(BF16)
    return high, (v - high.astype(F32)).astype(BF16)


def twice(v):
    return jnp.concatenate([v, v], axis=1)


def link_rows(decay):
    high, low = in_two(jnp.broadcast_to(decay, (8, HD)))
    return jnp.concatenate([high, low], axis=0)


def link_of(summ_ref, j):
    both = summ_ref[j, NS : NS + 16, :].astype(F32)
    return both[0:1] + both[8:9]


def head_sum(pair, p):
    lane, head = iota((128, 128), 0), iota((128, 128), 1)
    pick = jnp.where(head == 2 * p + lane // 64, 1.0, 0.0).astype(BF16)
    return dot(pair.astype(BF16), pick)


def triangle(kind):
    t, s = iota((LEN, LEN), 0), iota((LEN, LEN), 1)
    keep = {"incl": s <= t, "suffix": s >= t, "strict": s < t}[kind]
    return jnp.where(keep, 1.0, 0.0).astype(F32)


def fold8(v):
    return jnp.sum(v.reshape(v.shape[0] // 8, 8, v.shape[1]), axis=0)


def whole_spec(*dims):
    return pl.BlockSpec(dims, lambda i: (0,) * len(dims), pipeline_mode=pl.Buffered(1))


def rows_spec(r, c, back=None):
    if back is None:
        return pl.BlockSpec((r, c), lambda i: (i, 0))
    return pl.BlockSpec((r, c), lambda i: (back - i, 0))


TILE = 256
TILES = ROWS // TILE


def gather(go, W, X, cots, w_ref, x_ref, cot_ref, edge, locals_, between):
    x, c, z, y = place()
    xr, xl, xo = (x + 1) % 4, (x + 3) % 4, (x + 2) % 4
    zr, zl, zo = (z + 1) % 4, (z + 3) % 4, (z + 2) % 4
    yr, yl = (y + 1) % 4, (y + 3) % 4
    dxr, dxl = device(xr, c, z, y), device(xl, c, z, y)
    dzr, dzl = device(x, c, zr, y), device(x, c, zl, y)
    dyr, dyl = device(x, c, z, yr), device(x, c, z, yl)
    dco = device(x, 1 - c, z, y)
    own, own_x, own_c = locals_
    own.start()
    own_x.start()
    own_c.start()
    enter([dxr, dxl, dzr, dzl, dyr, dyl, dco])
    A, A1, A2 = pl.ds(0, HALF_A), pl.ds(0, HALF_A1), pl.ds(HALF_A1, HALF_A - HALF_A1)
    B = pl.ds(HALF_A, WIDE - HALF_A)
    B1, B2 = pl.ds(HALF_A, HALF_B1 - HALF_A), pl.ds(HALF_B1, WIDE - HALF_B1)
    H1, H2 = pl.ds(0, 128), pl.ds(128, 128)

    def same(ref, to):
        return go(ref, ref, to)

    def both_x(zz):
        return same(W.at[x, c, zz, :, A], dxr), same(W.at[x, c, zz, :, A], dxl)

    def both_z(xx):
        return same(W.at[xx, c, z, :, B], dzr), same(W.at[xx, c, z, :, B], dzl)

    def on_x(xx, cols):
        return W.at[xx, c, :, :, cols]

    def on_z(zz, cols):
        return W.at[:, c, zz, :, cols]

    a_r = go(w_ref.at[:, A], W.at[x, c, z, :, A], dzr)
    b_r = go(w_ref.at[:, B], W.at[x, c, z, :, B], dxr)
    a_l = go(w_ref.at[:, A], W.at[x, c, z, :, A], dzl)
    b_l = go(w_ref.at[:, B], W.at[x, c, z, :, B], dxl)
    x_r = go(x_ref, X.at[y], dyr)
    x_l = go(x_ref, X.at[y], dyl)
    own.wait()
    a2, b2, last = [both_x(z)], [both_z(x)], []
    a_r.wait_recv()
    a_fr = same(W.at[x, c, zl, :, A1], dzr)
    b_r.wait_recv()
    b_fr = same(W.at[xl, c, z, :, B1], dxr)
    a_l.wait_recv()
    a_fl = same(W.at[x, c, zr, :, A2], dzl)
    b_l.wait_recv()
    b_fl = same(W.at[xr, c, z, :, B2], dxl)
    a2.append(both_x(zl))
    b2.append(both_z(xl))
    a2.append(both_x(zr))
    b2.append(both_z(xr))
    a_fr.wait_recv()
    a_fl.wait_recv()
    a2.append(both_x(zo))
    b_fr.wait_recv()
    b_fl.wait_recv()
    b2.append(both_z(xo))
    last.append(same(on_x(x, A), dco))
    last.append(same(on_z(z, B), dco))
    fa, fb = [], []

    def onward(k):
        zz, xx = (z, zl, zr, zo)[k], (x, xl, xr, xo)[k]
        a2[k][0].wait_recv()
        fa.append(same(W.at[xl, c, zz, :, A1], dxr))
        b2[k][0].wait_recv()
        fb.append(same(W.at[xx, c, zl, :, B1], dzr))
        a2[k][1].wait_recv()
        fa.append(same(W.at[xr, c, zz, :, A2], dxl))
        b2[k][1].wait_recv()
        fb.append(same(W.at[xx, c, zr, :, B2], dzl))

    onward(0)
    between()
    onward(1)
    x_r.wait_recv()
    x_fr = same(X.at[yl, H1], dyr)
    x_l.wait_recv()
    x_fl = same(X.at[yr, H2], dyl)
    onward(2)
    onward(3)
    last.append(same(on_x(xl, A), dco))
    last.append(same(on_z(zl, B), dco))
    last.append(same(on_x(xr, A), dco))
    last.append(same(on_z(zr, B), dco))
    own_x.wait()
    x_fr.wait_recv()
    x_fl.wait_recv()
    e = go(X.at[3, pl.ds(240, 16)], edge, dzr)
    c_r = go(cot_ref, cots.at[y], dyr)
    c_l = go(cot_ref, cots.at[y], dyl)
    for k in (0, 2, 4, 6):
        fa[k].wait_recv()
    last.append(same(on_x(xo, A1), dco))
    for k in (0, 2, 4, 6):
        fb[k].wait_recv()
    last.append(same(on_z(zo, B1), dco))
    for k in (1, 3, 5, 7):
        fa[k].wait_recv()
    last.append(same(on_x(xo, A2), dco))
    for k in (1, 3, 5, 7):
        fb[k].wait_recv()
    last.append(same(on_z(zo, B2), dco))
    e.wait_recv()
    for copy in last:
        copy.wait_recv()
    more = []

    def cot_onward():
        c_r.wait_recv()
        more.append(same(cots.at[yl, H1], dyr))
        c_l.wait_recv()
        more.append(same(cots.at[yr, H2], dyl))

    def cot_end():
        own_c.wait()
        for copy in more:
            copy.wait_recv()

    return cot_onward, cot_end


def parts(v, size):
    q = jnp.floor((v + 0.5) * (1.0 / size))
    return q, v - size * q


def fiota(dims, axis):
    return iota(dims, axis).astype(F32)


def front_kernel(
    w_ref, x_ref, cot_ref, lens_ref, step_ref,
    W_out, X_out, cots, normed_ref, gate_ref, ci_ref, ds_ref, xbc_ref, xdt_ref, dt_ref, cum_ref, sig_ref, fresh_ref, pos_ref,
    edge_ref, conv_out, gain_out, summ_ref,
    W, X, E, Q, normed, gate, ci, ds, xbc, xdt, dts, cums, sigs, fresh, pos, scale, buf0, buf1, conv, state, decay,
    ssem, rsem, lsem, osem,
):
    x, c, z, y = place()
    go = Sends(ssem, rsem)
    locals_ = [
        pltpu.make_async_copy(w_ref, W.at[x, c, z], lsem.at[0]),
        pltpu.make_async_copy(x_ref, X.at[y], lsem.at[1]),
        pltpu.make_async_copy(cot_ref, cots.at[y], lsem.at[2]),
    ]

    def between():
        block, inner = parts(fiota((D, HD), 0), 48)
        _, head = parts(inner, 12)
        place_of = head * 64 + block * 2
        lane = fiota((D, HD), 1)
        for j in range(2):
            Q[j] = jnp.where(lane == place_of + j, 1.0, 0.0).astype(BF16)
        token = fiota((ROWS, 128), 0) + (z * ROWS).astype(F32)
        begin = jnp.zeros((ROWS, 128), F32)
        end = jnp.float32(0.0)
        for k in range(3):
            end = end + lens_ref[0, k].astype(F32)
            begin = jnp.where(token >= end, end, begin)
        pos[...] = token - begin

    cot_onward, cot_end = gather(go, W, X, cots, w_ref, x_ref, cot_ref, E, locals_, between)
    out_copies = [
        pltpu.make_async_copy(W, W_out, osem.at[0]),
        pltpu.make_async_copy(X, X_out, osem.at[1]),
    ]
    for copy in out_copies:
        copy.start()

    misc = W[:, :, :, :, C_MISC:WIDE].reshape(D, 128)
    row8, lane8 = iota((8, 128), 0), iota((8, 128), 1)
    pick = jnp.where(lane8 == jnp.where(row8 == 6, 34, 12 + row8), 1.0, 0.0).astype(BF16)
    across = dot_nt(pick, misc)
    r_block, r_in = parts(fiota((8, D), 1), 48)
    r_tap, _ = parts(r_in, 12)
    row = fiota((8, D), 0)
    found = jnp.zeros((8, HD), F32)
    for j in range(2):
        tap = jnp.where(row == r_tap, jnp.broadcast_to(across[j : j + 1], (8, D)), 0.0)
        tap = jnp.where(row < 4, tap, 0.0)
        bias = jnp.where((row == 4) & (r_tap == 0), jnp.broadcast_to(across[2 + j : 3 + j], (8, D)), 0.0)
        gains = jnp.where((row == 5) & (r_tap == 0), jnp.broadcast_to(across[4 + j : 5 + j], (8, D)), 0.0)
        found = found + dot((tap + bias + gains).astype(BF16), Q[j])
    conv[:, 0:HD] = found
    lane_in, col_in = fiota((128, 256), 0), fiota((128, 256), 1)
    _, col8 = parts(col_in, 8)
    col_block, _ = parts(fiota((D, 256), 1), 8)
    row_block, _ = parts(fiota((D, 256), 0), 48)
    here = row_block == col_block
    states = jnp.zeros((8, 256), F32)
    for first, lead in ((18, False), (26, True)):
        spread = dot(misc, jnp.where(lane_in == first + col8, 1.0, 0.0).astype(BF16))
        spread = jnp.where(here, spread, 0.0).astype(BF16)
        take = (row == 4) & (r_in == 0) if lead else (row < 4) & (row == r_in)
        states = states + dot(jnp.where(take, 1.0, 0.0).astype(BF16), spread)
    conv[:, HD:CONV] = states
    conv_out[...] = conv[...]
    gain_out[...] = jnp.zeros_like(gain_out)
    gain_out[0:1, :] = across[6:7]
    gain_out[1:2, 0:HD] = found[5:6]
    ngain = across[6:7]

    def norm(rows):
        wide = rows.astype(F32)
        r = lax.rsqrt(jnp.mean(wide * wide, axis=1, keepdims=True) + EPS)
        return (wide * r * ngain).astype(BF16)

    def weight(first, last):
        return W[:, :, :, :, first:last].reshape(D, last - first)

    edge = dot(norm(E[...]), weight(C_IN, C_MISC)).astype(BF16)
    edge_ref[...] = edge
    state[...] = jnp.zeros_like(state)
    decay[...] = jnp.ones_like(decay)
    bufs = (buf0, buf1)
    buf0[0:8, :] = edge.astype(F32)[8:16]

    def project(i):
        rows = slice(TILE * i, TILE * i + TILE)
        low = norm(X[i])
        normed[rows, :] = low
        gate[rows, :] = dot(low, weight(C_GATE, C_IN))
        conv_in = dot(low, weight(C_IN, C_MISC)).astype(BF16)
        ci[rows, :] = conv_in
        bufs[i % 2][8 : 8 + TILE, :] = conv_in.astype(F32)
        sigs[rows, :] = dot(low, weight(C_MISC, WIDE))

    def convolve(i):
        buf = bufs[i % 2]
        rows = slice(TILE * i, TILE * i + TILE)
        if i + 1 < TILES:
            bufs[(i + 1) % 2][0:8, :] = buf[TILE : TILE + 8, :]
        place_in = pos[rows, :]
        for j in range(CONV // 128):
            lanes = cols(j)
            acc = buf[8 : 8 + TILE, lanes] * conv[3:4, lanes] + conv[4:5, lanes]
            for back in (1, 2, 3):
                term = buf[8 - back : 8 - back + TILE, lanes] * conv[3 - back : 4 - back, lanes]
                acc = acc + jnp.where(place_in >= back, term, 0.0)
            sig = jax.nn.sigmoid(acc)
            ds[rows, lanes] = sig * (1.0 + acc * (1.0 - sig))
            xbc[rows, lanes] = (acc * sig).astype(BF16)
        lane = iota((TILE, 128), 1)
        pre = sigs[rows, :] + step_ref[0:1, :]
        small = jnp.exp(-jnp.abs(pre))
        log1p = jnp.where(
            small < 1e-3, small * (1.0 - 0.5 * small + (1.0 / 3.0) * small * small), jnp.log(1.0 + small)
        )
        dt = jnp.where(lane < HEADS, jnp.maximum(pre, 0.0) + log1p, 0.0)
        dts[rows, :] = dt
        sigs[rows, :] = jax.nn.sigmoid(pre)
        rate = dt * step_ref[1:2, :]
        for sub in range(TILE // LEN):
            inside = slice(LEN * sub, LEN * sub + LEN)
            rows = slice(TILE * i + LEN * sub, TILE * i + LEN * sub + LEN)
            cum = dot_full(triangle("incl"), rate[inside])
            cums[rows, :] = cum
            last = cum[LEN - 1 : LEN, :]
            pos_last = pos[TILE * i + LEN * sub + LEN - 1 : TILE * i + LEN * sub + LEN, :]
            row = iota((LEN, 128), 0).astype(F32)
            fade = jnp.where((LEN - 1) - row <= pos_last, jnp.exp2(last - cum), 0.0)
            whole = jnp.where(pos_last > LEN - 1, jnp.exp2(last), 0.0)
            basis_t = jnp.transpose(xbc[rows, HD : HD + NS].astype(F32)).astype(BF16)
            for p in range(PAIRS):
                low = (xbc[rows, cols(p)].astype(F32) * spread_heads(dt[inside], p)).astype(BF16)
                xdt[rows, cols(p)] = low
                ended = (low.astype(F32) * spread_heads(fade, p)).astype(BF16)
                new = dot(basis_t, ended)
                fresh[i * (TILE // LEN) + sub, :, cols(p)] = new
                factor = spread_heads(whole, p)
                state[:, cols(p)] = state[:, cols(p)] * factor + new
                decay[:, cols(p)] = decay[:, cols(p)] * factor

    pairs = [
        (normed, normed_ref), (gate, gate_ref), (ci, ci_ref), (ds, ds_ref), (xbc, xbc_ref), (xdt, xdt_ref), (dts, dt_ref),
        (cums, cum_ref), (sigs, sig_ref), (pos, pos_ref),
    ]

    def store(i):
        rows = slice(TILE * i, TILE * i + TILE)
        for k, (src, dst) in enumerate(pairs):
            out_copies.append(pltpu.make_async_copy(src.at[rows], dst.at[rows], osem.at[2 + 11 * i + k]))
        n = TILE // LEN
        here = slice(n * i, n * i + n)
        out_copies.append(pltpu.make_async_copy(fresh.at[here], fresh_ref.at[here], osem.at[2 + 11 * i + 10]))
        for copy in out_copies[-11:]:
            copy.start()

    project(0)
    for i in range(TILES):
        if i == 2:
            cot_onward()
        if i + 1 < TILES:
            project(i + 1)
        convolve(i)
        store(i)
    summ_ref[0:NS, :] = state[...].astype(BF16)
    summ_ref[NS : NS + 16, :] = link_rows(decay[...])
    cot_end()
    for copy in out_copies:
        copy.wait()
    go.finish()


def front(pack, rows, cot, lens, step):
    vmem = pl.BlockSpec(memory_space=pltpu.VMEM)
    anywhere = pl.BlockSpec(memory_space=ANY)
    outs = [
        ((ROWS, D), BF16), ((ROWS, HD), F32), ((ROWS, CONV), BF16), ((ROWS, CONV), F32), ((ROWS, CONV), BF16),
        ((ROWS, HD), BF16), ((ROWS, 128), F32), ((ROWS, 128), F32), ((ROWS, 128), F32), ((CHUNKS, NS, HD), F32),
        ((ROWS, 128), F32),
    ]
    return pl.pallas_call(
        front_kernel,
        out_shape=[shape((4, 2, 4, 48, WIDE), BF16), shape((4, 256, D), BF16), shape((4, 256, D), BF16)]
        + [shape(*o) for o in outs]
        + [shape((16, CONV), BF16), shape((8, CONV), F32), shape((8, D), F32), shape((NS + 16, HD), BF16)],
        in_specs=[anywhere] * 3 + [pl.BlockSpec(memory_space=pltpu.SMEM), vmem],
        out_specs=[anywhere] * 14 + [vmem] * 4,
        scratch_shapes=[
            pltpu.VMEM((4, 2, 4, 48, WIDE), BF16), pltpu.VMEM((4, 256, D), BF16), pltpu.VMEM((16, D), BF16),
            pltpu.VMEM((2, D, HD), BF16),
        ]
        + [pltpu.VMEM(*o) for o in outs]
        + [
            pltpu.VMEM((ROWS, 128), F32), pltpu.VMEM((8 + TILE, CONV), F32), pltpu.VMEM((8 + TILE, CONV), F32),
            pltpu.VMEM((8, CONV), F32), pltpu.VMEM((NS, HD), F32), pltpu.VMEM((1, HD), F32),
            pltpu.SemaphoreType.DMA((64,)), pltpu.SemaphoreType.DMA((64,)), pltpu.SemaphoreType.DMA((4,)),
            pltpu.SemaphoreType.DMA((48,)),
        ],
        compiler_params=comm_params(0, 60 << 20),
        name="front",
    )(pack, rows, cot, lens, step)


def forward_kernel(
    summ_in, xbc_ref, xdt_ref, cum_ref, pos_ref, fresh_ref, gate_ref, cot_ref, w_ref, skip_ref, gain_ref,
    enter_ref, branch_ref, dgate_ref, dmix_ref, out_ref, gfresh_ref, gsumm_ref, acc_ref,
    mixed, db, state, decay, summ, sums, ssem, rsem, lsem,
):
    step = pl.program_id(0)
    x, c, z, y = place()
    subs = TILE // LEN
    flow = Flow(ssem, rsem)
    others_z = [device(x, c, (z + k) % 4, y) for k in (1, 3, 2)]
    others_y = [device(x, c, z, (y + k) % 4) for k in (1, 3, 2)]
    for k in range(3):
        flow.add("z%d" % k, lambda: summ_in, lambda: summ.at[z], others_z[k])
        flow.add("y%d" % k, lambda: sums.at[y], lambda: sums.at[y], others_y[k])
    load = pltpu.make_async_copy(summ_in, summ.at[z], lsem.at[0])

    @pl.when(step == 0)
    def _():
        load.start()
        enter(others_z + others_y)
        flow.start("z0", "z1", "z2")
        acc_ref[...] = jnp.zeros_like(acc_ref)

    @pl.when(step < TILES)
    def _():
        here = pl.ds(pl.multiple_of(step * TILE, TILE), TILE)
        db[here, :] = dot(cot_ref[...], w_ref[...])
        t, s = iota((LEN, LEN), 0), iota((LEN, LEN), 1)
        gap = (t - s).astype(F32)
        for sub in range(subs):
            rows = slice(LEN * sub, LEN * sub + LEN)
            there = pl.ds(pl.multiple_of(step * TILE + LEN * sub, LEN), LEN)
            pos = pos_ref[rows, :]
            keep = (gap >= 0) & (gap <= pos)
            cum = cum_ref[rows, :]
            cum_t = jnp.transpose(cum)
            inner = dot_nt(xbc_ref[rows, HD + NS : CONV], xbc_ref[rows, HD : HD + NS])
            for p in range(PAIRS):
                lanes = cols(p)
                parts = []
                for h in (2 * p, 2 * p + 1):
                    span = jnp.where(keep, cum[:, h : h + 1] - cum_t[h : h + 1, :], -1e30)
                    parts.append((jnp.exp2(span) * inner).astype(BF16))
                local = dot(jnp.concatenate(parts, axis=1), stacked(xdt_ref[rows, lanes]))
                mixed[there, lanes] = local + skip_ref[:, lanes] * xbc_ref[rows, lanes].astype(F32)

    @pl.when(step == TILES)
    def _():
        flow.wait("z0", "z1", "z2")
        load.wait()
        start = jnp.zeros((NS, HD), F32)
        for j in range(3):
            start = jnp.where(j < z, start * link_of(summ, j) + summ[j, 0:NS, :].astype(F32), start)
        state[...] = start

    @pl.when((step >= TILES) & (step < 2 * TILES))
    def _():
        tile = step - TILES
        t, s = iota((LEN, LEN), 0), iota((LEN, LEN), 1)
        for sub in range(subs):
            rows = slice(LEN * sub, LEN * sub + LEN)
            there = pl.ds(pl.multiple_of(tile * TILE + LEN * sub, LEN), LEN)
            pos, cum = pos_ref[rows, :], cum_ref[rows, :]
            basis_c = xbc_ref[rows, HD + NS : CONV]
            fade = jnp.where(pos > t.astype(F32), jnp.exp2(cum), 0.0)
            whole = jnp.where(pos[LEN - 1 : LEN] > LEN - 1, jnp.exp2(cum[LEN - 1 : LEN]), 0.0)
            square = jnp.zeros((LEN, 128), F32)
            cross = jnp.zeros((LEN, 128), F32)
            for p in range(PAIRS):
                lanes = cols(p)
                entered = state[:, lanes].astype(BF16)
                enter_ref[sub, :, lanes] = entered
                whole_y = mixed[there, lanes] + dot(basis_c, entered) * spread_heads(fade, p)
                mixed[there, lanes] = whole_y
                gate = gate_ref[rows, lanes]
                gated = whole_y * gate * jax.nn.sigmoid(gate)
                square = square + gated * gated
                cross = cross + gated * gain_ref[:, lanes] * db[there, lanes]
                state[:, lanes] = state[:, lanes] * spread_heads(whole, p) + fresh_ref[sub, :, lanes]
            sq = jnp.sum(square, axis=1, keepdims=True)
            cr = jnp.sum(cross, axis=1, keepdims=True)
            both = jnp.where(s == 0, sq, jnp.where(s == 1, cr, 0.0))
            sums[y, tile * subs + sub] = jnp.transpose(both)[0:8]

    @pl.when(step == 2 * TILES - 1)
    def _():
        flow.start("y0", "y1", "y2")

    @pl.when(step == 2 * TILES)
    def _():
        flow.wait("y0", "y1", "y2")
        state[...] = jnp.zeros_like(state)
        decay[...] = jnp.ones_like(decay)

    @pl.when(step >= 2 * TILES)
    def _():
        tile = 3 * TILES - 1 - step
        for sub in reversed(range(subs)):
            rows = slice(LEN * sub, LEN * sub + LEN)
            there = pl.ds(pl.multiple_of(tile * TILE + LEN * sub, LEN), LEN)
            chunk = tile * subs + sub
            total = sums[0, chunk] + sums[1, chunk] + sums[2, chunk] + sums[3, chunk]
            both = jnp.transpose(jnp.concatenate([total, jnp.zeros((120, 128), F32)], axis=0))
            r = lax.rsqrt(both[:, 0:1] * (1.0 / E_ALL) + EPS)
            slope = r * r * r * both[:, 1:2] * (1.0 / E_ALL)
            pos, cum = pos_ref[rows, :], cum_ref[rows, :]
            fade = jnp.where(pos > iota((LEN, 128), 0).astype(F32), jnp.exp2(cum), 0.0)
            whole = jnp.where(pos[LEN - 1 : LEN] > LEN - 1, jnp.exp2(cum[LEN - 1 : LEN]), 0.0)
            basis_t = jnp.transpose(xbc_ref[rows, HD + NS : CONV].astype(F32)).astype(BF16)
            for p in range(PAIRS):
                lanes = cols(p)
                mix, gate, grad = mixed[there, lanes], gate_ref[rows, lanes], db[there, lanes]
                gain = gain_ref[:, lanes]
                sig = jax.nn.sigmoid(gate)
                silu = gate * sig
                gated = mix * silu
                scaled = gated * r
                branch_ref[rows, lanes] = (scaled * gain).astype(BF16)
                acc_ref[0:8, lanes] += fold8(grad * scaled)
                dgated = r * gain * grad - gated * slope
                dmix = dgated * silu
                dgate_ref[rows, lanes] = (dgated * mix * sig * (1.0 + gate * (1.0 - sig))).astype(BF16)
                dmix_ref[rows, lanes] = dmix
                acc_ref[8:16, lanes] += fold8(dmix * xbc_ref[rows, lanes].astype(F32))
                fresh = dot(basis_t, (dmix * spread_heads(fade, p)).astype(BF16))
                gfresh_ref[sub, :, lanes] = fresh
                factor = spread_heads(whole, p)
                state[:, lanes] = state[:, lanes] * factor + fresh
                decay[:, lanes] = decay[:, lanes] * factor
        out_ref[...] = dot_nt(branch_ref[...], w_ref[...]).astype(BF16)

    @pl.when(step == 3 * TILES - 1)
    def _():
        gsumm_ref[0:NS, :] = state[...].astype(BF16)
        gsumm_ref[NS : NS + 16, :] = link_rows(decay[...])
        flow.finish()


def forward(summ, xbc, xdt, cum, pos, fresh, gate, cot, W, skip, gain):
    sub, end = TILE // LEN, TILES - 1

    def sweep(i):
        return jnp.where(i < TILES, i, jnp.where(i < 2 * TILES, i - TILES, 3 * TILES - 1 - i))

    def first(i):
        return jnp.minimum(i, end)

    def second(i):
        return jnp.clip(i - TILES, 0, end)

    def third(i):
        return jnp.minimum(3 * TILES - 1 - i, end)

    def both(i):
        return jnp.where(i < 2 * TILES, jnp.maximum(i - TILES, 0), 3 * TILES - 1 - i)

    def rows(c, at):
        return pl.BlockSpec((TILE, c), lambda i: (at(i), 0))

    def states(at):
        return pl.BlockSpec((sub, NS, HD), lambda i: (at(i), 0, 0))

    return pl.pallas_call(
        forward_kernel,
        grid=(3 * TILES,),
        in_specs=[
            pl.BlockSpec(memory_space=ANY), rows(CONV, sweep), rows(HD, first), rows(128, sweep), rows(128, sweep),
            states(second), rows(HD, both), rows(D, first), whole_spec(D, HD), whole_spec(1, HD), whole_spec(1, HD),
        ],
        out_specs=[
            states(second), rows(HD, third), rows(HD, third), rows(HD, third), rows(D, third), states(third),
            whole_spec(NS + 16, HD), whole_spec(16, HD),
        ],
        out_shape=[
            shape((CHUNKS, NS, HD), BF16), shape((ROWS, HD), BF16), shape((ROWS, HD), BF16), shape((ROWS, HD), F32),
            shape((ROWS, D), BF16), shape((CHUNKS, NS, HD), F32), shape((NS + 16, HD), BF16), shape((16, HD), F32),
        ],
        scratch_shapes=[
            pltpu.VMEM((ROWS, HD), F32), pltpu.VMEM((ROWS, HD), F32), pltpu.VMEM((NS, HD), F32), pltpu.VMEM((1, HD), F32),
            pltpu.VMEM((4, NS + 16, HD), BF16), pltpu.VMEM((4, CHUNKS, 8, 128), F32),
        ] + sems(8),
        compiler_params=comm_params(1, 60 << 20),
        name="forward",
    )(summ, xbc, xdt, cum, pos, fresh, gate, cot, W, skip, gain)


def add(a, b):
    return a.astype(F32) + b.astype(F32)


class Reduce:
    def __init__(self, flow, tag, bufs, halves):
        self.flow, self.tag, self.bufs = flow, tag, bufs
        G, K, RA, SA, TA, UA, VA, RB, SB, TB, UB, VB = bufs
        nA, nA1, nB, nB1 = halves
        self.A, self.B = pl.ds(0, nA), pl.ds(nA, nB)
        self.A1, self.A2 = pl.ds(0, nA1), pl.ds(nA1, nA - nA1)
        self.B1, self.B2 = pl.ds(0, nB1), pl.ds(nB1, nB - nB1)
        self.GB1, self.GB2 = pl.ds(nA, nB1), pl.ds(nA + nB1, nB - nB1)
        x, c, z, y = place()
        self.c, self.at = c, (x, z)
        xr, xl, xo = (x + 1) % 4, (x + 3) % 4, (x + 2) % 4
        zr, zl, zo = (z + 1) % 4, (z + 3) % 4, (z + 2) % 4
        self.xs, self.zs = (xr, xl, xo), (zr, zl, zo)
        dxr, dxl = device(xr, c, z, y), device(xl, c, z, y)
        dzr, dzl = device(x, c, zr, y), device(x, c, zl, y)
        A, B, A1, A2, B1, B2, GB1, GB2 = self.A, self.B, self.A1, self.A2, self.B1, self.B2, self.GB1, self.GB2

        def put(name, src, dst, to):
            flow.add(tag + name, src, dst, to)

        for k in range(4):
            put("k%d" % k, lambda k=k: G.at[k, 1 - c], lambda k=k: K.at[k], device(x, 1 - c, z, y))
        put("ra1", lambda: G.at[xo, c, :, :, A1], lambda: RA.at[:, :, A1], dxr)
        put("ra2", lambda: G.at[xo, c, :, :, A2], lambda: RA.at[:, :, A2], dxl)
        put("rb1", lambda: G.at[:, c, zo, :, GB1], lambda: RB.at[:, :, B1], dzr)
        put("rb2", lambda: G.at[:, c, zo, :, GB2], lambda: RB.at[:, :, B2], dzl)
        put("sar", lambda: G.at[xr, c, :, :, A], lambda: SA.at[0], dxr)
        put("sal", lambda: G.at[xl, c, :, :, A], lambda: SA.at[1], dxl)
        put("sbr", lambda: G.at[:, c, zr, :, B], lambda: SB.at[0], dzr)
        put("sbl", lambda: G.at[:, c, zl, :, B], lambda: SB.at[1], dzl)
        put("ta1", lambda: TA.at[zo, :, A1], lambda: UA.at[:, A1], dzr)
        put("ta2", lambda: TA.at[zo, :, A2], lambda: UA.at[:, A2], dzl)
        put("tb1", lambda: TB.at[xo, :, B1], lambda: UB.at[:, B1], dxr)
        put("tb2", lambda: TB.at[xo, :, B2], lambda: UB.at[:, B2], dxl)
        put("var", lambda: TA.at[zr], lambda: VA.at[0], dzr)
        put("val", lambda: TA.at[zl], lambda: VA.at[1], dzl)
        put("vbr", lambda: TB.at[xr], lambda: VB.at[0], dxr)
        put("vbl", lambda: TB.at[xl], lambda: VB.at[1], dxl)

    def start(self, *names):
        self.flow.start(*[self.tag + name for name in names])

    def wait(self, *names):
        self.flow.wait(*[self.tag + name for name in names])

    def cores(self, k):
        self.start("k%d" % k)

    def first(self):
        G, K = self.bufs[:2]
        for k in range(4):
            self.wait("k%d" % k)
            for j in range(4):
                G[k, self.c, j] = add(G[k, self.c, j], K[k, j]).astype(BF16)
        self.start("ra1", "rb1", "ra2", "rb2")

    def second(self):
        G, K, RA, SA, TA, UA, VA, RB, SB, TB, UB, VB = self.bufs
        c, (xr, xl, _), (zr, zl, _) = self.c, self.xs, self.zs
        self.wait("ra1")
        G[xr, c, :, :, self.A1] = add(G[xr, c, :, :, self.A1], RA[:, :, self.A1]).astype(BF16)
        self.start("sar")
        self.wait("rb1")
        G[:, c, zr, :, self.GB1] = add(G[:, c, zr, :, self.GB1], RB[:, :, self.B1]).astype(BF16)
        self.start("sbr")
        self.wait("ra2")
        G[xl, c, :, :, self.A2] = add(G[xl, c, :, :, self.A2], RA[:, :, self.A2]).astype(BF16)
        self.start("sal")
        self.wait("rb2")
        G[:, c, zl, :, self.GB2] = add(G[:, c, zl, :, self.GB2], RB[:, :, self.B2]).astype(BF16)
        self.start("sbl")

    def third(self):
        G, K, RA, SA, TA, UA, VA, RB, SB, TB, UB, VB = self.bufs
        c, (x, z) = self.c, self.at
        self.wait("sar", "sal")
        TA[...] = (G[x, c, :, :, self.A].astype(F32) + add(SA[0], SA[1])).astype(BF16)
        self.start("ta1", "ta2")
        self.wait("sbr", "sbl")
        TB[...] = (G[:, c, z, :, self.B].astype(F32) + add(SB[0], SB[1])).astype(BF16)
        self.start("tb1", "tb2")

    def fourth(self):
        G, K, RA, SA, TA, UA, VA, RB, SB, TB, UB, VB = self.bufs
        (xr, xl, _), (zr, zl, _) = self.xs, self.zs
        self.wait("ta1")
        TA[zr, :, self.A1] = add(TA[zr, :, self.A1], UA[:, self.A1]).astype(BF16)
        self.start("var")
        self.wait("ta2")
        TA[zl, :, self.A2] = add(TA[zl, :, self.A2], UA[:, self.A2]).astype(BF16)
        self.start("val")
        self.wait("tb1")
        TB[xr, :, self.B1] = add(TB[xr, :, self.B1], UB[:, self.B1]).astype(BF16)
        self.start("vbr")
        self.wait("tb2")
        TB[xl, :, self.B2] = add(TB[xl, :, self.B2], UB[:, self.B2]).astype(BF16)
        self.start("vbl")

    def last(self, out_ref):
        G, K, RA, SA, TA, UA, VA, RB, SB, TB, UB, VB = self.bufs
        x, z = self.at
        self.wait("vbr", "vbl")
        out_ref[:, self.B] = TB[x].astype(F32) + add(VB[0], VB[1])
        self.wait("var", "val")
        out_ref[:, self.A] = TA[z].astype(F32) + add(VA[0], VA[1])


def reduce_bufs(halves):
    nA, nA1, nB, nB1 = halves

    def half(n):
        return [
            pltpu.VMEM((4, 48, n), BF16), pltpu.VMEM((2, 4, 48, n), BF16), pltpu.VMEM((4, 48, n), BF16),
            pltpu.VMEM((48, n), BF16), pltpu.VMEM((2, 48, n), BF16),
        ]

    return [pltpu.VMEM((4, 2, 4, 48, nA + nB), BF16), pltpu.VMEM((4, 4, 48, nA + nB), BF16)] + half(nA) + half(nB)


class RowSum:
    def __init__(self, flow, tag, N, M, Q, first_from=None):
        self.flow, self.tag, self.bufs = flow, tag, (N, M, Q)
        x, c, z, y = place()
        self.yr, self.yl, self.yo, self.y = (y + 1) % 4, (y + 3) % 4, (y + 2) % 4, y
        right, left = device(x, c, z, self.yr), device(x, c, z, self.yl)
        source = N if first_from is None else first_from
        self.h1, self.h2 = pl.ds(0, 128), pl.ds(128, 128)
        flow.add(tag + "1", lambda: source.at[self.yo, self.h1], lambda: M.at[0], right)
        flow.add(tag + "2", lambda: source.at[self.yo, self.h2], lambda: M.at[1], left)
        flow.add(tag + "3", lambda: N.at[self.yr], lambda: Q.at[0], right)
        flow.add(tag + "4", lambda: N.at[self.yl], lambda: Q.at[1], left)

    def first(self):
        self.flow.start(self.tag + "1", self.tag + "2")

    def second(self):
        N, M, Q = self.bufs
        self.flow.wait(self.tag + "1")
        N[self.yr, self.h1] = add(N[self.yr, self.h1], M[0]).astype(BF16)
        self.flow.start(self.tag + "3")
        self.flow.wait(self.tag + "2")
        N[self.yl, self.h2] = add(N[self.yl, self.h2], M[1]).astype(BF16)
        self.flow.start(self.tag + "4")

    def last(self, out_ref):
        N, M, Q = self.bufs
        self.flow.wait(self.tag + "3", self.tag + "4")
        out_ref[...] = N[self.y].astype(F32) + add(Q[0], Q[1])


def row_bufs():
    return [pltpu.VMEM((4, 256, D), BF16), pltpu.VMEM((2, 128, D), BF16), pltpu.VMEM((2, 256, D), BF16)]


MID = (768, 384, 768, 384)
TAIL = (640, 384, 512, 256)
PRE = 4


def middle_kernel(
    gsumm_ref, out_ref, cot_ref, normed_ref, branch_ref, dgate_ref,
    xbc_ref, xdt_ref, dt_ref, cum_ref, sig_ref, dmix_ref, enter_ref, gfresh_ref, ds_ref, ci_ref, pos_ref,
    edge_ref, conv_ref, step_ref, skip_ref,
    din_ref, cgrad_ref, hgrad_ref, dedge_ref, gout_ref, share_ref,
    state, dacc, posn, summ, edge_out, edge_in, *rest,
):
    bufs, (N, M, Q, ssem, rsem, lsem) = rest[:-6], rest[-6:]
    step = pl.program_id(0)
    steps = PRE + CHUNKS
    x, c, z, y = place()
    flow = Flow(ssem, rsem)
    reduce = Reduce(flow, "g", bufs, MID)
    rows = RowSum(flow, "n", N, M, Q, out_ref)
    others_z = [device(x, c, (z + k) % 4, y) for k in (1, 3, 2)]
    for k in range(3):
        flow.add("s%d" % k, lambda: gsumm_ref, lambda: summ.at[z], others_z[k])
    flow.add("e", lambda: edge_out, lambda: edge_in, others_z[1])
    load_n = pltpu.make_async_copy(out_ref, N, lsem.at[0])
    load_s = pltpu.make_async_copy(gsumm_ref, summ.at[z], lsem.at[1])

    @pl.when(step == 0)
    def _():
        load_s.start()
        load_n.start()
        enter(
            others_z
            + [device((x + 1) % 4, c, z, y), device((x + 3) % 4, c, z, y)]
            + [device(x, c, z, (y + 1) % 4), device(x, c, z, (y + 3) % 4), device(x, 1 - c, z, y)]
        )
        flow.start("s0", "s1", "s2")
        rows.first()

    for k in range(PRE):

        @pl.when(step == k)
        def _():
            G = bufs[0]
            out = dot(jnp.transpose(cot_ref[...]), branch_ref[...]).astype(BF16)
            gate = dot(jnp.transpose(normed_ref[...]), dgate_ref[...]).astype(BF16)
            G[k, :, :, :, 0:HD] = out.reshape(2, 4, 48, HD)
            G[k, :, :, :, HD : 2 * HD] = gate.reshape(2, 4, 48, HD)
            reduce.cores(k)

    @pl.when(step == PRE)
    def _():
        flow.wait("s0", "s1", "s2")
        load_s.wait()
        start = jnp.zeros((NS, HD), F32)
        for j in (3, 2, 1):
            link = link_of(summ, j)
            start = jnp.where(j > z, start * link + summ[j, 0:NS, :].astype(F32), start)
        state[...] = start
        dacc[LEN : LEN + 8, :] = jnp.zeros((8, CONV), F32)
        posn[LEN : LEN + 8, :] = jnp.zeros((8, 128), F32)
        cgrad_ref[...] = jnp.zeros_like(cgrad_ref)
        hgrad_ref[...] = jnp.zeros_like(hgrad_ref)
        reduce.first()

    @pl.when(step == PRE + 1)
    def _():
        load_n.wait()
        rows.second()

    @pl.when(step == PRE + 2)
    def _():
        reduce.second()

    @pl.when(step == PRE + 5)
    def _():
        reduce.third()

    @pl.when(step == PRE + 6)
    def _():
        reduce.fourth()

    @pl.when(step > PRE)
    def _():
        dacc[LEN : LEN + 8, :] = dacc[0:8, :]
        posn[LEN : LEN + 8, :] = posn[0:8, :]

    @pl.when(step >= PRE)
    def _():
        back_chunk(
            xbc_ref, xdt_ref, dt_ref, cum_ref, sig_ref, dmix_ref, enter_ref, gfresh_ref, ds_ref, ci_ref, pos_ref,
            conv_ref, step_ref, skip_ref, din_ref, cgrad_ref, hgrad_ref, state, dacc, posn,
        )

    @pl.when(step == steps - 1)
    def _():
        dacc[8:16, :] = dacc[0:8, :]
        dacc[0:8, :] = jnp.zeros((8, CONV), F32)
        posn[8:16, :] = posn[0:8, :]
        posn[0:8, :] = jnp.zeros((8, 128), F32)
        for j in range(CONV // 128):
            lanes = cols(j)
            ci = edge_ref[:, lanes].astype(F32)[8:16]
            d_in = jnp.zeros((8, 128), F32)
            for back in (1, 2, 3):
                moved = jnp.where(posn[back : back + 8, :] >= back, dacc[back : back + 8, lanes], 0.0)
                d_in = d_in + moved * conv_ref[3 - back : 4 - back, lanes]
                cgrad_ref[8 * (3 - back) : 8 * (3 - back) + 8, lanes] += moved * ci
            edge_out[:, lanes] = d_in
        flow.start("e")
        reduce.last(gout_ref)
        rows.last(share_ref)
        flow.wait("e")
        dedge_ref[...] = edge_in[...]
        flow.finish()


def back_chunk(
    xbc_ref, xdt_ref, dt_ref, cum_ref, sig_ref, dmix_ref, enter_ref, gfresh_ref, ds_ref, ci_ref, pos_ref,
    conv_ref, step_ref, skip_ref, din_ref, cgrad_ref, hgrad_ref, state, dacc, posn,
):
    pos = pos_ref[...]
    posn[0:LEN, :] = pos
    row, lane = iota((LEN, LEN), 0), iota((LEN, LEN), 1)
    gap = (lane - row).astype(F32)
    keep = (gap >= 0) & (gap <= jnp.transpose(pos))
    cum, dt = cum_ref[...], dt_ref[...]
    cum_t = jnp.transpose(cum)
    last = cum[LEN - 1 : LEN]
    pos_last = pos[LEN - 1 : LEN]
    fade = jnp.where(pos > row.astype(F32), jnp.exp2(cum), 0.0)
    ends = jnp.where((LEN - 1) - row.astype(F32) <= pos_last, jnp.exp2(last - cum), 0.0)
    whole = jnp.where(pos_last > LEN - 1, jnp.exp2(last), 0.0)
    basis = xbc_ref[:, HD : HD + NS]
    basis_c = xbc_ref[:, HD + NS : CONV]
    inner = dot_nt(basis, basis_c)
    inner2 = jnp.concatenate([inner, inner], axis=1)
    d_inner = jnp.zeros((LEN, LEN), F32)
    d_b = jnp.zeros((LEN, NS), F32)
    d_c = jnp.zeros((LEN, NS), F32)
    into = jnp.zeros((LEN, 128), F32)
    direct = jnp.zeros((LEN, 128), F32)
    carry = jnp.zeros((LEN, 128), F32)
    later = jnp.zeros((LEN, 128), F32)
    across = jnp.zeros((8, 128), F32)
    sums_t = []
    for p in range(PAIRS):
        lanes = cols(p)
        xs = xbc_ref[:, lanes].astype(F32)
        xdt = xdt_ref[:, lanes]
        dy_wide = dmix_ref[:, lanes]
        dy, dy_low = in_two(dy_wide)
        entered = enter_ref[0, :, lanes]
        after = state[:, lanes]
        after_low = after.astype(BF16)
        dys = stacked(dy)
        spans = []
        for h in (2 * p, 2 * p + 1):
            spans.append(jnp.where(keep, cum_t[h : h + 1, :] - cum[:, h : h + 1], -1e30))
        decays = jnp.exp2(jnp.concatenate(spans, axis=1))
        scores = (decays * inner2).astype(BF16)
        d_scores = dot_nt(twice(xdt), jnp.concatenate([dys, stacked(dy_low)], axis=1)) * decays
        d_inner = d_inner + d_scores[:, :LEN] + d_scores[:, LEN:]
        prod = d_scores * inner2
        sums_t.append(jnp.sum(prod[:, :LEN], axis=0, keepdims=True))
        sums_t.append(jnp.sum(prod[:, LEN:], axis=0, keepdims=True))
        first = jnp.sum(prod[:, :LEN], axis=1, keepdims=True)
        second = jnp.sum(prod[:, LEN:], axis=1, keepdims=True)
        into = into + jnp.where(lane == 2 * p, first, jnp.where(lane == 2 * p + 1, second, 0.0))
        end_pair = spread_heads(ends, p)
        fade_pair = spread_heads(fade, p)
        z_state = dot(basis, after_low) * end_pair
        z = dot(scores, dys) + z_state
        direct = direct + head_sum(xs * z, p)
        later = later + head_sum(xdt.astype(F32) * z_state, p)
        carry = carry + head_sum(dy_wide * dot(basis_c, entered) * fade_pair, p)
        across = across + head_sum(fold8(after * entered.astype(F32)), p)
        d_x = spread_heads(dt, p) * z + skip_ref[:, lanes] * dy_wide
        dacc[0:LEN, lanes] = d_x * ds_ref[:, lanes]
        d_b = d_b + dot_nt(jnp.concatenate(in_two(xdt.astype(F32) * end_pair), axis=1), twice(after_low))
        d_c = d_c + dot_nt(jnp.concatenate(in_two(dy_wide * fade_pair), axis=1), twice(entered))
        state[:, lanes] = after * spread_heads(whole, p) + gfresh_ref[0, :, lanes]
    low = d_inner.astype(BF16)
    d_b = d_b + dot(low, basis_c)
    d_c = d_c + dot_tn(low, basis)
    dacc[0:LEN, HD : HD + NS] = d_b * ds_ref[:, HD : HD + NS]
    dacc[0:LEN, HD + NS : CONV] = d_c * ds_ref[:, HD + NS : CONV]
    out_of = jnp.transpose(jnp.concatenate(sums_t + [jnp.zeros((128 - HEADS, LEN), F32)], axis=0))
    d_rate = (
        dot_full(triangle("suffix"), out_of - into + carry)
        + dot_full(triangle("strict"), later)
        + whole * jnp.sum(across, axis=0, keepdims=True)
    )
    d_step = (direct + d_rate * step_ref[2:3, :]) * sig_ref[...]
    hgrad_ref[0:8, :] += fold8(d_rate * dt)
    hgrad_ref[8:16, :] += fold8(d_step)
    din_ref[:, CONV : CONV + 128] = d_step.astype(BF16)

    for j in range(CONV // 128):
        lanes = cols(j)
        here = dacc[0:LEN, lanes]
        ci = ci_ref[:, lanes].astype(F32)
        d_in = here * conv_ref[3:4, lanes]
        cgrad_ref[24:32, lanes] += fold8(here * ci)
        cgrad_ref[32:40, lanes] += fold8(here)
        for back in (1, 2, 3):
            moved = jnp.where(posn[back : back + LEN, :] >= back, dacc[back : back + LEN, lanes], 0.0)
            d_in = d_in + moved * conv_ref[3 - back : 4 - back, lanes]
            cgrad_ref[8 * (3 - back) : 8 * (3 - back) + 8, lanes] += fold8(moved * ci)
        din_ref[:, lanes] = d_in.astype(BF16)


def middle(
    gsumm, out, cot, normed, branch, dgate, xbc, xdt, dt, cum, sig, dmix, entered, gfresh, ds, ci, pos, edge, conv, step, skip
):
    top = CHUNKS - 1

    def chunk(i):
        return jnp.minimum(top + PRE - i, top)

    def rows(c):
        return pl.BlockSpec((LEN, c), lambda i: (chunk(i), 0))

    def tiles():
        return pl.BlockSpec((ROWS, D // PRE), lambda i: (0, jnp.minimum(i, PRE - 1)))

    state = pl.BlockSpec((1, NS, HD), lambda i: (chunk(i), 0, 0))
    anywhere = pl.BlockSpec(memory_space=ANY)
    return pl.pallas_call(
        middle_kernel,
        grid=(PRE + CHUNKS,),
        in_specs=[
            anywhere, anywhere, tiles(), tiles(), whole_spec(ROWS, HD), whole_spec(ROWS, HD),
            rows(CONV), rows(HD), rows(128), rows(128), rows(128), rows(HD), state, state, rows(CONV), rows(CONV), rows(128),
            whole_spec(16, CONV), whole_spec(8, CONV), whole_spec(8, 128), whole_spec(1, HD),
        ],
        out_specs=[
            rows(CONV + 128), whole_spec(40, CONV), whole_spec(16, 128), whole_spec(8, CONV), whole_spec(48, 2 * HD),
            whole_spec(256, D),
        ],
        out_shape=[
            shape((ROWS, CONV + 128), BF16), shape((40, CONV), F32), shape((16, 128), F32), shape((8, CONV), F32),
            shape((48, 2 * HD), F32), shape((256, D), F32),
        ],
        scratch_shapes=[
            pltpu.VMEM((NS, HD), F32), pltpu.VMEM((LEN + 8, CONV), F32), pltpu.VMEM((LEN + 8, 128), F32),
            pltpu.VMEM((4, NS + 16, HD), BF16), pltpu.VMEM((8, CONV), F32), pltpu.VMEM((8, CONV), F32),
        ] + reduce_bufs(MID) + row_bufs() + sems(32),
        compiler_params=comm_params(3, 60 << 20),
        cost_estimate=pl.CostEstimate(flops=40 * ROWS * HD * 128, bytes_accessed=30 << 20, transcendentals=2 * ROWS * CONV),
        name="middle",
    )(gsumm, out, cot, normed, branch, dgate, xbc, xdt, dt, cum, sig, dmix, entered, gfresh, ds, ci, pos, edge, conv, step, skip)


def tail_kernel(
    dgate_ref, din_ref, w_ref, x_ref, normed_ref, edge_ref, cgrad_ref, tgrad_ref, hgrad_ref,
    gout_ref, share_ref, ysum_ref, plane_ref, every_ref,
    dgate, din, w, xs, normed, small, HZ, HX, HC, HY, Y, *rest,
):
    bufs, (N, M, Q, ssem, rsem, lsem) = rest[:-6], rest[-6:]
    x, c, z, y = place()
    xs_other = [device((x + k) % 4, c, z, y) for k in (1, 3, 2)]
    zs_other = [device(x, c, (z + k) % 4, y) for k in (1, 3, 2)]
    ys_other = [device(x, c, z, (y + k) % 4) for k in (1, 3, 2)]
    core = device(x, 1 - c, z, y)
    loads = [
        pltpu.make_async_copy(src, dst, lsem.at[k])
        for k, (src, dst) in enumerate(
            [(w_ref.at[:, C_GATE:WIDE], w), (dgate_ref, dgate), (din_ref, din), (x_ref, xs), (normed_ref, normed)]
        )
    ]
    for load in loads:
        load.start()
    enter(xs_other + zs_other + ys_other + [core])
    flow = Flow(ssem, rsem)
    reduce = Reduce(flow, "g", bufs, TAIL)
    rows = RowSum(flow, "n", N, M, Q)
    for k in range(3):
        flow.add("hz%d" % k, lambda: HZ.at[z], lambda: HZ.at[z], zs_other[k])
        flow.add("hx%d" % k, lambda: HX.at[x], lambda: HX.at[x], xs_other[k])
        flow.add("hy%d" % k, lambda: HY.at[y], lambda: HY.at[y], ys_other[k])
        flow.add("y%d" % k, lambda: Y.at[y], lambda: Y.at[y], ys_other[k])
    flow.add("hc", lambda: HC.at[c], lambda: HC.at[c], core)

    for load in loads[:3]:
        load.wait()
    end = din[ROWS - 16 : ROWS, 0:CONV].astype(F32)
    more = jnp.concatenate([jnp.zeros((8, CONV), F32), edge_ref[...]], axis=0)
    din[ROWS - 16 : ROWS, 0:CONV] = (end + more).astype(BF16)

    for k in range(40):
        j = k % 8
        small[k : k + 1, :] = jnp.sum(cgrad_ref[8 * (k // 8) : 8 * (k // 8) + 8, cols(j)], axis=0, keepdims=True)
    for j in range(6):
        small[40 + j : 41 + j, :] = jnp.sum(tgrad_ref[0:8, cols(j)], axis=0, keepdims=True)
        small[58 + j : 59 + j, :] = jnp.sum(tgrad_ref[8:16, cols(j)], axis=0, keepdims=True)
    small[64:65, :] = jnp.sum(hgrad_ref[0:8, :], axis=0, keepdims=True)
    small[65:66, :] = jnp.sum(hgrad_ref[8:16, :], axis=0, keepdims=True)
    small[66:72, :] = jnp.zeros((6, 128), F32)

    gains = jnp.zeros((8, D), F32)
    for k, block in enumerate((rows.yo, rows.yr, rows.yl, rows.y)):
        here = pl.ds(pl.multiple_of(block * 256, 256), 256)
        grad = dot_nt(dgate[here, :], w[:, 0:HD]) + dot_nt(din[here, :], w[:, HD : WIDE - C_GATE])
        N[block] = grad.astype(BF16)
        if k == 0:
            rows.first()
            loads[3].wait()
        wide = xs[here, :].astype(F32)
        r = lax.rsqrt(jnp.mean(wide * wide, axis=1, keepdims=True) + EPS)
        gains = gains + fold8(grad * wide * r)
    gains = jnp.sum(gains, axis=0, keepdims=True)
    for j in range(12):
        small[46 + j : 47 + j, :] = gains[:, cols(j)]
    HZ[z] = small[...]
    flow.start("hz0", "hz1", "hz2")
    loads[4].wait()
    G = bufs[0]
    for k in range(4):
        part = dot(jnp.transpose(normed[:, 384 * k : 384 * k + 384]), din[...]).astype(BF16)
        G[k] = part.reshape(2, 4, 48, CONV + 128)
        reduce.cores(k)
        if k == 0:
            rows.second()
    flow.wait("hz0", "hz1", "hz2")
    HX[x] = HZ[0] + HZ[1] + HZ[2] + HZ[3]
    flow.start("hx0", "hx1", "hx2")
    reduce.first()
    flow.wait("hx0", "hx1", "hx2")
    HC[c] = HX[0] + HX[1] + HX[2] + HX[3]
    flow.start("hc")
    reduce.second()
    flow.wait("hc")
    total = HC[0] + HC[1]
    HY[y] = total
    plane_ref[...] = total
    flow.start("hy0", "hy1", "hy2")
    reduce.third()
    flow.wait("hy0", "hy1", "hy2")
    every_ref[...] = HY[0] + HY[1] + HY[2] + HY[3]
    reduce.fourth()
    reduce.last(gout_ref)
    Y[y] = gout_ref[:, HD:CONV]
    flow.start("y0", "y1", "y2")
    rows.last(share_ref)
    flow.wait("y0", "y1", "y2")
    ysum_ref[...] = Y[0] + Y[1] + Y[2] + Y[3]
    flow.finish()


def tail(dgate, din, W, X, normed, edge, cgrad, tgrad, hgrad):
    vmem = pl.BlockSpec(memory_space=pltpu.VMEM)
    table = pltpu.VMEM((4, 72, 128), F32)
    return pl.pallas_call(
        tail_kernel,
        out_shape=(
            shape((48, CONV + 128), F32), shape((256, D), F32), shape((48, 2 * NS), F32), shape((72, 128), F32),
            shape((72, 128), F32),
        ),
        in_specs=[pl.BlockSpec(memory_space=ANY)] * 5 + [vmem] * 4,
        out_specs=[vmem] * 5,
        scratch_shapes=[
            pltpu.VMEM((ROWS, HD), BF16), pltpu.VMEM((ROWS, CONV + 128), BF16), pltpu.VMEM((D, WIDE - C_GATE), BF16),
            pltpu.VMEM((ROWS, D), BF16), pltpu.VMEM((ROWS, D), BF16), pltpu.VMEM((72, 128), F32),
            table, table, pltpu.VMEM((2, 72, 128), F32), table, pltpu.VMEM((4, 48, 2 * NS), F32),
        ] + reduce_bufs(TAIL) + row_bufs() + [
            pltpu.SemaphoreType.DMA((48,)), pltpu.SemaphoreType.DMA((48,)), pltpu.SemaphoreType.DMA((8,)),
        ],
        compiler_params=comm_params(5, 60 << 20),
        name="tail",
    )(dgate, din, W, X, normed, edge, cgrad, tgrad, hgrad)


def finish_kernel(
    x_ref, cot_ref, out_ref, share_ref, gain_ref, mid_ref, tail_ref, ysum_ref,
    lout_ref, grad_ref, gate_ref, in_ref, wout_ref, bc_ref,
):
    own = x_ref[...].astype(F32)
    lout_ref[...] = (own + out_ref[...]).astype(BF16)
    scale = lax.rsqrt(jnp.mean(own * own, axis=1, keepdims=True) + EPS)
    weighted = share_ref[...] * gain_ref[...]
    slope = scale * scale * scale * jnp.mean(own * weighted, axis=1, keepdims=True)
    grad_ref[...] = scale * weighted - own * slope + cot_ref[...].astype(F32)
    gate_ref[...] = mid_ref[:, HD : 2 * HD]
    in_ref[...] = tail_ref[:, 0:HD]
    wout_ref[...] = jnp.transpose(mid_ref[:, 0:HD])
    bc_ref[...] = ysum_ref[...]


def finish(rows, cot, out, share, gain, mid, tail, ysum):
    return pl.pallas_call(
        finish_kernel,
        out_shape=(
            shape((256, D), BF16), shape((256, D), F32), shape((48, HD), F32), shape((48, HD), F32), shape((HD, 48), F32),
            shape((48, 2 * NS), F32),
        ),
        in_specs=[pl.BlockSpec(memory_space=pltpu.VMEM)] * 8,
        out_specs=[pl.BlockSpec(memory_space=pltpu.VMEM)] * 6,
        compiler_params=pltpu.CompilerParams(vmem_limit_bytes=40 << 20),
        name="finish",
    )(rows, cot, out, share, gain, mid, tail, ysum)


def per_device(
    layer_input, out_cotangent, seq_lengths, norm_gain, proj_gate, proj_input, proj_step, proj_state, conv_inner,
    conv_inner_bias, conv_state, conv_state_bias, decay_log, step_bias, skip_scale, gate_gain, proj_out,
):
    ctx = lax.axis_index("ctx")
    tp = lax.axis_index("tp")

    def column(a):
        return jnp.pad(a, ((0, 48 - a.shape[0]), (0, 0)))

    misc = jnp.concatenate(
        [
            proj_step, conv_inner.reshape(48, 2), column(conv_inner_bias), column(gate_gain), column(conv_state),
            column(conv_state_bias[None, :]), norm_gain[:, None], jnp.zeros((48, 93), BF16),
        ],
        axis=1,
    )
    pack = jnp.concatenate([proj_out.T, proj_gate, proj_input, proj_state, misc], axis=1)

    rate = -jnp.exp(decay_log)
    step = jnp.pad(jnp.stack([step_bias, rate * LOG2E, rate]), ((0, 5), (0, 128 - HEADS)))
    skip = jnp.repeat(skip_scale, 64)[None, :]
    (
        W, X, cots, normed, gate, ci, ds, xbc, xdt, dt, cum, sig, fresh, pos, edge, conv, gains, summ,
    ) = front(pack, layer_input, out_cotangent, seq_lengths, step)
    W, X, cot_all = W.reshape(D, WIDE), X.reshape(ROWS, D), cots.reshape(ROWS, D)
    ngain, gain = gains[0:1], gains[1:2, :HD]
    entered, branch, dgate, dmix, out, gfresh, gsumm, tgrad = forward(
        summ, xbc, xdt, cum, pos, fresh, gate, cot_all, W, skip, gain
    )
    din, cgrad, hgrad, dedge, gmid, out_share = middle(
        gsumm, out.reshape(4, 256, D), cot_all, normed, branch, dgate,
        xbc, xdt, dt, cum, sig, dmix, entered, gfresh, ds, ci, pos, edge, conv, step, skip,
    )
    gtail, share, ysum, plane, every = tail(dgate, din, W, X, normed, dedge, cgrad, tgrad, hgrad)
    layer_output, input_grad, d_gate, d_input, d_out, d_state = finish(
        layer_input, out_cotangent, out_share, share, ngain, gmid, gtail, ysum
    )
    block = lax.axis_index("shard") * 4 + ctx
    conv_sum = plane[:40].reshape(5, CONV)[:, :HD].reshape(5, HEADS, 64)
    conv_sum = lax.dynamic_slice_in_dim(conv_sum, block * 2, 2, 2)
    gain_sum = lax.dynamic_slice_in_dim(plane[40:46].reshape(HEADS, 64), block * 2, 2, 1)
    state_sum = lax.dynamic_slice_in_dim(every[:40].reshape(5, CONV)[:, HD:], block * 8 + tp * 2, 2, 1)
    return (
        layer_output,
        input_grad,
        lax.dynamic_slice_in_dim(every[46:58].reshape(D), block * 48 + tp * 12, 12, 0),
        d_gate,
        d_input,
        gtail[:, CONV : CONV + HEADS],
        lax.dynamic_slice_in_dim(d_state, tp * 12, 12, 0),
        conv_sum[:4],
        conv_sum[4],
        state_sum[:4],
        state_sum[4],
        plane[64, :HEADS] * rate,
        plane[65, :HEADS],
        plane[58:64].reshape(HEADS, 64).sum(axis=1),
        gain_sum,
        d_out,
    )


def solution(mesh):
    both = ("shard", "ctx")
    every = ("shard", "ctx", "tp")
    return jax.shard_map(
        per_device,
        mesh=mesh,
        in_specs=(
            P(every, None), P(every, None), P("shard", None), P(both), P(both, "tp"), P(both, "tp"), P(both, "tp"),
            P(both, None), P(None, "tp", both), P("tp", both), P(None, both), P(both), P("tp"), P("tp"), P("tp"),
            P("tp", both), P("tp", both),
        ),
        out_specs=(
            P(every, None), P(every, None), P(every), P(both, "tp"), P(both, "tp"), P(both, "tp"), P(every, None),
            P(None, "tp", both), P("tp", both), P(None, every), P(every), P("tp"), P("tp"), P("tp"), P("tp", both),
            P("tp", both),
        ),
        check_vma=False,
    )
```

```python
import functools

import jax
import jax.numpy as jnp
from jax import lax
from jax.experimental import pallas as pl
from jax.experimental.pallas import tpu as pltpu
from jax.sharding import PartitionSpec as P

MESH = pl.DeviceIdType.MESH
ANY = pl.ANY
F32 = jnp.float32
BF16 = jnp.bfloat16
EPS = 1e-05
LOG2E = 1.4426950408889634
HIGH = lax.Precision.HIGHEST

D = 1536
ROWS = 1024
HD = 768
HEADS = 12
PAIRS = 6
NS = 128
CONV = 1024
LEN = 128
CHUNKS = 8
E_ALL = 3072
C_OUT, C_GATE, C_IN, C_BC, C_MISC, WIDE = 0, 768, 1536, 2304, 2560, 2688
HALF_A, HALF_A1, HALF_B1 = 1408, 768, 2048


def dot(a, b):
    return jnp.dot(a, b, preferred_element_type=F32)


def dot_nt(a, b):
    return lax.dot_general(a, b, (((1,), (1,)), ((), ())), preferred_element_type=F32)


def dot_tn(a, b):
    return lax.dot_general(a, b, (((0,), (0,)), ((), ())), preferred_element_type=F32)


def dot_full(a, b):
    return jnp.dot(a, b, precision=HIGH, preferred_element_type=F32)


def iota(shape, axis):
    return lax.broadcasted_iota(jnp.int32, shape, axis)


def place():
    s = lax.axis_index("shard")
    return s // 2, s % 2, lax.axis_index("ctx"), lax.axis_index("tp")


def device(x, c, z, y):
    return {"shard": x * 2 + c, "ctx": z, "tp": y}


def enter(others):
    barrier = pltpu.get_barrier_semaphore()
    for other in others:
        pl.semaphore_signal(barrier, inc=1, device_id=other, device_id_type=MESH)
    pl.semaphore_wait(barrier, len(others))


class Sends:
    def __init__(self, send_sem, recv_sem):
        self.send_sem, self.recv_sem, self.copies = send_sem, recv_sem, []

    def __call__(self, src, dst, to):
        k = len(self.copies)
        copy = pltpu.make_async_remote_copy(
            src_ref=src,
            dst_ref=dst,
            send_sem=self.send_sem.at[k],
            recv_sem=self.recv_sem.at[k],
            device_id=to,
            device_id_type=MESH,
        )
        copy.start()
        self.copies.append(copy)
        return copy

    def finish(self):
        for copy in self.copies:
            copy.wait_send()


class Flow:
    def __init__(self, send_sem, recv_sem):
        self.send_sem, self.recv_sem, self.known = send_sem, recv_sem, {}

    def add(self, name, src, dst, to):
        self.known[name] = (len(self.known), src, dst, to)

    def copy(self, name):
        k, src, dst, to = self.known[name]
        return pltpu.make_async_remote_copy(
            src_ref=src(),
            dst_ref=dst(),
            send_sem=self.send_sem.at[k],
            recv_sem=self.recv_sem.at[k],
            device_id=to,
            device_id_type=MESH,
        )

    def start(self, *names):
        for name in names:
            self.copy(name).start()

    def wait(self, *names):
        for name in names:
            self.copy(name).wait_recv()

    def finish(self):
        for name in self.known:
            self.copy(name).wait_send()


def sems(n):
    return [pltpu.SemaphoreType.DMA((n,)), pltpu.SemaphoreType.DMA((n,)), pltpu.SemaphoreType.DMA((4,))]


def comm_params(collective_id, vmem=None):
    return pltpu.CompilerParams(
        collective_id=collective_id, has_side_effects=True, vmem_limit_bytes=vmem
    )


def shape(dims, kind):
    return jax.ShapeDtypeStruct(dims, kind)


def spread_heads(v, p):
    r = v.shape[0]
    low = jnp.broadcast_to(v[:, 2 * p : 2 * p + 1], (r, 128))
    high = jnp.broadcast_to(v[:, 2 * p + 1 : 2 * p + 2], (r, 128))
    return jnp.where(iota((r, 128), 1) < 64, low, high)


def cols(p):
    return slice(128 * p, 128 * p + 128)


def stacked(pair):
    lane = iota(pair.shape, 1)
    zero = jnp.zeros_like(pair)
    return jnp.concatenate([jnp.where(lane < 64, pair, zero), jnp.where(lane < 64, zero, pair)], axis=0)


def in_two(v):
    high = v.astype(BF16)
    return high, (v - high.astype(F32)).astype(BF16)


def twice(v):
    return jnp.concatenate([v, v], axis=1)


def link_rows(decay):
    high, low = in_two(jnp.broadcast_to(decay, (8, HD)))
    return jnp.concatenate([high, low], axis=0)


def link_of(summ_ref, j):
    both = summ_ref[j, NS : NS + 16, :].astype(F32)
    return both[0:1] + both[8:9]


def head_sum(pair, p):
    lane, head = iota((128, 128), 0), iota((128, 128), 1)
    pick = jnp.where(head == 2 * p + lane // 64, 1.0, 0.0).astype(BF16)
    return dot(pair.astype(BF16), pick)


def triangle(kind):
    t, s = iota((LEN, LEN), 0), iota((LEN, LEN), 1)
    keep = {"incl": s <= t, "suffix": s >= t, "strict": s < t}[kind]
    return jnp.where(keep, 1.0, 0.0).astype(F32)


def fold8(v):
    return jnp.sum(v.reshape(v.shape[0] // 8, 8, v.shape[1]), axis=0)


def whole_spec(*dims):
    return pl.BlockSpec(dims, lambda i: (0,) * len(dims), pipeline_mode=pl.Buffered(1))


def rows_spec(r, c, back=None):
    if back is None:
        return pl.BlockSpec((r, c), lambda i: (i, 0))
    return pl.BlockSpec((r, c), lambda i: (back - i, 0))


TILE = 256
TILES = ROWS // TILE


def gather(go, W, X, cots, x_ref, cot_ref, edge, locals_, between):
    x, c, z, y = place()
    xr, xl, xo = (x + 1) % 4, (x + 3) % 4, (x + 2) % 4
    zr, zl, zo = (z + 1) % 4, (z + 3) % 4, (z + 2) % 4
    yr, yl = (y + 1) % 4, (y + 3) % 4
    dxr, dxl = device(xr, c, z, y), device(xl, c, z, y)
    dzr, dzl = device(x, c, zr, y), device(x, c, zl, y)
    dyr, dyl = device(x, c, z, yr), device(x, c, z, yl)
    dco = device(x, 1 - c, z, y)
    own, own_x, own_c = locals_
    for copy in own:
        copy.start()
    own_x.start()
    own_c.start()
    others_z = [dzr, dzl, device(x, c, zo, y)]
    enter([dxr, dxl, dyr, dyl, dco] + others_z)
    A, A1, A2 = pl.ds(0, HALF_A), pl.ds(0, HALF_A1), pl.ds(HALF_A1, HALF_A - HALF_A1)
    B = pl.ds(HALF_A, WIDE - HALF_A)
    B1, B2 = pl.ds(HALF_A, HALF_B1 - HALF_A), pl.ds(HALF_B1, WIDE - HALF_B1)
    H1, H2 = pl.ds(0, 128), pl.ds(128, 128)

    def same(ref, to):
        return go(ref, ref, to)

    def both_x(zz):
        return same(W.at[x, c, zz, :, A], dxr), same(W.at[x, c, zz, :, A], dxl)

    def both_z(xx):
        return same(W.at[xx, c, z, :, B], dzr), same(W.at[xx, c, z, :, B], dzl)

    def on_x(xx, cols):
        return W.at[xx, c, :, :, cols]

    def on_z(zz, cols):
        return W.at[:, c, zz, :, cols]

    x_r = go(x_ref, X.at[y], dyr)
    x_l = go(x_ref, X.at[y], dyl)
    for copy in own:
        copy.wait()
    a_r = same(W.at[x, c, z, :, A], dzr)
    b_r = same(W.at[x, c, z, :, B], dxr)
    a_l = same(W.at[x, c, z, :, A], dzl)
    b_l = same(W.at[x, c, z, :, B], dxl)
    a2, b2, last = [both_x(z)], [both_z(x)], []
    a_r.wait_recv()
    a_fr = same(W.at[x, c, zl, :, A1], dzr)
    b_r.wait_recv()
    b_fr = same(W.at[xl, c, z, :, B1], dxr)
    a_l.wait_recv()
    a_fl = same(W.at[x, c, zr, :, A2], dzl)
    b_l.wait_recv()
    b_fl = same(W.at[xr, c, z, :, B2], dxl)
    a2.append(both_x(zl))
    b2.append(both_z(xl))
    a2.append(both_x(zr))
    b2.append(both_z(xr))
    a_fr.wait_recv()
    a_fl.wait_recv()
    a2.append(both_x(zo))
    b_fr.wait_recv()
    b_fl.wait_recv()
    b2.append(both_z(xo))
    last.append(same(on_x(x, A), dco))
    last.append(same(on_z(z, B), dco))
    fa, fb = [], []

    def onward(k):
        zz, xx = (z, zl, zr, zo)[k], (x, xl, xr, xo)[k]
        a2[k][0].wait_recv()
        fa.append(same(W.at[xl, c, zz, :, A1], dxr))
        b2[k][0].wait_recv()
        fb.append(same(W.at[xx, c, zl, :, B1], dzr))
        a2[k][1].wait_recv()
        fa.append(same(W.at[xr, c, zz, :, A2], dxl))
        b2[k][1].wait_recv()
        fb.append(same(W.at[xx, c, zr, :, B2], dzl))

    onward(0)
    between()
    onward(1)
    x_r.wait_recv()
    x_fr = same(X.at[yl, H1], dyr)
    x_l.wait_recv()
    x_fl = same(X.at[yr, H2], dyl)
    onward(2)
    onward(3)
    last.append(same(on_x(xl, A), dco))
    last.append(same(on_z(zl, B), dco))
    last.append(same(on_x(xr, A), dco))
    last.append(same(on_z(zr, B), dco))
    own_x.wait()
    x_fr.wait_recv()
    x_fl.wait_recv()
    e = go(X.at[3, pl.ds(240, 16)], edge, dzr)
    c_r = go(cot_ref, cots.at[y], dyr)
    c_l = go(cot_ref, cots.at[y], dyl)
    for k in (0, 2, 4, 6):
        fa[k].wait_recv()
    last.append(same(on_x(xo, A1), dco))
    for k in (0, 2, 4, 6):
        fb[k].wait_recv()
    last.append(same(on_z(zo, B1), dco))
    for k in (1, 3, 5, 7):
        fa[k].wait_recv()
    last.append(same(on_x(xo, A2), dco))
    for k in (1, 3, 5, 7):
        fb[k].wait_recv()
    last.append(same(on_z(zo, B2), dco))
    e.wait_recv()
    for copy in last:
        copy.wait_recv()
    more = []

    def cot_onward():
        c_r.wait_recv()
        more.append(same(cots.at[yl, H1], dyr))
        c_l.wait_recv()
        more.append(same(cots.at[yr, H2], dyl))

    def cot_end():
        own_c.wait()
        for copy in more:
            copy.wait_recv()

    return cot_onward, cot_end, others_z


def parts(v, size):
    q = jnp.floor((v + 0.5) * (1.0 / size))
    return q, v - size * q


def fiota(dims, axis):
    return iota(dims, axis).astype(F32)


def front_kernel(
    x_ref, cot_ref, wout_ref, gate_w, in_w, bc_w, lens_ref, ps_ref, ci_w, cb_w, gg_w, cs_w, csb_w, ng_w, dec_ref, sb_ref, skip_ref,
    W_out, X_out, cots, normed_ref, gate_ref, ci_ref, ds_ref, xbc_ref, xdt_ref, dt_ref, cum_ref, sig_ref, fresh_ref, pos_ref,
    summs_ref, edge_ref, conv_out, ngain_out, gain_out, step_ref,
    W, X, E, Q, normed, gate, ci, ds, xbc, xdt, dts, cums, sigs, fresh, pos, scale, buf0, buf1, conv, state, decay, table, summ,
    ssem, rsem, lsem, osem,
):
    x, c, z, y = place()
    go = Sends(ssem, rsem)
    own = [
        pltpu.make_async_copy(src, W.at[x, c, z, :, pl.ds(first, src.shape[1])], lsem.at[k])
        for k, (src, first) in enumerate([(wout_ref, C_OUT), (gate_w, C_GATE), (in_w, C_IN), (bc_w, C_BC)])
    ]
    locals_ = [
        own,
        pltpu.make_async_copy(x_ref, X.at[y], lsem.at[4]),
        pltpu.make_async_copy(cot_ref, cots.at[y], lsem.at[5]),
    ]
    table[...] = jnp.zeros_like(table)
    table[0:HEADS, 0:48] = ps_ref[...].astype(F32)
    for k in range(4):
        table[12 + 2 * k : 14 + 2 * k, 0:HEADS] = ci_w[k].astype(F32)
    table[20:22, 0:HEADS] = cb_w[...].astype(F32)
    table[22:24, 0:HEADS] = gg_w[...].astype(F32)
    table[24:28, 0:8] = cs_w[...].astype(F32)
    table[28:29, 0:8] = csb_w[...].astype(F32)
    table[29:30, 0:48] = ng_w[...].astype(F32)
    W[x, c, z, :, C_MISC:WIDE] = jnp.transpose(table[...])[0:48].astype(BF16)
    rate = -jnp.exp(dec_ref[...])
    step_ref[...] = jnp.zeros_like(step_ref)
    step_ref[0:1, 0:HEADS] = sb_ref[...]
    step_ref[1:2, 0:HEADS] = rate * LOG2E
    step_ref[2:3, 0:HEADS] = rate
    step_ref[3:4, 0:HEADS] = skip_ref[...]

    def between():
        block, inner = parts(fiota((D, HD), 0), 48)
        _, head = parts(inner, 12)
        place_of = head * 64 + block * 2
        lane = fiota((D, HD), 1)
        for j in range(2):
            Q[j] = jnp.where(lane == place_of + j, 1.0, 0.0).astype(BF16)
        token = fiota((ROWS, 128), 0) + (z * ROWS).astype(F32)
        begin = jnp.zeros((ROWS, 128), F32)
        end = jnp.float32(0.0)
        for k in range(3):
            end = end + lens_ref[0, k].astype(F32)
            begin = jnp.where(token >= end, end, begin)
        pos[...] = token - begin

    cot_onward, cot_end, others_z = gather(go, W, X, cots, x_ref, cot_ref, E, locals_, between)
    out_copies = [
        pltpu.make_async_copy(W, W_out, osem.at[0]),
        pltpu.make_async_copy(X, X_out, osem.at[1]),
    ]
    for copy in out_copies:
        copy.start()

    misc = W[:, :, :, :, C_MISC:WIDE].reshape(D, 128)
    row8, lane8 = iota((8, 128), 0), iota((8, 128), 1)

    def across(column):
        return dot_nt(jnp.where(lane8 == column, 1.0, 0.0).astype(BF16), misc)

    _, r_in = parts(fiota((8, D), 1), 48)
    found = jnp.zeros((8, HD), F32)
    for j in range(2):
        taps = jnp.where(r_in < HEADS, across(12 + 2 * row8 + j), 0.0)
        found = found + dot(taps.astype(BF16), Q[j])
    conv[:, 0:HD] = found
    rest = across(jnp.where(row8 < 4, 24 + row8, jnp.where(row8 == 4, 28, 29)))
    col_block, col8 = parts(fiota((D, 256), 1), 8)
    row_block, row_in = parts(fiota((D, 256), 0), 48)
    spot = jnp.where((row_block == col_block) & (row_in == col8), 1.0, 0.0).astype(BF16)
    conv[:, HD:CONV] = dot(rest.astype(BF16), spot)
    ngain = rest[5:6]
    conv_out[...] = conv[...]
    ngain_out[...] = ngain
    gain_out[...] = found[5:6]

    def norm(rows):
        wide = rows.astype(F32)
        r = lax.rsqrt(jnp.mean(wide * wide, axis=1, keepdims=True) + EPS)
        return (wide * r * ngain).astype(BF16)

    def weight(first, last):
        return W[:, :, :, :, first:last].reshape(D, last - first)

    edge = dot(norm(E[...]), weight(C_IN, C_MISC)).astype(BF16)
    edge_ref[...] = edge
    state[...] = jnp.zeros_like(state)
    decay[...] = jnp.ones_like(decay)
    bufs = (buf0, buf1)
    buf0[0:8, :] = edge.astype(F32)[8:16]

    def project(i):
        rows = slice(TILE * i, TILE * i + TILE)
        low = norm(X[i])
        normed[rows, :] = low
        gate[rows, :] = dot(low, weight(C_GATE, C_IN))
        conv_in = dot(low, weight(C_IN, C_MISC)).astype(BF16)
        ci[rows, :] = conv_in
        bufs[i % 2][8 : 8 + TILE, :] = conv_in.astype(F32)
        sigs[rows, :] = dot(low, weight(C_MISC, WIDE))

    def convolve(i):
        buf = bufs[i % 2]
        rows = slice(TILE * i, TILE * i + TILE)
        if i + 1 < TILES:
            bufs[(i + 1) % 2][0:8, :] = buf[TILE : TILE + 8, :]
        place_in = pos[rows, :]
        for j in range(CONV // 128):
            lanes = cols(j)
            acc = buf[8 : 8 + TILE, lanes] * conv[3:4, lanes] + conv[4:5, lanes]
            for back in (1, 2, 3):
                term = buf[8 - back : 8 - back + TILE, lanes] * conv[3 - back : 4 - back, lanes]
                acc = acc + jnp.where(place_in >= back, term, 0.0)
            sig = jax.nn.sigmoid(acc)
            ds[rows, lanes] = sig * (1.0 + acc * (1.0 - sig))
            xbc[rows, lanes] = (acc * sig).astype(BF16)
        lane = iota((TILE, 128), 1)
        pre = sigs[rows, :] + step_ref[0:1, :]
        small = jnp.exp(-jnp.abs(pre))
        log1p = jnp.where(
            small < 1e-3, small * (1.0 - 0.5 * small + (1.0 / 3.0) * small * small), jnp.log(1.0 + small)
        )
        dt = jnp.where(lane < HEADS, jnp.maximum(pre, 0.0) + log1p, 0.0)
        dts[rows, :] = dt
        sigs[rows, :] = jax.nn.sigmoid(pre)
        rate = dt * step_ref[1:2, :]
        for sub in range(TILE // LEN):
            inside = slice(LEN * sub, LEN * sub + LEN)
            rows = slice(TILE * i + LEN * sub, TILE * i + LEN * sub + LEN)
            cum = dot_full(triangle("incl"), rate[inside])
            cums[rows, :] = cum
            last = cum[LEN - 1 : LEN, :]
            pos_last = pos[TILE * i + LEN * sub + LEN - 1 : TILE * i + LEN * sub + LEN, :]
            row = iota((LEN, 128), 0).astype(F32)
            fade = jnp.where((LEN - 1) - row <= pos_last, jnp.exp2(last - cum), 0.0)
            whole = jnp.where(pos_last > LEN - 1, jnp.exp2(last), 0.0)
            basis_t = jnp.transpose(xbc[rows, HD : HD + NS].astype(F32)).astype(BF16)
            for p in range(PAIRS):
                low = (xbc[rows, cols(p)].astype(F32) * spread_heads(dt[inside], p)).astype(BF16)
                xdt[rows, cols(p)] = low
                ended = (low.astype(F32) * spread_heads(fade, p)).astype(BF16)
                new = dot(basis_t, ended)
                fresh[i * (TILE // LEN) + sub, :, cols(p)] = new
                factor = spread_heads(whole, p)
                state[:, cols(p)] = state[:, cols(p)] * factor + new
                decay[:, cols(p)] = decay[:, cols(p)] * factor

    pairs = [
        (normed, normed_ref), (gate, gate_ref), (ci, ci_ref), (ds, ds_ref), (xbc, xbc_ref), (xdt, xdt_ref), (dts, dt_ref),
        (cums, cum_ref), (sigs, sig_ref), (pos, pos_ref),
    ]

    def store(i):
        rows = slice(TILE * i, TILE * i + TILE)
        for k, (src, dst) in enumerate(pairs):
            out_copies.append(pltpu.make_async_copy(src.at[rows], dst.at[rows], osem.at[2 + 11 * i + k]))
        n = TILE // LEN
        here = slice(n * i, n * i + n)
        out_copies.append(pltpu.make_async_copy(fresh.at[here], fresh_ref.at[here], osem.at[2 + 11 * i + 10]))
        for copy in out_copies[-11:]:
            copy.start()

    project(0)
    for i in range(TILES):
        if i == 2:
            cot_onward()
        if i + 1 < TILES:
            project(i + 1)
        convolve(i)
        store(i)
    summ[0:NS, :] = state[...].astype(BF16)
    summ[NS : NS + 16, :] = link_rows(decay[...])
    swaps = [go(summ, summs_ref.at[z], other) for other in others_z]
    out_copies.append(pltpu.make_async_copy(summ, summs_ref.at[z], osem.at[46]))
    out_copies[-1].start()
    cot_end()
    for copy in swaps:
        copy.wait_recv()
    for copy in out_copies:
        copy.wait()
    go.finish()


def front(big, lens, small):
    vmem = pl.BlockSpec(memory_space=pltpu.VMEM)
    anywhere = pl.BlockSpec(memory_space=ANY)
    outs = [
        ((ROWS, D), BF16), ((ROWS, HD), F32), ((ROWS, CONV), BF16), ((ROWS, CONV), F32), ((ROWS, CONV), BF16),
        ((ROWS, HD), BF16), ((ROWS, 128), F32), ((ROWS, 128), F32), ((ROWS, 128), F32), ((CHUNKS, NS, HD), F32),
        ((ROWS, 128), F32),
    ]
    return pl.pallas_call(
        front_kernel,
        out_shape=[shape((4, 2, 4, 48, WIDE), BF16), shape((4, 256, D), BF16), shape((4, 256, D), BF16)]
        + [shape(*o) for o in outs]
        + [shape((4, NS + 16, HD), BF16), shape((16, CONV), BF16), shape((8, CONV), F32), shape((1, D), F32)]
        + [shape((1, HD), F32), shape((8, 128), F32)],
        in_specs=[anywhere] * 6 + [pl.BlockSpec(memory_space=pltpu.SMEM)] + [vmem] * 10,
        out_specs=[anywhere] * 15 + [vmem] * 5,
        scratch_shapes=[
            pltpu.VMEM((4, 2, 4, 48, WIDE), BF16), pltpu.VMEM((4, 256, D), BF16), pltpu.VMEM((16, D), BF16),
            pltpu.VMEM((2, D, HD), BF16),
        ]
        + [pltpu.VMEM(*o) for o in outs]
        + [
            pltpu.VMEM((ROWS, 128), F32), pltpu.VMEM((8 + TILE, CONV), F32), pltpu.VMEM((8 + TILE, CONV), F32),
            pltpu.VMEM((8, CONV), F32), pltpu.VMEM((NS, HD), F32), pltpu.VMEM((1, HD), F32),
            pltpu.VMEM((128, 128), F32), pltpu.VMEM((NS + 16, HD), BF16),
            pltpu.SemaphoreType.DMA((72,)), pltpu.SemaphoreType.DMA((72,)), pltpu.SemaphoreType.DMA((8,)),
            pltpu.SemaphoreType.DMA((48,)),
        ],
        compiler_params=comm_params(0, 60 << 20),
        name="front",
    )(*big, lens, *small)


LAG = 2


def forward_kernel(
    summ, xbc_ref, xdt_ref, cum_ref, pos_ref, fresh_ref, gate_ref, cot_ref, w_ref, step_ref, gain_ref,
    xbc2_ref, cum2_ref, pos2_ref, gate2_ref,
    enter_ref, branch_ref, dgate_ref, dmix_ref, out_ref, gfresh_ref, gsumm_ref, acc_ref,
    mixed, db, state, back, decay, sums, ssem, rsem,
):
    step = pl.program_id(0)
    x, c, z, y = place()
    subs = TILE // LEN
    flow = Flow(ssem, rsem)
    others_y = [device(x, c, z, (y + k) % 4) for k in (1, 3, 2)]
    for i in range(TILES):
        for k in range(3):
            there = lambda i=i: sums.at[y, pl.ds(subs * i, subs)]
            flow.add("y%d%d" % (i, k), there, there, others_y[k])

    @pl.when(step == 0)
    def _():
        enter(others_y)
        acc_ref[...] = jnp.zeros_like(acc_ref)
        start = jnp.zeros((NS, HD), F32)
        for j in range(3):
            start = jnp.where(j < z, start * link_of(summ, j) + summ[j, 0:NS, :].astype(F32), start)
        state[...] = start
        back[...] = jnp.zeros_like(back)
        decay[...] = jnp.ones_like(decay)

    @pl.when(step < TILES)
    def _():
        here = pl.ds(pl.multiple_of(step * TILE, TILE), TILE)
        db[here, :] = dot(cot_ref[...], w_ref[...])
        t, s = iota((LEN, LEN), 0), iota((LEN, LEN), 1)
        gap = (t - s).astype(F32)
        for sub in range(subs):
            rows = slice(LEN * sub, LEN * sub + LEN)
            there = pl.ds(pl.multiple_of(step * TILE + LEN * sub, LEN), LEN)
            pos, cum = pos_ref[rows, :], cum_ref[rows, :]
            keep = (gap >= 0) & (gap <= pos)
            cum_t = jnp.transpose(cum)
            basis_c = xbc_ref[rows, HD + NS : CONV]
            inner = dot_nt(basis_c, xbc_ref[rows, HD : HD + NS])
            fade = jnp.where(pos > t.astype(F32), jnp.exp2(cum), 0.0)
            whole = jnp.where(pos[LEN - 1 : LEN] > LEN - 1, jnp.exp2(cum[LEN - 1 : LEN]), 0.0)
            square = jnp.zeros((LEN, 128), F32)
            cross = jnp.zeros((LEN, 128), F32)
            for p in range(PAIRS):
                lanes = cols(p)
                entered = state[:, lanes].astype(BF16)
                enter_ref[sub, :, lanes] = entered
                parts = []
                for h in (2 * p, 2 * p + 1):
                    span = jnp.where(keep, cum[:, h : h + 1] - cum_t[h : h + 1, :], -1e30)
                    parts.append((jnp.exp2(span) * inner).astype(BF16))
                local = dot(jnp.concatenate(parts, axis=1), stacked(xdt_ref[rows, lanes]))
                out = local + dot(basis_c, entered) * spread_heads(fade, p)
                whole_y = out + spread_heads(step_ref[...], p)[3:4] * xbc_ref[rows, lanes].astype(F32)
                mixed[there, lanes] = whole_y
                gate = gate_ref[rows, lanes]
                gated = whole_y * gate * jax.nn.sigmoid(gate)
                square = square + gated * gated
                cross = cross + gated * gain_ref[:, lanes] * db[there, lanes]
                state[:, lanes] = state[:, lanes] * spread_heads(whole, p) + fresh_ref[sub, :, lanes]
            sq = jnp.sum(square, axis=1, keepdims=True)
            cr = jnp.sum(cross, axis=1, keepdims=True)
            both = jnp.where(s == 0, sq, jnp.where(s == 1, cr, 0.0))
            sums[y, step * subs + sub] = jnp.transpose(both)[0:8]

    for i in range(TILES):

        @pl.when(step == i)
        def _():
            flow.start("y%d0" % i, "y%d1" % i, "y%d2" % i)

        @pl.when(step == i + LAG)
        def _():
            flow.wait("y%d0" % i, "y%d1" % i, "y%d2" % i)

    @pl.when(step >= LAG)
    def _():
        tile = step - LAG
        for sub in range(subs):
            rows = slice(LEN * sub, LEN * sub + LEN)
            there = pl.ds(pl.multiple_of(tile * TILE + LEN * sub, LEN), LEN)
            chunk = tile * subs + sub
            total = sums[0, chunk] + sums[1, chunk] + sums[2, chunk] + sums[3, chunk]
            both = jnp.transpose(jnp.concatenate([total, jnp.zeros((120, 128), F32)], axis=0))
            r = lax.rsqrt(both[:, 0:1] * (1.0 / E_ALL) + EPS)
            slope = r * r * r * both[:, 1:2] * (1.0 / E_ALL)
            pos, cum = pos2_ref[rows, :], cum2_ref[rows, :]
            fade = jnp.where(pos > iota((LEN, 128), 0).astype(F32), jnp.exp2(cum), 0.0)
            whole = jnp.where(pos[LEN - 1 : LEN] > LEN - 1, jnp.exp2(cum[LEN - 1 : LEN]), 0.0)
            basis_t = jnp.transpose(xbc2_ref[rows, HD + NS : CONV].astype(F32)).astype(BF16)
            for p in range(PAIRS):
                lanes = cols(p)
                mix, gate, grad = mixed[there, lanes], gate2_ref[rows, lanes], db[there, lanes]
                gain = gain_ref[:, lanes]
                sig = jax.nn.sigmoid(gate)
                silu = gate * sig
                gated = mix * silu
                scaled = gated * r
                branch_ref[rows, lanes] = (scaled * gain).astype(BF16)
                acc_ref[0:8, lanes] += fold8(grad * scaled)
                dgated = r * gain * grad - gated * slope
                dmix = dgated * silu
                dgate_ref[rows, lanes] = (dgated * mix * sig * (1.0 + gate * (1.0 - sig))).astype(BF16)
                dmix_ref[rows, lanes] = dmix
                acc_ref[8:16, lanes] += fold8(dmix * xbc2_ref[rows, lanes].astype(F32))
                fresh = dot(basis_t, (dmix * spread_heads(fade, p)).astype(BF16))
                gfresh_ref[sub, :, lanes] = fresh
                back[:, lanes] = back[:, lanes] + decay[:, lanes] * fresh
                decay[:, lanes] = decay[:, lanes] * spread_heads(whole, p)
        out_ref[...] = dot_nt(branch_ref[...], w_ref[...]).astype(BF16)

    @pl.when(step == TILES + LAG - 1)
    def _():
        gsumm_ref[0:NS, :] = back[...].astype(BF16)
        gsumm_ref[NS : NS + 16, :] = link_rows(decay[...])
        flow.finish()


def forward(summs, xbc, xdt, cum, pos, fresh, gate, cot, W, step, gain):
    sub = TILE // LEN

    def first(i):
        return jnp.minimum(i, TILES - 1)

    def second(i):
        return jnp.maximum(i - LAG, 0)

    def rows(c, at):
        return pl.BlockSpec((TILE, c), lambda i: (at(i), 0))

    def states(at):
        return pl.BlockSpec((sub, NS, HD), lambda i: (at(i), 0, 0))

    return pl.pallas_call(
        forward_kernel,
        grid=(TILES + LAG,),
        in_specs=[
            whole_spec(4, NS + 16, HD), rows(CONV, first), rows(HD, first), rows(128, first), rows(128, first),
            states(first), rows(HD, first), rows(D, first), whole_spec(D, HD), whole_spec(8, 128), whole_spec(1, HD),
            rows(CONV, second), rows(128, second), rows(128, second), rows(HD, second),
        ],
        out_specs=[
            states(first), rows(HD, second), rows(HD, second), rows(HD, second), rows(D, second), states(second),
            whole_spec(NS + 16, HD), whole_spec(16, HD),
        ],
        out_shape=[
            shape((CHUNKS, NS, HD), BF16), shape((ROWS, HD), BF16), shape((ROWS, HD), BF16), shape((ROWS, HD), F32),
            shape((ROWS, D), BF16), shape((CHUNKS, NS, HD), F32), shape((NS + 16, HD), BF16), shape((16, HD), F32),
        ],
        scratch_shapes=[
            pltpu.VMEM((ROWS, HD), F32), pltpu.VMEM((ROWS, HD), F32), pltpu.VMEM((NS, HD), F32), pltpu.VMEM((NS, HD), F32),
            pltpu.VMEM((1, HD), F32), pltpu.VMEM((4, CHUNKS, 8, 128), F32),
            pltpu.SemaphoreType.DMA((16,)), pltpu.SemaphoreType.DMA((16,)),
        ],
        compiler_params=comm_params(1, 60 << 20),
        name="forward",
    )(summs, xbc, xdt, cum, pos, fresh, gate, cot, W, step, gain, xbc, cum, pos, gate)


def add(a, b):
    return a.astype(F32) + b.astype(F32)


class Reduce:
    def __init__(self, flow, tag, bufs, halves):
        self.flow, self.tag, self.bufs = flow, tag, bufs
        G, K, RA, SA, TA, UA, VA, RB, SB, TB, UB, VB = bufs
        nA, nA1, nB, nB1 = halves
        self.A, self.B = pl.ds(0, nA), pl.ds(nA, nB)
        self.A1, self.A2 = pl.ds(0, nA1), pl.ds(nA1, nA - nA1)
        self.B1, self.B2 = pl.ds(0, nB1), pl.ds(nB1, nB - nB1)
        self.GB1, self.GB2 = pl.ds(nA, nB1), pl.ds(nA + nB1, nB - nB1)
        x, c, z, y = place()
        self.c, self.at = c, (x, z)
        xr, xl, xo = (x + 1) % 4, (x + 3) % 4, (x + 2) % 4
        zr, zl, zo = (z + 1) % 4, (z + 3) % 4, (z + 2) % 4
        self.xs, self.zs = (xr, xl, xo), (zr, zl, zo)
        dxr, dxl = device(xr, c, z, y), device(xl, c, z, y)
        dzr, dzl = device(x, c, zr, y), device(x, c, zl, y)
        A, B, A1, A2, B1, B2, GB1, GB2 = self.A, self.B, self.A1, self.A2, self.B1, self.B2, self.GB1, self.GB2

        def put(name, src, dst, to):
            flow.add(tag + name, src, dst, to)

        for k in range(4):
            put("k%d" % k, lambda k=k: G.at[k, 1 - c], lambda k=k: K.at[k], device(x, 1 - c, z, y))
        put("ra1", lambda: G.at[xo, c, :, :, A1], lambda: RA.at[:, :, A1], dxr)
        put("ra2", lambda: G.at[xo, c, :, :, A2], lambda: RA.at[:, :, A2], dxl)
        put("rb1", lambda: G.at[:, c, zo, :, GB1], lambda: RB.at[:, :, B1], dzr)
        put("rb2", lambda: G.at[:, c, zo, :, GB2], lambda: RB.at[:, :, B2], dzl)
        put("sar", lambda: G.at[xr, c, :, :, A], lambda: SA.at[0], dxr)
        put("sal", lambda: G.at[xl, c, :, :, A], lambda: SA.at[1], dxl)
        put("sbr", lambda: G.at[:, c, zr, :, B], lambda: SB.at[0], dzr)
        put("sbl", lambda: G.at[:, c, zl, :, B], lambda: SB.at[1], dzl)
        put("ta1", lambda: TA.at[zo, :, A1], lambda: UA.at[:, A1], dzr)
        put("ta2", lambda: TA.at[zo, :, A2], lambda: UA.at[:, A2], dzl)
        put("tb1", lambda: TB.at[xo, :, B1], lambda: UB.at[:, B1], dxr)
        put("tb2", lambda: TB.at[xo, :, B2], lambda: UB.at[:, B2], dxl)
        put("var", lambda: TA.at[zr], lambda: VA.at[0], dzr)
        put("val", lambda: TA.at[zl], lambda: VA.at[1], dzl)
        put("vbr", lambda: TB.at[xr], lambda: VB.at[0], dxr)
        put("vbl", lambda: TB.at[xl], lambda: VB.at[1], dxl)

    def start(self, *names):
        self.flow.start(*[self.tag + name for name in names])

    def wait(self, *names):
        self.flow.wait(*[self.tag + name for name in names])

    def cores(self, k):
        self.start("k%d" % k)

    def first(self):
        G, K = self.bufs[:2]
        for k in range(4):
            self.wait("k%d" % k)
            for j in range(4):
                G[k, self.c, j] = G[k, self.c, j] + K[k, j]
        self.start("ra1", "rb1", "ra2", "rb2")

    def second(self):
        G, K, RA, SA, TA, UA, VA, RB, SB, TB, UB, VB = self.bufs
        c, (xr, xl, _), (zr, zl, _) = self.c, self.xs, self.zs
        self.wait("ra1")
        G[xr, c, :, :, self.A1] = G[xr, c, :, :, self.A1] + RA[:, :, self.A1]
        self.start("sar")
        self.wait("rb1")
        G[:, c, zr, :, self.GB1] = G[:, c, zr, :, self.GB1] + RB[:, :, self.B1]
        self.start("sbr")
        self.wait("ra2")
        G[xl, c, :, :, self.A2] = G[xl, c, :, :, self.A2] + RA[:, :, self.A2]
        self.start("sal")
        self.wait("rb2")
        G[:, c, zl, :, self.GB2] = G[:, c, zl, :, self.GB2] + RB[:, :, self.B2]
        self.start("sbl")

    def third(self):
        G, K, RA, SA, TA, UA, VA, RB, SB, TB, UB, VB = self.bufs
        c, (x, z) = self.c, self.at
        self.wait("sar", "sal")
        TA[...] = (G[x, c, :, :, self.A].astype(F32) + add(SA[0], SA[1])).astype(BF16)
        self.start("ta1", "ta2")
        self.wait("sbr", "sbl")
        TB[...] = (G[:, c, z, :, self.B].astype(F32) + add(SB[0], SB[1])).astype(BF16)
        self.start("tb1", "tb2")

    def fourth(self):
        G, K, RA, SA, TA, UA, VA, RB, SB, TB, UB, VB = self.bufs
        (xr, xl, _), (zr, zl, _) = self.xs, self.zs
        self.wait("ta1")
        TA[zr, :, self.A1] = TA[zr, :, self.A1] + UA[:, self.A1]
        self.start("var")
        self.wait("ta2")
        TA[zl, :, self.A2] = TA[zl, :, self.A2] + UA[:, self.A2]
        self.start("val")
        self.wait("tb1")
        TB[xr, :, self.B1] = TB[xr, :, self.B1] + UB[:, self.B1]
        self.start("vbr")
        self.wait("tb2")
        TB[xl, :, self.B2] = TB[xl, :, self.B2] + UB[:, self.B2]
        self.start("vbl")

    def last(self, out_ref):
        G, K, RA, SA, TA, UA, VA, RB, SB, TB, UB, VB = self.bufs
        x, z = self.at
        self.wait("vbr", "vbl")
        out_ref[:, self.B] = TB[x].astype(F32) + add(VB[0], VB[1])
        self.wait("var", "val")
        out_ref[:, self.A] = TA[z].astype(F32) + add(VA[0], VA[1])


def reduce_bufs(halves):
    nA, nA1, nB, nB1 = halves

    def half(n):
        return [
            pltpu.VMEM((4, 48, n), BF16), pltpu.VMEM((2, 4, 48, n), BF16), pltpu.VMEM((4, 48, n), BF16),
            pltpu.VMEM((48, n), BF16), pltpu.VMEM((2, 48, n), BF16),
        ]

    return [pltpu.VMEM((4, 2, 4, 48, nA + nB), BF16), pltpu.VMEM((4, 4, 48, nA + nB), BF16)] + half(nA) + half(nB)


class RowSum:
    def __init__(self, flow, tag, N, M, Q, first_from=None):
        self.flow, self.tag, self.bufs = flow, tag, (N, M, Q)
        x, c, z, y = place()
        self.yr, self.yl, self.yo, self.y = (y + 1) % 4, (y + 3) % 4, (y + 2) % 4, y
        right, left = device(x, c, z, self.yr), device(x, c, z, self.yl)
        source = N if first_from is None else first_from
        self.h1, self.h2 = pl.ds(0, 128), pl.ds(128, 128)
        flow.add(tag + "1", lambda: source.at[self.yo, self.h1], lambda: M.at[0], right)
        flow.add(tag + "2", lambda: source.at[self.yo, self.h2], lambda: M.at[1], left)
        flow.add(tag + "3", lambda: N.at[self.yr], lambda: Q.at[0], right)
        flow.add(tag + "4", lambda: N.at[self.yl], lambda: Q.at[1], left)

    def first(self):
        self.flow.start(self.tag + "1", self.tag + "2")

    def second(self):
        N, M, Q = self.bufs
        self.flow.wait(self.tag + "1")
        N[self.yr, self.h1] = N[self.yr, self.h1] + M[0]
        self.flow.start(self.tag + "3")
        self.flow.wait(self.tag + "2")
        N[self.yl, self.h2] = N[self.yl, self.h2] + M[1]
        self.flow.start(self.tag + "4")

    def last(self, out_ref):
        N, M, Q = self.bufs
        self.flow.wait(self.tag + "3", self.tag + "4")
        out_ref[...] = N[self.y].astype(F32) + add(Q[0], Q[1])


def row_bufs():
    return [pltpu.VMEM((4, 256, D), BF16), pltpu.VMEM((2, 128, D), BF16), pltpu.VMEM((2, 256, D), BF16)]


MID = (768, 384, 768, 384)
TAIL = (640, 384, 512, 256)
PRE = 4


def middle_kernel(
    gsumm_ref, out_ref, cot_ref, normed_ref, branch_ref, dgate_ref,
    xbc_ref, xdt_ref, dt_ref, cum_ref, sig_ref, dmix_ref, enter_ref, gfresh_ref, ds_ref, ci_ref, pos_ref,
    edge_ref, conv_ref, step_ref,
    din_ref, cgrad_ref, hgrad_ref, dedge_ref, gout_ref, share_ref,
    state, dacc, posn, summ, edge_out, edge_in, *rest,
):
    bufs, (N, M, Q, ssem, rsem, lsem) = rest[:-6], rest[-6:]
    step = pl.program_id(0)
    steps = PRE + CHUNKS
    x, c, z, y = place()
    flow = Flow(ssem, rsem)
    reduce = Reduce(flow, "g", bufs, MID)
    rows = RowSum(flow, "n", N, M, Q, out_ref)
    others_z = [device(x, c, (z + k) % 4, y) for k in (1, 3, 2)]
    for k in range(3):
        flow.add("s%d" % k, lambda: gsumm_ref, lambda: summ.at[z], others_z[k])
    flow.add("e", lambda: edge_out, lambda: edge_in, others_z[1])
    load_n = pltpu.make_async_copy(out_ref, N, lsem.at[0])
    load_s = pltpu.make_async_copy(gsumm_ref, summ.at[z], lsem.at[1])

    @pl.when(step == 0)
    def _():
        load_s.start()
        load_n.start()
        enter(
            others_z
            + [device((x + 1) % 4, c, z, y), device((x + 3) % 4, c, z, y)]
            + [device(x, c, z, (y + 1) % 4), device(x, c, z, (y + 3) % 4), device(x, 1 - c, z, y)]
        )
        flow.start("s0", "s1", "s2")
        rows.first()

    for k in range(PRE):

        @pl.when(step == k)
        def _():
            G = bufs[0]
            out = dot(jnp.transpose(cot_ref[...]), branch_ref[...]).astype(BF16)
            gate = dot(jnp.transpose(normed_ref[...]), dgate_ref[...]).astype(BF16)
            G[k, :, :, :, 0:HD] = out.reshape(2, 4, 48, HD)
            G[k, :, :, :, HD : 2 * HD] = gate.reshape(2, 4, 48, HD)
            reduce.cores(k)

    @pl.when(step == PRE)
    def _():
        flow.wait("s0", "s1", "s2")
        load_s.wait()
        start = jnp.zeros((NS, HD), F32)
        for j in (3, 2, 1):
            link = link_of(summ, j)
            start = jnp.where(j > z, start * link + summ[j, 0:NS, :].astype(F32), start)
        state[...] = start
        dacc[LEN : LEN + 8, :] = jnp.zeros((8, CONV), F32)
        posn[LEN : LEN + 8, :] = jnp.zeros((8, 128), F32)
        cgrad_ref[...] = jnp.zeros_like(cgrad_ref)
        hgrad_ref[...] = jnp.zeros_like(hgrad_ref)
        reduce.first()

    @pl.when(step == PRE + 1)
    def _():
        load_n.wait()
        rows.second()

    @pl.when(step == PRE + 2)
    def _():
        reduce.second()

    @pl.when(step == PRE + 5)
    def _():
        reduce.third()

    @pl.when(step == PRE + 6)
    def _():
        reduce.fourth()

    @pl.when(step > PRE)
    def _():
        dacc[LEN : LEN + 8, :] = dacc[0:8, :]
        posn[LEN : LEN + 8, :] = posn[0:8, :]

    @pl.when(step >= PRE)
    def _():
        back_chunk(
            xbc_ref, xdt_ref, dt_ref, cum_ref, sig_ref, dmix_ref, enter_ref, gfresh_ref, ds_ref, ci_ref, pos_ref,
            conv_ref, step_ref, din_ref, cgrad_ref, hgrad_ref, state, dacc, posn,
        )

    @pl.when(step == steps - 1)
    def _():
        dacc[8:16, :] = dacc[0:8, :]
        dacc[0:8, :] = jnp.zeros((8, CONV), F32)
        posn[8:16, :] = posn[0:8, :]
        posn[0:8, :] = jnp.zeros((8, 128), F32)
        for j in range(CONV // 128):
            lanes = cols(j)
            ci = edge_ref[:, lanes].astype(F32)[8:16]
            d_in = jnp.zeros((8, 128), F32)
            for back in (1, 2, 3):
                moved = jnp.where(posn[back : back + 8, :] >= back, dacc[back : back + 8, lanes], 0.0)
                d_in = d_in + moved * conv_ref[3 - back : 4 - back, lanes]
                cgrad_ref[8 * (3 - back) : 8 * (3 - back) + 8, lanes] += moved * ci
            edge_out[:, lanes] = d_in
        flow.start("e")
        reduce.last(gout_ref)
        rows.last(share_ref)
        flow.wait("e")
        dedge_ref[...] = edge_in[...]
        flow.finish()


def back_chunk(
    xbc_ref, xdt_ref, dt_ref, cum_ref, sig_ref, dmix_ref, enter_ref, gfresh_ref, ds_ref, ci_ref, pos_ref,
    conv_ref, step_ref, din_ref, cgrad_ref, hgrad_ref, state, dacc, posn,
):
    pos = pos_ref[...]
    posn[0:LEN, :] = pos
    row, lane = iota((LEN, LEN), 0), iota((LEN, LEN), 1)
    gap = (lane - row).astype(F32)
    keep = (gap >= 0) & (gap <= jnp.transpose(pos))
    cum, dt = cum_ref[...], dt_ref[...]
    cum_t = jnp.transpose(cum)
    last = cum[LEN - 1 : LEN]
    pos_last = pos[LEN - 1 : LEN]
    fade = jnp.where(pos > row.astype(F32), jnp.exp2(cum), 0.0)
    ends = jnp.where((LEN - 1) - row.astype(F32) <= pos_last, jnp.exp2(last - cum), 0.0)
    whole = jnp.where(pos_last > LEN - 1, jnp.exp2(last), 0.0)
    basis = xbc_ref[:, HD : HD + NS]
    basis_c = xbc_ref[:, HD + NS : CONV]
    inner = dot_nt(basis, basis_c)
    inner2 = jnp.concatenate([inner, inner], axis=1)
    d_inner = jnp.zeros((LEN, LEN), F32)
    d_b = jnp.zeros((LEN, NS), F32)
    d_c = jnp.zeros((LEN, NS), F32)
    into = jnp.zeros((LEN, 128), F32)
    direct = jnp.zeros((LEN, 128), F32)
    carry = jnp.zeros((LEN, 128), F32)
    later = jnp.zeros((LEN, 128), F32)
    across = jnp.zeros((8, 128), F32)
    sums_t = []
    for p in range(PAIRS):
        lanes = cols(p)
        xs = xbc_ref[:, lanes].astype(F32)
        xdt = xdt_ref[:, lanes]
        dy_wide = dmix_ref[:, lanes]
        dy, dy_low = in_two(dy_wide)
        entered = enter_ref[0, :, lanes]
        after = state[:, lanes]
        after_low = after.astype(BF16)
        dys = stacked(dy)
        spans = []
        for h in (2 * p, 2 * p + 1):
            spans.append(jnp.where(keep, cum_t[h : h + 1, :] - cum[:, h : h + 1], -1e30))
        decays = jnp.exp2(jnp.concatenate(spans, axis=1))
        scores = (decays * inner2).astype(BF16)
        d_scores = dot_nt(twice(xdt), jnp.concatenate([dys, stacked(dy_low)], axis=1)) * decays
        d_inner = d_inner + d_scores[:, :LEN] + d_scores[:, LEN:]
        prod = d_scores * inner2
        sums_t.append(jnp.sum(prod[:, :LEN], axis=0, keepdims=True))
        sums_t.append(jnp.sum(prod[:, LEN:], axis=0, keepdims=True))
        first = jnp.sum(prod[:, :LEN], axis=1, keepdims=True)
        second = jnp.sum(prod[:, LEN:], axis=1, keepdims=True)
        into = into + jnp.where(lane == 2 * p, first, jnp.where(lane == 2 * p + 1, second, 0.0))
        end_pair = spread_heads(ends, p)
        fade_pair = spread_heads(fade, p)
        z_state = dot(basis, after_low) * end_pair
        z = dot(scores, dys) + z_state
        direct = direct + head_sum(xs * z, p)
        later = later + head_sum(xdt.astype(F32) * z_state, p)
        carry = carry + head_sum(dy_wide * dot(basis_c, entered) * fade_pair, p)
        across = across + head_sum(fold8(after * entered.astype(F32)), p)
        d_x = spread_heads(dt, p) * z + spread_heads(step_ref[...], p)[3:4] * dy_wide
        dacc[0:LEN, lanes] = d_x * ds_ref[:, lanes]
        d_b = d_b + dot_nt(jnp.concatenate(in_two(xdt.astype(F32) * end_pair), axis=1), twice(after_low))
        d_c = d_c + dot_nt(jnp.concatenate(in_two(dy_wide * fade_pair), axis=1), twice(entered))
        state[:, lanes] = after * spread_heads(whole, p) + gfresh_ref[0, :, lanes]
    low = d_inner.astype(BF16)
    d_b = d_b + dot(low, basis_c)
    d_c = d_c + dot_tn(low, basis)
    dacc[0:LEN, HD : HD + NS] = d_b * ds_ref[:, HD : HD + NS]
    dacc[0:LEN, HD + NS : CONV] = d_c * ds_ref[:, HD + NS : CONV]
    out_of = jnp.transpose(jnp.concatenate(sums_t + [jnp.zeros((128 - HEADS, LEN), F32)], axis=0))
    d_rate = (
        dot_full(triangle("suffix"), out_of - into + carry)
        + dot_full(triangle("strict"), later)
        + whole * jnp.sum(across, axis=0, keepdims=True)
    )
    d_step = (direct + d_rate * step_ref[2:3, :]) * sig_ref[...]
    hgrad_ref[0:8, :] += fold8(d_rate * dt)
    hgrad_ref[8:16, :] += fold8(d_step)
    din_ref[:, CONV : CONV + 128] = d_step.astype(BF16)

    for j in range(CONV // 128):
        lanes = cols(j)
        here = dacc[0:LEN, lanes]
        ci = ci_ref[:, lanes].astype(F32)
        d_in = here * conv_ref[3:4, lanes]
        cgrad_ref[24:32, lanes] += fold8(here * ci)
        cgrad_ref[32:40, lanes] += fold8(here)
        for back in (1, 2, 3):
            moved = jnp.where(posn[back : back + LEN, :] >= back, dacc[back : back + LEN, lanes], 0.0)
            d_in = d_in + moved * conv_ref[3 - back : 4 - back, lanes]
            cgrad_ref[8 * (3 - back) : 8 * (3 - back) + 8, lanes] += fold8(moved * ci)
        din_ref[:, lanes] = d_in.astype(BF16)


def middle(
    gsumm, out, cot, normed, branch, dgate, xbc, xdt, dt, cum, sig, dmix, entered, gfresh, ds, ci, pos, edge, conv, step
):
    top = CHUNKS - 1

    def chunk(i):
        return jnp.minimum(top + PRE - i, top)

    def rows(c):
        return pl.BlockSpec((LEN, c), lambda i: (chunk(i), 0))

    def tiles():
        return pl.BlockSpec((ROWS, D // PRE), lambda i: (0, jnp.minimum(i, PRE - 1)))

    state = pl.BlockSpec((1, NS, HD), lambda i: (chunk(i), 0, 0))
    anywhere = pl.BlockSpec(memory_space=ANY)
    return pl.pallas_call(
        middle_kernel,
        grid=(PRE + CHUNKS,),
        in_specs=[
            anywhere, anywhere, tiles(), tiles(), whole_spec(ROWS, HD), whole_spec(ROWS, HD),
            rows(CONV), rows(HD), rows(128), rows(128), rows(128), rows(HD), state, state, rows(CONV), rows(CONV), rows(128),
            whole_spec(16, CONV), whole_spec(8, CONV), whole_spec(8, 128),
        ],
        out_specs=[
            rows(CONV + 128), whole_spec(40, CONV), whole_spec(16, 128), whole_spec(8, CONV), whole_spec(48, 2 * HD),
            whole_spec(256, D),
        ],
        out_shape=[
            shape((ROWS, CONV + 128), BF16), shape((40, CONV), F32), shape((16, 128), F32), shape((8, CONV), F32),
            shape((48, 2 * HD), F32), shape((256, D), F32),
        ],
        scratch_shapes=[
            pltpu.VMEM((NS, HD), F32), pltpu.VMEM((LEN + 8, CONV), F32), pltpu.VMEM((LEN + 8, 128), F32),
            pltpu.VMEM((4, NS + 16, HD), BF16), pltpu.VMEM((8, CONV), F32), pltpu.VMEM((8, CONV), F32),
        ] + reduce_bufs(MID) + row_bufs() + sems(32),
        compiler_params=comm_params(3, 60 << 20),
        cost_estimate=pl.CostEstimate(flops=40 * ROWS * HD * 128, bytes_accessed=30 << 20, transcendentals=2 * ROWS * CONV),
        name="middle",
    )(gsumm, out, cot, normed, branch, dgate, xbc, xdt, dt, cum, sig, dmix, entered, gfresh, ds, ci, pos, edge, conv, step)


def tail_kernel(
    dgate_ref, din_ref, w_ref, x_ref, normed_ref, edge_ref, cgrad_ref, tgrad_ref, hgrad_ref,
    gout_ref, share_ref, ysum_ref, plane_ref, every_ref,
    dgate, din, w, xs, normed, small, HZ, HX, HC, HY, Y, *rest,
):
    bufs, (N, M, Q, ssem, rsem, lsem) = rest[:-6], rest[-6:]
    x, c, z, y = place()
    xs_other = [device((x + k) % 4, c, z, y) for k in (1, 3, 2)]
    zs_other = [device(x, c, (z + k) % 4, y) for k in (1, 3, 2)]
    ys_other = [device(x, c, z, (y + k) % 4) for k in (1, 3, 2)]
    core = device(x, 1 - c, z, y)
    loads = [
        pltpu.make_async_copy(src, dst, lsem.at[k])
        for k, (src, dst) in enumerate(
            [(w_ref.at[:, C_GATE:WIDE], w), (dgate_ref, dgate), (din_ref, din), (x_ref, xs), (normed_ref, normed)]
        )
    ]
    for load in loads:
        load.start()
    enter(xs_other + zs_other + ys_other + [core])
    flow = Flow(ssem, rsem)
    reduce = Reduce(flow, "g", bufs, TAIL)
    rows = RowSum(flow, "n", N, M, Q)
    for k in range(3):
        flow.add("hz%d" % k, lambda: HZ.at[z], lambda: HZ.at[z], zs_other[k])
        flow.add("hx%d" % k, lambda: HX.at[x], lambda: HX.at[x], xs_other[k])
        flow.add("hy%d" % k, lambda: HY.at[y], lambda: HY.at[y], ys_other[k])
        flow.add("y%d" % k, lambda: Y.at[y], lambda: Y.at[y], ys_other[k])
    flow.add("hc", lambda: HC.at[c], lambda: HC.at[c], core)

    for load in loads[:3]:
        load.wait()
    end = din[ROWS - 16 : ROWS, 0:CONV].astype(F32)
    more = jnp.concatenate([jnp.zeros((8, CONV), F32), edge_ref[...]], axis=0)
    din[ROWS - 16 : ROWS, 0:CONV] = (end + more).astype(BF16)

    for k in range(40):
        j = k % 8
        small[k : k + 1, :] = jnp.sum(cgrad_ref[8 * (k // 8) : 8 * (k // 8) + 8, cols(j)], axis=0, keepdims=True)
    for j in range(6):
        small[40 + j : 41 + j, :] = jnp.sum(tgrad_ref[0:8, cols(j)], axis=0, keepdims=True)
        small[58 + j : 59 + j, :] = jnp.sum(tgrad_ref[8:16, cols(j)], axis=0, keepdims=True)
    small[64:65, :] = jnp.sum(hgrad_ref[0:8, :], axis=0, keepdims=True)
    small[65:66, :] = jnp.sum(hgrad_ref[8:16, :], axis=0, keepdims=True)
    small[66:72, :] = jnp.zeros((6, 128), F32)

    G = bufs[0]
    gains = []

    def row_block(block):
        here = pl.ds(pl.multiple_of(block * 256, 256), 256)
        grad = dot_nt(dgate[here, :], w[:, 0:HD]) + dot_nt(din[here, :], w[:, HD : WIDE - C_GATE])
        N[block] = grad.astype(BF16)
        return here, grad

    def gain_part(here, grad):
        wide = xs[here, :].astype(F32)
        r = lax.rsqrt(jnp.mean(wide * wide, axis=1, keepdims=True) + EPS)
        gains.append(fold8(grad * wide * r))

    kept = row_block(rows.yo)
    rows.first()
    loads[3].wait()
    gain_part(*kept)
    loads[4].wait()
    for k in range(4):
        part = dot(jnp.transpose(normed[:, 384 * k : 384 * k + 384]), din[...]).astype(BF16)
        G[k] = part.reshape(2, 4, 48, CONV + 128)
        reduce.cores(k)
    gain_part(*row_block(rows.yr))
    reduce.first()
    gain_part(*row_block(rows.yl))
    rows.second()
    gain_part(*row_block(rows.y))
    gains = jnp.sum(gains[0] + gains[1] + gains[2] + gains[3], axis=0, keepdims=True)
    for j in range(12):
        small[46 + j : 47 + j, :] = gains[:, cols(j)]
    HZ[z] = small[...]
    flow.start("hz0", "hz1", "hz2")
    reduce.second()
    flow.wait("hz0", "hz1", "hz2")
    HX[x] = HZ[0] + HZ[1] + HZ[2] + HZ[3]
    flow.start("hx0", "hx1", "hx2")
    flow.wait("hx0", "hx1", "hx2")
    HC[c] = HX[0] + HX[1] + HX[2] + HX[3]
    flow.start("hc")
    reduce.third()
    flow.wait("hc")
    total = HC[0] + HC[1]
    HY[y] = total
    plane_ref[...] = total
    flow.start("hy0", "hy1", "hy2")
    reduce.fourth()
    flow.wait("hy0", "hy1", "hy2")
    every_ref[...] = HY[0] + HY[1] + HY[2] + HY[3]
    reduce.last(gout_ref)
    Y[y] = gout_ref[:, HD:CONV]
    flow.start("y0", "y1", "y2")
    rows.last(share_ref)
    flow.wait("y0", "y1", "y2")
    ysum_ref[...] = Y[0] + Y[1] + Y[2] + Y[3]
    flow.finish()


def tail(dgate, din, W, X, normed, edge, cgrad, tgrad, hgrad):
    vmem = pl.BlockSpec(memory_space=pltpu.VMEM)
    table = pltpu.VMEM((4, 72, 128), F32)
    return pl.pallas_call(
        tail_kernel,
        out_shape=(
            shape((48, CONV + 128), F32), shape((256, D), F32), shape((48, 2 * NS), F32), shape((72, 128), F32),
            shape((72, 128), F32),
        ),
        in_specs=[pl.BlockSpec(memory_space=ANY)] * 5 + [vmem] * 4,
        out_specs=[vmem] * 5,
        scratch_shapes=[
            pltpu.VMEM((ROWS, HD), BF16), pltpu.VMEM((ROWS, CONV + 128), BF16), pltpu.VMEM((D, WIDE - C_GATE), BF16),
            pltpu.VMEM((ROWS, D), BF16), pltpu.VMEM((ROWS, D), BF16), pltpu.VMEM((72, 128), F32),
            table, table, pltpu.VMEM((2, 72, 128), F32), table, pltpu.VMEM((4, 48, 2 * NS), F32),
        ] + reduce_bufs(TAIL) + row_bufs() + [
            pltpu.SemaphoreType.DMA((48,)), pltpu.SemaphoreType.DMA((48,)), pltpu.SemaphoreType.DMA((8,)),
        ],
        compiler_params=comm_params(5, 60 << 20),
        name="tail",
    )(dgate, din, W, X, normed, edge, cgrad, tgrad, hgrad)


def finish_kernel(
    x_ref, cot_ref, out_ref, share_ref, gain_ref, mid_ref, tail_ref, ysum_ref, plane_ref, every_ref, step_ref,
    lout_ref, grad_ref, ngain_ref, gate_ref, in_ref, ps_ref, bc_ref, ci_ref, cb_ref, cs_ref, csb_ref, dec_ref, sb_ref,
    skip_ref, gg_ref, wout_ref,
):
    x, c, z, y = place()
    block = (((x * 2 + c) * 4) + z).astype(F32)
    tp = y.astype(F32)
    own = x_ref[...].astype(F32)
    lout_ref[...] = (own + out_ref[...]).astype(BF16)
    scale = lax.rsqrt(jnp.mean(own * own, axis=1, keepdims=True) + EPS)
    weighted = share_ref[...] * gain_ref[...]
    slope = scale * scale * scale * jnp.mean(own * weighted, axis=1, keepdims=True)
    grad_ref[...] = scale * weighted - own * slope + cot_ref[...].astype(F32)
    gate_ref[...] = mid_ref[:, HD : 2 * HD]
    in_ref[...] = tail_ref[:, 0:HD]
    wout_ref[...] = jnp.transpose(mid_ref[:, 0:HD])
    steps = jnp.concatenate([tail_ref[:, CONV : CONV + 128], jnp.zeros((80, 128), F32)], axis=0)
    ps_ref[...] = jnp.transpose(steps)[0:HEADS, 0:48]

    def one(keep):
        return jnp.where(keep, 1.0, 0.0).astype(F32)

    def full_nt(a, b):
        return lax.dot_general(a, b, (((1,), (1,)), ((), ())), precision=HIGH, preferred_element_type=F32)

    bc_ref[...] = dot_full(one(fiota((16, 48), 1) == fiota((16, 48), 0) + 12 * tp), ysum_ref[...])[0:12]
    plane, every = plane_ref[...], every_ref[...]
    lane, row = fiota((8, 128), 1), fiota((8, 128), 0)
    source, head = fiota((72, 128), 0), fiota((72, 128), 1)
    half, odd = parts(head, 2)
    picked = [full_nt(one(lane == 64 * q + 2 * block + row), plane) for q in (0, 1)]
    sums = [full_nt(one((lane >= 64 * q) & (lane < 64 * q + 64)), plane) for q in (0, 1)]

    def heads_of(first, rows):
        total = jnp.zeros((8, 128), F32)
        for q in (0, 1):
            total = total + dot_full(rows[q], one((source == first + half) & (odd == q)))
        return total

    for k in range(4):
        ci_ref[k] = heads_of(8 * k, picked)[0:2, 0:HEADS]
    cb_ref[...] = heads_of(32, picked)[0:2, 0:HEADS]
    gg_ref[...] = heads_of(40, picked)[0:2, 0:HEADS]
    skip_ref[...] = heads_of(58, sums)[0:1, 0:HEADS]
    dec_ref[...] = plane[64:65, 0:HEADS] * step_ref[2:3, 0:HEADS]
    sb_ref[...] = plane[65:66, 0:HEADS]
    at = 8 * block + 2 * tp
    upper, at = parts(at, 128)
    by_tap = full_nt(one(lane == at + row), every)
    cs_ref[...] = dot_full(by_tap, one(source == 8 * head + 6 + upper))[0:2, 0:4]
    rows8 = dot_full(one((fiota((8, 72), 1) == 8 * fiota((8, 72), 0) + 6 + upper)), every)
    csb_ref[...] = full_nt(rows8, one(fiota((128, 128), 1) == at + fiota((128, 128), 0)))[4:5, 0:2]
    flat = 48 * block + 12 * tp + head
    line, spot = parts(flat, 128)
    spread = full_nt(every, one(fiota((128, 128), 1) == spot[0:1].reshape(1, 128).T))
    ngain_ref[...] = jnp.sum(jnp.where(source == 46 + line, spread, 0.0), axis=0, keepdims=True)[:, 0:12]


def finish(*args):
    outs = [
        ((256, D), BF16), ((256, D), F32), ((1, 12), F32), ((48, HD), F32), ((48, HD), F32), ((HEADS, 48), F32),
        ((12, 2 * NS), F32), ((4, 2, HEADS), F32), ((2, HEADS), F32), ((2, 4), F32), ((1, 2), F32), ((1, HEADS), F32),
        ((1, HEADS), F32), ((1, HEADS), F32), ((2, HEADS), F32), ((HD, 48), F32),
    ]
    return pl.pallas_call(
        finish_kernel,
        grid=(1,),
        out_shape=[shape(*o) for o in outs],
        in_specs=[whole_spec(*a.shape) for a in args],
        out_specs=[whole_spec(*o[0]) for o in outs],
        compiler_params=pltpu.CompilerParams(vmem_limit_bytes=40 << 20),
        name="finish",
    )(*args)


def per_device(
    layer_input, out_cotangent, seq_lengths, norm_gain, proj_gate, proj_input, proj_step, proj_state, conv_inner,
    conv_inner_bias, conv_state, conv_state_bias, decay_log, step_bias, skip_scale, gate_gain, proj_out,
):
    (
        W, X, cots, normed, gate, ci, ds, xbc, xdt, dt, cum, sig, fresh, pos, summs, edge, conv, ngain, gain, step,
    ) = front(
        (layer_input, out_cotangent, proj_out.T, proj_gate, proj_input, proj_state),
        seq_lengths,
        (
            proj_step.T, conv_inner.transpose(0, 2, 1), conv_inner_bias.T, gate_gain.T, conv_state, conv_state_bias[None],
            norm_gain[None], decay_log[None], step_bias[None], skip_scale[None],
        ),
    )
    W, X, cot_all = W.reshape(D, WIDE), X.reshape(ROWS, D), cots.reshape(ROWS, D)
    entered, branch, dgate, dmix, out, gfresh, gsumm, tgrad = forward(
        summs, xbc, xdt, cum, pos, fresh, gate, cot_all, W, step, gain
    )
    din, cgrad, hgrad, dedge, gmid, out_share = middle(
        gsumm, out.reshape(4, 256, D), cot_all, normed, branch, dgate,
        xbc, xdt, dt, cum, sig, dmix, entered, gfresh, ds, ci, pos, edge, conv, step,
    )
    gtail, share, ysum, plane, every = tail(dgate, din, W, X, normed, dedge, cgrad, tgrad, hgrad)
    (
        layer_output, input_grad, g_norm, g_gate, g_in, g_step, g_state, g_conv, g_bias, g_cs, g_csb, g_decay, g_sb, g_skip,
        g_gain, g_out,
    ) = finish(layer_input, out_cotangent, out_share, share, ngain, gmid, gtail, ysum, plane, every, step)
    return (
        layer_output, input_grad, g_norm[0], g_gate, g_in, g_step.T, g_state, g_conv.transpose(0, 2, 1), g_bias.T, g_cs.T,
        g_csb[0], g_decay[0], g_sb[0], g_skip[0], g_gain.T, g_out,
    )


def solution(mesh):
    both = ("shard", "ctx")
    every = ("shard", "ctx", "tp")
    return jax.shard_map(
        per_device,
        mesh=mesh,
        in_specs=(
            P(every, None), P(every, None), P("shard", None), P(both), P(both, "tp"), P(both, "tp"), P(both, "tp"),
            P(both, None), P(None, "tp", both), P("tp", both), P(None, both), P(both), P("tp"), P("tp"), P("tp"),
            P("tp", both), P("tp", both),
        ),
        out_specs=(
            P(every, None), P(every, None), P(every), P(both, "tp"), P(both, "tp"), P(both, "tp"), P(every, None),
            P(None, "tp", both), P("tp", both), P(None, every), P(every), P("tp"), P("tp"), P("tp"), P("tp", both),
            P("tp", both),
        ),
        check_vma=False,
    )
```

```python
import functools

import jax
import jax.numpy as jnp
from jax import lax
from jax.experimental import pallas as pl
from jax.experimental.pallas import tpu as pltpu
from jax.sharding import PartitionSpec as P

MESH = pl.DeviceIdType.MESH
ANY = pl.ANY
F32 = jnp.float32
BF16 = jnp.bfloat16
EPS = 1e-05
LOG2E = 1.4426950408889634
HIGH = lax.Precision.HIGHEST

D = 1536
ROWS = 1024
HD = 768
HEADS = 12
PAIRS = 6
NS = 128
CONV = 1024
LEN = 128
CHUNKS = 8
E_ALL = 3072
C_OUT, C_GATE, C_IN, C_BC, C_MISC, WIDE = 0, 768, 1536, 2304, 2560, 2688
HALF_A, HALF_A1, HALF_B1 = 1408, 768, 2048


def dot(a, b):
    return jnp.dot(a, b, preferred_element_type=F32)


def dot_nt(a, b):
    return lax.dot_general(a, b, (((1,), (1,)), ((), ())), preferred_element_type=F32)


def dot_tn(a, b):
    return lax.dot_general(a, b, (((0,), (0,)), ((), ())), preferred_element_type=F32)


def dot_full(a, b):
    return jnp.dot(a, b, precision=HIGH, preferred_element_type=F32)


def iota(shape, axis):
    return lax.broadcasted_iota(jnp.int32, shape, axis)


def place():
    s = lax.axis_index("shard")
    return s // 2, s % 2, lax.axis_index("ctx"), lax.axis_index("tp")


def device(x, c, z, y):
    return {"shard": x * 2 + c, "ctx": z, "tp": y}


def enter(others):
    barrier = pltpu.get_barrier_semaphore()
    for other in others:
        pl.semaphore_signal(barrier, inc=1, device_id=other, device_id_type=MESH)
    pl.semaphore_wait(barrier, len(others))


class Sends:
    def __init__(self, send_sem, recv_sem):
        self.send_sem, self.recv_sem, self.copies = send_sem, recv_sem, []

    def __call__(self, src, dst, to):
        k = len(self.copies)
        copy = pltpu.make_async_remote_copy(
            src_ref=src,
            dst_ref=dst,
            send_sem=self.send_sem.at[k],
            recv_sem=self.recv_sem.at[k],
            device_id=to,
            device_id_type=MESH,
        )
        copy.start()
        self.copies.append(copy)
        return copy

    def finish(self):
        for copy in self.copies:
            copy.wait_send()


class Flow:
    def __init__(self, send_sem, recv_sem):
        self.send_sem, self.recv_sem, self.known = send_sem, recv_sem, {}

    def add(self, name, src, dst, to):
        self.known[name] = (len(self.known), src, dst, to)

    def copy(self, name):
        k, src, dst, to = self.known[name]
        return pltpu.make_async_remote_copy(
            src_ref=src(),
            dst_ref=dst(),
            send_sem=self.send_sem.at[k],
            recv_sem=self.recv_sem.at[k],
            device_id=to,
            device_id_type=MESH,
        )

    def start(self, *names):
        for name in names:
            self.copy(name).start()

    def wait(self, *names):
        for name in names:
            self.copy(name).wait_recv()

    def finish(self):
        for name in self.known:
            self.copy(name).wait_send()


def sems(n):
    return [pltpu.SemaphoreType.DMA((n,)), pltpu.SemaphoreType.DMA((n,)), pltpu.SemaphoreType.DMA((4,))]


def comm_params(collective_id, vmem=None):
    return pltpu.CompilerParams(
        collective_id=collective_id, has_side_effects=True, vmem_limit_bytes=vmem
    )


def shape(dims, kind):
    return jax.ShapeDtypeStruct(dims, kind)


def spread_heads(v, p):
    r = v.shape[0]
    low = jnp.broadcast_to(v[:, 2 * p : 2 * p + 1], (r, 128))
    high = jnp.broadcast_to(v[:, 2 * p + 1 : 2 * p + 2], (r, 128))
    return jnp.where(iota((r, 128), 1) < 64, low, high)


def cols(p):
    return slice(128 * p, 128 * p + 128)


def stacked(pair):
    lane = iota(pair.shape, 1)
    zero = jnp.zeros_like(pair)
    return jnp.concatenate([jnp.where(lane < 64, pair, zero), jnp.where(lane < 64, zero, pair)], axis=0)


def in_two(v):
    high = v.astype(BF16)
    return high, (v - high.astype(F32)).astype(BF16)


def twice(v):
    return jnp.concatenate([v, v], axis=1)


def link_rows(decay):
    high, low = in_two(jnp.broadcast_to(decay, (8, HD)))
    return jnp.concatenate([high, low], axis=0)


def link_of(summ_ref, j):
    both = summ_ref[j, NS : NS + 16, :].astype(F32)
    return both[0:1] + both[8:9]


def head_pick(p):
    lane, head = iota((128, 128), 0), iota((128, 128), 1)
    return jnp.where(head == 2 * p + lane // 64, 1.0, 0.0).astype(BF16)


def head_sum(pair, p):
    return dot(pair.astype(BF16), head_pick(p))


def triangle(kind):
    t, s = iota((LEN, LEN), 0), iota((LEN, LEN), 1)
    keep = {"incl": s <= t, "suffix": s >= t, "strict": s < t}[kind]
    return jnp.where(keep, 1.0, 0.0).astype(F32)


def fold8(v):
    return jnp.sum(v.reshape(v.shape[0] // 8, 8, v.shape[1]), axis=0)


def whole_spec(*dims):
    return pl.BlockSpec(dims, lambda i: (0,) * len(dims), pipeline_mode=pl.Buffered(1))


def rows_spec(r, c, back=None):
    if back is None:
        return pl.BlockSpec((r, c), lambda i: (i, 0))
    return pl.BlockSpec((r, c), lambda i: (back - i, 0))


TILE = 256
TILES = ROWS // TILE


def gather(go, W, X, cots, x_ref, cot_ref, edge, locals_, between):
    x, c, z, y = place()
    xr, xl, xo = (x + 1) % 4, (x + 3) % 4, (x + 2) % 4
    zr, zl, zo = (z + 1) % 4, (z + 3) % 4, (z + 2) % 4
    yr, yl = (y + 1) % 4, (y + 3) % 4
    dxr, dxl = device(xr, c, z, y), device(xl, c, z, y)
    dzr, dzl = device(x, c, zr, y), device(x, c, zl, y)
    dyr, dyl = device(x, c, z, yr), device(x, c, z, yl)
    dco = device(x, 1 - c, z, y)
    own, own_x, own_c = locals_
    for copy in own:
        copy.start()
    own_x.start()
    own_c.start()
    others_z = [dzr, dzl, device(x, c, zo, y)]
    enter([dxr, dxl, dyr, dyl, dco] + others_z)
    A, A1, A2 = pl.ds(0, HALF_A), pl.ds(0, HALF_A1), pl.ds(HALF_A1, HALF_A - HALF_A1)
    B = pl.ds(HALF_A, WIDE - HALF_A)
    B1, B2 = pl.ds(HALF_A, HALF_B1 - HALF_A), pl.ds(HALF_B1, WIDE - HALF_B1)
    H1, H2 = pl.ds(0, 128), pl.ds(128, 128)

    def same(ref, to):
        return go(ref, ref, to)

    def both_x(zz):
        return same(W.at[x, c, zz, :, A], dxr), same(W.at[x, c, zz, :, A], dxl)

    def both_z(xx):
        return same(W.at[xx, c, z, :, B], dzr), same(W.at[xx, c, z, :, B], dzl)

    def on_x(xx, cols):
        return W.at[xx, c, :, :, cols]

    def on_z(zz, cols):
        return W.at[:, c, zz, :, cols]

    x_r = go(x_ref, X.at[y], dyr)
    x_l = go(x_ref, X.at[y], dyl)
    for copy in own:
        copy.wait()
    a_r = same(W.at[x, c, z, :, A], dzr)
    b_r = same(W.at[x, c, z, :, B], dxr)
    a_l = same(W.at[x, c, z, :, A], dzl)
    b_l = same(W.at[x, c, z, :, B], dxl)
    a2, b2, last = [both_x(z)], [both_z(x)], []
    a_r.wait_recv()
    a_fr = same(W.at[x, c, zl, :, A1], dzr)
    b_r.wait_recv()
    b_fr = same(W.at[xl, c, z, :, B1], dxr)
    a_l.wait_recv()
    a_fl = same(W.at[x, c, zr, :, A2], dzl)
    b_l.wait_recv()
    b_fl = same(W.at[xr, c, z, :, B2], dxl)
    a2.append(both_x(zl))
    b2.append(both_z(xl))
    a2.append(both_x(zr))
    b2.append(both_z(xr))
    a_fr.wait_recv()
    a_fl.wait_recv()
    a2.append(both_x(zo))
    b_fr.wait_recv()
    b_fl.wait_recv()
    b2.append(both_z(xo))
    last.append(same(on_x(x, A), dco))
    last.append(same(on_z(z, B), dco))
    fa, fb = [], []

    def onward(k):
        zz, xx = (z, zl, zr, zo)[k], (x, xl, xr, xo)[k]
        a2[k][0].wait_recv()
        fa.append(same(W.at[xl, c, zz, :, A1], dxr))
        b2[k][0].wait_recv()
        fb.append(same(W.at[xx, c, zl, :, B1], dzr))
        a2[k][1].wait_recv()
        fa.append(same(W.at[xr, c, zz, :, A2], dxl))
        b2[k][1].wait_recv()
        fb.append(same(W.at[xx, c, zr, :, B2], dzl))

    onward(0)
    between()
    onward(1)
    x_r.wait_recv()
    x_fr = same(X.at[yl, H1], dyr)
    x_l.wait_recv()
    x_fl = same(X.at[yr, H2], dyl)
    onward(2)
    onward(3)
    last.append(same(on_x(xl, A), dco))
    last.append(same(on_z(zl, B), dco))
    last.append(same(on_x(xr, A), dco))
    last.append(same(on_z(zr, B), dco))
    own_x.wait()
    x_fr.wait_recv()
    x_fl.wait_recv()
    e = go(X.at[3, pl.ds(240, 16)], edge, dzr)
    c_r = go(cot_ref, cots.at[y], dyr)
    c_l = go(cot_ref, cots.at[y], dyl)
    for k in (0, 2, 4, 6):
        fa[k].wait_recv()
    last.append(same(on_x(xo, A1), dco))
    for k in (0, 2, 4, 6):
        fb[k].wait_recv()
    last.append(same(on_z(zo, B1), dco))
    for k in (1, 3, 5, 7):
        fa[k].wait_recv()
    last.append(same(on_x(xo, A2), dco))
    for k in (1, 3, 5, 7):
        fb[k].wait_recv()
    last.append(same(on_z(zo, B2), dco))
    e.wait_recv()
    for copy in last:
        copy.wait_recv()
    more = []

    def cot_onward():
        c_r.wait_recv()
        more.append(same(cots.at[yl, H1], dyr))
        c_l.wait_recv()
        more.append(same(cots.at[yr, H2], dyl))

    def cot_end():
        own_c.wait()
        for copy in more:
            copy.wait_recv()

    return cot_onward, cot_end, others_z


def parts(v, size):
    q = jnp.floor((v + 0.5) * (1.0 / size))
    return q, v - size * q


def fiota(dims, axis):
    return iota(dims, axis).astype(F32)


def front_kernel(
    x_ref, cot_ref, wout_ref, gate_w, in_w, bc_w, lens_ref, ps_ref, ci_w, cb_w, gg_w, cs_w, csb_w, ng_w, dec_ref, sb_ref, skip_ref,
    W_out, X_out, cots, normed_ref, gate_ref, ci_ref, ds_ref, xbc_ref, xdt_ref, dt_ref, cum_ref, sig_ref, fresh_ref, pos_ref,
    near_ref, summs_ref, edge_ref, conv_out, ngain_out, gain_out, step_ref,
    W, X, E, Q, normed, gate, ci, ds, xbc, xdt, dts, cums, sigs, fresh, pos, scale, buf0, buf1, conv, state, decay, table, summ, near,
    ssem, rsem, lsem, osem,
):
    x, c, z, y = place()
    go = Sends(ssem, rsem)
    own = [
        pltpu.make_async_copy(src, W.at[x, c, z, :, pl.ds(first, src.shape[1])], lsem.at[k])
        for k, (src, first) in enumerate([(wout_ref, C_OUT), (gate_w, C_GATE), (in_w, C_IN), (bc_w, C_BC)])
    ]
    locals_ = [
        own,
        pltpu.make_async_copy(x_ref, X.at[y], lsem.at[4]),
        pltpu.make_async_copy(cot_ref, cots.at[y], lsem.at[5]),
    ]
    table[...] = jnp.zeros_like(table)
    table[0:HEADS, 0:48] = ps_ref[...].astype(F32)
    for k in range(4):
        table[12 + 2 * k : 14 + 2 * k, 0:HEADS] = ci_w[k].astype(F32)
    table[20:22, 0:HEADS] = cb_w[...].astype(F32)
    table[22:24, 0:HEADS] = gg_w[...].astype(F32)
    table[24:28, 0:8] = cs_w[...].astype(F32)
    table[28:29, 0:8] = csb_w[...].astype(F32)
    table[29:30, 0:48] = ng_w[...].astype(F32)
    W[x, c, z, :, C_MISC:WIDE] = jnp.transpose(table[...])[0:48].astype(BF16)
    rate = -jnp.exp(dec_ref[...])
    step_ref[...] = jnp.zeros_like(step_ref)
    step_ref[0:1, 0:HEADS] = sb_ref[...]
    step_ref[1:2, 0:HEADS] = rate * LOG2E
    step_ref[2:3, 0:HEADS] = rate
    step_ref[3:4, 0:HEADS] = skip_ref[...]

    def between():
        block, inner = parts(fiota((D, HD), 0), 48)
        _, head = parts(inner, 12)
        place_of = head * 64 + block * 2
        lane = fiota((D, HD), 1)
        for j in range(2):
            Q[j] = jnp.where(lane == place_of + j, 1.0, 0.0).astype(BF16)
        token = fiota((ROWS, 128), 0) + (z * ROWS).astype(F32)
        begin = jnp.zeros((ROWS, 128), F32)
        end = jnp.float32(0.0)
        for k in range(3):
            end = end + lens_ref[0, k].astype(F32)
            begin = jnp.where(token >= end, end, begin)
        pos[...] = token - begin

    cot_onward, cot_end, others_z = gather(go, W, X, cots, x_ref, cot_ref, E, locals_, between)
    out_copies = [
        pltpu.make_async_copy(W, W_out, osem.at[0]),
        pltpu.make_async_copy(X, X_out, osem.at[1]),
    ]
    for copy in out_copies:
        copy.start()

    misc = W[:, :, :, :, C_MISC:WIDE].reshape(D, 128)
    row8, lane8 = iota((8, 128), 0), iota((8, 128), 1)

    def across(column):
        return dot_nt(jnp.where(lane8 == column, 1.0, 0.0).astype(BF16), misc)

    _, r_in = parts(fiota((8, D), 1), 48)
    found = jnp.zeros((8, HD), F32)
    for j in range(2):
        taps = jnp.where(r_in < HEADS, across(12 + 2 * row8 + j), 0.0)
        found = found + dot(taps.astype(BF16), Q[j])
    conv[:, 0:HD] = found
    rest = across(jnp.where(row8 < 4, 24 + row8, jnp.where(row8 == 4, 28, 29)))
    col_block, col8 = parts(fiota((D, 256), 1), 8)
    row_block, row_in = parts(fiota((D, 256), 0), 48)
    spot = jnp.where((row_block == col_block) & (row_in == col8), 1.0, 0.0).astype(BF16)
    conv[:, HD:CONV] = dot(rest.astype(BF16), spot)
    ngain = rest[5:6]
    conv_out[...] = conv[...]
    ngain_out[...] = ngain
    gain_out[...] = found[5:6]

    def norm(rows):
        wide = rows.astype(F32)
        r = lax.rsqrt(jnp.mean(wide * wide, axis=1, keepdims=True) + EPS)
        return (wide * r * ngain).astype(BF16)

    def weight(first, last):
        return W[:, :, :, :, first:last].reshape(D, last - first)

    edge = dot(norm(E[...]), weight(C_IN, C_MISC)).astype(BF16)
    edge_ref[...] = edge
    state[...] = jnp.zeros_like(state)
    decay[...] = jnp.ones_like(decay)
    bufs = (buf0, buf1)
    buf0[0:8, :] = edge.astype(F32)[8:16]

    def project(i):
        rows = slice(TILE * i, TILE * i + TILE)
        low = norm(X[i])
        normed[rows, :] = low
        conv_in = dot(low, weight(C_IN, C_MISC)).astype(BF16)
        ci[rows, :] = conv_in
        bufs[i % 2][8 : 8 + TILE, :] = conv_in.astype(F32)
        sigs[rows, :] = dot(low, weight(C_MISC, WIDE))

    def convolve(i):
        buf = bufs[i % 2]
        rows = slice(TILE * i, TILE * i + TILE)
        if i + 1 < TILES:
            bufs[(i + 1) % 2][0:8, :] = buf[TILE : TILE + 8, :]
        place_in = pos[rows, :]
        for j in range(CONV // 128):
            lanes = cols(j)
            acc = buf[8 : 8 + TILE, lanes] * conv[3:4, lanes] + conv[4:5, lanes]
            for back in (1, 2, 3):
                term = buf[8 - back : 8 - back + TILE, lanes] * conv[3 - back : 4 - back, lanes]
                acc = acc + jnp.where(place_in >= back, term, 0.0)
            sig = jax.nn.sigmoid(acc)
            ds[rows, lanes] = sig * (1.0 + acc * (1.0 - sig))
            xbc[rows, lanes] = (acc * sig).astype(BF16)
        lane = iota((TILE, 128), 1)
        pre = sigs[rows, :] + step_ref[0:1, :]
        small = jnp.exp(-jnp.abs(pre))
        log1p = jnp.where(
            small < 1e-3, small * (1.0 - 0.5 * small + (1.0 / 3.0) * small * small), jnp.log(1.0 + small)
        )
        dt = jnp.where(lane < HEADS, jnp.maximum(pre, 0.0) + log1p, 0.0)
        dts[rows, :] = dt
        sigs[rows, :] = jax.nn.sigmoid(pre)
        rate = dt * step_ref[1:2, :]
        for sub in range(TILE // LEN):
            inside = slice(LEN * sub, LEN * sub + LEN)
            rows = slice(TILE * i + LEN * sub, TILE * i + LEN * sub + LEN)
            cum = dot_full(triangle("incl"), rate[inside])
            cums[rows, :] = cum
            last = cum[LEN - 1 : LEN, :]
            pos_last = pos[TILE * i + LEN * sub + LEN - 1 : TILE * i + LEN * sub + LEN, :]
            row = iota((LEN, 128), 0).astype(F32)
            fade = jnp.where((LEN - 1) - row <= pos_last, jnp.exp2(last - cum), 0.0)
            whole = jnp.where(pos_last > LEN - 1, jnp.exp2(last), 0.0)
            basis_t = jnp.transpose(xbc[rows, HD : HD + NS].astype(F32)).astype(BF16)
            for p in range(PAIRS):
                low = (xbc[rows, cols(p)].astype(F32) * spread_heads(dt[inside], p)).astype(BF16)
                xdt[rows, cols(p)] = low
                ended = (low.astype(F32) * spread_heads(fade, p)).astype(BF16)
                new = dot(basis_t, ended)
                fresh[i * (TILE // LEN) + sub, :, cols(p)] = new
                factor = spread_heads(whole, p)
                state[:, cols(p)] = state[:, cols(p)] * factor + new
                decay[:, cols(p)] = decay[:, cols(p)] * factor

    pairs = [
        (normed, normed_ref), (ci, ci_ref), (ds, ds_ref), (xbc, xbc_ref), (xdt, xdt_ref), (dts, dt_ref),
        (cums, cum_ref), (sigs, sig_ref), (pos, pos_ref),
    ]

    def store(i):
        rows = slice(TILE * i, TILE * i + TILE)
        for k, (src, dst) in enumerate(pairs):
            out_copies.append(pltpu.make_async_copy(src.at[rows], dst.at[rows], osem.at[2 + 11 * i + k]))
        n = TILE // LEN
        here = slice(n * i, n * i + n)
        out_copies.append(pltpu.make_async_copy(fresh.at[here], fresh_ref.at[here], osem.at[2 + 11 * i + 10]))
        for copy in out_copies[-10:]:
            copy.start()

    project(0)
    for i in range(TILES):
        if i == 2:
            cot_onward()
        if i + 1 < TILES:
            project(i + 1)
        convolve(i)
        store(i)
    summ[0:NS, :] = state[...].astype(BF16)
    summ[NS : NS + 16, :] = link_rows(decay[...])
    swaps = [go(summ, summs_ref.at[z], other) for other in others_z]
    out_copies.append(pltpu.make_async_copy(summ, summs_ref.at[z], osem.at[46]))
    out_copies[-1].start()
    for i in range(TILES):
        rows = slice(TILE * i, TILE * i + TILE)
        gate[rows, :] = dot(normed[rows, :], weight(C_GATE, C_IN))
        out_copies.append(pltpu.make_async_copy(gate.at[rows], gate_ref.at[rows], osem.at[2 + 11 * i + 9]))
        out_copies[-1].start()
    t, low_s = iota((LEN, LEN), 0), iota((LEN, LEN), 1)
    gap = (t - low_s).astype(F32)

    def local_chunk(i, _):
        rows = pl.ds(pl.multiple_of(LEN * i, LEN), LEN)
        place_in, cum = pos[rows, :], cums[rows, :]
        keep = (gap >= 0) & (gap <= place_in)
        cum_t = jnp.transpose(cum)
        inner = dot_nt(xbc[rows, HD + NS : CONV], xbc[rows, HD : HD + NS])
        for p in range(PAIRS):
            scores = []
            for h in (2 * p, 2 * p + 1):
                span = jnp.where(keep, cum[:, h : h + 1] - cum_t[h : h + 1, :], -1e30)
                scores.append((jnp.exp2(span) * inner).astype(BF16))
            local = dot(jnp.concatenate(scores, axis=1), stacked(xdt[rows, cols(p)]))
            skip = spread_heads(step_ref[...], p)[3:4]
            near[rows, cols(p)] = local + skip * xbc[rows, cols(p)].astype(F32)
        return 0

    lax.fori_loop(0, CHUNKS, local_chunk, 0)
    out_copies.append(pltpu.make_async_copy(near, near_ref, osem.at[47]))
    out_copies[-1].start()
    cot_end()
    for copy in swaps:
        copy.wait_recv()
    for copy in out_copies:
        copy.wait()
    go.finish()


def front(big, lens, small):
    vmem = pl.BlockSpec(memory_space=pltpu.VMEM)
    anywhere = pl.BlockSpec(memory_space=ANY)
    outs = [
        ((ROWS, D), BF16), ((ROWS, HD), F32), ((ROWS, CONV), BF16), ((ROWS, CONV), F32), ((ROWS, CONV), BF16),
        ((ROWS, HD), BF16), ((ROWS, 128), F32), ((ROWS, 128), F32), ((ROWS, 128), F32), ((CHUNKS, NS, HD), F32),
        ((ROWS, 128), F32),
    ]
    return pl.pallas_call(
        front_kernel,
        out_shape=[shape((4, 2, 4, 48, WIDE), BF16), shape((4, 256, D), BF16), shape((4, 256, D), BF16)]
        + [shape(*o) for o in outs]
        + [shape((ROWS, HD), F32), shape((4, NS + 16, HD), BF16), shape((16, CONV), BF16), shape((8, CONV), F32), shape((1, D), F32)]
        + [shape((1, HD), F32), shape((8, 128), F32)],
        in_specs=[anywhere] * 6 + [pl.BlockSpec(memory_space=pltpu.SMEM)] + [vmem] * 10,
        out_specs=[anywhere] * 16 + [vmem] * 5,
        scratch_shapes=[
            pltpu.VMEM((4, 2, 4, 48, WIDE), BF16), pltpu.VMEM((4, 256, D), BF16), pltpu.VMEM((16, D), BF16),
            pltpu.VMEM((2, D, HD), BF16),
        ]
        + [pltpu.VMEM(*o) for o in outs]
        + [
            pltpu.VMEM((ROWS, 128), F32), pltpu.VMEM((8 + TILE, CONV), F32), pltpu.VMEM((8 + TILE, CONV), F32),
            pltpu.VMEM((8, CONV), F32), pltpu.VMEM((NS, HD), F32), pltpu.VMEM((1, HD), F32),
            pltpu.VMEM((128, 128), F32), pltpu.VMEM((NS + 16, HD), BF16), pltpu.VMEM((ROWS, HD), F32),
            pltpu.SemaphoreType.DMA((72,)), pltpu.SemaphoreType.DMA((72,)), pltpu.SemaphoreType.DMA((8,)),
            pltpu.SemaphoreType.DMA((48,)),
        ],
        compiler_params=comm_params(0, 60 << 20),
        name="front",
    )(*big, lens, *small)


LAG = 2


def forward_kernel(
    summ, xbc_ref, near_ref, cum_ref, pos_ref, fresh_ref, gate_ref, cot_ref, w_ref, gain_ref,
    xbc2_ref, cum2_ref, pos2_ref, gate2_ref,
    enter_ref, branch_ref, dgate_ref, dmix_ref, gfresh_ref, gsumm_ref, acc_ref,
    mixed, db, state, back, decay, sums, ssem, rsem,
):
    step = pl.program_id(0)
    x, c, z, y = place()
    subs = TILE // LEN
    flow = Flow(ssem, rsem)
    others_y = [device(x, c, z, (y + k) % 4) for k in (1, 3, 2)]
    for i in range(TILES):
        for k in range(3):
            there = lambda i=i: sums.at[y, pl.ds(subs * i, subs)]
            flow.add("y%d%d" % (i, k), there, there, others_y[k])

    @pl.when(step == 0)
    def _():
        enter(others_y)
        acc_ref[...] = jnp.zeros_like(acc_ref)
        start = jnp.zeros((NS, HD), F32)
        for j in range(3):
            start = jnp.where(j < z, start * link_of(summ, j) + summ[j, 0:NS, :].astype(F32), start)
        state[...] = start
        back[...] = jnp.zeros_like(back)
        decay[...] = jnp.ones_like(decay)

    @pl.when(step < TILES)
    def _():
        here = pl.ds(pl.multiple_of(step * TILE, TILE), TILE)
        db[here, :] = dot(cot_ref[...], w_ref[...])
        t, s = iota((LEN, LEN), 0), iota((LEN, LEN), 1)
        for sub in range(subs):
            rows = slice(LEN * sub, LEN * sub + LEN)
            there = pl.ds(pl.multiple_of(step * TILE + LEN * sub, LEN), LEN)
            pos, cum = pos_ref[rows, :], cum_ref[rows, :]
            basis_c = xbc_ref[rows, HD + NS : CONV]
            fade = jnp.where(pos > t.astype(F32), jnp.exp2(cum), 0.0)
            whole = jnp.where(pos[LEN - 1 : LEN] > LEN - 1, jnp.exp2(cum[LEN - 1 : LEN]), 0.0)
            square = jnp.zeros((LEN, 128), F32)
            cross = jnp.zeros((LEN, 128), F32)
            for p in range(PAIRS):
                lanes = cols(p)
                entered = state[:, lanes].astype(BF16)
                enter_ref[sub, :, lanes] = entered
                whole_y = near_ref[rows, lanes] + dot(basis_c, entered) * spread_heads(fade, p)
                mixed[there, lanes] = whole_y
                gate = gate_ref[rows, lanes]
                gated = whole_y * gate * jax.nn.sigmoid(gate)
                square = square + gated * gated
                cross = cross + gated * gain_ref[:, lanes] * db[there, lanes]
                state[:, lanes] = state[:, lanes] * spread_heads(whole, p) + fresh_ref[sub, :, lanes]
            sq = jnp.sum(square, axis=1, keepdims=True)
            cr = jnp.sum(cross, axis=1, keepdims=True)
            both = jnp.where(s == 0, sq, jnp.where(s == 1, cr, 0.0))
            sums[y, step * subs + sub] = jnp.transpose(both)[0:8]

    for i in range(TILES):

        @pl.when(step == i)
        def _():
            flow.start("y%d0" % i, "y%d1" % i, "y%d2" % i)

        @pl.when(step == i + LAG)
        def _():
            flow.wait("y%d0" % i, "y%d1" % i, "y%d2" % i)

    @pl.when(step >= LAG)
    def _():
        tile = step - LAG
        for sub in range(subs):
            rows = slice(LEN * sub, LEN * sub + LEN)
            there = pl.ds(pl.multiple_of(tile * TILE + LEN * sub, LEN), LEN)
            chunk = tile * subs + sub
            total = sums[0, chunk] + sums[1, chunk] + sums[2, chunk] + sums[3, chunk]
            both = jnp.transpose(jnp.concatenate([total, jnp.zeros((120, 128), F32)], axis=0))
            r = lax.rsqrt(both[:, 0:1] * (1.0 / E_ALL) + EPS)
            slope = r * r * r * both[:, 1:2] * (1.0 / E_ALL)
            pos, cum = pos2_ref[rows, :], cum2_ref[rows, :]
            fade = jnp.where(pos > iota((LEN, 128), 0).astype(F32), jnp.exp2(cum), 0.0)
            whole = jnp.where(pos[LEN - 1 : LEN] > LEN - 1, jnp.exp2(cum[LEN - 1 : LEN]), 0.0)
            basis_t = jnp.transpose(xbc2_ref[rows, HD + NS : CONV].astype(F32)).astype(BF16)
            for p in range(PAIRS):
                lanes = cols(p)
                mix, gate, grad = mixed[there, lanes], gate2_ref[rows, lanes], db[there, lanes]
                gain = gain_ref[:, lanes]
                sig = jax.nn.sigmoid(gate)
                silu = gate * sig
                gated = mix * silu
                scaled = gated * r
                branch_ref[rows, lanes] = (scaled * gain).astype(BF16)
                acc_ref[0:8, lanes] += fold8(grad * scaled)
                dgated = r * gain * grad - gated * slope
                dmix = dgated * silu
                dgate_ref[rows, lanes] = (dgated * mix * sig * (1.0 + gate * (1.0 - sig))).astype(BF16)
                dmix_ref[rows, lanes] = dmix
                acc_ref[8:16, lanes] += fold8(dmix * xbc2_ref[rows, lanes].astype(F32))
                fresh = dot(basis_t, (dmix * spread_heads(fade, p)).astype(BF16))
                gfresh_ref[sub, :, lanes] = fresh
                back[:, lanes] = back[:, lanes] + decay[:, lanes] * fresh
                decay[:, lanes] = decay[:, lanes] * spread_heads(whole, p)

    @pl.when(step == TILES + LAG - 1)
    def _():
        gsumm_ref[0:NS, :] = back[...].astype(BF16)
        gsumm_ref[NS : NS + 16, :] = link_rows(decay[...])
        flow.finish()


def forward(summs, xbc, near, cum, pos, fresh, gate, cot, W, gain):
    sub = TILE // LEN

    def first(i):
        return jnp.minimum(i, TILES - 1)

    def second(i):
        return jnp.maximum(i - LAG, 0)

    def rows(c, at):
        return pl.BlockSpec((TILE, c), lambda i: (at(i), 0))

    def states(at):
        return pl.BlockSpec((sub, NS, HD), lambda i: (at(i), 0, 0))

    return pl.pallas_call(
        forward_kernel,
        grid=(TILES + LAG,),
        in_specs=[
            whole_spec(4, NS + 16, HD), rows(CONV, first), rows(HD, first), rows(128, first), rows(128, first),
            states(first), rows(HD, first), rows(D, first), whole_spec(D, HD), whole_spec(1, HD),
            rows(CONV, second), rows(128, second), rows(128, second), rows(HD, second),
        ],
        out_specs=[
            states(first), rows(HD, second), rows(HD, second), rows(HD, second), states(second),
            whole_spec(NS + 16, HD), whole_spec(16, HD),
        ],
        out_shape=[
            shape((CHUNKS, NS, HD), BF16), shape((ROWS, HD), BF16), shape((ROWS, HD), BF16), shape((ROWS, HD), F32),
            shape((CHUNKS, NS, HD), F32), shape((NS + 16, HD), BF16), shape((16, HD), F32),
        ],
        scratch_shapes=[
            pltpu.VMEM((ROWS, HD), F32), pltpu.VMEM((ROWS, HD), F32), pltpu.VMEM((NS, HD), F32), pltpu.VMEM((NS, HD), F32),
            pltpu.VMEM((1, HD), F32), pltpu.VMEM((4, CHUNKS, 8, 128), F32),
            pltpu.SemaphoreType.DMA((16,)), pltpu.SemaphoreType.DMA((16,)),
        ],
        compiler_params=comm_params(1, 60 << 20),
        name="forward",
    )(summs, xbc, near, cum, pos, fresh, gate, cot, W, gain, xbc, cum, pos, gate)


def add(a, b):
    return a.astype(F32) + b.astype(F32)


class Reduce:
    def __init__(self, flow, tag, bufs, halves):
        self.flow, self.tag, self.bufs = flow, tag, bufs
        G, K, RA, SA, TA, UA, VA, RB, SB, TB, UB, VB = bufs
        nA, nA1, nB, nB1 = halves
        self.A, self.B = pl.ds(0, nA), pl.ds(nA, nB)
        self.A1, self.A2 = pl.ds(0, nA1), pl.ds(nA1, nA - nA1)
        self.B1, self.B2 = pl.ds(0, nB1), pl.ds(nB1, nB - nB1)
        self.GB1, self.GB2 = pl.ds(nA, nB1), pl.ds(nA + nB1, nB - nB1)
        x, c, z, y = place()
        self.c, self.at = c, (x, z)
        xr, xl, xo = (x + 1) % 4, (x + 3) % 4, (x + 2) % 4
        zr, zl, zo = (z + 1) % 4, (z + 3) % 4, (z + 2) % 4
        self.xs, self.zs = (xr, xl, xo), (zr, zl, zo)
        dxr, dxl = device(xr, c, z, y), device(xl, c, z, y)
        dzr, dzl = device(x, c, zr, y), device(x, c, zl, y)
        A, B, A1, A2, B1, B2, GB1, GB2 = self.A, self.B, self.A1, self.A2, self.B1, self.B2, self.GB1, self.GB2

        def put(name, src, dst, to):
            flow.add(tag + name, src, dst, to)

        for k in range(4):
            put("k%d" % k, lambda k=k: G.at[k, 1 - c], lambda k=k: K.at[k], device(x, 1 - c, z, y))
        put("ra1", lambda: G.at[xo, c, :, :, A1], lambda: RA.at[:, :, A1], dxr)
        put("ra2", lambda: G.at[xo, c, :, :, A2], lambda: RA.at[:, :, A2], dxl)
        put("rb1", lambda: G.at[:, c, zo, :, GB1], lambda: RB.at[:, :, B1], dzr)
        put("rb2", lambda: G.at[:, c, zo, :, GB2], lambda: RB.at[:, :, B2], dzl)
        put("sar", lambda: G.at[xr, c, :, :, A], lambda: SA.at[0], dxr)
        put("sal", lambda: G.at[xl, c, :, :, A], lambda: SA.at[1], dxl)
        put("sbr", lambda: G.at[:, c, zr, :, B], lambda: SB.at[0], dzr)
        put("sbl", lambda: G.at[:, c, zl, :, B], lambda: SB.at[1], dzl)
        put("ta1", lambda: TA.at[zo, :, A1], lambda: UA.at[:, A1], dzr)
        put("ta2", lambda: TA.at[zo, :, A2], lambda: UA.at[:, A2], dzl)
        put("tb1", lambda: TB.at[xo, :, B1], lambda: UB.at[:, B1], dxr)
        put("tb2", lambda: TB.at[xo, :, B2], lambda: UB.at[:, B2], dxl)
        put("var", lambda: TA.at[zr], lambda: VA.at[0], dzr)
        put("val", lambda: TA.at[zl], lambda: VA.at[1], dzl)
        put("vbr", lambda: TB.at[xr], lambda: VB.at[0], dxr)
        put("vbl", lambda: TB.at[xl], lambda: VB.at[1], dxl)

    def start(self, *names):
        self.flow.start(*[self.tag + name for name in names])

    def wait(self, *names):
        self.flow.wait(*[self.tag + name for name in names])

    def cores(self, k):
        self.start("k%d" % k)

    def first(self):
        G, K = self.bufs[:2]
        for k in range(4):
            self.wait("k%d" % k)

        def join(i, _):
            k, j = i // 4, i % 4
            G[k, self.c, j] = add(G[k, self.c, j], K[k, j]).astype(BF16)
            return 0

        lax.fori_loop(0, 16, join, 0)
        self.start("ra1", "rb1", "ra2", "rb2")

    def second(self):
        G, K, RA, SA, TA, UA, VA, RB, SB, TB, UB, VB = self.bufs
        c, (xr, xl, _), (zr, zl, _) = self.c, self.xs, self.zs
        self.wait("ra1")
        G[xr, c, :, :, self.A1] = G[xr, c, :, :, self.A1] + RA[:, :, self.A1]
        self.start("sar")
        self.wait("rb1")
        G[:, c, zr, :, self.GB1] = G[:, c, zr, :, self.GB1] + RB[:, :, self.B1]
        self.start("sbr")
        self.wait("ra2")
        G[xl, c, :, :, self.A2] = G[xl, c, :, :, self.A2] + RA[:, :, self.A2]
        self.start("sal")
        self.wait("rb2")
        G[:, c, zl, :, self.GB2] = G[:, c, zl, :, self.GB2] + RB[:, :, self.B2]
        self.start("sbl")

    def third(self):
        G, K, RA, SA, TA, UA, VA, RB, SB, TB, UB, VB = self.bufs
        c, (x, z) = self.c, self.at
        self.wait("sar", "sal")
        TA[...] = (G[x, c, :, :, self.A].astype(F32) + add(SA[0], SA[1])).astype(BF16)
        self.start("ta1", "ta2")
        self.wait("sbr", "sbl")
        TB[...] = (G[:, c, z, :, self.B].astype(F32) + add(SB[0], SB[1])).astype(BF16)
        self.start("tb1", "tb2")

    def fourth(self):
        G, K, RA, SA, TA, UA, VA, RB, SB, TB, UB, VB = self.bufs
        (xr, xl, _), (zr, zl, _) = self.xs, self.zs
        self.wait("ta1")
        TA[zr, :, self.A1] = TA[zr, :, self.A1] + UA[:, self.A1]
        self.start("var")
        self.wait("ta2")
        TA[zl, :, self.A2] = TA[zl, :, self.A2] + UA[:, self.A2]
        self.start("val")
        self.wait("tb1")
        TB[xr, :, self.B1] = TB[xr, :, self.B1] + UB[:, self.B1]
        self.start("vbr")
        self.wait("tb2")
        TB[xl, :, self.B2] = TB[xl, :, self.B2] + UB[:, self.B2]
        self.start("vbl")

    def last(self, out_ref):
        G, K, RA, SA, TA, UA, VA, RB, SB, TB, UB, VB = self.bufs
        x, z = self.at
        self.wait("vbr", "vbl")
        out_ref[:, self.B] = TB[x].astype(F32) + add(VB[0], VB[1])
        self.wait("var", "val")
        out_ref[:, self.A] = TA[z].astype(F32) + add(VA[0], VA[1])


def reduce_bufs(halves):
    nA, nA1, nB, nB1 = halves

    def half(n):
        return [
            pltpu.VMEM((4, 48, n), BF16), pltpu.VMEM((2, 4, 48, n), BF16), pltpu.VMEM((4, 48, n), BF16),
            pltpu.VMEM((48, n), BF16), pltpu.VMEM((2, 48, n), BF16),
        ]

    return [pltpu.VMEM((4, 2, 4, 48, nA + nB), BF16), pltpu.VMEM((4, 4, 48, nA + nB), BF16)] + half(nA) + half(nB)


class RowSum:
    def __init__(self, flow, tag, N, M, Q):
        self.flow, self.tag, self.bufs = flow, tag, (N, M, Q)
        x, c, z, y = place()
        self.yr, self.yl, self.yo, self.y = (y + 1) % 4, (y + 3) % 4, (y + 2) % 4, y
        right, left = device(x, c, z, self.yr), device(x, c, z, self.yl)
        self.h1, self.h2 = pl.ds(0, 128), pl.ds(128, 128)
        flow.add(tag + "1", lambda: N.at[self.yo, self.h1], lambda: M.at[0], right)
        flow.add(tag + "2", lambda: N.at[self.yo, self.h2], lambda: M.at[1], left)
        flow.add(tag + "3", lambda: N.at[self.yr], lambda: Q.at[0], right)
        flow.add(tag + "4", lambda: N.at[self.yl], lambda: Q.at[1], left)

    def first(self):
        self.flow.start(self.tag + "1", self.tag + "2")

    def second(self):
        N, M, Q = self.bufs
        self.flow.wait(self.tag + "1")
        N[self.yr, self.h1] = N[self.yr, self.h1] + M[0]
        self.flow.start(self.tag + "3")
        self.flow.wait(self.tag + "2")
        N[self.yl, self.h2] = N[self.yl, self.h2] + M[1]
        self.flow.start(self.tag + "4")

    def last(self, out_ref):
        N, M, Q = self.bufs
        self.flow.wait(self.tag + "3", self.tag + "4")
        out_ref[...] = N[self.y].astype(F32) + add(Q[0], Q[1])


def row_bufs():
    return [pltpu.VMEM((4, 256, D), BF16), pltpu.VMEM((2, 128, D), BF16), pltpu.VMEM((2, 256, D), BF16)]


MID = (768, 384, 768, 384)
TAIL = (640, 384, 512, 256)
PRE = 4


def middle_kernel(
    gsumm_ref, w_ref, cot_ref, normed_ref, branch_ref, dgate_ref,
    xbc_ref, xdt_ref, dt_ref, cum_ref, sig_ref, dmix_ref, enter_ref, gfresh_ref, ds_ref, ci_ref, pos_ref,
    edge_ref, conv_ref, step_ref,
    din_ref, cgrad_ref, hgrad_ref, dedge_ref, gout_ref, share_ref,
    state, dacc, posn, picks, summ, edge_out, edge_in, *rest,
):
    bufs, (N, M, Q, ssem, rsem, lsem) = rest[:-6], rest[-6:]
    step = pl.program_id(0)
    steps = PRE + CHUNKS
    x, c, z, y = place()
    flow = Flow(ssem, rsem)
    reduce = Reduce(flow, "g", bufs, MID)
    rows = RowSum(flow, "n", N, M, Q)
    others_z = [device(x, c, (z + k) % 4, y) for k in (1, 3, 2)]
    for k in range(3):
        flow.add("s%d" % k, lambda: gsumm_ref, lambda: summ.at[z], others_z[k])
    flow.add("e", lambda: edge_out, lambda: edge_in, others_z[1])
    load_s = pltpu.make_async_copy(gsumm_ref, summ.at[z], lsem.at[1])

    @pl.when(step == 0)
    def _():
        load_s.start()
        enter(
            others_z
            + [device((x + 1) % 4, c, z, y), device((x + 3) % 4, c, z, y)]
            + [device(x, c, z, (y + 1) % 4), device(x, c, z, (y + 3) % 4), device(x, 1 - c, z, y)]
        )
        flow.start("s0", "s1", "s2")
        for p in range(PAIRS):
            picks[p] = head_pick(p)

    for k in range(PRE):

        @pl.when(step == k)
        def _():
            block = (rows.yo, rows.yr, rows.yl, rows.y)[k]
            here = pl.ds(pl.multiple_of(block * 256, 256), 256)
            N[block] = dot_nt(branch_ref[here, :], w_ref[...]).astype(BF16)
            if k == 0:
                rows.first()
            G = bufs[0]
            out = dot(jnp.transpose(cot_ref[...]), branch_ref[...]).astype(BF16)
            gate = dot(jnp.transpose(normed_ref[...]), dgate_ref[...]).astype(BF16)
            G[k, :, :, :, 0:HD] = out.reshape(2, 4, 48, HD)
            G[k, :, :, :, HD : 2 * HD] = gate.reshape(2, 4, 48, HD)
            reduce.cores(k)

    @pl.when(step == PRE)
    def _():
        flow.wait("s0", "s1", "s2")
        load_s.wait()
        start = jnp.zeros((NS, HD), F32)
        for j in (3, 2, 1):
            link = link_of(summ, j)
            start = jnp.where(j > z, start * link + summ[j, 0:NS, :].astype(F32), start)
        state[...] = start
        dacc[LEN : LEN + 8, :] = jnp.zeros((8, CONV), F32)
        posn[LEN : LEN + 8, :] = jnp.zeros((8, 128), F32)
        cgrad_ref[...] = jnp.zeros_like(cgrad_ref)
        hgrad_ref[...] = jnp.zeros_like(hgrad_ref)
        reduce.first()

    @pl.when(step == PRE + 1)
    def _():
        rows.second()

    @pl.when(step == PRE + 2)
    def _():
        reduce.second()

    @pl.when(step == PRE + 5)
    def _():
        reduce.third()

    @pl.when(step == PRE + 6)
    def _():
        reduce.fourth()

    @pl.when(step > PRE)
    def _():
        dacc[LEN : LEN + 8, :] = dacc[0:8, :]
        posn[LEN : LEN + 8, :] = posn[0:8, :]

    @pl.when(step >= PRE)
    def _():
        back_chunk(
            xbc_ref, xdt_ref, dt_ref, cum_ref, sig_ref, dmix_ref, enter_ref, gfresh_ref, ds_ref, ci_ref, pos_ref,
            conv_ref, step_ref, din_ref, cgrad_ref, hgrad_ref, state, dacc, posn, picks,
        )

    @pl.when(step == steps - 1)
    def _():
        dacc[8:16, :] = dacc[0:8, :]
        dacc[0:8, :] = jnp.zeros((8, CONV), F32)
        posn[8:16, :] = posn[0:8, :]
        posn[0:8, :] = jnp.zeros((8, 128), F32)
        for j in range(CONV // 128):
            lanes = cols(j)
            ci = edge_ref[:, lanes].astype(F32)[8:16]
            d_in = jnp.zeros((8, 128), F32)
            for back in (1, 2, 3):
                moved = jnp.where(posn[back : back + 8, :] >= back, dacc[back : back + 8, lanes], 0.0)
                d_in = d_in + moved * conv_ref[3 - back : 4 - back, lanes]
                cgrad_ref[8 * (3 - back) : 8 * (3 - back) + 8, lanes] += moved * ci
            edge_out[:, lanes] = d_in
        flow.start("e")
        reduce.last(gout_ref)
        rows.last(share_ref)
        flow.wait("e")
        dedge_ref[...] = edge_in[...]
        flow.finish()


def back_chunk(
    xbc_ref, xdt_ref, dt_ref, cum_ref, sig_ref, dmix_ref, enter_ref, gfresh_ref, ds_ref, ci_ref, pos_ref,
    conv_ref, step_ref, din_ref, cgrad_ref, hgrad_ref, state, dacc, posn, picks,
):
    pos = pos_ref[...]
    posn[0:LEN, :] = pos
    row, lane = iota((LEN, LEN), 0), iota((LEN, LEN), 1)
    gap = (lane - row).astype(F32)
    keep = (gap >= 0) & (gap <= jnp.transpose(pos))
    cum, dt = cum_ref[...], dt_ref[...]
    cum_t = jnp.transpose(cum)
    last = cum[LEN - 1 : LEN]
    pos_last = pos[LEN - 1 : LEN]
    fade = jnp.where(pos > row.astype(F32), jnp.exp2(cum), 0.0)
    ends = jnp.where((LEN - 1) - row.astype(F32) <= pos_last, jnp.exp2(last - cum), 0.0)
    whole = jnp.where(pos_last > LEN - 1, jnp.exp2(last), 0.0)
    basis = xbc_ref[:, HD : HD + NS]
    basis_c = xbc_ref[:, HD + NS : CONV]
    inner = dot_nt(basis, basis_c)
    inner2 = jnp.concatenate([inner, inner], axis=1)
    d_inner = jnp.zeros((LEN, LEN), F32)
    d_b = jnp.zeros((LEN, NS), F32)
    d_c = jnp.zeros((LEN, NS), F32)
    into = jnp.zeros((LEN, 128), F32)
    by_head = jnp.zeros((3 * LEN, 128), F32)
    across = jnp.zeros((8, 128), F32)
    sums_t = []
    for p in range(PAIRS):
        lanes = cols(p)
        xs = xbc_ref[:, lanes].astype(F32)
        xdt = xdt_ref[:, lanes]
        dy_wide = dmix_ref[:, lanes]
        dy, dy_low = in_two(dy_wide)
        entered = enter_ref[0, :, lanes]
        after = state[:, lanes]
        after_low = after.astype(BF16)
        dys = stacked(dy)
        spans = []
        for h in (2 * p, 2 * p + 1):
            spans.append(jnp.where(keep, cum_t[h : h + 1, :] - cum[:, h : h + 1], -1e30))
        decays = jnp.exp2(jnp.concatenate(spans, axis=1))
        scores = (decays * inner2).astype(BF16)
        d_scores = dot_nt(twice(xdt), jnp.concatenate([dys, stacked(dy_low)], axis=1)) * decays
        d_inner = d_inner + d_scores[:, :LEN] + d_scores[:, LEN:]
        prod = d_scores * inner2
        sums_t.append(jnp.sum(prod[:, :LEN], axis=0, keepdims=True))
        sums_t.append(jnp.sum(prod[:, LEN:], axis=0, keepdims=True))
        end_pair = spread_heads(ends, p)
        fade_pair = spread_heads(fade, p)
        z_state = dot(basis, after_low) * end_pair
        z = dot(scores, dys) + z_state
        first = jnp.sum(prod[:, :LEN], axis=1, keepdims=True)
        second = jnp.sum(prod[:, LEN:], axis=1, keepdims=True)
        into = into + jnp.where(lane == 2 * p, first, jnp.where(lane == 2 * p + 1, second, 0.0))
        products = [
            (xs * z).astype(BF16),
            (xdt.astype(F32) * z_state).astype(BF16),
            (dy_wide * dot(basis_c, entered) * fade_pair).astype(BF16),
        ]
        by_head = by_head + dot(jnp.concatenate(products, axis=0), picks[p])
        across = across + dot(fold8(after * entered.astype(F32)).astype(BF16), picks[p])
        d_x = spread_heads(dt, p) * z + spread_heads(step_ref[...], p)[3:4] * dy_wide
        dacc[0:LEN, lanes] = d_x * ds_ref[:, lanes]
        d_b = d_b + dot_nt(jnp.concatenate(in_two(xdt.astype(F32) * end_pair), axis=1), twice(after_low))
        d_c = d_c + dot_nt(jnp.concatenate(in_two(dy_wide * fade_pair), axis=1), twice(entered))
        state[:, lanes] = after * spread_heads(whole, p) + gfresh_ref[0, :, lanes]
    low = d_inner.astype(BF16)
    d_b = d_b + dot(low, basis_c)
    d_c = d_c + dot_tn(low, basis)
    dacc[0:LEN, HD : HD + NS] = d_b * ds_ref[:, HD : HD + NS]
    dacc[0:LEN, HD + NS : CONV] = d_c * ds_ref[:, HD + NS : CONV]
    direct, later, carry = by_head[:LEN], by_head[LEN : 2 * LEN], by_head[2 * LEN :]
    out_of = jnp.transpose(jnp.concatenate(sums_t + [jnp.zeros((128 - HEADS, LEN), F32)], axis=0))
    d_rate = (
        dot_full(triangle("suffix"), out_of - into + carry)
        + dot_full(triangle("strict"), later)
        + whole * jnp.sum(across, axis=0, keepdims=True)
    )
    d_step = (direct + d_rate * step_ref[2:3, :]) * sig_ref[...]
    hgrad_ref[0:8, :] += fold8(d_rate * dt)
    hgrad_ref[8:16, :] += fold8(d_step)
    din_ref[:, CONV : CONV + 128] = d_step.astype(BF16)

    within = [posn[back : back + LEN, :] >= back for back in (1, 2, 3)]
    for j in range(CONV // 128):
        lanes = cols(j)
        here = dacc[0:LEN, lanes]
        ci = ci_ref[:, lanes].astype(F32)
        d_in = here * conv_ref[3:4, lanes]
        cgrad_ref[24:32, lanes] += fold8(here * ci)
        cgrad_ref[32:40, lanes] += fold8(here)
        for back in (1, 2, 3):
            moved = jnp.where(within[back - 1], dacc[back : back + LEN, lanes], 0.0)
            d_in = d_in + moved * conv_ref[3 - back : 4 - back, lanes]
            cgrad_ref[8 * (3 - back) : 8 * (3 - back) + 8, lanes] += fold8(moved * ci)
        din_ref[:, lanes] = d_in.astype(BF16)


def middle(
    gsumm, W, cot, normed, branch, dgate, xbc, xdt, dt, cum, sig, dmix, entered, gfresh, ds, ci, pos, edge, conv, step
):
    top = CHUNKS - 1

    def chunk(i):
        return jnp.minimum(top + PRE - i, top)

    def rows(c):
        return pl.BlockSpec((LEN, c), lambda i: (chunk(i), 0))

    def tiles():
        return pl.BlockSpec((ROWS, D // PRE), lambda i: (0, jnp.minimum(i, PRE - 1)))

    state = pl.BlockSpec((1, NS, HD), lambda i: (chunk(i), 0, 0))
    anywhere = pl.BlockSpec(memory_space=ANY)
    return pl.pallas_call(
        middle_kernel,
        grid=(PRE + CHUNKS,),
        in_specs=[
            anywhere, whole_spec(D, HD), tiles(), tiles(), whole_spec(ROWS, HD), whole_spec(ROWS, HD),
            rows(CONV), rows(HD), rows(128), rows(128), rows(128), rows(HD), state, state, rows(CONV), rows(CONV), rows(128),
            whole_spec(16, CONV), whole_spec(8, CONV), whole_spec(8, 128),
        ],
        out_specs=[
            rows(CONV + 128), whole_spec(40, CONV), whole_spec(16, 128), whole_spec(8, CONV), whole_spec(48, 2 * HD),
            whole_spec(256, D),
        ],
        out_shape=[
            shape((ROWS, CONV + 128), BF16), shape((40, CONV), F32), shape((16, 128), F32), shape((8, CONV), F32),
            shape((48, 2 * HD), F32), shape((256, D), F32),
        ],
        scratch_shapes=[
            pltpu.VMEM((NS, HD), F32), pltpu.VMEM((LEN + 8, CONV), F32), pltpu.VMEM((LEN + 8, 128), F32),
            pltpu.VMEM((PAIRS, 128, 128), BF16),
            pltpu.VMEM((4, NS + 16, HD), BF16), pltpu.VMEM((8, CONV), F32), pltpu.VMEM((8, CONV), F32),
        ] + reduce_bufs(MID) + row_bufs() + sems(32),
        compiler_params=comm_params(3, 60 << 20),
        cost_estimate=pl.CostEstimate(flops=40 * ROWS * HD * 128, bytes_accessed=30 << 20, transcendentals=2 * ROWS * CONV),
        name="middle",
    )(gsumm, W, cot, normed, branch, dgate, xbc, xdt, dt, cum, sig, dmix, entered, gfresh, ds, ci, pos, edge, conv, step)


def tail_kernel(
    dgate_ref, din_ref, w_ref, x_ref, normed_ref, edge_ref, cgrad_ref, tgrad_ref, hgrad_ref,
    gout_ref, share_ref, ysum_ref, plane_ref, every_ref,
    dgate, din, w, xs, normed, small, HZ, HX, HC, HY, Y, *rest,
):
    bufs, (N, M, Q, ssem, rsem, lsem) = rest[:-6], rest[-6:]
    x, c, z, y = place()
    xs_other = [device((x + k) % 4, c, z, y) for k in (1, 3, 2)]
    zs_other = [device(x, c, (z + k) % 4, y) for k in (1, 3, 2)]
    ys_other = [device(x, c, z, (y + k) % 4) for k in (1, 3, 2)]
    core = device(x, 1 - c, z, y)
    loads = [
        pltpu.make_async_copy(src, dst, lsem.at[k])
        for k, (src, dst) in enumerate(
            [(w_ref.at[:, C_GATE:WIDE], w), (dgate_ref, dgate), (din_ref, din), (x_ref, xs), (normed_ref, normed)]
        )
    ]
    for load in loads:
        load.start()
    enter(xs_other + zs_other + ys_other + [core])
    flow = Flow(ssem, rsem)
    reduce = Reduce(flow, "g", bufs, TAIL)
    rows = RowSum(flow, "n", N, M, Q)
    for k in range(3):
        flow.add("hz%d" % k, lambda: HZ.at[z], lambda: HZ.at[z], zs_other[k])
        flow.add("hx%d" % k, lambda: HX.at[x], lambda: HX.at[x], xs_other[k])
        flow.add("hy%d" % k, lambda: HY.at[y], lambda: HY.at[y], ys_other[k])
        flow.add("y%d" % k, lambda: Y.at[y], lambda: Y.at[y], ys_other[k])
    flow.add("hc", lambda: HC.at[c], lambda: HC.at[c], core)

    for load in loads[:3]:
        load.wait()
    end = din[ROWS - 16 : ROWS, 0:CONV].astype(F32)
    more = jnp.concatenate([jnp.zeros((8, CONV), F32), edge_ref[...]], axis=0)
    din[ROWS - 16 : ROWS, 0:CONV] = (end + more).astype(BF16)

    G = bufs[0]
    gains = []

    def row_block(block):
        here = pl.ds(pl.multiple_of(block * 256, 256), 256)
        grad = dot_nt(dgate[here, :], w[:, 0:HD]) + dot_nt(din[here, :], w[:, HD : WIDE - C_GATE])
        N[block] = grad.astype(BF16)
        return here, grad

    def gain_part(here, grad):
        wide = xs[here, :].astype(F32)
        r = lax.rsqrt(jnp.mean(wide * wide, axis=1, keepdims=True) + EPS)
        gains.append(fold8(grad * wide * r))

    kept = row_block(rows.yo)
    rows.first()
    loads[3].wait()
    gain_part(*kept)
    loads[4].wait()
    for k in range(4):
        part = dot(jnp.transpose(normed[:, 384 * k : 384 * k + 384]), din[...]).astype(BF16)
        G[k] = part.reshape(2, 4, 48, CONV + 128)
        reduce.cores(k)
    gain_part(*row_block(rows.yr))
    reduce.first()
    gain_part(*row_block(rows.yl))
    rows.second()
    gain_part(*row_block(rows.y))
    for k in range(40):
        j = k % 8
        small[k : k + 1, :] = jnp.sum(cgrad_ref[8 * (k // 8) : 8 * (k // 8) + 8, cols(j)], axis=0, keepdims=True)
    for j in range(6):
        small[40 + j : 41 + j, :] = jnp.sum(tgrad_ref[0:8, cols(j)], axis=0, keepdims=True)
        small[58 + j : 59 + j, :] = jnp.sum(tgrad_ref[8:16, cols(j)], axis=0, keepdims=True)
    small[64:65, :] = jnp.sum(hgrad_ref[0:8, :], axis=0, keepdims=True)
    small[65:66, :] = jnp.sum(hgrad_ref[8:16, :], axis=0, keepdims=True)
    small[66:72, :] = jnp.zeros((6, 128), F32)

    gains = jnp.sum(gains[0] + gains[1] + gains[2] + gains[3], axis=0, keepdims=True)
    for j in range(12):
        small[46 + j : 47 + j, :] = gains[:, cols(j)]
    HZ[z] = small[...]
    flow.start("hz0", "hz1", "hz2")
    reduce.second()
    flow.wait("hz0", "hz1", "hz2")
    HX[x] = HZ[0] + HZ[1] + HZ[2] + HZ[3]
    flow.start("hx0", "hx1", "hx2")
    flow.wait("hx0", "hx1", "hx2")
    HC[c] = HX[0] + HX[1] + HX[2] + HX[3]
    flow.start("hc")
    reduce.third()
    flow.wait("hc")
    total = HC[0] + HC[1]
    HY[y] = total
    plane_ref[...] = total
    flow.start("hy0", "hy1", "hy2")
    reduce.fourth()
    flow.wait("hy0", "hy1", "hy2")
    every_ref[...] = HY[0] + HY[1] + HY[2] + HY[3]
    reduce.last(gout_ref)
    Y[y] = gout_ref[:, HD:CONV]
    flow.start("y0", "y1", "y2")
    rows.last(share_ref)
    flow.wait("y0", "y1", "y2")
    ysum_ref[...] = Y[0] + Y[1] + Y[2] + Y[3]
    flow.finish()


def tail(dgate, din, W, X, normed, edge, cgrad, tgrad, hgrad):
    vmem = pl.BlockSpec(memory_space=pltpu.VMEM)
    table = pltpu.VMEM((4, 72, 128), F32)
    return pl.pallas_call(
        tail_kernel,
        out_shape=(
            shape((48, CONV + 128), F32), shape((256, D), F32), shape((48, 2 * NS), F32), shape((72, 128), F32),
            shape((72, 128), F32),
        ),
        in_specs=[pl.BlockSpec(memory_space=ANY)] * 5 + [vmem] * 4,
        out_specs=[vmem] * 5,
        scratch_shapes=[
            pltpu.VMEM((ROWS, HD), BF16), pltpu.VMEM((ROWS, CONV + 128), BF16), pltpu.VMEM((D, WIDE - C_GATE), BF16),
            pltpu.VMEM((ROWS, D), BF16), pltpu.VMEM((ROWS, D), BF16), pltpu.VMEM((72, 128), F32),
            table, table, pltpu.VMEM((2, 72, 128), F32), table, pltpu.VMEM((4, 48, 2 * NS), F32),
        ] + reduce_bufs(TAIL) + row_bufs() + [
            pltpu.SemaphoreType.DMA((48,)), pltpu.SemaphoreType.DMA((48,)), pltpu.SemaphoreType.DMA((8,)),
        ],
        compiler_params=comm_params(5, 60 << 20),
        name="tail",
    )(dgate, din, W, X, normed, edge, cgrad, tgrad, hgrad)


def finish_kernel(
    x_ref, cot_ref, out_ref, share_ref, gain_ref, mid_ref, tail_ref, ysum_ref, plane_ref, every_ref, step_ref,
    lout_ref, grad_ref, ngain_ref, gate_ref, in_ref, ps_ref, bc_ref, ci_ref, cb_ref, cs_ref, csb_ref, dec_ref, sb_ref,
    skip_ref, gg_ref, wout_ref,
):
    x, c, z, y = place()
    block = (((x * 2 + c) * 4) + z).astype(F32)
    tp = y.astype(F32)
    own = x_ref[...].astype(F32)
    lout_ref[...] = (own + out_ref[...]).astype(BF16)
    scale = lax.rsqrt(jnp.mean(own * own, axis=1, keepdims=True) + EPS)
    weighted = share_ref[...] * gain_ref[...]
    slope = scale * scale * scale * jnp.mean(own * weighted, axis=1, keepdims=True)
    grad_ref[...] = scale * weighted - own * slope + cot_ref[...].astype(F32)
    gate_ref[...] = mid_ref[:, HD : 2 * HD]
    in_ref[...] = tail_ref[:, 0:HD]
    wout_ref[...] = jnp.transpose(mid_ref[:, 0:HD])
    steps = jnp.concatenate([tail_ref[:, CONV : CONV + 128], jnp.zeros((80, 128), F32)], axis=0)
    ps_ref[...] = jnp.transpose(steps)[0:HEADS, 0:48]

    def one(keep):
        return jnp.where(keep, 1.0, 0.0).astype(F32)

    def full_nt(a, b):
        return lax.dot_general(a, b, (((1,), (1,)), ((), ())), precision=HIGH, preferred_element_type=F32)

    bc_ref[...] = dot_full(one(fiota((16, 48), 1) == fiota((16, 48), 0) + 12 * tp), ysum_ref[...])[0:12]
    plane, every = plane_ref[...], every_ref[...]
    lane, row = fiota((8, 128), 1), fiota((8, 128), 0)
    source, head = fiota((72, 128), 0), fiota((72, 128), 1)
    half, odd = parts(head, 2)
    picked = [full_nt(one(lane == 64 * q + 2 * block + row), plane) for q in (0, 1)]
    sums = [full_nt(one((lane >= 64 * q) & (lane < 64 * q + 64)), plane) for q in (0, 1)]

    def heads_of(first, rows):
        total = jnp.zeros((8, 128), F32)
        for q in (0, 1):
            total = total + dot_full(rows[q], one((source == first + half) & (odd == q)))
        return total

    for k in range(4):
        ci_ref[k] = heads_of(8 * k, picked)[0:2, 0:HEADS]
    cb_ref[...] = heads_of(32, picked)[0:2, 0:HEADS]
    gg_ref[...] = heads_of(40, picked)[0:2, 0:HEADS]
    skip_ref[...] = heads_of(58, sums)[0:1, 0:HEADS]
    dec_ref[...] = plane[64:65, 0:HEADS] * step_ref[2:3, 0:HEADS]
    sb_ref[...] = plane[65:66, 0:HEADS]
    at = 8 * block + 2 * tp
    upper, at = parts(at, 128)
    by_tap = full_nt(one(lane == at + row), every)
    cs_ref[...] = dot_full(by_tap, one(source == 8 * head + 6 + upper))[0:2, 0:4]
    rows8 = dot_full(one((fiota((8, 72), 1) == 8 * fiota((8, 72), 0) + 6 + upper)), every)
    csb_ref[...] = full_nt(rows8, one(fiota((128, 128), 1) == at + fiota((128, 128), 0)))[4:5, 0:2]
    flat = 48 * block + 12 * tp + head
    line, spot = parts(flat, 128)
    spread = full_nt(every, one(fiota((128, 128), 1) == spot[0:1].reshape(1, 128).T))
    ngain_ref[...] = jnp.sum(jnp.where(source == 46 + line, spread, 0.0), axis=0, keepdims=True)[:, 0:12]


def finish(*args):
    outs = [
        ((256, D), BF16), ((256, D), F32), ((1, 12), F32), ((48, HD), F32), ((48, HD), F32), ((HEADS, 48), F32),
        ((12, 2 * NS), F32), ((4, 2, HEADS), F32), ((2, HEADS), F32), ((2, 4), F32), ((1, 2), F32), ((1, HEADS), F32),
        ((1, HEADS), F32), ((1, HEADS), F32), ((2, HEADS), F32), ((HD, 48), F32),
    ]
    return pl.pallas_call(
        finish_kernel,
        grid=(1,),
        out_shape=[shape(*o) for o in outs],
        in_specs=[whole_spec(*a.shape) for a in args],
        out_specs=[whole_spec(*o[0]) for o in outs],
        compiler_params=pltpu.CompilerParams(vmem_limit_bytes=60 << 20),
        name="finish",
    )(*args)


def per_device(
    layer_input, out_cotangent, seq_lengths, norm_gain, proj_gate, proj_input, proj_step, proj_state, conv_inner,
    conv_inner_bias, conv_state, conv_state_bias, decay_log, step_bias, skip_scale, gate_gain, proj_out,
):
    (
        W, X, cots, normed, gate, ci, ds, xbc, xdt, dt, cum, sig, fresh, pos, near, summs, edge, conv, ngain, gain, step,
    ) = front(
        (layer_input, out_cotangent, proj_out.T, proj_gate, proj_input, proj_state),
        seq_lengths,
        (
            proj_step.T, conv_inner.transpose(0, 2, 1), conv_inner_bias.T, gate_gain.T, conv_state, conv_state_bias[None],
            norm_gain[None], decay_log[None], step_bias[None], skip_scale[None],
        ),
    )
    W, X, cot_all = W.reshape(D, WIDE), X.reshape(ROWS, D), cots.reshape(ROWS, D)
    entered, branch, dgate, dmix, gfresh, gsumm, tgrad = forward(
        summs, xbc, near, cum, pos, fresh, gate, cot_all, W, gain
    )
    din, cgrad, hgrad, dedge, gmid, out_share = middle(
        gsumm, W, cot_all, normed, branch, dgate,
        xbc, xdt, dt, cum, sig, dmix, entered, gfresh, ds, ci, pos, edge, conv, step,
    )
    gtail, share, ysum, plane, every = tail(dgate, din, W, X, normed, dedge, cgrad, tgrad, hgrad)
    (
        layer_output, input_grad, g_norm, g_gate, g_in, g_step, g_state, g_conv, g_bias, g_cs, g_csb, g_decay, g_sb, g_skip,
        g_gain, g_out,
    ) = finish(layer_input, out_cotangent, out_share, share, ngain, gmid, gtail, ysum, plane, every, step)
    return (
        layer_output, input_grad, g_norm[0], g_gate, g_in, g_step.T, g_state, g_conv.transpose(0, 2, 1), g_bias.T, g_cs.T,
        g_csb[0], g_decay[0], g_sb[0], g_skip[0], g_gain.T, g_out,
    )


def solution(mesh):
    both = ("shard", "ctx")
    every = ("shard", "ctx", "tp")
    return jax.shard_map(
        per_device,
        mesh=mesh,
        in_specs=(
            P(every, None), P(every, None), P("shard", None), P(both), P(both, "tp"), P(both, "tp"), P(both, "tp"),
            P(both, None), P(None, "tp", both), P("tp", both), P(None, both), P(both), P("tp"), P("tp"), P("tp"),
            P("tp", both), P("tp", both),
        ),
        out_specs=(
            P(every, None), P(every, None), P(every), P(both, "tp"), P(both, "tp"), P(both, "tp"), P(every, None),
            P(None, "tp", both), P("tp", both), P(None, every), P(every), P("tp"), P("tp"), P("tp"), P("tp", both),
            P("tp", both),
        ),
        check_vma=False,
    )
```

```python
import functools

import jax
import jax.numpy as jnp
from jax import lax
from jax.experimental import pallas as pl
from jax.experimental.pallas import tpu as pltpu
from jax.sharding import PartitionSpec as P

MESH = pl.DeviceIdType.MESH
ANY = pl.ANY
F32 = jnp.float32
BF16 = jnp.bfloat16
EPS = 1e-05
LOG2E = 1.4426950408889634
HIGH = lax.Precision.HIGHEST

D = 1536
ROWS = 1024
HD = 768
HEADS = 12
PAIRS = 6
NS = 128
CONV = 1024
LEN = 128
CHUNKS = 8
E_ALL = 3072
C_OUT, C_GATE, C_IN, C_BC, C_MISC, WIDE = 0, 768, 1536, 2304, 2560, 2688
HALF_A, HALF_A1, HALF_B1 = 1408, 768, 2048


def dot(a, b):
    return jnp.dot(a, b, preferred_element_type=F32)


def dot_nt(a, b):
    return lax.dot_general(a, b, (((1,), (1,)), ((), ())), preferred_element_type=F32)


def dot_tn(a, b):
    return lax.dot_general(a, b, (((0,), (0,)), ((), ())), preferred_element_type=F32)


def dot_full(a, b):
    return jnp.dot(a, b, precision=HIGH, preferred_element_type=F32)


def iota(shape, axis):
    return lax.broadcasted_iota(jnp.int32, shape, axis)


def place():
    s = lax.axis_index("shard")
    return s // 2, s % 2, lax.axis_index("ctx"), lax.axis_index("tp")


def device(x, c, z, y):
    return {"shard": x * 2 + c, "ctx": z, "tp": y}


def enter(others):
    barrier = pltpu.get_barrier_semaphore()
    for other in others:
        pl.semaphore_signal(barrier, inc=1, device_id=other, device_id_type=MESH)
    pl.semaphore_wait(barrier, len(others))


class Sends:
    def __init__(self, send_sem, recv_sem):
        self.send_sem, self.recv_sem, self.copies = send_sem, recv_sem, []

    def __call__(self, src, dst, to):
        k = len(self.copies)
        copy = pltpu.make_async_remote_copy(
            src_ref=src,
            dst_ref=dst,
            send_sem=self.send_sem.at[k],
            recv_sem=self.recv_sem.at[k],
            device_id=to,
            device_id_type=MESH,
        )
        copy.start()
        self.copies.append(copy)
        return copy

    def finish(self):
        for copy in self.copies:
            copy.wait_send()


class Flow:
    def __init__(self, send_sem, recv_sem):
        self.send_sem, self.recv_sem, self.known = send_sem, recv_sem, {}

    def add(self, name, src, dst, to):
        self.known[name] = (len(self.known), src, dst, to)

    def copy(self, name):
        k, src, dst, to = self.known[name]
        return pltpu.make_async_remote_copy(
            src_ref=src(),
            dst_ref=dst(),
            send_sem=self.send_sem.at[k],
            recv_sem=self.recv_sem.at[k],
            device_id=to,
            device_id_type=MESH,
        )

    def start(self, *names):
        for name in names:
            self.copy(name).start()

    def wait(self, *names):
        for name in names:
            self.copy(name).wait_recv()

    def finish(self):
        for name in self.known:
            self.copy(name).wait_send()


def sems(n):
    return [pltpu.SemaphoreType.DMA((n,)), pltpu.SemaphoreType.DMA((n,)), pltpu.SemaphoreType.DMA((4,))]


def comm_params(collective_id, vmem=None):
    return pltpu.CompilerParams(
        collective_id=collective_id, has_side_effects=True, vmem_limit_bytes=vmem
    )


def shape(dims, kind):
    return jax.ShapeDtypeStruct(dims, kind)


def spread_heads(v, p):
    r = v.shape[0]
    low = jnp.broadcast_to(v[:, 2 * p : 2 * p + 1], (r, 128))
    high = jnp.broadcast_to(v[:, 2 * p + 1 : 2 * p + 2], (r, 128))
    return jnp.where(iota((r, 128), 1) < 64, low, high)


def fill_places(places):
    source, target = iota((256, 256), 0), iota((256, 256), 1)
    for q in range(PAIRS // 2):
        places[q] = jnp.where(source % 128 == 4 * q + target // 64, 1.0, 0.0).astype(BF16)


class Spread:
    def __init__(self, places, *columns):
        self.places, self.count = places, len(columns)
        self.values = jnp.concatenate([jnp.concatenate(in_two(v), axis=1) for v in columns], axis=0)

    def __call__(self, p):
        if p % 2 == 0:
            self.now = dot(self.values, self.places[p // 2])
        here = slice(128 * (p % 2), 128 * (p % 2) + 128)
        found = [self.now[LEN * k : LEN * k + LEN, here] for k in range(self.count)]
        return found if self.count > 1 else found[0]


def cols(p):
    return slice(128 * p, 128 * p + 128)


def stacked(pair):
    lane = iota(pair.shape, 1)
    zero = jnp.zeros_like(pair)
    return jnp.concatenate([jnp.where(lane < 64, pair, zero), jnp.where(lane < 64, zero, pair)], axis=0)


def in_two(v):
    high = v.astype(BF16)
    return high, (v - high.astype(F32)).astype(BF16)


def twice(v):
    return jnp.concatenate([v, v], axis=1)


def link_rows(decay):
    high, low = in_two(jnp.broadcast_to(decay, (8, HD)))
    return jnp.concatenate([high, low], axis=0)


def link_of(summ_ref, j):
    both = summ_ref[j, NS : NS + 16, :].astype(F32)
    return both[0:1] + both[8:9]


def head_pick(p):
    lane, head = iota((128, 128), 0), iota((128, 128), 1)
    return jnp.where(head == 2 * p + lane // 64, 1.0, 0.0).astype(BF16)


def head_sum(pair, p):
    return dot(pair.astype(BF16), head_pick(p))


def triangle(kind):
    t, s = iota((LEN, LEN), 0), iota((LEN, LEN), 1)
    keep = {"incl": s <= t, "suffix": s >= t, "strict": s < t}[kind]
    return jnp.where(keep, 1.0, 0.0).astype(F32)


def ordered(*terms):
    left, right = [], []
    for kind, v in terms:
        high, low = in_two(v)
        rest = (v - high.astype(F32) - low.astype(F32)).astype(BF16)
        left += [triangle(kind).astype(BF16)] * 3
        right += [high, low, rest]
    return dot(jnp.concatenate(left, axis=1), jnp.concatenate(right, axis=0))


def fold8(v):
    return jnp.sum(v.reshape(v.shape[0] // 8, 8, v.shape[1]), axis=0)


def whole_spec(*dims):
    return pl.BlockSpec(dims, lambda i: (0,) * len(dims), pipeline_mode=pl.Buffered(1))


def rows_spec(r, c, back=None):
    if back is None:
        return pl.BlockSpec((r, c), lambda i: (i, 0))
    return pl.BlockSpec((r, c), lambda i: (back - i, 0))


TILE = 256
TILES = ROWS // TILE


def gather(go, W, X, cots, x_ref, cot_ref, edge, locals_, between):
    x, c, z, y = place()
    xr, xl, xo = (x + 1) % 4, (x + 3) % 4, (x + 2) % 4
    zr, zl, zo = (z + 1) % 4, (z + 3) % 4, (z + 2) % 4
    yr, yl = (y + 1) % 4, (y + 3) % 4
    dxr, dxl = device(xr, c, z, y), device(xl, c, z, y)
    dzr, dzl = device(x, c, zr, y), device(x, c, zl, y)
    dyr, dyl = device(x, c, z, yr), device(x, c, z, yl)
    dco = device(x, 1 - c, z, y)
    own, own_x, own_c = locals_
    for copy in own:
        copy.start()
    own_x.start()
    own_c.start()
    others_z = [dzr, dzl, device(x, c, zo, y)]
    enter([dxr, dxl, dyr, dyl, dco] + others_z)
    A, A1, A2 = pl.ds(0, HALF_A), pl.ds(0, HALF_A1), pl.ds(HALF_A1, HALF_A - HALF_A1)
    B = pl.ds(HALF_A, WIDE - HALF_A)
    B1, B2 = pl.ds(HALF_A, HALF_B1 - HALF_A), pl.ds(HALF_B1, WIDE - HALF_B1)
    H1, H2 = pl.ds(0, 128), pl.ds(128, 128)

    def same(ref, to):
        return go(ref, ref, to)

    def both_x(zz):
        return same(W.at[x, c, zz, :, A], dxr), same(W.at[x, c, zz, :, A], dxl)

    def both_z(xx):
        return same(W.at[xx, c, z, :, B], dzr), same(W.at[xx, c, z, :, B], dzl)

    def on_x(xx, cols):
        return W.at[xx, c, :, :, cols]

    def on_z(zz, cols):
        return W.at[:, c, zz, :, cols]

    x_r = go(x_ref, X.at[y], dyr)
    x_l = go(x_ref, X.at[y], dyl)
    for copy in own:
        copy.wait()
    a_r = same(W.at[x, c, z, :, A], dzr)
    b_r = same(W.at[x, c, z, :, B], dxr)
    a_l = same(W.at[x, c, z, :, A], dzl)
    b_l = same(W.at[x, c, z, :, B], dxl)
    a2, b2, last = [both_x(z)], [both_z(x)], []
    a_r.wait_recv()
    a_fr = same(W.at[x, c, zl, :, A1], dzr)
    b_r.wait_recv()
    b_fr = same(W.at[xl, c, z, :, B1], dxr)
    a_l.wait_recv()
    a_fl = same(W.at[x, c, zr, :, A2], dzl)
    b_l.wait_recv()
    b_fl = same(W.at[xr, c, z, :, B2], dxl)
    a2.append(both_x(zl))
    b2.append(both_z(xl))
    a2.append(both_x(zr))
    b2.append(both_z(xr))
    a_fr.wait_recv()
    a_fl.wait_recv()
    a2.append(both_x(zo))
    b_fr.wait_recv()
    b_fl.wait_recv()
    b2.append(both_z(xo))
    last.append(same(on_x(x, A), dco))
    last.append(same(on_z(z, B), dco))
    fa, fb = [], []

    def onward(k):
        zz, xx = (z, zl, zr, zo)[k], (x, xl, xr, xo)[k]
        a2[k][0].wait_recv()
        fa.append(same(W.at[xl, c, zz, :, A1], dxr))
        b2[k][0].wait_recv()
        fb.append(same(W.at[xx, c, zl, :, B1], dzr))
        a2[k][1].wait_recv()
        fa.append(same(W.at[xr, c, zz, :, A2], dxl))
        b2[k][1].wait_recv()
        fb.append(same(W.at[xx, c, zr, :, B2], dzl))

    onward(0)
    between()
    onward(1)
    x_r.wait_recv()
    x_fr = same(X.at[yl, H1], dyr)
    x_l.wait_recv()
    x_fl = same(X.at[yr, H2], dyl)
    onward(2)
    onward(3)
    last.append(same(on_x(xl, A), dco))
    last.append(same(on_z(zl, B), dco))
    last.append(same(on_x(xr, A), dco))
    last.append(same(on_z(zr, B), dco))
    own_x.wait()
    x_fr.wait_recv()
    x_fl.wait_recv()
    e = go(X.at[3, pl.ds(240, 16)], edge, dzr)
    c_r = go(cot_ref, cots.at[y], dyr)
    c_l = go(cot_ref, cots.at[y], dyl)
    for k in (0, 2, 4, 6):
        fa[k].wait_recv()
    last.append(same(on_x(xo, A1), dco))
    for k in (0, 2, 4, 6):
        fb[k].wait_recv()
    last.append(same(on_z(zo, B1), dco))
    for k in (1, 3, 5, 7):
        fa[k].wait_recv()
    last.append(same(on_x(xo, A2), dco))
    for k in (1, 3, 5, 7):
        fb[k].wait_recv()
    last.append(same(on_z(zo, B2), dco))
    e.wait_recv()
    for copy in last:
        copy.wait_recv()
    more = []

    def cot_onward():
        c_r.wait_recv()
        more.append(same(cots.at[yl, H1], dyr))
        c_l.wait_recv()
        more.append(same(cots.at[yr, H2], dyl))

    def cot_end():
        own_c.wait()
        for copy in more:
            copy.wait_recv()

    return cot_onward, cot_end, others_z


def parts(v, size):
    q = jnp.floor((v + 0.5) * (1.0 / size))
    return q, v - size * q


def fiota(dims, axis):
    return iota(dims, axis).astype(F32)


def front_kernel(
    x_ref, cot_ref, wout_ref, gate_w, in_w, bc_w, lens_ref, ps_ref, ci_w, cb_w, gg_w, cs_w, csb_w, ng_w, dec_ref, sb_ref, skip_ref,
    W_out, X_out, cots, normed_ref, gate_ref, ci_ref, ds_ref, xbc_ref, xdt_ref, dt_ref, cum_ref, sig_ref, fresh_ref, pos_ref,
    near_ref, summs_ref, edge_ref, conv_out, ngain_out, gain_out, step_ref,
    W, X, E, Q, normed, gate, ci, ds, xbc, xdt, dts, cums, sigs, fresh, pos, scale, buf0, buf1, conv, state, decay, table, summ, near, spot, places,
    ssem, rsem, lsem, osem,
):
    x, c, z, y = place()
    go = Sends(ssem, rsem)
    own = [
        pltpu.make_async_copy(src, W.at[x, c, z, :, pl.ds(first, src.shape[1])], lsem.at[k])
        for k, (src, first) in enumerate([(wout_ref, C_OUT), (gate_w, C_GATE), (in_w, C_IN), (bc_w, C_BC)])
    ]
    locals_ = [
        own,
        pltpu.make_async_copy(x_ref, X.at[y], lsem.at[4]),
        pltpu.make_async_copy(cot_ref, cots.at[y], lsem.at[5]),
    ]
    table[...] = jnp.zeros_like(table)
    table[0:HEADS, 0:48] = ps_ref[...].astype(F32)
    for k in range(4):
        table[12 + 2 * k : 14 + 2 * k, 0:HEADS] = ci_w[k].astype(F32)
    table[20:22, 0:HEADS] = cb_w[...].astype(F32)
    table[22:24, 0:HEADS] = gg_w[...].astype(F32)
    table[24:28, 0:8] = cs_w[...].astype(F32)
    table[28:29, 0:8] = csb_w[...].astype(F32)
    table[29:30, 0:48] = ng_w[...].astype(F32)
    W[x, c, z, :, C_MISC:WIDE] = jnp.transpose(table[...])[0:48].astype(BF16)
    rate = -jnp.exp(dec_ref[...])
    step_ref[...] = jnp.zeros_like(step_ref)
    step_ref[0:1, 0:HEADS] = sb_ref[...]
    step_ref[1:2, 0:HEADS] = rate * LOG2E
    step_ref[2:3, 0:HEADS] = rate
    step_ref[3:4, 0:HEADS] = skip_ref[...]

    def between():
        fill_places(places)
        block, inner = parts(fiota((D, HD), 0), 48)
        _, head = parts(inner, 12)
        place_of = head * 64 + block * 2
        lane = fiota((D, HD), 1)
        for j in range(2):
            Q[j] = jnp.where(lane == place_of + j, 1.0, 0.0).astype(BF16)
        col_block, col8 = parts(fiota((D, 256), 1), 8)
        row_block, row_in = parts(fiota((D, 256), 0), 48)
        spot[...] = jnp.where((row_block == col_block) & (row_in == col8), 1.0, 0.0).astype(BF16)
        token = fiota((ROWS, 128), 0) + (z * ROWS).astype(F32)
        begin = jnp.zeros((ROWS, 128), F32)
        end = jnp.float32(0.0)
        for k in range(3):
            end = end + lens_ref[0, k].astype(F32)
            begin = jnp.where(token >= end, end, begin)
        pos[...] = token - begin

    cot_onward, cot_end, others_z = gather(go, W, X, cots, x_ref, cot_ref, E, locals_, between)
    out_copies = [
        pltpu.make_async_copy(W, W_out, osem.at[0]),
        pltpu.make_async_copy(X, X_out, osem.at[1]),
    ]
    for copy in out_copies:
        copy.start()

    misc = W[:, :, :, :, C_MISC:WIDE].reshape(D, 128)
    row8, lane8 = iota((8, 128), 0), iota((8, 128), 1)

    def across(column):
        return dot_nt(jnp.where(lane8 == column, 1.0, 0.0).astype(BF16), misc)

    _, r_in = parts(fiota((8, D), 1), 48)
    found = jnp.zeros((8, HD), F32)
    for j in range(2):
        taps = jnp.where(r_in < HEADS, across(12 + 2 * row8 + j), 0.0)
        found = found + dot(taps.astype(BF16), Q[j])
    conv[:, 0:HD] = found
    rest = across(jnp.where(row8 < 4, 24 + row8, jnp.where(row8 == 4, 28, 29)))
    conv[:, HD:CONV] = dot(rest.astype(BF16), spot[...])
    ngain = rest[5:6]
    conv_out[...] = conv[...]
    ngain_out[...] = ngain
    gain_out[...] = found[5:6]

    def norm(rows):
        wide = rows.astype(F32)
        r = lax.rsqrt(jnp.mean(wide * wide, axis=1, keepdims=True) + EPS)
        return (wide * r * ngain).astype(BF16)

    def weight(first, last):
        return W[:, :, :, :, first:last].reshape(D, last - first)

    edge = dot(norm(E[...]), weight(C_IN, C_MISC)).astype(BF16)
    edge_ref[...] = edge
    state[...] = jnp.zeros_like(state)
    decay[...] = jnp.ones_like(decay)
    bufs = (buf0, buf1)
    buf0[0:8, :] = edge.astype(F32)[8:16]

    def project(i):
        rows = slice(TILE * i, TILE * i + TILE)
        low = norm(X[i])
        normed[rows, :] = low
        conv_in = dot(low, weight(C_IN, C_MISC)).astype(BF16)
        ci[rows, :] = conv_in
        bufs[i % 2][8 : 8 + TILE, :] = conv_in.astype(F32)
        sigs[rows, :] = dot(low, weight(C_MISC, WIDE))

    def convolve(i):
        buf = bufs[i % 2]
        rows = slice(TILE * i, TILE * i + TILE)
        if i + 1 < TILES:
            bufs[(i + 1) % 2][0:8, :] = buf[TILE : TILE + 8, :]
        place_in = pos[rows, :]
        for j in range(CONV // 128):
            lanes = cols(j)
            acc = buf[8 : 8 + TILE, lanes] * conv[3:4, lanes] + conv[4:5, lanes]
            for back in (1, 2, 3):
                term = buf[8 - back : 8 - back + TILE, lanes] * conv[3 - back : 4 - back, lanes]
                acc = acc + jnp.where(place_in >= back, term, 0.0)
            sig = jax.nn.sigmoid(acc)
            ds[rows, lanes] = sig * (1.0 + acc * (1.0 - sig))
            xbc[rows, lanes] = (acc * sig).astype(BF16)
        lane = iota((TILE, 128), 1)
        pre = sigs[rows, :] + step_ref[0:1, :]
        small = jnp.exp(-jnp.abs(pre))
        log1p = jnp.where(
            small < 1e-3, small * (1.0 - 0.5 * small + (1.0 / 3.0) * small * small), jnp.log(1.0 + small)
        )
        dt = jnp.where(lane < HEADS, jnp.maximum(pre, 0.0) + log1p, 0.0)
        dts[rows, :] = dt
        sigs[rows, :] = jax.nn.sigmoid(pre)
        rate = dt * step_ref[1:2, :]
        for sub in range(TILE // LEN):
            inside = slice(LEN * sub, LEN * sub + LEN)
            rows = slice(TILE * i + LEN * sub, TILE * i + LEN * sub + LEN)
            cum = dot_full(triangle("incl"), rate[inside])
            cums[rows, :] = cum
            last = cum[LEN - 1 : LEN, :]
            pos_last = pos[TILE * i + LEN * sub + LEN - 1 : TILE * i + LEN * sub + LEN, :]
            row = iota((LEN, 128), 0).astype(F32)
            fade = jnp.where((LEN - 1) - row <= pos_last, jnp.exp2(last - cum), 0.0)
            whole = jnp.where(pos_last > LEN - 1, jnp.exp2(last), 0.0)
            basis_t = jnp.transpose(xbc[rows, HD : HD + NS].astype(F32)).astype(BF16)
            spread = Spread(places, dt[inside], fade)
            for p in range(PAIRS):
                dt_pair, fade_pair = spread(p)
                low = (xbc[rows, cols(p)].astype(F32) * dt_pair).astype(BF16)
                xdt[rows, cols(p)] = low
                ended = (low.astype(F32) * fade_pair).astype(BF16)
                new = dot(basis_t, ended)
                fresh[i * (TILE // LEN) + sub, :, cols(p)] = new
                factor = spread_heads(whole, p)
                state[:, cols(p)] = state[:, cols(p)] * factor + new
                decay[:, cols(p)] = decay[:, cols(p)] * factor

    pairs = [
        (normed, normed_ref), (ci, ci_ref), (ds, ds_ref), (xbc, xbc_ref), (xdt, xdt_ref), (dts, dt_ref),
        (cums, cum_ref), (sigs, sig_ref), (pos, pos_ref),
    ]

    def store(i):
        rows = slice(TILE * i, TILE * i + TILE)
        for k, (src, dst) in enumerate(pairs):
            out_copies.append(pltpu.make_async_copy(src.at[rows], dst.at[rows], osem.at[2 + 11 * i + k]))
        n = TILE // LEN
        here = slice(n * i, n * i + n)
        out_copies.append(pltpu.make_async_copy(fresh.at[here], fresh_ref.at[here], osem.at[2 + 11 * i + 10]))
        for copy in out_copies[-10:]:
            copy.start()

    project(0)
    for i in range(TILES):
        if i == 2:
            cot_onward()
        if i + 1 < TILES:
            project(i + 1)
        convolve(i)
        store(i)
    summ[0:NS, :] = state[...].astype(BF16)
    summ[NS : NS + 16, :] = link_rows(decay[...])
    swaps = [go(summ, summs_ref.at[z], other) for other in others_z]
    out_copies.append(pltpu.make_async_copy(summ, summs_ref.at[z], osem.at[46]))
    out_copies[-1].start()
    for i in range(TILES):
        rows = slice(TILE * i, TILE * i + TILE)
        gate[rows, :] = dot(normed[rows, :], weight(C_GATE, C_IN))
        out_copies.append(pltpu.make_async_copy(gate.at[rows], gate_ref.at[rows], osem.at[2 + 11 * i + 9]))
        out_copies[-1].start()
    t, low_s = iota((LEN, LEN), 0), iota((LEN, LEN), 1)
    gap = (t - low_s).astype(F32)

    def local_chunk(i, _):
        rows = pl.ds(pl.multiple_of(LEN * i, LEN), LEN)
        place_in, cum = pos[rows, :], cums[rows, :]
        keep = (gap >= 0) & (gap <= place_in)
        cum_t = jnp.transpose(cum)
        inner = dot_nt(xbc[rows, HD + NS : CONV], xbc[rows, HD : HD + NS])
        for p in range(PAIRS):
            scores = []
            for h in (2 * p, 2 * p + 1):
                span = jnp.where(keep, cum[:, h : h + 1] - cum_t[h : h + 1, :], -1e30)
                scores.append((jnp.exp2(span) * inner).astype(BF16))
            local = dot(jnp.concatenate(scores, axis=1), stacked(xdt[rows, cols(p)]))
            skip = spread_heads(step_ref[...], p)[3:4]
            near[rows, cols(p)] = local + skip * xbc[rows, cols(p)].astype(F32)
        return 0

    lax.fori_loop(0, CHUNKS, local_chunk, 0)
    out_copies.append(pltpu.make_async_copy(near, near_ref, osem.at[47]))
    out_copies[-1].start()
    cot_end()
    for copy in swaps:
        copy.wait_recv()
    for copy in out_copies:
        copy.wait()
    go.finish()


def front(big, lens, small):
    vmem = pl.BlockSpec(memory_space=pltpu.VMEM)
    anywhere = pl.BlockSpec(memory_space=ANY)
    outs = [
        ((ROWS, D), BF16), ((ROWS, HD), F32), ((ROWS, CONV), BF16), ((ROWS, CONV), F32), ((ROWS, CONV), BF16),
        ((ROWS, HD), BF16), ((ROWS, 128), F32), ((ROWS, 128), F32), ((ROWS, 128), F32), ((CHUNKS, NS, HD), F32),
        ((ROWS, 128), F32),
    ]
    return pl.pallas_call(
        front_kernel,
        out_shape=[shape((4, 2, 4, 48, WIDE), BF16), shape((4, 256, D), BF16), shape((4, 256, D), BF16)]
        + [shape(*o) for o in outs]
        + [shape((ROWS, HD), F32), shape((4, NS + 16, HD), BF16), shape((16, CONV), BF16), shape((8, CONV), F32), shape((1, D), F32)]
        + [shape((1, HD), F32), shape((8, 128), F32)],
        in_specs=[anywhere] * 6 + [pl.BlockSpec(memory_space=pltpu.SMEM)] + [vmem] * 10,
        out_specs=[anywhere] * 16 + [vmem] * 5,
        scratch_shapes=[
            pltpu.VMEM((4, 2, 4, 48, WIDE), BF16), pltpu.VMEM((4, 256, D), BF16), pltpu.VMEM((16, D), BF16),
            pltpu.VMEM((2, D, HD), BF16),
        ]
        + [pltpu.VMEM(*o) for o in outs]
        + [
            pltpu.VMEM((ROWS, 128), F32), pltpu.VMEM((8 + TILE, CONV), F32), pltpu.VMEM((8 + TILE, CONV), F32),
            pltpu.VMEM((8, CONV), F32), pltpu.VMEM((NS, HD), F32), pltpu.VMEM((1, HD), F32),
            pltpu.VMEM((128, 128), F32), pltpu.VMEM((NS + 16, HD), BF16), pltpu.VMEM((ROWS, HD), F32),
            pltpu.VMEM((D, 256), BF16), pltpu.VMEM((PAIRS // 2, 256, 256), BF16),
            pltpu.SemaphoreType.DMA((72,)), pltpu.SemaphoreType.DMA((72,)), pltpu.SemaphoreType.DMA((8,)),
            pltpu.SemaphoreType.DMA((48,)),
        ],
        compiler_params=comm_params(0, 60 << 20),
        name="front",
    )(*big, lens, *small)


LAG = 2


def forward_kernel(
    summ, xbc_ref, near_ref, cum_ref, pos_ref, fresh_ref, gate_ref, cot_ref, w_ref, gain_ref,
    xbc2_ref, cum2_ref, pos2_ref, gate2_ref,
    enter_ref, branch_ref, dgate_ref, dmix_ref, gfresh_ref, gsumm_ref, acc_ref,
    mixed, db, state, back, decay, sums, places, ssem, rsem,
):
    step = pl.program_id(0)
    x, c, z, y = place()
    subs = TILE // LEN
    flow = Flow(ssem, rsem)
    others_y = [device(x, c, z, (y + k) % 4) for k in (1, 3, 2)]
    for i in range(TILES):
        for k in range(3):
            there = lambda i=i: sums.at[y, pl.ds(subs * i, subs)]
            flow.add("y%d%d" % (i, k), there, there, others_y[k])

    @pl.when(step == 0)
    def _():
        enter(others_y)
        fill_places(places)
        acc_ref[...] = jnp.zeros_like(acc_ref)
        start = jnp.zeros((NS, HD), F32)
        for j in range(3):
            start = jnp.where(j < z, start * link_of(summ, j) + summ[j, 0:NS, :].astype(F32), start)
        state[...] = start
        back[...] = jnp.zeros_like(back)
        decay[...] = jnp.ones_like(decay)

    @pl.when(step < TILES)
    def _():
        here = pl.ds(pl.multiple_of(step * TILE, TILE), TILE)
        db[here, :] = dot(cot_ref[...], w_ref[...])
        t, s = iota((LEN, LEN), 0), iota((LEN, LEN), 1)
        for sub in range(subs):
            rows = slice(LEN * sub, LEN * sub + LEN)
            there = pl.ds(pl.multiple_of(step * TILE + LEN * sub, LEN), LEN)
            pos, cum = pos_ref[rows, :], cum_ref[rows, :]
            basis_c = xbc_ref[rows, HD + NS : CONV]
            fade = jnp.where(pos > t.astype(F32), jnp.exp2(cum), 0.0)
            whole = jnp.where(pos[LEN - 1 : LEN] > LEN - 1, jnp.exp2(cum[LEN - 1 : LEN]), 0.0)
            spread = Spread(places, fade)
            square = jnp.zeros((LEN, 128), F32)
            cross = jnp.zeros((LEN, 128), F32)
            for p in range(PAIRS):
                lanes = cols(p)
                entered = state[:, lanes].astype(BF16)
                enter_ref[sub, :, lanes] = entered
                whole_y = near_ref[rows, lanes] + dot(basis_c, entered) * spread(p)
                mixed[there, lanes] = whole_y
                gate = gate_ref[rows, lanes]
                gated = whole_y * gate * jax.nn.sigmoid(gate)
                square = square + gated * gated
                cross = cross + gated * gain_ref[:, lanes] * db[there, lanes]
                state[:, lanes] = state[:, lanes] * spread_heads(whole, p) + fresh_ref[sub, :, lanes]
            sq = jnp.sum(square, axis=1, keepdims=True)
            cr = jnp.sum(cross, axis=1, keepdims=True)
            both = jnp.where(s == 0, sq, jnp.where(s == 1, cr, 0.0))
            sums[y, step * subs + sub] = jnp.transpose(both)[0:8]

    for i in range(TILES):

        @pl.when(step == i)
        def _():
            flow.start("y%d0" % i, "y%d1" % i, "y%d2" % i)

        @pl.when(step == i + LAG)
        def _():
            flow.wait("y%d0" % i, "y%d1" % i, "y%d2" % i)

    @pl.when(step >= LAG)
    def _():
        tile = step - LAG
        for sub in range(subs):
            rows = slice(LEN * sub, LEN * sub + LEN)
            there = pl.ds(pl.multiple_of(tile * TILE + LEN * sub, LEN), LEN)
            chunk = tile * subs + sub
            total = sums[0, chunk] + sums[1, chunk] + sums[2, chunk] + sums[3, chunk]
            both = jnp.transpose(jnp.concatenate([total, jnp.zeros((120, 128), F32)], axis=0))
            r = lax.rsqrt(both[:, 0:1] * (1.0 / E_ALL) + EPS)
            slope = r * r * r * both[:, 1:2] * (1.0 / E_ALL)
            pos, cum = pos2_ref[rows, :], cum2_ref[rows, :]
            fade = jnp.where(pos > iota((LEN, 128), 0).astype(F32), jnp.exp2(cum), 0.0)
            whole = jnp.where(pos[LEN - 1 : LEN] > LEN - 1, jnp.exp2(cum[LEN - 1 : LEN]), 0.0)
            basis_t = jnp.transpose(xbc2_ref[rows, HD + NS : CONV].astype(F32)).astype(BF16)
            spread = Spread(places, fade)
            for p in range(PAIRS):
                lanes = cols(p)
                mix, gate, grad = mixed[there, lanes], gate2_ref[rows, lanes], db[there, lanes]
                gain = gain_ref[:, lanes]
                sig = jax.nn.sigmoid(gate)
                silu = gate * sig
                gated = mix * silu
                scaled = gated * r
                branch_ref[rows, lanes] = (scaled * gain).astype(BF16)
                acc_ref[0:8, lanes] += fold8(grad * scaled)
                dgated = r * gain * grad - gated * slope
                dmix = dgated * silu
                dgate_ref[rows, lanes] = (dgated * mix * sig * (1.0 + gate * (1.0 - sig))).astype(BF16)
                dmix_ref[rows, lanes] = dmix
                acc_ref[8:16, lanes] += fold8(dmix * xbc2_ref[rows, lanes].astype(F32))
                fresh = dot(basis_t, (dmix * spread(p)).astype(BF16))
                gfresh_ref[sub, :, lanes] = fresh
                back[:, lanes] = back[:, lanes] + decay[:, lanes] * fresh
                decay[:, lanes] = decay[:, lanes] * spread_heads(whole, p)

    @pl.when(step == TILES + LAG - 1)
    def _():
        gsumm_ref[0:NS, :] = back[...].astype(BF16)
        gsumm_ref[NS : NS + 16, :] = link_rows(decay[...])
        flow.finish()


def forward(summs, xbc, near, cum, pos, fresh, gate, cot, W, gain):
    sub = TILE // LEN

    def first(i):
        return jnp.minimum(i, TILES - 1)

    def second(i):
        return jnp.maximum(i - LAG, 0)

    def rows(c, at):
        return pl.BlockSpec((TILE, c), lambda i: (at(i), 0))

    def states(at):
        return pl.BlockSpec((sub, NS, HD), lambda i: (at(i), 0, 0))

    return pl.pallas_call(
        forward_kernel,
        grid=(TILES + LAG,),
        in_specs=[
            whole_spec(4, NS + 16, HD), rows(CONV, first), rows(HD, first), rows(128, first), rows(128, first),
            states(first), rows(HD, first), rows(D, first), whole_spec(D, HD), whole_spec(1, HD),
            rows(CONV, second), rows(128, second), rows(128, second), rows(HD, second),
        ],
        out_specs=[
            states(first), rows(HD, second), rows(HD, second), rows(HD, second), states(second),
            whole_spec(NS + 16, HD), whole_spec(16, HD),
        ],
        out_shape=[
            shape((CHUNKS, NS, HD), BF16), shape((ROWS, HD), BF16), shape((ROWS, HD), BF16), shape((ROWS, HD), F32),
            shape((CHUNKS, NS, HD), F32), shape((NS + 16, HD), BF16), shape((16, HD), F32),
        ],
        scratch_shapes=[
            pltpu.VMEM((ROWS, HD), F32), pltpu.VMEM((ROWS, HD), F32), pltpu.VMEM((NS, HD), F32), pltpu.VMEM((NS, HD), F32),
            pltpu.VMEM((1, HD), F32), pltpu.VMEM((4, CHUNKS, 8, 128), F32), pltpu.VMEM((PAIRS // 2, 256, 256), BF16),
            pltpu.SemaphoreType.DMA((16,)), pltpu.SemaphoreType.DMA((16,)),
        ],
        compiler_params=comm_params(1, 60 << 20),
        name="forward",
    )(summs, xbc, near, cum, pos, fresh, gate, cot, W, gain, xbc, cum, pos, gate)


def add(a, b):
    return a.astype(F32) + b.astype(F32)


class Reduce:
    def __init__(self, flow, tag, bufs, halves):
        self.flow, self.tag, self.bufs = flow, tag, bufs
        G, K, RA, SA, TA, UA, VA, RB, SB, TB, UB, VB = bufs
        nA, nA1, nB, nB1 = halves
        self.A, self.B = pl.ds(0, nA), pl.ds(nA, nB)
        self.A1, self.A2 = pl.ds(0, nA1), pl.ds(nA1, nA - nA1)
        self.B1, self.B2 = pl.ds(0, nB1), pl.ds(nB1, nB - nB1)
        self.GB1, self.GB2 = pl.ds(nA, nB1), pl.ds(nA + nB1, nB - nB1)
        x, c, z, y = place()
        self.c, self.at = c, (x, z)
        xr, xl, xo = (x + 1) % 4, (x + 3) % 4, (x + 2) % 4
        zr, zl, zo = (z + 1) % 4, (z + 3) % 4, (z + 2) % 4
        self.xs, self.zs = (xr, xl, xo), (zr, zl, zo)
        dxr, dxl = device(xr, c, z, y), device(xl, c, z, y)
        dzr, dzl = device(x, c, zr, y), device(x, c, zl, y)
        A, B, A1, A2, B1, B2, GB1, GB2 = self.A, self.B, self.A1, self.A2, self.B1, self.B2, self.GB1, self.GB2

        def put(name, src, dst, to):
            flow.add(tag + name, src, dst, to)

        for k in range(4):
            put("k%d" % k, lambda k=k: G.at[k, 1 - c], lambda k=k: K.at[k], device(x, 1 - c, z, y))
        put("ra1", lambda: G.at[xo, c, :, :, A1], lambda: RA.at[:, :, A1], dxr)
        put("ra2", lambda: G.at[xo, c, :, :, A2], lambda: RA.at[:, :, A2], dxl)
        put("rb1", lambda: G.at[:, c, zo, :, GB1], lambda: RB.at[:, :, B1], dzr)
        put("rb2", lambda: G.at[:, c, zo, :, GB2], lambda: RB.at[:, :, B2], dzl)
        put("sar", lambda: G.at[xr, c, :, :, A], lambda: SA.at[0], dxr)
        put("sal", lambda: G.at[xl, c, :, :, A], lambda: SA.at[1], dxl)
        put("sbr", lambda: G.at[:, c, zr, :, B], lambda: SB.at[0], dzr)
        put("sbl", lambda: G.at[:, c, zl, :, B], lambda: SB.at[1], dzl)
        put("ta1", lambda: TA.at[zo, :, A1], lambda: UA.at[:, A1], dzr)
        put("ta2", lambda: TA.at[zo, :, A2], lambda: UA.at[:, A2], dzl)
        put("tb1", lambda: TB.at[xo, :, B1], lambda: UB.at[:, B1], dxr)
        put("tb2", lambda: TB.at[xo, :, B2], lambda: UB.at[:, B2], dxl)
        put("var", lambda: TA.at[zr], lambda: VA.at[0], dzr)
        put("val", lambda: TA.at[zl], lambda: VA.at[1], dzl)
        put("vbr", lambda: TB.at[xr], lambda: VB.at[0], dxr)
        put("vbl", lambda: TB.at[xl], lambda: VB.at[1], dxl)

    def start(self, *names):
        self.flow.start(*[self.tag + name for name in names])

    def wait(self, *names):
        self.flow.wait(*[self.tag + name for name in names])

    def cores(self, k):
        self.start("k%d" % k)

    def first(self):
        G, K = self.bufs[:2]
        for k in range(4):
            self.wait("k%d" % k)

        c, (xr, xl, xo), (zr, zl, zo), (x, z) = self.c, self.xs, self.zs, self.at
        A, B = self.A, self.B

        def join_a(k):
            def one(j, _):
                G[k, c, j, :, A] = add(G[k, c, j, :, A], K[k, j, :, A]).astype(BF16)
                return 0

            lax.fori_loop(0, 4, one, 0)

        def join_b(j):
            def one(k, _):
                G[k, c, j, :, B] = add(G[k, c, j, :, B], K[k, j, :, B]).astype(BF16)
                return 0

            lax.fori_loop(0, 4, one, 0)

        join_a(xo)
        self.start("ra1", "ra2")
        join_b(zo)
        self.start("rb1", "rb2")
        for k, j in ((xr, zr), (xl, zl), (x, z)):
            join_a(k)
            join_b(j)

    def second(self):
        G, K, RA, SA, TA, UA, VA, RB, SB, TB, UB, VB = self.bufs
        c, (xr, xl, _), (zr, zl, _) = self.c, self.xs, self.zs
        self.wait("ra1")
        G[xr, c, :, :, self.A1] = G[xr, c, :, :, self.A1] + RA[:, :, self.A1]
        self.start("sar")
        self.wait("rb1")
        G[:, c, zr, :, self.GB1] = G[:, c, zr, :, self.GB1] + RB[:, :, self.B1]
        self.start("sbr")
        self.wait("ra2")
        G[xl, c, :, :, self.A2] = G[xl, c, :, :, self.A2] + RA[:, :, self.A2]
        self.start("sal")
        self.wait("rb2")
        G[:, c, zl, :, self.GB2] = G[:, c, zl, :, self.GB2] + RB[:, :, self.B2]
        self.start("sbl")

    def third(self):
        G, K, RA, SA, TA, UA, VA, RB, SB, TB, UB, VB = self.bufs
        c, (x, z) = self.c, self.at
        self.wait("sar", "sal")
        TA[...] = (G[x, c, :, :, self.A].astype(F32) + add(SA[0], SA[1])).astype(BF16)
        self.start("ta1", "ta2")
        self.wait("sbr", "sbl")
        TB[...] = (G[:, c, z, :, self.B].astype(F32) + add(SB[0], SB[1])).astype(BF16)
        self.start("tb1", "tb2")

    def fourth(self):
        G, K, RA, SA, TA, UA, VA, RB, SB, TB, UB, VB = self.bufs
        (xr, xl, _), (zr, zl, _) = self.xs, self.zs
        self.wait("ta1")
        TA[zr, :, self.A1] = TA[zr, :, self.A1] + UA[:, self.A1]
        self.start("var")
        self.wait("ta2")
        TA[zl, :, self.A2] = TA[zl, :, self.A2] + UA[:, self.A2]
        self.start("val")
        self.wait("tb1")
        TB[xr, :, self.B1] = TB[xr, :, self.B1] + UB[:, self.B1]
        self.start("vbr")
        self.wait("tb2")
        TB[xl, :, self.B2] = TB[xl, :, self.B2] + UB[:, self.B2]
        self.start("vbl")

    def last(self, out_ref):
        G, K, RA, SA, TA, UA, VA, RB, SB, TB, UB, VB = self.bufs
        x, z = self.at
        self.wait("vbr", "vbl")
        out_ref[:, self.B] = TB[x].astype(F32) + add(VB[0], VB[1])
        self.wait("var", "val")
        out_ref[:, self.A] = TA[z].astype(F32) + add(VA[0], VA[1])


def reduce_bufs(halves):
    nA, nA1, nB, nB1 = halves

    def half(n):
        return [
            pltpu.VMEM((4, 48, n), BF16), pltpu.VMEM((2, 4, 48, n), BF16), pltpu.VMEM((4, 48, n), BF16),
            pltpu.VMEM((48, n), BF16), pltpu.VMEM((2, 48, n), BF16),
        ]

    return [pltpu.VMEM((4, 2, 4, 48, nA + nB), BF16), pltpu.VMEM((4, 4, 48, nA + nB), BF16)] + half(nA) + half(nB)


class RowSum:
    def __init__(self, flow, tag, N, M, Q):
        self.flow, self.tag, self.bufs = flow, tag, (N, M, Q)
        x, c, z, y = place()
        self.yr, self.yl, self.yo, self.y = (y + 1) % 4, (y + 3) % 4, (y + 2) % 4, y
        right, left = device(x, c, z, self.yr), device(x, c, z, self.yl)
        self.h1, self.h2 = pl.ds(0, 128), pl.ds(128, 128)
        flow.add(tag + "1", lambda: N.at[self.yo, self.h1], lambda: M.at[0], right)
        flow.add(tag + "2", lambda: N.at[self.yo, self.h2], lambda: M.at[1], left)
        flow.add(tag + "3", lambda: N.at[self.yr], lambda: Q.at[0], right)
        flow.add(tag + "4", lambda: N.at[self.yl], lambda: Q.at[1], left)

    def first(self):
        self.flow.start(self.tag + "1", self.tag + "2")

    def second(self):
        N, M, Q = self.bufs
        self.flow.wait(self.tag + "1")
        N[self.yr, self.h1] = N[self.yr, self.h1] + M[0]
        self.flow.start(self.tag + "3")
        self.flow.wait(self.tag + "2")
        N[self.yl, self.h2] = N[self.yl, self.h2] + M[1]
        self.flow.start(self.tag + "4")

    def last(self, out_ref):
        N, M, Q = self.bufs
        self.flow.wait(self.tag + "3", self.tag + "4")
        out_ref[...] = N[self.y].astype(F32) + add(Q[0], Q[1])


def row_bufs():
    return [pltpu.VMEM((4, 256, D), BF16), pltpu.VMEM((2, 128, D), BF16), pltpu.VMEM((2, 256, D), BF16)]


MID = (768, 384, 768, 384)
TAIL = (640, 384, 512, 256)
PRE = 4


def middle_kernel(
    gsumm_ref, w_ref, cot_ref, normed_ref, branch_ref, dgate_ref,
    xbc_ref, xdt_ref, dt_ref, cum_ref, sig_ref, dmix_ref, enter_ref, gfresh_ref, ds_ref, ci_ref, pos_ref,
    edge_ref, conv_ref, step_ref,
    din_ref, cgrad_ref, hgrad_ref, dedge_ref, gout_ref, share_ref,
    state, dacc, posn, picks, places, summ, edge_out, edge_in, *rest,
):
    bufs, (N, M, Q, ssem, rsem, lsem) = rest[:-6], rest[-6:]
    step = pl.program_id(0)
    steps = PRE + CHUNKS
    x, c, z, y = place()
    flow = Flow(ssem, rsem)
    reduce = Reduce(flow, "g", bufs, MID)
    rows = RowSum(flow, "n", N, M, Q)
    others_z = [device(x, c, (z + k) % 4, y) for k in (1, 3, 2)]
    for k in range(3):
        flow.add("s%d" % k, lambda: gsumm_ref, lambda: summ.at[z], others_z[k])
    flow.add("e", lambda: edge_out, lambda: edge_in, others_z[1])
    load_s = pltpu.make_async_copy(gsumm_ref, summ.at[z], lsem.at[1])

    @pl.when(step == 0)
    def _():
        load_s.start()
        enter(
            others_z
            + [device((x + 1) % 4, c, z, y), device((x + 3) % 4, c, z, y)]
            + [device(x, c, z, (y + 1) % 4), device(x, c, z, (y + 3) % 4), device(x, 1 - c, z, y)]
        )
        flow.start("s0", "s1", "s2")
        lanes, heads = iota((256, 128), 0), iota((256, 128), 1)
        fill_places(places)
        for q in range(PAIRS // 2):
            picks[q] = jnp.where(heads == 4 * q + lanes // 64, 1.0, 0.0).astype(BF16)

    for k in range(PRE):

        @pl.when(step == k)
        def _():
            block = (rows.yo, rows.yr, rows.yl, rows.y)[k]
            here = pl.ds(pl.multiple_of(block * 256, 256), 256)
            N[block] = dot_nt(branch_ref[here, :], w_ref[...]).astype(BF16)
            if k == 0:
                rows.first()
            G = bufs[0]
            out = dot(jnp.transpose(cot_ref[...]), branch_ref[...]).astype(BF16)
            gate = dot(jnp.transpose(normed_ref[...]), dgate_ref[...]).astype(BF16)
            G[k, :, :, :, 0:HD] = out.reshape(2, 4, 48, HD)
            G[k, :, :, :, HD : 2 * HD] = gate.reshape(2, 4, 48, HD)
            reduce.cores(k)

    @pl.when(step == PRE)
    def _():
        flow.wait("s0", "s1", "s2")
        load_s.wait()
        start = jnp.zeros((NS, HD), F32)
        for j in (3, 2, 1):
            link = link_of(summ, j)
            start = jnp.where(j > z, start * link + summ[j, 0:NS, :].astype(F32), start)
        state[...] = start
        dacc[LEN : LEN + 8, :] = jnp.zeros((8, CONV), F32)
        posn[LEN : LEN + 8, :] = jnp.zeros((8, 128), F32)
        cgrad_ref[...] = jnp.zeros_like(cgrad_ref)
        hgrad_ref[...] = jnp.zeros_like(hgrad_ref)
        reduce.first()

    @pl.when(step == PRE + 1)
    def _():
        rows.second()

    @pl.when(step == PRE + 2)
    def _():
        reduce.second()

    @pl.when(step == PRE + 5)
    def _():
        reduce.third()

    @pl.when(step == PRE + 6)
    def _():
        reduce.fourth()

    @pl.when(step > PRE)
    def _():
        dacc[LEN : LEN + 8, :] = dacc[0:8, :]
        posn[LEN : LEN + 8, :] = posn[0:8, :]

    @pl.when(step >= PRE)
    def _():
        back_chunk(
            xbc_ref, xdt_ref, dt_ref, cum_ref, sig_ref, dmix_ref, enter_ref, gfresh_ref, ds_ref, ci_ref, pos_ref,
            conv_ref, step_ref, din_ref, cgrad_ref, hgrad_ref, state, dacc, posn, picks, places,
        )

    @pl.when(step == steps - 1)
    def _():
        dacc[8:16, :] = dacc[0:8, :]
        dacc[0:8, :] = jnp.zeros((8, CONV), F32)
        posn[8:16, :] = posn[0:8, :]
        posn[0:8, :] = jnp.zeros((8, 128), F32)
        for j in range(CONV // 128):
            lanes = cols(j)
            ci = edge_ref[:, lanes].astype(F32)[8:16]
            d_in = jnp.zeros((8, 128), F32)
            for back in (1, 2, 3):
                moved = jnp.where(posn[back : back + 8, :] >= back, dacc[back : back + 8, lanes], 0.0)
                d_in = d_in + moved * conv_ref[3 - back : 4 - back, lanes]
                cgrad_ref[8 * (3 - back) : 8 * (3 - back) + 8, lanes] += moved * ci
            edge_out[:, lanes] = d_in
        flow.start("e")
        reduce.last(gout_ref)
        rows.last(share_ref)
        flow.wait("e")
        dedge_ref[...] = edge_in[...]
        flow.finish()


def back_chunk(
    xbc_ref, xdt_ref, dt_ref, cum_ref, sig_ref, dmix_ref, enter_ref, gfresh_ref, ds_ref, ci_ref, pos_ref,
    conv_ref, step_ref, din_ref, cgrad_ref, hgrad_ref, state, dacc, posn, picks, places,
):
    pos = pos_ref[...]
    posn[0:LEN, :] = pos
    row, lane = iota((LEN, LEN), 0), iota((LEN, LEN), 1)
    gap = (lane - row).astype(F32)
    keep = (gap >= 0) & (gap <= jnp.transpose(pos))
    cum, dt = cum_ref[...], dt_ref[...]
    cum_t = jnp.transpose(cum)
    last = cum[LEN - 1 : LEN]
    pos_last = pos[LEN - 1 : LEN]
    fade = jnp.where(pos > row.astype(F32), jnp.exp2(cum), 0.0)
    ends = jnp.where((LEN - 1) - row.astype(F32) <= pos_last, jnp.exp2(last - cum), 0.0)
    whole = jnp.where(pos_last > LEN - 1, jnp.exp2(last), 0.0)
    basis = xbc_ref[:, HD : HD + NS]
    basis_c = xbc_ref[:, HD + NS : CONV]
    inner = dot_nt(basis, basis_c)
    inner2 = jnp.concatenate([inner, inner], axis=1)
    d_inner = jnp.zeros((LEN, LEN), F32)
    d_b = jnp.zeros((LEN, NS), F32)
    d_c = jnp.zeros((LEN, NS), F32)
    into = jnp.zeros((LEN, 128), F32)
    by_head = jnp.zeros((3 * LEN, 128), F32)
    across = jnp.zeros((8, 128), F32)
    sums_t = []
    spread = Spread(places, ends, fade, dt)
    for p in range(PAIRS):
        lanes = cols(p)
        xs = xbc_ref[:, lanes].astype(F32)
        xdt = xdt_ref[:, lanes]
        dy_wide = dmix_ref[:, lanes]
        dy, dy_low = in_two(dy_wide)
        entered = enter_ref[0, :, lanes]
        after = state[:, lanes]
        after_low = after.astype(BF16)
        dys = stacked(dy)
        spans = []
        for h in (2 * p, 2 * p + 1):
            spans.append(jnp.where(keep, cum_t[h : h + 1, :] - cum[:, h : h + 1], -1e30))
        decays = jnp.exp2(jnp.concatenate(spans, axis=1))
        scores = (decays * inner2).astype(BF16)
        d_scores = dot_nt(twice(xdt), jnp.concatenate([dys, stacked(dy_low)], axis=1)) * decays
        d_inner = d_inner + d_scores[:, :LEN] + d_scores[:, LEN:]
        prod = d_scores * inner2
        sums_t.append(jnp.sum(prod[:, :LEN], axis=0, keepdims=True))
        sums_t.append(jnp.sum(prod[:, LEN:], axis=0, keepdims=True))
        end_pair, fade_pair, dt_pair = spread(p)
        z_state = dot(basis, after_low) * end_pair
        z = dot(scores, dys) + z_state
        first = jnp.sum(prod[:, :LEN], axis=1, keepdims=True)
        second = jnp.sum(prod[:, LEN:], axis=1, keepdims=True)
        into = into + jnp.where(lane == 2 * p, first, jnp.where(lane == 2 * p + 1, second, 0.0))
        products = [
            (xs * z).astype(BF16),
            (xdt.astype(F32) * z_state).astype(BF16),
            (dy_wide * dot(basis_c, entered) * fade_pair).astype(BF16),
        ]
        products.append(fold8(after * entered.astype(F32)).astype(BF16))
        if p % 2 == 0:
            before = products
        else:
            two = [jnp.concatenate(both, axis=1) for both in zip(before, products)]
            by_head = by_head + dot(jnp.concatenate(two[:3], axis=0), picks[p // 2])
            across = across + dot(two[3], picks[p // 2])
        d_x = dt_pair * z + spread_heads(step_ref[...], p)[3:4] * dy_wide
        dacc[0:LEN, lanes] = d_x * ds_ref[:, lanes]
        d_b = d_b + dot_nt(jnp.concatenate(in_two(xdt.astype(F32) * end_pair), axis=1), twice(after_low))
        d_c = d_c + dot_nt(jnp.concatenate(in_two(dy_wide * fade_pair), axis=1), twice(entered))
        state[:, lanes] = after * spread_heads(whole, p) + gfresh_ref[0, :, lanes]
    low = d_inner.astype(BF16)
    d_b = d_b + dot(low, basis_c)
    d_c = d_c + dot_tn(low, basis)
    dacc[0:LEN, HD : HD + NS] = d_b * ds_ref[:, HD : HD + NS]
    dacc[0:LEN, HD + NS : CONV] = d_c * ds_ref[:, HD + NS : CONV]
    direct, later, carry = by_head[:LEN], by_head[LEN : 2 * LEN], by_head[2 * LEN :]
    out_of = jnp.transpose(jnp.concatenate(sums_t + [jnp.zeros((128 - HEADS, LEN), F32)], axis=0))
    d_rate = (
        ordered(("suffix", out_of - into + carry), ("strict", later))
        + whole * jnp.sum(across, axis=0, keepdims=True)
    )
    d_step = (direct + d_rate * step_ref[2:3, :]) * sig_ref[...]
    hgrad_ref[0:8, :] += fold8(d_rate * dt)
    hgrad_ref[8:16, :] += fold8(d_step)
    din_ref[:, CONV : CONV + 128] = d_step.astype(BF16)

    within = [posn[back : back + LEN, :] >= back for back in (1, 2, 3)]
    for j in range(CONV // 128):
        lanes = cols(j)
        here = dacc[0:LEN, lanes]
        ci = ci_ref[:, lanes].astype(F32)
        d_in = here * conv_ref[3:4, lanes]
        cgrad_ref[24:32, lanes] += fold8(here * ci)
        cgrad_ref[32:40, lanes] += fold8(here)
        for back in (1, 2, 3):
            moved = jnp.where(within[back - 1], dacc[back : back + LEN, lanes], 0.0)
            d_in = d_in + moved * conv_ref[3 - back : 4 - back, lanes]
            cgrad_ref[8 * (3 - back) : 8 * (3 - back) + 8, lanes] += fold8(moved * ci)
        din_ref[:, lanes] = d_in.astype(BF16)


def middle(
    gsumm, W, cot, normed, branch, dgate, xbc, xdt, dt, cum, sig, dmix, entered, gfresh, ds, ci, pos, edge, conv, step
):
    top = CHUNKS - 1

    def chunk(i):
        return jnp.minimum(top + PRE - i, top)

    def rows(c):
        return pl.BlockSpec((LEN, c), lambda i: (chunk(i), 0))

    def tiles():
        return pl.BlockSpec((ROWS, D // PRE), lambda i: (0, jnp.minimum(i, PRE - 1)))

    state = pl.BlockSpec((1, NS, HD), lambda i: (chunk(i), 0, 0))
    anywhere = pl.BlockSpec(memory_space=ANY)
    return pl.pallas_call(
        middle_kernel,
        grid=(PRE + CHUNKS,),
        in_specs=[
            anywhere, whole_spec(D, HD), tiles(), tiles(), whole_spec(ROWS, HD), whole_spec(ROWS, HD),
            rows(CONV), rows(HD), rows(128), rows(128), rows(128), rows(HD), state, state, rows(CONV), rows(CONV), rows(128),
            whole_spec(16, CONV), whole_spec(8, CONV), whole_spec(8, 128),
        ],
        out_specs=[
            rows(CONV + 128), whole_spec(40, CONV), whole_spec(16, 128), whole_spec(8, CONV), whole_spec(48, 2 * HD),
            whole_spec(256, D),
        ],
        out_shape=[
            shape((ROWS, CONV + 128), BF16), shape((40, CONV), F32), shape((16, 128), F32), shape((8, CONV), F32),
            shape((48, 2 * HD), F32), shape((256, D), F32),
        ],
        scratch_shapes=[
            pltpu.VMEM((NS, HD), F32), pltpu.VMEM((LEN + 8, CONV), F32), pltpu.VMEM((LEN + 8, 128), F32),
            pltpu.VMEM((PAIRS // 2, 256, 128), BF16), pltpu.VMEM((PAIRS // 2, 256, 256), BF16),
            pltpu.VMEM((4, NS + 16, HD), BF16), pltpu.VMEM((8, CONV), F32), pltpu.VMEM((8, CONV), F32),
        ] + reduce_bufs(MID) + row_bufs() + sems(32),
        compiler_params=comm_params(3, 60 << 20),
        cost_estimate=pl.CostEstimate(flops=40 * ROWS * HD * 128, bytes_accessed=30 << 20, transcendentals=2 * ROWS * CONV),
        name="middle",
    )(gsumm, W, cot, normed, branch, dgate, xbc, xdt, dt, cum, sig, dmix, entered, gfresh, ds, ci, pos, edge, conv, step)


def tail_kernel(
    dgate_ref, din_ref, w_ref, x_ref, normed_ref, edge_ref, cgrad_ref, tgrad_ref, hgrad_ref,
    gout_ref, share_ref, ysum_ref, plane_ref, every_ref,
    dgate, din, w, xs, normed, grads, small, HZ, HX, HC, HY, Y, *rest,
):
    bufs, (N, M, Q, ssem, rsem, lsem) = rest[:-6], rest[-6:]
    x, c, z, y = place()
    xs_other = [device((x + k) % 4, c, z, y) for k in (1, 3, 2)]
    zs_other = [device(x, c, (z + k) % 4, y) for k in (1, 3, 2)]
    ys_other = [device(x, c, z, (y + k) % 4) for k in (1, 3, 2)]
    core = device(x, 1 - c, z, y)
    loads = [
        pltpu.make_async_copy(src, dst, lsem.at[k])
        for k, (src, dst) in enumerate(
            [(w_ref.at[:, C_GATE:WIDE], w), (dgate_ref, dgate), (din_ref, din), (x_ref, xs), (normed_ref, normed)]
        )
    ]
    for load in loads:
        load.start()
    enter(xs_other + zs_other + ys_other + [core])
    flow = Flow(ssem, rsem)
    reduce = Reduce(flow, "g", bufs, TAIL)
    rows = RowSum(flow, "n", N, M, Q)
    for k in range(3):
        flow.add("hz%d" % k, lambda: HZ.at[z], lambda: HZ.at[z], zs_other[k])
        flow.add("hx%d" % k, lambda: HX.at[x], lambda: HX.at[x], xs_other[k])
        flow.add("hy%d" % k, lambda: HY.at[y], lambda: HY.at[y], ys_other[k])
        flow.add("y%d" % k, lambda: Y.at[y], lambda: Y.at[y], ys_other[k])
    flow.add("hc", lambda: HC.at[c], lambda: HC.at[c], core)

    for load in loads[:3]:
        load.wait()
    end = din[ROWS - 16 : ROWS, 0:CONV].astype(F32)
    more = jnp.concatenate([jnp.zeros((8, CONV), F32), edge_ref[...]], axis=0)
    din[ROWS - 16 : ROWS, 0:CONV] = (end + more).astype(BF16)

    G = bufs[0]
    gains = []
    blocks = (rows.yo, rows.yr, rows.yl, rows.y)

    def row_block(block):
        here = pl.ds(pl.multiple_of(block * 256, 256), 256)
        grad = dot_nt(dgate[here, :], w[:, 0:HD]) + dot_nt(din[here, :], w[:, HD : WIDE - C_GATE])
        N[block] = grad.astype(BF16)
        grads[here, :] = grad

    def gain_part(block):
        here = pl.ds(pl.multiple_of(block * 256, 256), 256)
        wide = xs[here, :].astype(F32)
        r = lax.rsqrt(jnp.mean(wide * wide, axis=1, keepdims=True) + EPS)
        gains.append(fold8(grads[here, :] * wide * r))

    row_block(rows.yo)
    rows.first()
    loads[4].wait()
    for k in range(4):
        part = dot(jnp.transpose(normed[:, 384 * k : 384 * k + 384]), din[...]).astype(BF16)
        G[k] = part.reshape(2, 4, 48, CONV + 128)
        reduce.cores(k)
    row_block(rows.yr)
    reduce.first()
    row_block(rows.yl)
    rows.second()
    reduce.second()
    row_block(rows.y)
    loads[3].wait()
    for block in blocks:
        gain_part(block)
    for k in range(40):
        j = k % 8
        small[k : k + 1, :] = jnp.sum(cgrad_ref[8 * (k // 8) : 8 * (k // 8) + 8, cols(j)], axis=0, keepdims=True)
    for j in range(6):
        small[40 + j : 41 + j, :] = jnp.sum(tgrad_ref[0:8, cols(j)], axis=0, keepdims=True)
        small[58 + j : 59 + j, :] = jnp.sum(tgrad_ref[8:16, cols(j)], axis=0, keepdims=True)
    small[64:65, :] = jnp.sum(hgrad_ref[0:8, :], axis=0, keepdims=True)
    small[65:66, :] = jnp.sum(hgrad_ref[8:16, :], axis=0, keepdims=True)
    small[66:72, :] = jnp.zeros((6, 128), F32)

    gains = jnp.sum(gains[0] + gains[1] + gains[2] + gains[3], axis=0, keepdims=True)
    for j in range(12):
        small[46 + j : 47 + j, :] = gains[:, cols(j)]
    HZ[z] = small[...]
    flow.start("hz0", "hz1", "hz2")
    reduce.third()
    flow.wait("hz0", "hz1", "hz2")
    HX[x] = HZ[0] + HZ[1] + HZ[2] + HZ[3]
    flow.start("hx0", "hx1", "hx2")
    reduce.fourth()
    flow.wait("hx0", "hx1", "hx2")
    HC[c] = HX[0] + HX[1] + HX[2] + HX[3]
    flow.start("hc")
    reduce.last(gout_ref)
    Y[y] = gout_ref[:, HD:CONV]
    flow.start("y0", "y1", "y2")
    flow.wait("hc")
    total = HC[0] + HC[1]
    HY[y] = total
    plane_ref[...] = total
    flow.start("hy0", "hy1", "hy2")
    rows.last(share_ref)
    flow.wait("y0", "y1", "y2")
    ysum_ref[...] = Y[0] + Y[1] + Y[2] + Y[3]
    flow.wait("hy0", "hy1", "hy2")
    every_ref[...] = HY[0] + HY[1] + HY[2] + HY[3]
    flow.finish()


def tail(dgate, din, W, X, normed, edge, cgrad, tgrad, hgrad):
    vmem = pl.BlockSpec(memory_space=pltpu.VMEM)
    table = pltpu.VMEM((4, 72, 128), F32)
    return pl.pallas_call(
        tail_kernel,
        out_shape=(
            shape((48, CONV + 128), F32), shape((256, D), F32), shape((48, 2 * NS), F32), shape((72, 128), F32),
            shape((72, 128), F32),
        ),
        in_specs=[pl.BlockSpec(memory_space=ANY)] * 5 + [vmem] * 4,
        out_specs=[vmem] * 5,
        scratch_shapes=[
            pltpu.VMEM((ROWS, HD), BF16), pltpu.VMEM((ROWS, CONV + 128), BF16), pltpu.VMEM((D, WIDE - C_GATE), BF16),
            pltpu.VMEM((ROWS, D), BF16), pltpu.VMEM((ROWS, D), BF16), pltpu.VMEM((ROWS, D), F32), pltpu.VMEM((72, 128), F32),
            table, table, pltpu.VMEM((2, 72, 128), F32), table, pltpu.VMEM((4, 48, 2 * NS), F32),
        ] + reduce_bufs(TAIL) + row_bufs() + [
            pltpu.SemaphoreType.DMA((48,)), pltpu.SemaphoreType.DMA((48,)), pltpu.SemaphoreType.DMA((8,)),
        ],
        compiler_params=comm_params(5, 60 << 20),
        name="tail",
    )(dgate, din, W, X, normed, edge, cgrad, tgrad, hgrad)


def finish_kernel(
    x_ref, cot_ref, out_ref, share_ref, gain_ref, mid_ref, tail_ref, ysum_ref, plane_ref, every_ref, step_ref,
    lout_ref, grad_ref, ngain_ref, gate_ref, in_ref, ps_ref, bc_ref, ci_ref, cb_ref, cs_ref, csb_ref, dec_ref, sb_ref,
    skip_ref, gg_ref, wout_ref,
):
    own = x_ref[...].astype(F32)
    lout_ref[...] = (own + out_ref[...]).astype(BF16)
    scale = lax.rsqrt(jnp.mean(own * own, axis=1, keepdims=True) + EPS)
    weighted = share_ref[...] * gain_ref[...]
    slope = scale * scale * scale * jnp.mean(own * weighted, axis=1, keepdims=True)
    grad_ref[...] = scale * weighted - own * slope + cot_ref[...].astype(F32)

    @pl.when(pl.program_id(0) == 0)
    def _():
        x, c, z, y = place()
        block = (((x * 2 + c) * 4) + z).astype(F32)
        tp = y.astype(F32)
        gate_ref[...] = mid_ref[:, HD : 2 * HD]
        in_ref[...] = tail_ref[:, 0:HD]
        wout_ref[...] = mid_ref[:, 0:HD]
        steps = jnp.concatenate([tail_ref[:, CONV : CONV + 128], jnp.zeros((80, 128), F32)], axis=0)
        ps_ref[...] = jnp.transpose(steps)[0:HEADS, 0:48]

        def one(keep):
            return jnp.where(keep, 1.0, 0.0).astype(F32)

        def full_nt(a, b):
            return lax.dot_general(a, b, (((1,), (1,)), ((), ())), precision=HIGH, preferred_element_type=F32)

        bc_ref[...] = dot_full(one(fiota((16, 48), 1) == fiota((16, 48), 0) + 12 * tp), ysum_ref[...])[0:12]
        plane, every = plane_ref[...], every_ref[...]
        lane, row = fiota((8, 128), 1), fiota((8, 128), 0)
        source, head = fiota((72, 128), 0), fiota((72, 128), 1)
        half, odd = parts(head, 2)
        picked = [full_nt(one(lane == 64 * q + 2 * block + row), plane) for q in (0, 1)]
        sums = [full_nt(one((lane >= 64 * q) & (lane < 64 * q + 64)), plane) for q in (0, 1)]

        def heads_of(first, rows):
            total = jnp.zeros((8, 128), F32)
            for q in (0, 1):
                total = total + dot_full(rows[q], one((source == first + half) & (odd == q)))
            return total

        for k in range(4):
            ci_ref[k] = heads_of(8 * k, picked)[0:2, 0:HEADS]
        cb_ref[...] = heads_of(32, picked)[0:2, 0:HEADS]
        gg_ref[...] = heads_of(40, picked)[0:2, 0:HEADS]
        skip_ref[...] = heads_of(58, sums)[0:1, 0:HEADS]
        dec_ref[...] = plane[64:65, 0:HEADS] * step_ref[2:3, 0:HEADS]
        sb_ref[...] = plane[65:66, 0:HEADS]
        at = 8 * block + 2 * tp
        upper, at = parts(at, 128)
        by_tap = full_nt(one(lane == at + row), every)
        cs_ref[...] = dot_full(by_tap, one(source == 8 * head + 6 + upper))[0:2, 0:4]
        rows8 = dot_full(one((fiota((8, 72), 1) == 8 * fiota((8, 72), 0) + 6 + upper)), every)
        csb_ref[...] = full_nt(rows8, one(fiota((128, 128), 1) == at + fiota((128, 128), 0)))[4:5, 0:2]
        flat = 48 * block + 12 * tp + head
        line, spot = parts(flat, 128)
        spread = full_nt(every, one(fiota((128, 128), 1) == spot[0:1].reshape(1, 128).T))
        ngain_ref[...] = jnp.sum(jnp.where(source == 46 + line, spread, 0.0), axis=0, keepdims=True)[:, 0:12]


def finish(*args):
    outs = [
        ((256, D), BF16), ((256, D), F32), ((1, 12), F32), ((48, HD), F32), ((48, HD), F32), ((HEADS, 48), F32),
        ((12, 2 * NS), F32), ((4, 2, HEADS), F32), ((2, HEADS), F32), ((2, 4), F32), ((1, 2), F32), ((1, HEADS), F32),
        ((1, HEADS), F32), ((1, HEADS), F32), ((2, HEADS), F32), ((48, HD), F32),
    ]
    return pl.pallas_call(
        finish_kernel,
        grid=(1,),
        out_shape=[shape(*o) for o in outs],
        in_specs=[rows_spec(256, D)] * 4 + [whole_spec(*a.shape) for a in args[4:]],
        out_specs=[rows_spec(256, D)] * 2 + [whole_spec(*o[0]) for o in outs[2:]],
        compiler_params=pltpu.CompilerParams(vmem_limit_bytes=60 << 20),
        name="finish",
    )(*args)


def per_device(
    layer_input, out_cotangent, seq_lengths, norm_gain, proj_gate, proj_input, proj_step, proj_state, conv_inner,
    conv_inner_bias, conv_state, conv_state_bias, decay_log, step_bias, skip_scale, gate_gain, proj_out,
):
    (
        W, X, cots, normed, gate, ci, ds, xbc, xdt, dt, cum, sig, fresh, pos, near, summs, edge, conv, ngain, gain, step,
    ) = front(
        (layer_input, out_cotangent, proj_out.T, proj_gate, proj_input, proj_state),
        seq_lengths,
        (
            proj_step.T, conv_inner.transpose(0, 2, 1), conv_inner_bias.T, gate_gain.T, conv_state, conv_state_bias[None],
            norm_gain[None], decay_log[None], step_bias[None], skip_scale[None],
        ),
    )
    W, X, cot_all = W.reshape(D, WIDE), X.reshape(ROWS, D), cots.reshape(ROWS, D)
    entered, branch, dgate, dmix, gfresh, gsumm, tgrad = forward(
        summs, xbc, near, cum, pos, fresh, gate, cot_all, W, gain
    )
    din, cgrad, hgrad, dedge, gmid, out_share = middle(
        gsumm, W, cot_all, normed, branch, dgate,
        xbc, xdt, dt, cum, sig, dmix, entered, gfresh, ds, ci, pos, edge, conv, step,
    )
    gtail, share, ysum, plane, every = tail(dgate, din, W, X, normed, dedge, cgrad, tgrad, hgrad)
    (
        layer_output, input_grad, g_norm, g_gate, g_in, g_step, g_state, g_conv, g_bias, g_cs, g_csb, g_decay, g_sb, g_skip,
        g_gain, g_out,
    ) = finish(layer_input, out_cotangent, out_share, share, ngain, gmid, gtail, ysum, plane, every, step)
    return (
        layer_output, input_grad, g_norm[0], g_gate, g_in, g_step.T, g_state, g_conv.transpose(0, 2, 1), g_bias.T, g_cs.T,
        g_csb[0], g_decay[0], g_sb[0], g_skip[0], g_gain.T, g_out.T,
    )


def solution(mesh):
    both = ("shard", "ctx")
    every = ("shard", "ctx", "tp")
    return jax.shard_map(
        per_device,
        mesh=mesh,
        in_specs=(
            P(every, None), P(every, None), P("shard", None), P(both), P(both, "tp"), P(both, "tp"), P(both, "tp"),
            P(both, None), P(None, "tp", both), P("tp", both), P(None, both), P(both), P("tp"), P("tp"), P("tp"),
            P("tp", both), P("tp", both),
        ),
        out_specs=(
            P(every, None), P(every, None), P(every), P(both, "tp"), P(both, "tp"), P(both, "tp"), P(every, None),
            P(None, "tp", both), P("tp", both), P(None, every), P(every), P("tp"), P("tp"), P("tp"), P("tp", both),
            P("tp", both),
        ),
        check_vma=False,
    )
```
